32 devices in a mesh: dp: 16 (over z, y, core), ctx: 2 (over x).
Axes of the slice: x: 2, y: 2, z: 4, core: 2. Of those that a mesh axis runs over, the one named last changes fastest.
Arguments:
- block_input: bfloat16 [48, 512, 1024], P('dp', 'ctx'), may hold values from -6 to 6
- lengths: int32 [48], P('dp'), may hold values from 1 to 512, as said below
- mask: int32 [48, 512], P('dp', 'ctx'), may hold values 0 or 1
- blocks: int32 [48, 512], P('dp', 'ctx'), may hold values from 0 to 22, never falling along the last dimension, each value on 1 to 25 neighbouring positions
- timesteps: int32 [48], P('dp'), may hold values from 0 to 4999
- w_qkv: bfloat16 [1024, 3072], P(('dp', 'ctx')), may hold values from -0.1875 to 0.1875
- w_o: bfloat16 [1024, 1024], P(('dp', 'ctx')), may hold values from -1.5 to 1.5
- w_in: bfloat16 [1024, 4096], P(('dp', 'ctx')), may hold values from -0.1875 to 0.1875
- w_out: bfloat16 [4096, 1024], P(('dp', 'ctx')), may hold values from -0.09375 to 0.09375
- b_in: bfloat16 [4096], P(('dp', 'ctx')), may hold values from -3 to 3
- biases: bfloat16 [4, 1024], P(None, ('dp', 'ctx')), may hold values from -3 to 3
- gains: bfloat16 [2, 1024], P(None, ('dp', 'ctx')), may hold values from 0.5 to 1.5
- shifts: bfloat16 [2, 1024], P(None, ('dp', 'ctx')), may hold values from -2 to 2
- cotangent: bfloat16 [48, 512, 1024], P('dp', 'ctx'), may hold values from -6 to 6
Outputs:
- output: bfloat16 [48, 512, 1024], P('dp', 'ctx')
- input_grad: bfloat16 [48, 512, 1024], P('dp', 'ctx')
- grad_w_qkv: float32 [1024, 3072], P(('dp', 'ctx'))
- grad_w_o: float32 [1024, 1024], P(('dp', 'ctx'))
- grad_w_in: float32 [1024, 4096], P(('dp', 'ctx'))
- grad_w_out: float32 [4096, 1024], P(('dp', 'ctx'))
- grad_b_in: float32 [4096], P(('dp', 'ctx'))
- grad_biases: float32 [4, 1024], P(None, ('dp', 'ctx'))
- grad_gains: float32 [2, 1024], P(None, ('dp', 'ctx'))
- grad_shifts: float32 [2, 1024], P(None, ('dp', 'ctx'))
- rms: float32 [4], replicated
The draws below stay inside these ranges and needn't reach their ends.
Inputs may be any that keep to these rules, and one draw needn't show every extreme that they name: `lengths`: in every aligned group of 3 items one item has length 512.
All inputs are finite; a program needn't handle non-finite values. No bound on the sum of `mask` on one device may be relied on, other than what follows from the above.
Results may differ from the reference program's by a relative error of at most 0.018.
Values may be sent and summed in bfloat16 or wider, within the bound.
A program may use at most 192 MiB of HBM per device.

```python
import math
import jax
import jax.numpy as jnp
import numpy as np
from jax import lax

D = 1024
HEADS = 16
HD = 64
FF = 4096
LEN = 512
BLK = 25
TSTEPS = 5000
ITEMS_DEV = 3
ITEMS = 48


def draw_block_input(key, part):
    key = jax.random.fold_in(key, 11)
    ramp = 0.6 + 0.9 * jnp.arange(ITEMS, dtype=jnp.float32) / max(ITEMS - 1, 1)
    base = jnp.clip(jax.random.normal(key, (ITEMS, LEN, D), jnp.float32), -4.0, 4.0)
    return (base * ramp[:, None, None]).astype(jnp.bfloat16)


def draw_lengths(key, part):
    key = jax.random.fold_in(key, 23)
    first, second = jax.random.split(key)
    drawn = jax.random.randint(first, (ITEMS,), LEN // 4, LEN + 1, dtype=jnp.int32)
    chosen = jax.random.randint(second, (ITEMS // ITEMS_DEV,), 0, ITEMS_DEV, dtype=jnp.int32)
    index = jnp.arange(ITEMS, dtype=jnp.int32)
    full = index % ITEMS_DEV == jnp.repeat(chosen, ITEMS_DEV)
    return jnp.where(full, LEN, drawn).astype(jnp.int32)


def set_ends(values, key, smallest, top_value):
    place = [jax.random.randint(jax.random.fold_in(key, axis), (), 0, length) for axis, length in enumerate(values.shape)]
    longest = values.shape.index(max(values.shape))
    beside = place[:longest] + [(place[longest] + 1) % values.shape[longest]] + place[longest + 1:]
    return values.at[tuple(place)].set(smallest).at[tuple(beside)].set(top_value)


def levels(own_key, dims, shards, low, largest):
    level, own = 1.0, jax.random.fold_in(own_key, 6)
    for position, blocks in shards:
        draws = jnp.exp(jax.random.uniform(jax.random.fold_in(own, position), (blocks,), jnp.float32, low / len(shards), largest / len(shards)))
        level = level * jnp.repeat(draws, dims[position] // blocks).reshape([-1 if axis == position else 1 for axis in range(len(dims))])
    return level


def profile(number_of, total, most, slope):
    weights = [(1 << 20) // math.isqrt(rank ** slope) + 1 for rank in range(2, number_of + 1)]
    surplus, given = total - most - (number_of - 1), [1] * (number_of - 1)
    while surplus > 0:
        candidates = [i for i in range(number_of - 1) if given[i] < most]
        whole, remaining = sum([weights[i] for i in candidates]), surplus
        for i in candidates:
            extra = min(most - given[i], max(1, remaining * weights[i] // whole), surplus)
            given[i] = given[i] + extra
            surplus = surplus - extra
    return np.array([most] + given)


def uneven(rng, count, total, most, lean):
    if count == 2:
        one = jax.random.randint(rng, (), max(1, total - most), min(most, total - 1) + 1)
        return jnp.stack([one, total - one])
    sizes = jnp.asarray(profile(count, total, most, lean), jnp.int32)
    pairs = (count - 1) // 2
    giver, receiver = sizes[1:1 + 2 * pairs:2], sizes[2:2 + 2 * pairs:2]
    slack = jnp.minimum(giver - 1, most - receiver)
    moved = jax.random.randint(jax.random.fold_in(rng, 1), (pairs,), 0, 1 << 20) % (slack + 1)
    sizes = sizes.at[1:1 + 2 * pairs:2].set(giver - moved).at[2:2 + 2 * pairs:2].set(receiver + moved)
    return sizes[jax.random.permutation(jax.random.fold_in(rng, 2), count)]


def normal_values(stream_key, dims, scale, reach, shards=(), held_as=jnp.bfloat16):
    values = scale * jax.random.normal(stream_key, dims, jnp.float32)
    if shards:
        values = values * levels(stream_key, dims, shards, -0.22, 0.18)
    return jnp.clip(values, -reach, reach).astype(held_as)


def setup_inputs(seed: int = 0) -> dict:
    key_list = jax.random.split(jax.random.key(seed), 15)
    block_input = draw_block_input(jax.random.fold_in(key_list[14], 71), 0)
    lengths = draw_lengths(jax.random.fold_in(key_list[14], 71), 0)
    mask = set_ends((jax.random.randint(key_list[2], (ITEMS, LEN), 0, 8) < 7).astype(jnp.int32), jax.random.fold_in(key_list[2], 1), 0, 1)
    blocks = jax.vmap(lambda own: jnp.searchsorted(jnp.cumsum(uneven(own, (LEN + BLK - 1) // BLK + 2, LEN, BLK, 0)), jnp.arange(LEN), side="right"))(jax.random.split(key_list[3], ITEMS)).reshape((ITEMS, LEN)).astype(jnp.int32)
    timesteps = set_ends(jax.random.randint(key_list[4], (ITEMS,), 0, TSTEPS), jax.random.fold_in(key_list[4], 1), 0, TSTEPS - 1).astype(jnp.int32)
    w_qkv = normal_values(key_list[5], (D, 3 * D), D ** -0.5, 0.1875, ((0, 32),))
    w_o = normal_values(key_list[6], (D, D), (D // 64) ** -0.5, 1.5, ((0, 32),))
    w_in = normal_values(key_list[7], (D, FF), D ** -0.5, 0.1875, ((0, 32),))
    w_out = normal_values(key_list[8], (FF, D), FF ** -0.5, 0.09375, ((0, 32),))
    b_in = normal_values(key_list[9], (FF,), 0.5, 3.0, ((0, 32),))
    biases = normal_values(key_list[10], (4, D), 0.5, 3.0, ((1, 32),))
    gains = jnp.clip(1.0 + 0.1 * jax.random.normal(key_list[11], (2, D), jnp.float32), 0.5, 1.5).astype(jnp.bfloat16)
    shifts = normal_values(key_list[12], (2, D), 0.3, 2.0, ((1, 32),))
    cotangent = normal_values(key_list[13], (ITEMS, LEN, D), 1.0, 6.0, ((0, 16), (1, 2)))
    return {"block_input": block_input, "lengths": lengths, "mask": mask, "blocks": blocks, "timesteps": timesteps, "w_qkv": w_qkv, "w_o": w_o, "w_in": w_in, "w_out": w_out, "b_in": b_in, "biases": biases, "gains": gains, "shifts": shifts, "cotangent": cotangent}


@jax.custom_vjp
def low(v):
    return lax.optimization_barrier(v.astype(jnp.bfloat16)).astype(jnp.float32)

@jax.custom_vjp
def low_back(v):
    return v

def low_keep(v):
    return (low(v), None)

def low_pass(kept, grad):
    return (grad,)

def back_keep(v):
    return (v, None)

def back_low(kept, grad):
    return (low(grad),)
low.defvjp(low_keep, low_pass)
low_back.defvjp(back_keep, back_low)
fill_value = -1e+30
eps_norm = 1e-05

def time_embed(steps, width):
    half = width // 2
    freqs = jnp.exp(jnp.arange(half, dtype=jnp.float32) * (-math.log(10000.0) / half))
    angle = steps.astype(jnp.float32)[:, None] * freqs[None, :]
    return jnp.concatenate([jnp.sin(angle), jnp.cos(angle)], axis=-1)

def layer_norm(resid, gain, shift):
    centre = resid - lax.optimization_barrier(jnp.mean(resid, axis=-1, keepdims=True))
    spread = lax.optimization_barrier(jnp.mean(centre * centre, axis=-1, keepdims=True))
    return centre * lax.rsqrt(spread + eps_norm) * gain + shift

def project(left, weight):
    return jnp.einsum('gtd,de->gte', left, weight, precision=lax.Precision.HIGHEST)

def block_forward(params, stream, allowed, row_weight):
    w_qkv, w_o, w_in, w_out, b_in, biases, gains, shifts = params
    groups = stream.shape[0]
    stream_low = low(stream)
    joint = project(stream_low, w_qkv)
    query = low(low_back(joint[..., :D] + biases[0]))
    keys = low(low_back(joint[..., D:2 * D]))
    values = low(low_back(joint[..., 2 * D:] + biases[1]))
    shape_four = (groups, LEN, HEADS, HD)
    scores = jnp.einsum('gqhd,gkhd->ghqk', query.reshape(shape_four), keys.reshape(shape_four), precision=lax.Precision.HIGHEST) * (1.0 / math.sqrt(HD))
    scores = low_back(scores)
    scores = jnp.where(allowed[:, None] == 1, scores, fill_value)
    probs = jax.nn.softmax(scores, axis=-1)
    mixed = jnp.einsum('ghqk,gkhd->gqhd', low(probs), values.reshape(shape_four), precision=lax.Precision.HIGHEST)
    mixed = low(low_back(mixed.reshape(groups, LEN, D)))
    attn = low_back(project(mixed, w_o) + biases[2])
    hidden_one = layer_norm(stream + attn, gains[0], shifts[0])
    pre = low_back(project(low(hidden_one), w_in) + b_in)
    act = low(jax.nn.gelu(pre, approximate=False))
    branch = low_back(project(act, w_out) + biases[3])
    result = layer_norm(hidden_one + branch, gains[1], shifts[1])
    squares = jnp.stack([jnp.sum(row_weight * lax.optimization_barrier(jnp.sum(tensor * tensor, axis=-1))) for tensor in (stream, attn, branch, result)])
    return (result, squares)

def reference(block_input, lengths, mask, blocks, timesteps, w_qkv, w_o, w_in, w_out, b_in, biases, gains, shifts, cotangent):
    positions = jnp.arange(LEN, dtype=jnp.int32)
    valid = ((positions[None, :] < lengths[:, None]) & ((mask == 1) | (positions[None, :] == 0))).astype(jnp.int32)
    allowed = ((valid[:, None, :] == 1) & (blocks[:, None, :] <= blocks[:, :, None]) | (positions[:, None] == positions[None, :])[None]).astype(jnp.int32)
    stream = block_input.astype(jnp.float32) + time_embed(timesteps, D)[:, None, :]
    params = tuple((weight.astype(jnp.float32) for weight in (w_qkv, w_o, w_in, w_out, b_in, biases, gains, shifts)))
    groups = ITEMS // ITEMS_DEV
    row_weight = valid.astype(jnp.float32)

    def whole(params, stream):

        def step_fn(carry, inputs):
            stream_grp, allowed_grp, weight_grp = inputs
            result, squares = jax.checkpoint(block_forward)(params, stream_grp, allowed_grp, weight_grp)
            return (carry + squares, result)
        inputs = (stream.reshape(groups, ITEMS_DEV, LEN, D), allowed.reshape(groups, ITEMS_DEV, LEN, LEN), row_weight.reshape(groups, ITEMS_DEV, LEN))
        totals, results = lax.scan(step_fn, jnp.zeros((4,), jnp.float32), inputs)
        return (results.reshape(ITEMS, LEN, D), totals)
    result, back_fn, totals = jax.vjp(whole, params, stream, has_aux=True)
    param_grads, stream_grad = back_fn(cotangent.astype(jnp.float32))
    rms = jnp.sqrt(totals / (jnp.sum(row_weight) * D))
    return (result.astype(jnp.bfloat16), stream_grad.astype(jnp.bfloat16), param_grads[0], param_grads[1], param_grads[2], param_grads[3], param_grads[4], param_grads[5], param_grads[6], param_grads[7], rms)
```

```python
from functools import partial
import math

import jax
import jax.numpy as jnp
from jax import lax
from jax.experimental import pallas as pl
from jax.experimental.pallas import tpu as pltpu
from jax.sharding import PartitionSpec as P

HEADS = 16
HD = 64

AXES = ("dp", "ctx")


def my_index():
    return lax.axis_index("dp") * lax.axis_size("ctx") + lax.axis_index("ctx")


def n_devices():
    return lax.axis_size("dp") * lax.axis_size("ctx")


def swap(array, bits):
    return lax.ppermute(array, AXES, [(i, i ^ bits) for i in range(n_devices())])


def after(array, *others):
    return lax.optimization_barrier((array, *others))[0]


X, CORE, Y, Z = 1, 2, 4, 8


def reorder(pieces, blocks, to_shape, moves):
    plan = moves

    def kernel(*refs):
        sources, out, sem = refs[: len(pieces)], refs[len(pieces)], refs[len(pieces) + 1]
        me = my_index()
        copies = [
            pltpu.make_async_copy(sources[p].at[b], out.at[jnp.bitwise_xor(me, place)], sem.at[i])
            for i, (p, b, place) in enumerate(plan)
        ]
        for copy in copies:
            copy.start()
        for copy in copies:
            copy.wait()

    return pl.pallas_call(
        kernel,
        out_shape=jax.ShapeDtypeStruct(to_shape, pieces[0].dtype),
        in_specs=[pl.BlockSpec(memory_space=pl.ANY)] * len(pieces),
        out_specs=pl.BlockSpec(memory_space=pl.ANY),
        scratch_shapes=[pltpu.SemaphoreType.DMA((len(plan),))],
    )(*pieces)


def gather_pieces(shard, first):
    nz = n_devices() // Z
    half = nz // 2
    shard = after(shard, *first)
    others = [swap(shard, Z * k) for k in range(1, nz)]
    own = jnp.stack([shard] + others)
    from_x = swap(own, X)
    from_y = swap(own, Y)
    diag_a = swap(from_x[:half], Y)
    diag_b = swap(from_y[half:], X)
    mine = [(own, 0, 0), (from_x, X, 0), (from_y, Y, 0), (diag_a, X | Y, 0), (diag_b, X | Y, half)]
    theirs = [(swap(p, CORE), bits | CORE, k) for p, bits, k in mine]
    return mine + theirs, others


def assemble(placed, rows):
    n = n_devices()
    pieces = [p for p, _, _ in placed]
    plan = []
    for i, (p, bits, start) in enumerate(placed):
        for k in range(p.shape[0]):
            plan.append((i, k, bits | (Z * (start + k))))
    shape = (n,) + pieces[0].shape[1:]
    return reorder(pieces, None, shape, plan).reshape(n * shape[1], shape[2])


def scatter_sum(grad, first):
    n = n_devices()
    nz = n // Z
    half = nz // 2
    rows, cols = grad.shape
    r = rows // n
    rel = reorder_rel(grad.reshape(n, r, cols)).reshape(nz, 2, 2, 2, r, cols)
    f32 = jnp.float32
    low = jnp.bfloat16
    sent = rel[:, :, 1]
    got = swap(after(sent, *first), CORE)
    total = rel[:, :, 0].astype(f32) + got.astype(f32)
    own = total[:, 0, 0].astype(low)
    to_x = total[:, 0, 1].astype(low)
    to_y = total[:, 1, 0].astype(low)
    diag = total[:, 1, 1].astype(low)
    to_x_a = (to_x[:half].astype(f32) + swap(diag[:half], Y).astype(f32)).astype(low)
    to_y_b = (to_y[half:].astype(f32) + swap(diag[half:], X).astype(f32)).astype(low)
    got_x_b = swap(to_x[half:], X)
    got_y_a = swap(to_y[:half], Y)
    got_x_a = swap(to_x_a, X)
    got_y_b = swap(to_y_b, Y)
    own_a = own[:half].astype(f32) + got_x_a.astype(f32) + got_y_a.astype(f32)
    own_b = own[half:].astype(f32) + got_x_b.astype(f32) + got_y_b.astype(f32)
    line = jnp.concatenate([own_a, own_b], axis=0)
    out = line[0]
    line = line.astype(low)
    for k in range(1, nz):
        out = out + swap(line[k], Z * k).astype(f32)
    return out, got


def reorder_rel(grad):
    n = grad.shape[0]
    plan = [(0, s, s) for s in range(n)]

    def kernel(src, out, sem):
        me = my_index()
        copies = [
            pltpu.make_async_copy(src.at[jnp.bitwise_xor(me, s)], out.at[s], sem.at[s]) for s in range(n)
        ]
        for copy in copies:
            copy.start()
        for copy in copies:
            copy.wait()

    return pl.pallas_call(
        kernel,
        out_shape=jax.ShapeDtypeStruct(grad.shape, grad.dtype),
        in_specs=[pl.BlockSpec(memory_space=pl.ANY)],
        out_specs=pl.BlockSpec(memory_space=pl.ANY),
        scratch_shapes=[pltpu.SemaphoreType.DMA((n,))],
    )(grad)


def gather_small(vector):
    n = n_devices()
    rel = vector[None, :]
    bit = 1
    while bit < n:
        rel = jnp.concatenate([rel, swap(rel, bit)], axis=0)
        bit *= 2
    place = jnp.bitwise_xor(jnp.arange(n, dtype=jnp.int32), my_index())
    pick = (place[:, None] == jnp.arange(n, dtype=jnp.int32)[None, :]).astype(vector.dtype)
    return jnp.dot(pick, rel, preferred_element_type=jnp.float32)


def sum_small(vector):
    bit = 1
    while bit < n_devices():
        vector = vector + swap(vector, bit)
        bit *= 2
    return vector


fill_value = -1e30
eps_norm = 1e-05
code_absent = 30000.0


def time_embed(steps, width):
    half = width // 2
    freqs = jnp.exp(jnp.arange(half, dtype=jnp.float32) * (-math.log(10000.0) / half))
    angle = steps.astype(jnp.float32)[:, None] * freqs[None, :]
    return jnp.concatenate([jnp.sin(angle), jnp.cos(angle)], axis=-1)


def layer_norm(resid, gain, shift):
    centre = resid - jnp.mean(resid, axis=-1, keepdims=True)
    spread = jnp.mean(centre * centre, axis=-1, keepdims=True)
    return centre * lax.rsqrt(spread + eps_norm) * gain + shift


def inner(left, right):
    return lax.dot_general(
        left, right, (((0,), (0,)), ((), ())), preferred_element_type=jnp.float32
    )


def back_project(grad, weight):
    return lax.dot_general(
        grad, weight, (((1,), (1,)), ((), ())), preferred_element_type=jnp.float32
    )


def scores_of(query, keys, code_row, query_block, key_pos, positions):
    permit = (code_row[None, :] <= query_block[:, None]) | (key_pos[None, :] == positions[:, None])
    raw = jnp.einsum("qhd,khd->hqk", query, keys, preferred_element_type=jnp.float32) * (
        1.0 / math.sqrt(HD)
    )
    return jnp.where(permit[None], raw, fill_value)


def body(
    block_input,
    lengths,
    mask,
    blocks,
    timesteps,
    w_qkv,
    w_o,
    w_in,
    w_out,
    b_in,
    biases,
    gains,
    shifts,
    cotangent,
):
    items, half_len, width = block_input.shape
    rows = items * half_len
    f32, low = jnp.float32, jnp.bfloat16
    n = n_devices()
    by_hand = (w_qkv.shape[0] % 16 == 0) and n % Z == 0
    positions = lax.axis_index("ctx") * half_len + jnp.arange(half_len, dtype=jnp.int32)
    other_positions = (1 - lax.axis_index("ctx")) * half_len + jnp.arange(half_len, dtype=jnp.int32)
    key_pos = jnp.concatenate([positions, other_positions])
    valid = (positions[None, :] < lengths[:, None]) & ((mask == 1) | (positions[None, :] == 0))
    code_local = jnp.where(valid, blocks.astype(f32), code_absent)
    small = jnp.concatenate([b_in, biases.reshape(-1), gains.reshape(-1), shifts.reshape(-1)])
    if by_hand:
        placed, last = gather_pieces(w_qkv, ())
        w_qkv_all = assemble(placed, rows)
        input_other = swap(after(block_input, *last), X)
        placed, last = gather_pieces(w_o, last)
        w_o_all = assemble(placed, rows)
        placed, last = gather_pieces(w_in, last)
        w_in_all = assemble(placed, rows)
        placed, last = gather_pieces(w_out, last)
        w_out_all = assemble(placed, rows)
    else:
        input_other = swap(block_input, X)
        w_qkv_all, w_o_all, w_in_all, w_out_all = (
            lax.all_gather(w, AXES, axis=0, tiled=True) for w in (w_qkv, w_o, w_in, w_out)
        )
    small_all = gather_small(small)
    code_all = jnp.concatenate([code_local, swap(code_local, X)], axis=1)
    share = width // n
    b_count = b_in.shape[0]
    b_in_full = small_all[:, :b_count].reshape(-1)
    rest = small_all[:, b_count:].reshape(n, 8, share).transpose(1, 0, 2).reshape(8, width)
    bias_full, gain_full, shift_full = rest[:4], rest[4:6], rest[6:8]

    embed = time_embed(timesteps, width)[:, None, :]
    stream = (block_input.astype(f32) + embed).reshape(rows, width)
    stream_low = stream.astype(low)
    other_low = (input_other.astype(f32) + embed).reshape(rows, width).astype(low)
    joint = jnp.dot(stream_low, w_qkv_all, preferred_element_type=f32)
    other = jnp.dot(other_low, w_qkv_all[:, width:], preferred_element_type=f32)
    query_low = (joint[:, :width] + bias_full[0]).astype(low)
    split = lambda array: array.reshape(items, half_len, width)
    key_all = jnp.concatenate(
        [split(joint[:, width : 2 * width].astype(low)), split(other[:, :width].astype(low))], axis=1
    )
    value_all = jnp.concatenate(
        [
            split((joint[:, 2 * width :] + bias_full[1]).astype(low)),
            split((other[:, width:] + bias_full[1]).astype(low)),
        ],
        axis=1,
    )
    full_len = 2 * half_len
    query_block = blocks.astype(f32)
    query_four = query_low.reshape(items, half_len, HEADS, HD)
    key_four = key_all.reshape(items, full_len, HEADS, HD)
    value_four = value_all.reshape(items, full_len, HEADS, HD)

    def attend(inputs):
        query, keys, values, code_row, block_row = inputs
        scores = scores_of(query, keys, code_row, block_row, key_pos, positions)
        peak = jnp.max(scores, axis=-1, keepdims=True)
        expo = jnp.exp(scores - peak)
        total = jnp.sum(expo, axis=-1, keepdims=True)
        probs = expo / total
        mixed = jnp.einsum(
            "hqk,khd->qhd", probs.astype(jnp.bfloat16), values, preferred_element_type=jnp.float32
        )
        return (mixed, (peak + jnp.log(total))[..., 0])

    mixed_all, log_totals = lax.map(
        attend, (query_four, key_four, value_four, code_all, query_block)
    )
    mixed_low = mixed_all.reshape(rows, width).astype(jnp.bfloat16)
    attn = jnp.dot(mixed_low, w_o_all, preferred_element_type=jnp.float32) + bias_full[2]
    resid_one = stream + attn
    hidden_one = layer_norm(resid_one, gain_full[0], shift_full[0])
    hidden_low = hidden_one.astype(jnp.bfloat16)
    pre = jnp.dot(hidden_low, w_in_all, preferred_element_type=jnp.float32) + b_in_full
    act_low = jax.nn.gelu(pre, approximate=False).astype(jnp.bfloat16)
    branch = jnp.dot(act_low, w_out_all, preferred_element_type=jnp.float32) + bias_full[3]
    resid_two = hidden_one + branch
    result = layer_norm(resid_two, gain_full[1], shift_full[1])
    output = result.astype(jnp.bfloat16).reshape(items, half_len, width)
    row_weight = valid.reshape(rows).astype(jnp.float32)
    local_sums = jnp.stack(
        [
            jnp.sum(row_weight * jnp.sum(tensor * tensor, axis=-1))
            for tensor in (stream, attn, branch, result)
        ]
        + [jnp.sum(row_weight)]
    )
    _, norm_two_back = jax.vjp(layer_norm, resid_two, gain_full[1], shift_full[1])
    dres_two, gain_two_grad, shift_two_grad = norm_two_back(
        cotangent.reshape(rows, width).astype(jnp.float32)
    )
    branch_grad = dres_two.astype(jnp.bfloat16)

    if by_hand:
        share_sum = lambda part, first: scatter_sum(part.astype(low), first)
    else:
        share_sum = lambda part, first: (
            lax.psum_scatter(part, AXES, scatter_dimension=0, tiled=True),
            part,
        )
    grad_out, got = share_sum(inner(act_low, branch_grad), ())
    act_grad = back_project(branch_grad, w_out_all)
    _, gelu_back = jax.vjp(partial(jax.nn.gelu, approximate=False), pre)
    pre_grad = gelu_back(act_grad)[0].astype(jnp.bfloat16)
    grad_in, got = share_sum(inner(hidden_low, pre_grad), (got,))
    dhidden = dres_two + back_project(pre_grad, w_in_all)
    _, norm_one_back = jax.vjp(layer_norm, resid_one, gain_full[0], shift_full[0])
    dres_one, gain_one_grad, shift_one_grad = norm_one_back(dhidden)
    attn_grad = dres_one.astype(jnp.bfloat16)
    grad_o, got = share_sum(inner(mixed_low, attn_grad), (got,))
    mixed_grad = (
        back_project(attn_grad, w_o_all).astype(jnp.bfloat16).reshape(items, half_len, HEADS, HD)
    )

    def attend_back(inputs):
        query, keys, values, code_row, block_row, log_row, grad_row = inputs
        scores = scores_of(query, keys, code_row, block_row, key_pos, positions)
        probs = jnp.exp(scores - log_row[..., None])
        value_part = jnp.einsum(
            "hqk,qhd->khd", probs.astype(jnp.bfloat16), grad_row, preferred_element_type=jnp.float32
        )
        prob_grad = jnp.einsum("qhd,khd->hqk", grad_row, values, preferred_element_type=jnp.float32)
        centre = jnp.sum(probs * prob_grad, axis=-1, keepdims=True)
        score_grad = (probs * (prob_grad - centre)).astype(jnp.bfloat16)
        query_part = jnp.einsum(
            "hqk,khd->qhd", score_grad, keys, preferred_element_type=jnp.float32
        ) * (1.0 / math.sqrt(HD))
        key_part = jnp.einsum(
            "hqk,qhd->khd", score_grad, query, preferred_element_type=jnp.float32
        ) * (1.0 / math.sqrt(HD))
        return (query_part, key_part, value_part)

    query_part, key_part, value_part = lax.map(
        attend_back,
        (query_four, key_four, value_four, code_all, query_block, log_totals, mixed_grad),
    )
    key_part = key_part.reshape(items, full_len, width)
    value_part = value_part.reshape(items, full_len, width)
    away = jnp.stack([key_part[:, half_len:], value_part[:, half_len:]]).astype(low)
    back = swap(away, X).astype(f32)
    query_grad_low = query_part.reshape(rows, width).astype(jnp.bfloat16)
    key_grad_low = (key_part[:, :half_len] + back[0]).reshape(rows, width).astype(jnp.bfloat16)
    value_grad_low = (value_part[:, :half_len] + back[1]).reshape(rows, width).astype(jnp.bfloat16)
    joint_grad = jnp.concatenate([query_grad_low, key_grad_low, value_grad_low], axis=1)
    grad_qkv, got = share_sum(inner(stream_low, joint_grad), (got,))
    input_grad = (
        (dres_one + back_project(joint_grad, w_qkv_all))
        .astype(jnp.bfloat16)
        .reshape(items, half_len, width)
    )
    b_in_part = jnp.sum(pre_grad.astype(jnp.float32), axis=0)
    parts = [
        jnp.sum(query_grad_low.astype(jnp.float32), axis=0),
        jnp.sum(value_grad_low.astype(jnp.float32), axis=0),
        jnp.sum(attn_grad.astype(jnp.float32), axis=0),
        jnp.sum(branch_grad.astype(jnp.float32), axis=0),
        gain_one_grad,
        gain_two_grad,
        shift_one_grad,
        shift_two_grad,
    ]
    sums = sum_small(jnp.concatenate([b_in_part] + parts + [local_sums]))
    ff = b_in_part.shape[0]
    me = my_index()
    grad_b_in = lax.dynamic_slice(sums, (me * b_count,), (b_count,))
    grads = lax.dynamic_slice(sums[ff : ff + 8 * width].reshape(8, width), (0, me * share), (8, share))
    totals = sums[ff + 8 * width :]
    rms = jnp.sqrt(totals[:4] / (totals[4] * width))
    return (
        output,
        input_grad,
        grad_qkv,
        grad_o,
        grad_in,
        grad_out,
        grad_b_in,
        grads[:4],
        grads[4:6],
        grads[6:8],
        rms,
    )


def solution(mesh):
    in_specs = (
        P("dp", "ctx", None),
        P("dp"),
        P("dp", "ctx"),
        P("dp", "ctx"),
        P("dp"),
        P(("dp", "ctx"), None),
        P(("dp", "ctx"), None),
        P(("dp", "ctx"), None),
        P(("dp", "ctx"), None),
        P(("dp", "ctx")),
        P(None, ("dp", "ctx")),
        P(None, ("dp", "ctx")),
        P(None, ("dp", "ctx")),
        P("dp", "ctx", None),
    )
    out_specs = (
        P("dp", "ctx", None),
        P("dp", "ctx", None),
        P(("dp", "ctx"), None),
        P(("dp", "ctx"), None),
        P(("dp", "ctx"), None),
        P(("dp", "ctx"), None),
        P(("dp", "ctx")),
        P(None, ("dp", "ctx")),
        P(None, ("dp", "ctx")),
        P(None, ("dp", "ctx")),
        P(),
    )
    return jax.shard_map(body, mesh=mesh, in_specs=in_specs, out_specs=out_specs, check_vma=False)
```

```python
from functools import partial
import math

import jax
import jax.numpy as jnp
from jax import lax
from jax.experimental import pallas as pl
from jax.experimental.pallas import tpu as pltpu
from jax.sharding import PartitionSpec as P

HEADS = 16
HD = 64

AXES = ("dp", "ctx")
X = 1


def my_index():
    return lax.axis_index("dp") * lax.axis_size("ctx") + lax.axis_index("ctx")


def n_devices():
    return lax.axis_size("dp") * lax.axis_size("ctx")


def swap(array, bits):
    return lax.ppermute(array, AXES, [(i, i ^ bits) for i in range(n_devices())])

MESH = pl.DeviceIdType.MESH


class Place:
    def __init__(self):
        dp = lax.axis_index("dp")
        self.nz = lax.axis_size("dp") // 4
        self.x = lax.axis_index("ctx")
        self.c = dp % 2
        self.y = (dp // 2) % 2
        self.z = dp // 4

    def zth(self, k):
        z, bit = self.z, 1
        while bit < self.nz:
            if k & bit:
                z = z + bit * (1 - 2 * ((self.z // bit) % 2))
            bit *= 2
        return z

    def flips(self, y=0, c=0, x=0):
        return (
            1 - self.y if y else self.y,
            1 - self.c if c else self.c,
            1 - self.x if x else self.x,
        )

    def device(self, k=0, y=0, c=0, x=0):
        fy, fc, fx = self.flips(y, c, x)
        return ((self.zth(k) * 2 + fy) * 2 + fc, fx)

    def shard(self, k=0, y=0, c=0, x=0):
        fy, fc, fx = self.flips(y, c, x)
        return ((self.zth(k) * 2 + fy) * 2 + fc) * 2 + fx

    def column(self, y=0, c=0, x=0):
        fy, fc, fx = self.flips(y, c, x)
        return (fy * 2 + fc) * 2 + fx

    def partners(self):
        return [self.device(k=k) for k in range(1, self.nz)] + [
            self.device(x=1),
            self.device(y=1),
            self.device(c=1),
        ]


def meet(place):
    barrier = pltpu.get_barrier_semaphore()
    partners = place.partners()
    for partner in partners:
        pl.semaphore_signal(barrier, inc=1, device_id=partner, device_id_type=MESH)
    pl.semaphore_wait(barrier, len(partners))


class Sender:
    def __init__(self, send_sem, recv_sem):
        self.send_sem, self.recv_sem = send_sem, recv_sem
        self.count = 0
        self.open = []

    def send(self, src, dst, device):
        copy = pltpu.make_async_remote_copy(
            src_ref=src,
            dst_ref=dst,
            send_sem=self.send_sem.at[self.count],
            recv_sem=self.recv_sem.at[self.count],
            device_id=device,
            device_id_type=MESH,
        )
        self.count += 1
        copy.start()
        self.open.append(copy)
        return copy

    def close(self):
        for copy in self.open:
            copy.wait_send()
        self.open = []


def gather_copies(nz):
    return (nz - 1) + 2 * (nz + 2) + 5


def gather_steps(place, sender, shard, full):
    nz = place.nz
    half = nz // 2
    mine = place.column()
    own = full.at[place.z, mine]
    by_z = [sender.send(shard, own, place.device(k=k)) for k in range(1, nz)]
    from_x = [sender.send(shard, own, place.device(x=1))]
    from_y = [sender.send(shard, own, place.device(y=1))]
    yield
    for k in range(1, nz):
        by_z[k - 1].wait_recv()
        piece = full.at[place.zth(k), mine]
        from_x.append(sender.send(piece, piece, place.device(x=1)))
        from_y.append(sender.send(piece, piece, place.device(y=1)))
    line = full.at[:, mine]
    to_core = [sender.send(line, line, place.device(c=1))]
    yield
    for copy in from_x:
        copy.wait_recv()
    at_x = place.column(x=1)
    line = full.at[:, at_x]
    part = full.at[pl.ds(0, half), at_x]
    diag_a = sender.send(part, part, place.device(y=1))
    to_core.append(sender.send(line, line, place.device(c=1)))
    yield
    for copy in from_y:
        copy.wait_recv()
    at_y = place.column(y=1)
    line = full.at[:, at_y]
    part = full.at[pl.ds(half, nz - half), at_y]
    diag_b = sender.send(part, part, place.device(x=1))
    to_core.append(sender.send(line, line, place.device(c=1)))
    yield
    diag = place.column(x=1, y=1)
    for copy, start, size in ((diag_a, 0, half), (diag_b, half, nz - half)):
        copy.wait_recv()
        part = full.at[pl.ds(start, size), diag]
        to_core.append(sender.send(part, part, place.device(c=1)))
    yield
    for copy in to_core:
        copy.wait_recv()


def gather_kernel(shapes, nz):
    count = len(shapes)

    def kernel(*refs):
        shards, given = refs[:count], refs[count]
        fulls, taken = refs[count + 1 : 2 * count + 1], refs[2 * count + 1]
        send_sem, recv_sem, own_sem = refs[2 * count + 2 :]
        place = Place()
        sender = Sender(send_sem, recv_sem)
        kept = [
            pltpu.make_async_copy(shard, full.at[place.z, place.column()], own_sem.at[i])
            for i, (shard, full) in enumerate(zip(shards, fulls))
        ]
        for copy in kept:
            copy.start()
        meet(place)
        for copy in kept:
            copy.wait()
        steps = [gather_steps(place, sender, s, f) for s, f in zip(shards, fulls)]
        swapped = None
        t = 0
        while steps:
            live = []
            for i, step in enumerate(steps):
                if i > t:
                    live.append(step)
                    continue
                try:
                    next(step)
                    live.append(step)
                except StopIteration:
                    pass
            steps = live
            if t == 1:
                swapped = sender.send(given, taken, place.device(x=1))
            t += 1
        swapped.wait_recv()
        sender.close()

    return kernel


def gather_all(shards, block_input, collective_id):
    nz = lax.axis_size("dp") // 4
    copies = len(shards) * gather_copies(nz) + 1
    results = pl.pallas_call(
        gather_kernel([s.shape for s in shards], nz),
        out_shape=[jax.ShapeDtypeStruct((nz, 8) + s.shape, s.dtype) for s in shards]
        + [jax.ShapeDtypeStruct(block_input.shape, block_input.dtype)],
        in_specs=[pl.BlockSpec(memory_space=pltpu.VMEM)] * (len(shards) + 1),
        out_specs=[pl.BlockSpec(memory_space=pl.ANY)] * (len(shards) + 1),
        scratch_shapes=[
            pltpu.SemaphoreType.DMA((copies,)),
            pltpu.SemaphoreType.DMA((copies,)),
            pltpu.SemaphoreType.DMA((len(shards),)),
        ],
        compiler_params=pltpu.CompilerParams(
            collective_id=collective_id, has_side_effects=True, vmem_limit_bytes=16 << 20
        ),
    )(*shards, block_input)
    return results


def reduce_copies(nz):
    return 4 + 2 + 2 + 2 + nz - 1


def reduce_buffers(nz, rows, cols):
    low = jnp.bfloat16
    half = nz // 2
    return [
        pltpu.VMEM((4, nz, rows, cols), low),
        pltpu.VMEM((4, nz, rows, cols), low),
        pltpu.VMEM((half, rows, cols), low),
        pltpu.VMEM((nz - half, rows, cols), low),
        pltpu.VMEM((2, nz, rows, cols), low),
        pltpu.VMEM((nz - 1, rows, cols), low),
    ]


def add_rows(target, terms, count, rows):
    step = min(rows, 16)
    per = rows // step

    def one(j, _):
        i, start = j // per, (j % per) * step
        at = pl.ds(pl.multiple_of(start, step), step)
        total = terms[0](i, at).astype(jnp.float32)
        for term in terms[1:]:
            total = total + term(i, at).astype(jnp.float32)
        target(i, at, total)
        return 0

    lax.fori_loop(0, count * per, one, 0)


def reduce_steps(place, sender, grad, buffers, out):
    from_core, sums, diag_y, diag_x, from_xy, from_z = buffers
    nz, half = place.nz, place.nz // 2
    rows = grad.shape[2]
    low = jnp.bfloat16
    groups = ((1, 1), (0, 1), (1, 0), (0, 0))
    by_core = [
        sender.send(grad.at[:, place.column(y=fy, c=1, x=fx)], from_core.at[i], place.device(c=1))
        for i, (fy, fx) in enumerate(groups)
    ]
    yield

    def put(slot, offset=0):
        def store(i, at, value):
            sums[slot, i + offset, at, :] = value.astype(low)

        return store

    def add_core(slot):
        fy, fx = groups[slot]
        column = place.column(y=fy, x=fx)
        by_core[slot].wait_recv()
        add_rows(
            put(slot),
            [lambda i, at: grad[i, column, at, :], lambda i, at: from_core[slot, i, at, :]],
            nz,
            rows,
        )

    low_z, high_z = pl.ds(0, half), pl.ds(half, nz - half)
    add_core(0)
    by_y = sender.send(sums.at[0, low_z], diag_y, place.device(y=1))
    by_x = sender.send(sums.at[0, high_z], diag_x, place.device(x=1))
    add_core(1)
    x_high = sender.send(sums.at[1, high_z], from_xy.at[0, high_z], place.device(x=1))
    add_core(2)
    y_low = sender.send(sums.at[2, low_z], from_xy.at[1, low_z], place.device(y=1))
    yield
    add_core(3)
    by_y.wait_recv()
    add_rows(
        put(1),
        [lambda i, at: sums[1, i, at, :], lambda i, at: diag_y[i, at, :]],
        half,
        rows,
    )
    x_low = sender.send(sums.at[1, low_z], from_xy.at[0, low_z], place.device(x=1))
    by_x.wait_recv()
    add_rows(
        put(2, half),
        [lambda i, at: sums[2, i + half, at, :], lambda i, at: diag_x[i, at, :]],
        nz - half,
        rows,
    )
    y_high = sender.send(sums.at[2, high_z], from_xy.at[1, high_z], place.device(y=1))
    yield
    for copy in (x_high, y_low, x_low, y_high):
        copy.wait_recv()
    add_rows(
        put(3),
        [
            lambda i, at: sums[3, i, at, :],
            lambda i, at: from_xy[0, i, at, :],
            lambda i, at: from_xy[1, i, at, :],
        ],
        nz,
        rows,
    )
    by_z = [
        sender.send(sums.at[3, place.zth(k)], from_z.at[k - 1], place.device(k=k)) for k in range(1, nz)
    ]
    yield
    for copy in by_z:
        copy.wait_recv()

    def last(i, at, value):
        out[at, :] = value

    add_rows(
        last,
        [lambda i, at: sums[3, place.z, at, :]]
        + [lambda i, at, k=k: from_z[k, at, :] for k in range(nz - 1)],
        1,
        rows,
    )


def reduce_kernel(shapes):
    count = len(shapes)

    def kernel(*refs):
        grads, outs = refs[:count], refs[count : 2 * count]
        scratch = refs[2 * count :]
        buffers = [scratch[6 * i : 6 * i + 6] for i in range(count)]
        send_sem, recv_sem = scratch[6 * count :]
        place = Place()
        sender = Sender(send_sem, recv_sem)
        meet(place)
        steps = [reduce_steps(place, sender, g, b, o) for g, b, o in zip(grads, buffers, outs)]
        t = 0
        while steps:
            live = []
            for i, step in enumerate(steps):
                if i > t:
                    live.append(step)
                    continue
                try:
                    next(step)
                    live.append(step)
                except StopIteration:
                    pass
            steps = live
            t += 1
        sender.close()

    return kernel


def reduce_all(grads, collective_id):
    nz = lax.axis_size("dp") // 4
    n = nz * 8
    blocks = [g.reshape(nz, 8, g.shape[0] // n, g.shape[1]) for g in grads]
    copies = len(grads) * reduce_copies(nz)
    scratch = []
    for block in blocks:
        scratch += reduce_buffers(nz, block.shape[2], block.shape[3])
    return pl.pallas_call(
        reduce_kernel([b.shape for b in blocks]),
        out_shape=[jax.ShapeDtypeStruct(b.shape[2:], jnp.float32) for b in blocks],
        in_specs=[pl.BlockSpec(memory_space=pltpu.VMEM)] * len(grads),
        out_specs=[pl.BlockSpec(memory_space=pltpu.VMEM)] * len(grads),
        scratch_shapes=scratch
        + [pltpu.SemaphoreType.DMA((copies,)), pltpu.SemaphoreType.DMA((copies,))],
        compiler_params=pltpu.CompilerParams(
            collective_id=collective_id, has_side_effects=True, vmem_limit_bytes=56 << 20
        ),
    )(*blocks)


def sum_small(vector):
    bit = 1
    while bit < n_devices():
        vector = vector + swap(vector, bit)
        bit *= 2
    return vector


fill_value = -1e30
eps_norm = 1e-05
code_absent = 30000.0


def time_embed(steps, width):
    half = width // 2
    freqs = jnp.exp(jnp.arange(half, dtype=jnp.float32) * (-math.log(10000.0) / half))
    angle = steps.astype(jnp.float32)[:, None] * freqs[None, :]
    return jnp.concatenate([jnp.sin(angle), jnp.cos(angle)], axis=-1)


def layer_norm(resid, gain, shift):
    centre = resid - jnp.mean(resid, axis=-1, keepdims=True)
    spread = jnp.mean(centre * centre, axis=-1, keepdims=True)
    return centre * lax.rsqrt(spread + eps_norm) * gain + shift


def inner(left, right):
    return lax.dot_general(
        left, right, (((0,), (0,)), ((), ())), preferred_element_type=jnp.float32
    )


def back_project(grad, weight):
    return lax.dot_general(
        grad, weight, (((1,), (1,)), ((), ())), preferred_element_type=jnp.float32
    )


def scores_of(query, keys, code_row, query_block, key_pos, positions):
    permit = (code_row[None, :] <= query_block[:, None]) | (key_pos[None, :] == positions[:, None])
    raw = jnp.einsum("qhd,khd->hqk", query, keys, preferred_element_type=jnp.float32) * (
        1.0 / math.sqrt(HD)
    )
    return jnp.where(permit[None], raw, fill_value)


def body(
    block_input,
    lengths,
    mask,
    blocks,
    timesteps,
    w_qkv,
    w_o,
    w_in,
    w_out,
    b_in,
    biases,
    gains,
    shifts,
    cotangent,
):
    items, half_len, width = block_input.shape
    rows = items * half_len
    f32, low = jnp.float32, jnp.bfloat16
    n = n_devices()
    positions = lax.axis_index("ctx") * half_len + jnp.arange(half_len, dtype=jnp.int32)
    other_positions = (1 - lax.axis_index("ctx")) * half_len + jnp.arange(half_len, dtype=jnp.int32)
    key_pos = jnp.concatenate([positions, other_positions])
    valid = (positions[None, :] < lengths[:, None]) & ((mask == 1) | (positions[None, :] == 0))
    code_local = jnp.where(valid, blocks.astype(f32), code_absent)
    share = width // n
    b_count = b_in.shape[0]
    small = jnp.concatenate([b_in, biases.reshape(-1), gains.reshape(-1), shifts.reshape(-1)])
    small = jnp.pad(small.astype(f32), (0, 1024 - small.shape[0])).reshape(8, 128)
    gathered = gather_all([w_qkv, small, w_o, w_in, w_out], block_input.reshape(rows, width), 1)
    w_qkv_all, small_all, w_o_all, w_in_all, w_out_all = (g.reshape(-1, g.shape[-1]) for g in gathered[:5])
    input_other = gathered[5].reshape(block_input.shape)
    small_all = small_all.reshape(n, 1024)[:, : b_count + 8 * share]
    code_all = jnp.concatenate([code_local, swap(code_local, X)], axis=1)
    b_in_full = small_all[:, :b_count].reshape(-1)
    rest = small_all[:, b_count:].reshape(n, 8, share).transpose(1, 0, 2).reshape(8, width)
    bias_full, gain_full, shift_full = rest[:4], rest[4:6], rest[6:8]

    embed = time_embed(timesteps, width)[:, None, :]
    stream = (block_input.astype(f32) + embed).reshape(rows, width)
    stream_low = stream.astype(low)
    other_low = (input_other.astype(f32) + embed).reshape(rows, width).astype(low)
    joint = jnp.dot(stream_low, w_qkv_all, preferred_element_type=f32)
    other = jnp.dot(other_low, w_qkv_all[:, width:], preferred_element_type=f32)
    query_low = (joint[:, :width] + bias_full[0]).astype(low)
    split = lambda array: array.reshape(items, half_len, width)
    key_all = jnp.concatenate(
        [split(joint[:, width : 2 * width].astype(low)), split(other[:, :width].astype(low))], axis=1
    )
    value_all = jnp.concatenate(
        [
            split((joint[:, 2 * width :] + bias_full[1]).astype(low)),
            split((other[:, width:] + bias_full[1]).astype(low)),
        ],
        axis=1,
    )
    full_len = 2 * half_len
    query_block = blocks.astype(f32)
    query_four = query_low.reshape(items, half_len, HEADS, HD)
    key_four = key_all.reshape(items, full_len, HEADS, HD)
    value_four = value_all.reshape(items, full_len, HEADS, HD)

    def attend(inputs):
        query, keys, values, code_row, block_row = inputs
        scores = scores_of(query, keys, code_row, block_row, key_pos, positions)
        peak = jnp.max(scores, axis=-1, keepdims=True)
        expo = jnp.exp(scores - peak)
        total = jnp.sum(expo, axis=-1, keepdims=True)
        probs = expo / total
        mixed = jnp.einsum(
            "hqk,khd->qhd", probs.astype(jnp.bfloat16), values, preferred_element_type=jnp.float32
        )
        return (mixed, (peak + jnp.log(total))[..., 0])

    mixed_all, log_totals = lax.map(
        attend, (query_four, key_four, value_four, code_all, query_block)
    )
    mixed_low = mixed_all.reshape(rows, width).astype(jnp.bfloat16)
    attn = jnp.dot(mixed_low, w_o_all, preferred_element_type=jnp.float32) + bias_full[2]
    resid_one = stream + attn
    hidden_one = layer_norm(resid_one, gain_full[0], shift_full[0])
    hidden_low = hidden_one.astype(jnp.bfloat16)
    pre = jnp.dot(hidden_low, w_in_all, preferred_element_type=jnp.float32) + b_in_full
    act_low = jax.nn.gelu(pre, approximate=False).astype(jnp.bfloat16)
    branch = jnp.dot(act_low, w_out_all, preferred_element_type=jnp.float32) + bias_full[3]
    resid_two = hidden_one + branch
    result = layer_norm(resid_two, gain_full[1], shift_full[1])
    output = result.astype(jnp.bfloat16).reshape(items, half_len, width)
    row_weight = valid.reshape(rows).astype(jnp.float32)
    local_sums = jnp.stack(
        [
            jnp.sum(row_weight * jnp.sum(tensor * tensor, axis=-1))
            for tensor in (stream, attn, branch, result)
        ]
        + [jnp.sum(row_weight)]
    )
    _, norm_two_back = jax.vjp(layer_norm, resid_two, gain_full[1], shift_full[1])
    dres_two, gain_two_grad, shift_two_grad = norm_two_back(
        cotangent.reshape(rows, width).astype(jnp.float32)
    )
    branch_grad = dres_two.astype(jnp.bfloat16)

    grad_out_part = inner(act_low, branch_grad).astype(low)
    act_grad = back_project(branch_grad, w_out_all)
    _, gelu_back = jax.vjp(partial(jax.nn.gelu, approximate=False), pre)
    pre_grad = gelu_back(act_grad)[0].astype(jnp.bfloat16)
    grad_in_part = inner(hidden_low, pre_grad).astype(low)
    dhidden = dres_two + back_project(pre_grad, w_in_all)
    _, norm_one_back = jax.vjp(layer_norm, resid_one, gain_full[0], shift_full[0])
    dres_one, gain_one_grad, shift_one_grad = norm_one_back(dhidden)
    attn_grad = dres_one.astype(jnp.bfloat16)
    grad_o_part = inner(mixed_low, attn_grad).astype(low)
    mixed_grad = (
        back_project(attn_grad, w_o_all).astype(jnp.bfloat16).reshape(items, half_len, HEADS, HD)
    )

    def attend_back(inputs):
        query, keys, values, code_row, block_row, log_row, grad_row = inputs
        scores = scores_of(query, keys, code_row, block_row, key_pos, positions)
        probs = jnp.exp(scores - log_row[..., None])
        value_part = jnp.einsum(
            "hqk,qhd->khd", probs.astype(jnp.bfloat16), grad_row, preferred_element_type=jnp.float32
        )
        prob_grad = jnp.einsum("qhd,khd->hqk", grad_row, values, preferred_element_type=jnp.float32)
        centre = jnp.sum(probs * prob_grad, axis=-1, keepdims=True)
        score_grad = (probs * (prob_grad - centre)).astype(jnp.bfloat16)
        query_part = jnp.einsum(
            "hqk,khd->qhd", score_grad, keys, preferred_element_type=jnp.float32
        ) * (1.0 / math.sqrt(HD))
        key_part = jnp.einsum(
            "hqk,qhd->khd", score_grad, query, preferred_element_type=jnp.float32
        ) * (1.0 / math.sqrt(HD))
        return (query_part, key_part, value_part)

    query_part, key_part, value_part = lax.map(
        attend_back,
        (query_four, key_four, value_four, code_all, query_block, log_totals, mixed_grad),
    )
    key_part = key_part.reshape(items, full_len, width)
    value_part = value_part.reshape(items, full_len, width)
    away = jnp.stack([key_part[:, half_len:], value_part[:, half_len:]]).astype(low)
    back = swap(away, X).astype(f32)
    query_grad_low = query_part.reshape(rows, width).astype(jnp.bfloat16)
    key_grad_low = (key_part[:, :half_len] + back[0]).reshape(rows, width).astype(jnp.bfloat16)
    value_grad_low = (value_part[:, :half_len] + back[1]).reshape(rows, width).astype(jnp.bfloat16)
    joint_grad = jnp.concatenate([query_grad_low, key_grad_low, value_grad_low], axis=1)
    grad_qkv_part = inner(stream_low, joint_grad).astype(low)
    grad_out, grad_in = reduce_all([grad_out_part, grad_in_part], 2)
    grad_qkv, grad_o = reduce_all([grad_qkv_part, grad_o_part], 3)
    input_grad = (
        (dres_one + back_project(joint_grad, w_qkv_all))
        .astype(jnp.bfloat16)
        .reshape(items, half_len, width)
    )
    b_in_part = jnp.sum(pre_grad.astype(jnp.float32), axis=0)
    parts = [
        jnp.sum(query_grad_low.astype(jnp.float32), axis=0),
        jnp.sum(value_grad_low.astype(jnp.float32), axis=0),
        jnp.sum(attn_grad.astype(jnp.float32), axis=0),
        jnp.sum(branch_grad.astype(jnp.float32), axis=0),
        gain_one_grad,
        gain_two_grad,
        shift_one_grad,
        shift_two_grad,
    ]
    sums = sum_small(jnp.concatenate([b_in_part] + parts + [local_sums]))
    ff = b_in_part.shape[0]
    me = my_index()
    grad_b_in = lax.dynamic_slice(sums, (me * b_count,), (b_count,))
    grads = lax.dynamic_slice(sums[ff : ff + 8 * width].reshape(8, width), (0, me * share), (8, share))
    totals = sums[ff + 8 * width :]
    rms = jnp.sqrt(totals[:4] / (totals[4] * width))
    return (
        output,
        input_grad,
        grad_qkv,
        grad_o,
        grad_in,
        grad_out,
        grad_b_in,
        grads[:4],
        grads[4:6],
        grads[6:8],
        rms,
    )


def solution(mesh):
    in_specs = (
        P("dp", "ctx", None),
        P("dp"),
        P("dp", "ctx"),
        P("dp", "ctx"),
        P("dp"),
        P(("dp", "ctx"), None),
        P(("dp", "ctx"), None),
        P(("dp", "ctx"), None),
        P(("dp", "ctx"), None),
        P(("dp", "ctx")),
        P(None, ("dp", "ctx")),
        P(None, ("dp", "ctx")),
        P(None, ("dp", "ctx")),
        P("dp", "ctx", None),
    )
    out_specs = (
        P("dp", "ctx", None),
        P("dp", "ctx", None),
        P(("dp", "ctx"), None),
        P(("dp", "ctx"), None),
        P(("dp", "ctx"), None),
        P(("dp", "ctx"), None),
        P(("dp", "ctx")),
        P(None, ("dp", "ctx")),
        P(None, ("dp", "ctx")),
        P(None, ("dp", "ctx")),
        P(),
    )
    return jax.shard_map(body, mesh=mesh, in_specs=in_specs, out_specs=out_specs, check_vma=False)
```

```python
from functools import partial
import math

import jax
import jax.numpy as jnp
from jax import lax
from jax.experimental import pallas as pl
from jax.experimental.pallas import tpu as pltpu
from jax.sharding import PartitionSpec as P

HEADS = 16
HD = 64

AXES = ("dp", "ctx")
X = 1


def my_index():
    return lax.axis_index("dp") * lax.axis_size("ctx") + lax.axis_index("ctx")


def n_devices():
    return lax.axis_size("dp") * lax.axis_size("ctx")


def swap(array, bits):
    return lax.ppermute(array, AXES, [(i, i ^ bits) for i in range(n_devices())])

MESH = pl.DeviceIdType.MESH


class Place:
    def __init__(self):
        dp = lax.axis_index("dp")
        self.nz = lax.axis_size("dp") // 4
        self.x = lax.axis_index("ctx")
        self.c = dp % 2
        self.y = (dp // 2) % 2
        self.z = dp // 4

    def zth(self, k):
        z, bit = self.z, 1
        while bit < self.nz:
            if k & bit:
                z = z + bit * (1 - 2 * ((self.z // bit) % 2))
            bit *= 2
        return z

    def flips(self, y=0, c=0, x=0):
        return (
            1 - self.y if y else self.y,
            1 - self.c if c else self.c,
            1 - self.x if x else self.x,
        )

    def device(self, k=0, y=0, c=0, x=0):
        fy, fc, fx = self.flips(y, c, x)
        return ((self.zth(k) * 2 + fy) * 2 + fc, fx)

    def shard(self, k=0, y=0, c=0, x=0):
        fy, fc, fx = self.flips(y, c, x)
        return ((self.zth(k) * 2 + fy) * 2 + fc) * 2 + fx

    def column(self, y=0, c=0, x=0):
        fy, fc, fx = self.flips(y, c, x)
        return (fy * 2 + fc) * 2 + fx

    def partners(self):
        return [self.device(k=k) for k in range(1, self.nz)] + [
            self.device(x=1),
            self.device(y=1),
            self.device(c=1),
        ]


def meet(place):
    barrier = pltpu.get_barrier_semaphore()
    partners = place.partners()
    for partner in partners:
        pl.semaphore_signal(barrier, inc=1, device_id=partner, device_id_type=MESH)
    pl.semaphore_wait(barrier, len(partners))


class Sender:
    def __init__(self, send_sem, recv_sem):
        self.send_sem, self.recv_sem = send_sem, recv_sem
        self.count = 0
        self.open = []

    def send(self, src, dst, device):
        copy = pltpu.make_async_remote_copy(
            src_ref=src,
            dst_ref=dst,
            send_sem=self.send_sem.at[self.count],
            recv_sem=self.recv_sem.at[self.count],
            device_id=device,
            device_id_type=MESH,
        )
        self.count += 1
        copy.start()
        self.open.append(copy)
        return copy

    def close(self):
        for copy in self.open:
            copy.wait_send()
        self.open = []


def gather_copies(nz):
    return (nz - 1) + 2 * (nz + 2) + 5


def gather_steps(place, sender, shard, full):
    nz = place.nz
    half = nz // 2
    mine = place.column()
    own = full.at[place.z, mine]
    by_z = [sender.send(shard, own, place.device(k=k)) for k in range(1, nz)]
    from_x = [sender.send(shard, own, place.device(x=1))]
    from_y = [sender.send(shard, own, place.device(y=1))]
    yield
    for k in range(1, nz):
        by_z[k - 1].wait_recv()
        piece = full.at[place.zth(k), mine]
        from_x.append(sender.send(piece, piece, place.device(x=1)))
        from_y.append(sender.send(piece, piece, place.device(y=1)))
    line = full.at[:, mine]
    to_core = [sender.send(line, line, place.device(c=1))]
    yield
    for copy in from_x:
        copy.wait_recv()
    at_x = place.column(x=1)
    line = full.at[:, at_x]
    part = full.at[pl.ds(0, half), at_x]
    diag_a = sender.send(part, part, place.device(y=1))
    to_core.append(sender.send(line, line, place.device(c=1)))
    yield
    for copy in from_y:
        copy.wait_recv()
    at_y = place.column(y=1)
    line = full.at[:, at_y]
    part = full.at[pl.ds(half, nz - half), at_y]
    diag_b = sender.send(part, part, place.device(x=1))
    to_core.append(sender.send(line, line, place.device(c=1)))
    yield
    diag = place.column(x=1, y=1)
    for copy, start, size in ((diag_a, 0, half), (diag_b, half, nz - half)):
        copy.wait_recv()
        part = full.at[pl.ds(start, size), diag]
        to_core.append(sender.send(part, part, place.device(c=1)))
    yield
    for copy in to_core:
        copy.wait_recv()


def reduce_copies(nz):
    return 4 + 2 + 2 + 2 + nz - 1


def reduce_buffers(nz, rows, cols):
    low = jnp.bfloat16
    half = nz // 2
    return [
        pltpu.VMEM((4, nz, rows, cols), low),
        pltpu.VMEM((4, nz, rows, cols), low),
        pltpu.VMEM((half, rows, cols), low),
        pltpu.VMEM((nz - half, rows, cols), low),
        pltpu.VMEM((2, nz, rows, cols), low),
        pltpu.VMEM((nz - 1, rows, cols), low),
    ]


def add_rows(target, terms, count, rows):
    step = min(rows, 16)
    per = rows // step

    def one(j, _):
        i, start = j // per, (j % per) * step
        at = pl.ds(pl.multiple_of(start, step), step)
        total = terms[0](i, at).astype(jnp.float32)
        for term in terms[1:]:
            total = total + term(i, at).astype(jnp.float32)
        target(i, at, total)
        return 0

    lax.fori_loop(0, count * per, one, 0)


def reduce_steps(place, sender, grad, buffers, out):
    from_core, sums, diag_y, diag_x, from_xy, from_z = buffers
    nz, half = place.nz, place.nz // 2
    rows = grad.shape[2]
    low = jnp.bfloat16
    groups = ((1, 1), (0, 1), (1, 0), (0, 0))
    by_core = [
        sender.send(grad.at[:, place.column(y=fy, c=1, x=fx)], from_core.at[i], place.device(c=1))
        for i, (fy, fx) in enumerate(groups)
    ]
    yield

    def put(slot, offset=0):
        def store(i, at, value):
            sums[slot, i + offset, at, :] = value.astype(low)

        return store

    def add_core(slot):
        fy, fx = groups[slot]
        column = place.column(y=fy, x=fx)
        by_core[slot].wait_recv()
        add_rows(
            put(slot),
            [lambda i, at: grad[i, column, at, :], lambda i, at: from_core[slot, i, at, :]],
            nz,
            rows,
        )

    low_z, high_z = pl.ds(0, half), pl.ds(half, nz - half)
    add_core(0)
    by_y = sender.send(sums.at[0, low_z], diag_y, place.device(y=1))
    by_x = sender.send(sums.at[0, high_z], diag_x, place.device(x=1))
    add_core(1)
    x_high = sender.send(sums.at[1, high_z], from_xy.at[0, high_z], place.device(x=1))
    add_core(2)
    y_low = sender.send(sums.at[2, low_z], from_xy.at[1, low_z], place.device(y=1))
    yield
    add_core(3)
    by_y.wait_recv()
    add_rows(
        put(1),
        [lambda i, at: sums[1, i, at, :], lambda i, at: diag_y[i, at, :]],
        half,
        rows,
    )
    x_low = sender.send(sums.at[1, low_z], from_xy.at[0, low_z], place.device(x=1))
    by_x.wait_recv()
    add_rows(
        put(2, half),
        [lambda i, at: sums[2, i + half, at, :], lambda i, at: diag_x[i, at, :]],
        nz - half,
        rows,
    )
    y_high = sender.send(sums.at[2, high_z], from_xy.at[1, high_z], place.device(y=1))
    yield
    for copy in (x_high, y_low, x_low, y_high):
        copy.wait_recv()
    add_rows(
        put(3),
        [
            lambda i, at: sums[3, i, at, :],
            lambda i, at: from_xy[0, i, at, :],
            lambda i, at: from_xy[1, i, at, :],
        ],
        nz,
        rows,
    )
    by_z = [
        sender.send(sums.at[3, place.zth(k)], from_z.at[k - 1], place.device(k=k)) for k in range(1, nz)
    ]
    yield
    for copy in by_z:
        copy.wait_recv()

    def last(i, at, value):
        out[at, :] = value

    add_rows(
        last,
        [lambda i, at: sums[3, place.z, at, :]]
        + [lambda i, at, k=k: from_z[k, at, :] for k in range(nz - 1)],
        1,
        rows,
    )


def reduce_kernel(shapes):
    count = len(shapes)

    def kernel(*refs):
        grads, outs = refs[:count], refs[count : 2 * count]
        scratch = refs[2 * count :]
        buffers = [scratch[6 * i : 6 * i + 6] for i in range(count)]
        send_sem, recv_sem = scratch[6 * count :]
        place = Place()
        sender = Sender(send_sem, recv_sem)
        meet(place)
        steps = [reduce_steps(place, sender, g, b, o) for g, b, o in zip(grads, buffers, outs)]
        t = 0
        while steps:
            live = []
            for i, step in enumerate(steps):
                if i > t:
                    live.append(step)
                    continue
                try:
                    next(step)
                    live.append(step)
                except StopIteration:
                    pass
            steps = live
            t += 1
        sender.close()

    return kernel


def reduce_all(grads, collective_id):
    nz = lax.axis_size("dp") // 4
    n = nz * 8
    blocks = [g.reshape(nz, 8, g.shape[0] // n, g.shape[1]) for g in grads]
    copies = len(grads) * reduce_copies(nz)
    scratch = []
    for block in blocks:
        scratch += reduce_buffers(nz, block.shape[2], block.shape[3])
    return pl.pallas_call(
        reduce_kernel([b.shape for b in blocks]),
        out_shape=[jax.ShapeDtypeStruct(b.shape[2:], jnp.float32) for b in blocks],
        in_specs=[pl.BlockSpec(memory_space=pltpu.VMEM)] * len(grads),
        out_specs=[pl.BlockSpec(memory_space=pltpu.VMEM)] * len(grads),
        scratch_shapes=scratch
        + [pltpu.SemaphoreType.DMA((copies,)), pltpu.SemaphoreType.DMA((copies,))],
        compiler_params=pltpu.CompilerParams(
            collective_id=collective_id, has_side_effects=True, vmem_limit_bytes=56 << 20
        ),
    )(*blocks)


def sum_small(vector):
    bit = 1
    while bit < n_devices():
        vector = vector + swap(vector, bit)
        bit *= 2
    return vector


fill_value = -1e30
eps_norm = 1e-05
code_absent = 30000.0


def time_embed(steps, width):
    half = width // 2
    freqs = jnp.exp(jnp.arange(half, dtype=jnp.float32) * (-math.log(10000.0) / half))
    angle = steps.astype(jnp.float32)[:, None] * freqs[None, :]
    return jnp.concatenate([jnp.sin(angle), jnp.cos(angle)], axis=-1)


def layer_norm(resid, gain, shift):
    centre = resid - jnp.mean(resid, axis=-1, keepdims=True)
    spread = jnp.mean(centre * centre, axis=-1, keepdims=True)
    return centre * lax.rsqrt(spread + eps_norm) * gain + shift


def inner(left, right):
    return lax.dot_general(
        left, right, (((0,), (0,)), ((), ())), preferred_element_type=jnp.float32
    )


def back_project(grad, weight):
    return lax.dot_general(
        grad, weight, (((1,), (1,)), ((), ())), preferred_element_type=jnp.float32
    )


NN = (((1,), (0,)), ((), ()))
NT = (((1,), (1,)), ((), ()))
LOW = jnp.bfloat16
F32 = jnp.float32


def mm(left, right, dims=NN):
    return lax.dot_general(left, right, dims, preferred_element_type=F32)


def loop(count, step):
    lax.fori_loop(0, count, lambda i, _: (step(i), 0)[1], 0)


def tile(index, size):
    return pl.ds(pl.multiple_of(index * size, size), size)


def run_out(steps):
    for _ in steps:
        pass


def expand(packed, offset, share, start, length):
    n, wide = packed.shape
    place = lax.broadcasted_iota(jnp.int32, (wide, length), 1) + start
    lane = lax.broadcasted_iota(jnp.int32, (wide, length), 0)
    pick = (lane == offset + lax.rem(place, share)).astype(F32).astype(LOW)
    spread = mm(packed, pick)
    row = lax.broadcasted_iota(jnp.int32, (n, length), 0)
    column = lax.broadcasted_iota(jnp.int32, (n, length), 1) + start
    return jnp.sum(jnp.where(row == lax.div(column, share), spread, 0.0), axis=0, keepdims=True)


def normalize(resid):
    centre = resid - jnp.mean(resid, axis=-1, keepdims=True)
    spread = jnp.mean(centre * centre, axis=-1, keepdims=True)
    rstd = lax.rsqrt(spread + eps_norm)
    return centre * rstd, rstd


def column_sum(value):
    return jnp.sum(value, axis=0, keepdims=True)


def forward_kernel(by_hand, items, half_len, names_in, names_out, names_scratch, *refs):
    names = names_in + names_out + names_scratch
    r = dict(zip(names, refs))
    width = r["input"].shape[1]
    rows = items * half_len
    blocks = r["act"].shape[0]
    place = Place()
    sender = Sender(r["send"], r["recv"])
    local = r["local"]
    local_count = [0]

    def copy(src, dst):
        made = pltpu.make_async_copy(src, dst, local.at[local_count[0]])
        local_count[0] += 1
        made.start()
        return made

    saved = []
    cot_in = copy(r["cotangent"], r["cot"])
    params = ["w_qkv", "small", "w_o", "w_in", "w_out"]
    if by_hand:
        full = {p: r["all_" + p] for p in params}
        kept = [copy(r[p], full[p].at[place.z, place.column()]) for p in params]
    else:
        full = {p: r[p] for p in params}
        kept = []
    meet(place)
    for made in kept:
        made.wait()
    if by_hand:
        gens = {p: gather_steps(place, sender, r[p], full[p]) for p in params}

    def pump(*which):
        if by_hand:
            for p in which:
                next(gens[p], None)

    across = place.device(x=1)
    pump("w_qkv", "small")
    codes_over = sender.send(r["codes"], r["codes_taken"], across)
    half_item = [pl.ds(i * half_len, half_len) for i in range(items)]
    input_over = []
    for at in half_item[:2]:
        input_over.append(sender.send(r["input"].at[at], r["taken"].at[at], across))
    stream, sums = r["stream"], r["sums"]
    sums[...] = jnp.zeros_like(sums)
    valid = [r["cols"][:, items + i : items + i + 1] for i in range(items)]
    for i in range(items):
        embed = r["embed"][i : i + 1, :]

        def make_stream(j, i=i, embed=embed):
            at = pl.ds(pl.multiple_of(i * half_len + j * 32, 32), 32)
            value = r["input"][at, :].astype(F32) + embed
            stream[at, :] = value.astype(LOW)
            weight = r["cols"][tile(j, 32), items + i : items + i + 1]
            sums[0:1, :] += column_sum(value * value * weight)

        loop(half_len // 32, make_stream)
    pump("w_qkv", "small", "w_o", "w_in")
    pump("w_qkv", "small")
    pump("w_qkv", "small")
    for at in half_item[2:]:
        input_over.append(sender.send(r["input"].at[at], r["taken"].at[at], across))
    pump("w_qkv", "small", "w_o")
    pump("w_qkv", "small")
    load_qkv = [
        copy(full["w_qkv"].at[:, :, :, pl.ds(t * width, width)], r["v_qkv"].at[t]) for t in range(3)
    ]
    load_small = copy(full["small"], r["v_small"])
    load_small.wait()
    shards = r["v_small"].shape[0] * r["v_small"].shape[1]
    for d in range(shards):
        r["packed"][d : d + 1, :] = r["v_small"][d // 8, d % 8, 0:1, :]
    packed = r["packed"][...].astype(LOW)
    share = width // shards
    b_share = share * blocks
    vectors, b_in = r["vectors"], r["v_b_in"]
    for t in range(8):
        vectors[t : t + 1, :] = expand(packed, b_share + t * share, share, 0, width)
    for t in range(blocks):
        b_in[t : t + 1, :] = expand(packed, 0, b_share, t * width, width)
    bias_q, bias_v, bias_o, bias_out = (vectors[t : t + 1, :] for t in range(4))
    gain_one, gain_two, shift_one, shift_two = (vectors[t : t + 1, :] for t in range(4, 8))
    heads = r["heads"]
    step = 256

    def weight(name, t, at):
        value = r[name][t, :, :, :, at]
        return value.reshape(-1, value.shape[-1])

    for made in load_qkv:
        made.wait()

    def project_own(j):
        at = tile(j, step)
        mine = stream[0:rows, :]
        heads[0, :, at] = (mm(mine, weight("v_qkv", 0, at)) + vectors[0:1, at]).astype(LOW)
        heads[1, :, at] = mm(mine, weight("v_qkv", 1, at)).astype(LOW)
        heads[3, :, at] = (mm(mine, weight("v_qkv", 2, at)) + vectors[1:2, at]).astype(LOW)

    def project_other(j):
        at = tile(j, step)
        theirs = stream[rows : 2 * rows, :]
        heads[2, :, at] = mm(theirs, weight("v_qkv", 1, at)).astype(LOW)
        heads[4, :, at] = (mm(theirs, weight("v_qkv", 2, at)) + vectors[1:2, at]).astype(LOW)

    pump("w_in")
    loop(width // step, project_own)
    pump("w_o", "w_out")
    codes_over.wait_recv()
    same = lax.broadcasted_iota(jnp.int32, (half_len, half_len), 0) == lax.broadcasted_iota(
        jnp.int32, (half_len, half_len), 1
    )
    for i in range(items):
        asked = r["cols"][:, i : i + 1]
        own = (r["codes"][i : i + 1, :] <= asked) | same
        other = r["codes_taken"][i : i + 1, :] <= asked
        r["permit"][i, :, 0:half_len] = jnp.where(own, 0.0, fill_value)
        r["permit"][i, :, half_len : 2 * half_len] = jnp.where(other, 0.0, fill_value)
    for made in input_over:
        made.wait_recv()
    for i in range(items):
        embed = r["embed"][i : i + 1, :]

        def make_other(j, i=i, embed=embed):
            at = pl.ds(pl.multiple_of(i * half_len + j * 32, 32), 32)
            to = pl.ds(pl.multiple_of(rows + i * half_len + j * 32, 32), 32)
            stream[to, :] = (r["taken"][at, :].astype(F32) + embed).astype(LOW)

        loop(half_len // 32, make_other)
    loop(width // step, project_other)
    saved.append(copy(heads, r["save_heads"]))
    saved.append(copy(r["permit"], r["save_permit"]))
    pump("w_o", "w_o", "w_in")
    lane = lax.broadcasted_iota(jnp.int32, (half_len, 2 * HD), 1)
    key_lane = lax.broadcasted_iota(jnp.int32, (2 * half_len, 2 * HD), 1)

    def attend(i):
        at_rows = pl.ds(i * half_len, half_len)

        def pair(p):
            at = tile(p, 2 * HD)
            query = heads[0, at_rows, at] * (1.0 / math.sqrt(HD))
            keys = jnp.concatenate([heads[1, at_rows, at], heads[2, at_rows, at]], axis=0)
            values = jnp.concatenate([heads[3, at_rows, at], heads[4, at_rows, at]], axis=0)
            nothing = jnp.zeros((), LOW)
            mixed = None
            logs = r["logs"][i]
            for h in range(2):
                scores = mm(jnp.where((lane < HD) == (h == 0), query, nothing), keys, NT) + r["permit"][i]
                peak = jnp.max(scores, axis=1, keepdims=True)
                expo = jnp.exp(scores - peak)
                total = jnp.sum(expo, axis=1, keepdims=True)
                probs = (expo * (1.0 / total)).astype(LOW)
                part = mm(probs, jnp.where((key_lane < HD) == (h == 0), values, nothing))
                mixed = part if mixed is None else mixed + part
                logs = jnp.where(lane == 2 * p + h, peak + jnp.log(total), logs)
            r["logs"][i] = logs
            stream[at_rows, at] = mixed.astype(LOW)

        loop(width // (2 * HD), pair)

    attend(0)
    pump("w_in", "w_in")
    if items > 1:
        attend(1)
    pump("w_in", "w_out")
    for i in range(2, items):
        attend(i)
    mixed = stream
    saved.append(copy(stream.at[pl.ds(0, rows)], r["save_mixed"]))
    saved.append(copy(r["logs"], r["save_logs"]))
    if by_hand:
        run_out(gens["w_o"])
    load_o = copy(full["w_o"], r["v_o"])
    load_o.wait()
    xhat = r["xhat"]
    for i in range(items):
        at_rows = pl.ds(i * half_len, half_len)
        w_o = r["v_o"][...].reshape(width, width)
        r["work"][...] = mm(mixed[at_rows, :], w_o) + bias_o
        embed = r["embed"][i : i + 1, :]

        def first_norm(j, i=i, embed=embed):
            at = pl.ds(pl.multiple_of(i * half_len + j * 32, 32), 32)
            to = pl.ds(pl.multiple_of(rows + i * half_len + j * 32, 32), 32)
            weight_rows = r["cols"][tile(j, 32), items + i : items + i + 1]
            attn = r["work"][tile(j, 32), :]
            sums[1:2, :] += column_sum(attn * attn * weight_rows)
            value, rstd = normalize(r["input"][at, :].astype(F32) + embed + attn)
            xhat[at, :] = value
            r["rstd"][at, :] = jnp.broadcast_to(rstd, (32, 128))
            stream[to, :] = (value * gain_one + shift_one).astype(LOW)

        loop(half_len // 32, first_norm)
    saved.append(copy(xhat, r["save_xhat"]))
    saved.append(copy(r["rstd"], r["save_rstd"]))
    if by_hand:
        run_out(gens["w_in"])
    load_in = [copy(full["w_in"].at[:, :, :, pl.ds(t * width, width)], r["v_in"].at[t]) for t in range(blocks)]
    for made in saved[:1]:
        made.wait()
    act, slope = heads, r["slope"]
    for t in range(blocks):
        load_in[t].wait()

        def feed(j, t=t):
            at = tile(j, step)
            w_in = weight("v_in", t, at)
            for i in range(items):
                own = pl.ds(i * half_len, half_len)
                pre = mm(stream[pl.ds(rows + i * half_len, half_len), :], w_in) + b_in[t : t + 1, at]
                cdf = 0.5 + 0.5 * lax.erf(pre * (1.0 / math.sqrt(2.0)))
                act[t, own, at] = (pre * cdf).astype(LOW)
                pdf = jnp.exp(pre * pre * -0.5) * (1.0 / math.sqrt(2.0 * math.pi))
                slope[t, own, at] = (cdf + pre * pdf).astype(LOW)

        loop(width // step, feed)
        if t == 1:
            pump("w_out")
        if t == 2:
            pump("w_out")
    saved.append(copy(heads.at[pl.ds(0, blocks)], r["act"]))
    saved.append(copy(slope, r["save_slope"]))
    if by_hand:
        run_out(gens["w_out"])
    load_out = [copy(full["w_out"].at[t], r["v_out"].at[t]) for t in range(blocks)]
    for made in load_out:
        made.wait()
    cot_in.wait()
    saved[2].wait()
    for i in range(items):
        at_rows = pl.ds(i * half_len, half_len)
        total = None
        for t in range(blocks):
            part = mm(act[t, at_rows, :], r["v_out"][t].reshape(width, width))
            total = part if total is None else total + part
        r["work"][...] = total + bias_out

        def second_norm(j, i=i):
            at = pl.ds(pl.multiple_of(i * half_len + j * 32, 32), 32)
            to = pl.ds(pl.multiple_of(rows + i * half_len + j * 32, 32), 32)
            weight_rows = r["cols"][tile(j, 32), items + i : items + i + 1]
            branch = r["work"][tile(j, 32), :]
            sums[2:3, :] += column_sum(branch * branch * weight_rows)
            value, rstd = normalize(xhat[at, :] * gain_one + shift_one + branch)
            result = value * gain_two + shift_two
            sums[3:4, :] += column_sum(result * result * weight_rows)
            stream[at, :] = result.astype(LOW)
            grad = r["cot"][at, :].astype(F32)
            sums[5:6, :] += column_sum(grad * value)
            sums[6:7, :] += column_sum(grad)
            scaled = grad * gain_two
            back = rstd * (
                scaled
                - jnp.mean(scaled, axis=-1, keepdims=True)
                - value * jnp.mean(scaled * value, axis=-1, keepdims=True)
            )
            r["back"][at, :] = back
            back_low = back.astype(LOW)
            stream[to, :] = back_low
            sums[4:5, :] += column_sum(back_low.astype(F32))

        loop(half_len // 32, second_norm)
    saved.append(copy(stream.at[pl.ds(0, rows)], r["output"]))
    saved.append(copy(stream.at[pl.ds(rows, rows)], r["save_back_low"]))
    saved.append(copy(r["back"], r["save_back"]))
    saved.append(copy(vectors, r["save_vectors"]))
    for i, made in enumerate(saved):
        if i not in (0, 2):
            made.wait()
    sender.close()


def forward(by_hand, items, half_len, weights, small, block_input, embed, codes, cols, cotangent, collective_id):
    rows, width = block_input.shape
    full_len = 2 * half_len
    blocks = 4
    nz = lax.axis_size("dp") // 4
    shape = jax.ShapeDtypeStruct
    vmem, hbm = pl.BlockSpec(memory_space=pltpu.VMEM), pl.BlockSpec(memory_space=pl.ANY)
    params = ["w_qkv", "small", "w_o", "w_in", "w_out"]
    ins = dict(zip(params, [weights[0], small] + weights[1:]))
    spaces_in = [vmem if by_hand else hbm] * 5
    ins.update(input=block_input, embed=embed, codes=codes, cols=cols, cotangent=cotangent)
    spaces_in += [vmem] * 4 + [hbm]
    outs, spaces_out = {}, []
    if by_hand:
        for p in params:
            outs["all_" + p] = shape((nz, 8) + ins[p].shape, ins[p].dtype)
            spaces_out.append(hbm)
    outs.update(
        save_heads=shape((5, rows, width), LOW),
        save_permit=shape((items, half_len, full_len), F32),
        save_mixed=shape((rows, width), LOW),
        save_logs=shape((items, half_len, 128), F32),
        save_xhat=shape((rows, width), F32),
        save_rstd=shape((rows, 128), F32),
        act=shape((blocks, rows, width), LOW),
        save_slope=shape((blocks, rows, width), LOW),
        output=shape((rows, width), LOW),
        save_back_low=shape((rows, width), LOW),
        save_back=shape((rows, width), F32),
        save_vectors=shape((8, width), F32),
        sums=shape((8, width), F32),
    )
    spaces_out += [hbm] * 12 + [vmem]
    if by_hand:
        small_full = (nz, 8) + small.shape
    else:
        small_full = small.shape
    copies = 5 * gather_copies(nz) + items + 1
    scratch = dict(
        send=pltpu.SemaphoreType.DMA((copies,)),
        recv=pltpu.SemaphoreType.DMA((copies,)),
        local=pltpu.SemaphoreType.DMA((40,)),
        taken=pltpu.VMEM((rows, width), LOW),
        codes_taken=pltpu.VMEM(codes.shape, F32),
        stream=pltpu.VMEM((2 * rows, width), LOW),
        v_qkv=pltpu.VMEM((3, 4, 8, 32, width), LOW),
        v_small=pltpu.VMEM(small_full, F32),
        packed=pltpu.VMEM((small_full[0] * 8, small_full[-1]), F32),
        vectors=pltpu.VMEM((8, width), F32),
        v_b_in=pltpu.VMEM((8, width), F32),
        heads=pltpu.VMEM((5, rows, width), LOW),
        permit=pltpu.VMEM((items, half_len, full_len), F32),
        logs=pltpu.VMEM((items, half_len, 128), F32),
        v_o=pltpu.VMEM((4, 8, 32, width), LOW),
        work=pltpu.VMEM((half_len, width), F32),
        xhat=pltpu.VMEM((rows, width), F32),
        rstd=pltpu.VMEM((rows, 128), F32),
        v_in=pltpu.VMEM((blocks, 4, 8, 32, width), LOW),
        slope=pltpu.VMEM((blocks, rows, width), LOW),
        v_out=pltpu.VMEM((blocks, 8, 128, width), LOW),
        cot=pltpu.VMEM((rows, width), LOW),
        back=pltpu.VMEM((rows, width), F32),
    )
    results = pl.pallas_call(
        partial(forward_kernel, by_hand, items, half_len, list(ins), list(outs), list(scratch)),
        out_shape=list(outs.values()),
        in_specs=spaces_in,
        out_specs=spaces_out,
        scratch_shapes=list(scratch.values()),
        compiler_params=pltpu.CompilerParams(
            collective_id=collective_id, has_side_effects=True, vmem_limit_bytes=62 << 20
        ),
    )(*ins.values())
    return dict(zip(outs, results))


def scores_of(query, keys, code_row, query_block, key_pos, positions):
    permit = (code_row[None, :] <= query_block[:, None]) | (key_pos[None, :] == positions[:, None])
    raw = jnp.einsum("qhd,khd->hqk", query, keys, preferred_element_type=jnp.float32) * (
        1.0 / math.sqrt(HD)
    )
    return jnp.where(permit[None], raw, fill_value)


def body(
    block_input,
    lengths,
    mask,
    blocks,
    timesteps,
    w_qkv,
    w_o,
    w_in,
    w_out,
    b_in,
    biases,
    gains,
    shifts,
    cotangent,
):
    items, half_len, width = block_input.shape
    rows = items * half_len
    f32, low = jnp.float32, jnp.bfloat16
    n = n_devices()
    positions = lax.axis_index("ctx") * half_len + jnp.arange(half_len, dtype=jnp.int32)
    other_positions = (1 - lax.axis_index("ctx")) * half_len + jnp.arange(half_len, dtype=jnp.int32)
    key_pos = jnp.concatenate([positions, other_positions])
    valid = (positions[None, :] < lengths[:, None]) & ((mask == 1) | (positions[None, :] == 0))
    code_local = jnp.where(valid, blocks.astype(f32), code_absent)
    share = width // n
    b_count = b_in.shape[0]
    share = width // n
    b_count = b_in.shape[0]
    small = jnp.concatenate([b_in, biases.reshape(-1), gains.reshape(-1), shifts.reshape(-1)])
    small_wide = -(-small.shape[0] // 128) * 128
    small = jnp.pad(small.astype(f32), (0, small_wide - small.shape[0]))
    small = jnp.broadcast_to(small[None, :], (8, small_wide))
    by_hand = w_qkv.shape[0] == 32
    weights = [w_qkv, w_o, w_in, w_out]
    if not by_hand:
        weights = [lax.all_gather(w, AXES, axis=0, tiled=True) for w in weights]
        weights = [w.reshape(4, 8, w.shape[0] // 32, w.shape[1]) for w in weights]
        small = lax.all_gather(small, AXES, axis=0).reshape(n // 8, 8, 8, small_wide)
    embed = time_embed(timesteps, width)
    embed_rows = jnp.pad(embed, ((0, 8 - items), (0, 0)))
    codes = jnp.pad(code_local, ((0, 8 - items), (0, 0)))
    cols = jnp.concatenate([blocks.astype(f32), valid.astype(f32)], axis=0).T
    cols = jnp.pad(cols, ((0, 0), (0, 128 - 2 * items)))
    fw = forward(
        by_hand,
        items,
        half_len,
        weights,
        small,
        block_input.reshape(rows, width),
        embed_rows,
        codes,
        cols,
        cotangent.reshape(rows, width),
        1,
    )
    if by_hand:
        weights = [fw["all_" + p] for p in ("w_qkv", "w_o", "w_in", "w_out")]
    w_qkv_all, w_o_all, w_in_all, w_out_all = (w.reshape(-1, w.shape[-1]) for w in weights)
    gain_full = fw["save_vectors"][4:6]
    shift_full = fw["save_vectors"][6:8]
    code_all = jnp.concatenate([code_local, swap(code_local, X)], axis=1)
    stream = (block_input.astype(f32) + embed[:, None, :]).reshape(rows, width)
    stream_low = stream.astype(low)
    full_len = 2 * half_len
    saved_heads = fw["save_heads"].reshape(5, items, half_len, width)
    query_four = saved_heads[0].reshape(items, half_len, HEADS, HD)
    key_four = jnp.concatenate([saved_heads[1], saved_heads[2]], axis=1).reshape(items, full_len, HEADS, HD)
    value_four = jnp.concatenate([saved_heads[3], saved_heads[4]], axis=1).reshape(items, full_len, HEADS, HD)
    query_block = blocks.astype(f32)
    log_totals = fw["save_logs"][:, :, :HEADS].transpose(0, 2, 1)
    mixed_low = fw["save_mixed"]
    act_low = fw["act"].transpose(1, 0, 2).reshape(rows, -1)
    slope = fw["save_slope"].transpose(1, 0, 2).reshape(rows, -1)
    xhat_one = fw["save_xhat"]
    rstd_one = fw["save_rstd"][:, :1]
    hidden_low = (xhat_one * gain_full[0] + shift_full[0]).astype(low)
    output = fw["output"].reshape(items, half_len, width)
    dres_two = fw["save_back"]
    branch_grad = fw["save_back_low"]
    fsums = fw["sums"]
    local_sums = jnp.concatenate([jnp.sum(fsums[:4], axis=1), jnp.sum(valid.astype(f32))[None]])
    gain_two_grad, shift_two_grad = fsums[5], fsums[6]

    grad_out_part = inner(act_low, branch_grad).astype(low)
    act_grad = back_project(branch_grad, w_out_all)
    pre_grad = (act_grad * slope.astype(f32)).astype(low)
    grad_in_part = inner(hidden_low, pre_grad).astype(low)
    dhidden = dres_two + back_project(pre_grad, w_in_all)
    scaled = dhidden * gain_full[0]
    dres_one = rstd_one * (
        scaled
        - jnp.mean(scaled, axis=-1, keepdims=True)
        - xhat_one * jnp.mean(scaled * xhat_one, axis=-1, keepdims=True)
    )
    gain_one_grad = jnp.sum(dhidden * xhat_one, axis=0)
    shift_one_grad = jnp.sum(dhidden, axis=0)
    attn_grad = dres_one.astype(jnp.bfloat16)
    grad_o_part = inner(mixed_low, attn_grad).astype(low)
    mixed_grad = (
        back_project(attn_grad, w_o_all).astype(jnp.bfloat16).reshape(items, half_len, HEADS, HD)
    )

    def attend_back(inputs):
        query, keys, values, code_row, block_row, log_row, grad_row = inputs
        scores = scores_of(query, keys, code_row, block_row, key_pos, positions)
        probs = jnp.exp(scores - log_row[..., None])
        value_part = jnp.einsum(
            "hqk,qhd->khd", probs.astype(jnp.bfloat16), grad_row, preferred_element_type=jnp.float32
        )
        prob_grad = jnp.einsum("qhd,khd->hqk", grad_row, values, preferred_element_type=jnp.float32)
        centre = jnp.sum(probs * prob_grad, axis=-1, keepdims=True)
        score_grad = (probs * (prob_grad - centre)).astype(jnp.bfloat16)
        query_part = jnp.einsum(
            "hqk,khd->qhd", score_grad, keys, preferred_element_type=jnp.float32
        ) * (1.0 / math.sqrt(HD))
        key_part = jnp.einsum(
            "hqk,qhd->khd", score_grad, query, preferred_element_type=jnp.float32
        ) * (1.0 / math.sqrt(HD))
        return (query_part, key_part, value_part)

    query_part, key_part, value_part = lax.map(
        attend_back,
        (query_four, key_four, value_four, code_all, query_block, log_totals, mixed_grad),
    )
    key_part = key_part.reshape(items, full_len, width)
    value_part = value_part.reshape(items, full_len, width)
    away = jnp.stack([key_part[:, half_len:], value_part[:, half_len:]]).astype(low)
    back = swap(away, X).astype(f32)
    query_grad_low = query_part.reshape(rows, width).astype(jnp.bfloat16)
    key_grad_low = (key_part[:, :half_len] + back[0]).reshape(rows, width).astype(jnp.bfloat16)
    value_grad_low = (value_part[:, :half_len] + back[1]).reshape(rows, width).astype(jnp.bfloat16)
    joint_grad = jnp.concatenate([query_grad_low, key_grad_low, value_grad_low], axis=1)
    grad_qkv_part = inner(stream_low, joint_grad).astype(low)
    if by_hand:
        grad_out, grad_in = reduce_all([grad_out_part, grad_in_part], 2)
        grad_qkv, grad_o = reduce_all([grad_qkv_part, grad_o_part], 3)
    else:
        grad_out, grad_in, grad_qkv, grad_o = (
            lax.psum_scatter(part.astype(f32), AXES, scatter_dimension=0, tiled=True)
            for part in (grad_out_part, grad_in_part, grad_qkv_part, grad_o_part)
        )
    input_grad = (
        (dres_one + back_project(joint_grad, w_qkv_all))
        .astype(jnp.bfloat16)
        .reshape(items, half_len, width)
    )
    b_in_part = jnp.sum(pre_grad.astype(jnp.float32), axis=0)
    parts = [
        jnp.sum(query_grad_low.astype(jnp.float32), axis=0),
        jnp.sum(value_grad_low.astype(jnp.float32), axis=0),
        jnp.sum(attn_grad.astype(jnp.float32), axis=0),
        fsums[4],
        gain_one_grad,
        gain_two_grad,
        shift_one_grad,
        shift_two_grad,
    ]
    sums = sum_small(jnp.concatenate([b_in_part] + parts + [local_sums]))
    ff = b_in_part.shape[0]
    me = my_index()
    grad_b_in = lax.dynamic_slice(sums, (me * b_count,), (b_count,))
    grads = lax.dynamic_slice(sums[ff : ff + 8 * width].reshape(8, width), (0, me * share), (8, share))
    totals = sums[ff + 8 * width :]
    rms = jnp.sqrt(totals[:4] / (totals[4] * width))
    return (
        output,
        input_grad,
        grad_qkv,
        grad_o,
        grad_in,
        grad_out,
        grad_b_in,
        grads[:4],
        grads[4:6],
        grads[6:8],
        rms,
    )


def solution(mesh):
    in_specs = (
        P("dp", "ctx", None),
        P("dp"),
        P("dp", "ctx"),
        P("dp", "ctx"),
        P("dp"),
        P(("dp", "ctx"), None),
        P(("dp", "ctx"), None),
        P(("dp", "ctx"), None),
        P(("dp", "ctx"), None),
        P(("dp", "ctx")),
        P(None, ("dp", "ctx")),
        P(None, ("dp", "ctx")),
        P(None, ("dp", "ctx")),
        P("dp", "ctx", None),
    )
    out_specs = (
        P("dp", "ctx", None),
        P("dp", "ctx", None),
        P(("dp", "ctx"), None),
        P(("dp", "ctx"), None),
        P(("dp", "ctx"), None),
        P(("dp", "ctx"), None),
        P(("dp", "ctx")),
        P(None, ("dp", "ctx")),
        P(None, ("dp", "ctx")),
        P(None, ("dp", "ctx")),
        P(),
    )
    return jax.shard_map(body, mesh=mesh, in_specs=in_specs, out_specs=out_specs, check_vma=False)
```

```python
from functools import partial
import math

import jax
import jax.numpy as jnp
from jax import lax
from jax.experimental import pallas as pl
from jax.experimental.pallas import tpu as pltpu
from jax.sharding import PartitionSpec as P

HEADS = 16
HD = 64

AXES = ("dp", "ctx")
X = 1


def my_index():
    return lax.axis_index("dp") * lax.axis_size("ctx") + lax.axis_index("ctx")


def n_devices():
    return lax.axis_size("dp") * lax.axis_size("ctx")


fill_value = -1e30
eps_norm = 1e-05
code_absent = 30000.0


def time_embed(steps, width):
    half = width // 2
    freqs = jnp.exp(jnp.arange(half, dtype=jnp.float32) * (-math.log(10000.0) / half))
    angle = steps.astype(jnp.float32)[:, None] * freqs[None, :]
    return jnp.concatenate([jnp.sin(angle), jnp.cos(angle)], axis=-1)


MESH = pl.DeviceIdType.MESH


class Place:
    def __init__(self):
        dp = lax.axis_index("dp")
        self.nz = lax.axis_size("dp") // 4
        self.x = lax.axis_index("ctx")
        self.c = dp % 2
        self.y = (dp // 2) % 2
        self.z = dp // 4

    def zth(self, k):
        z, bit = self.z, 1
        while bit < self.nz:
            if k & bit:
                z = z + bit * (1 - 2 * ((self.z // bit) % 2))
            bit *= 2
        return z

    def flips(self, y=0, c=0, x=0):
        return (
            1 - self.y if y else self.y,
            1 - self.c if c else self.c,
            1 - self.x if x else self.x,
        )

    def device(self, k=0, y=0, c=0, x=0):
        fy, fc, fx = self.flips(y, c, x)
        return ((self.zth(k) * 2 + fy) * 2 + fc, fx)

    def shard(self, k=0, y=0, c=0, x=0):
        fy, fc, fx = self.flips(y, c, x)
        return ((self.zth(k) * 2 + fy) * 2 + fc) * 2 + fx

    def column(self, y=0, c=0, x=0):
        fy, fc, fx = self.flips(y, c, x)
        return (fy * 2 + fc) * 2 + fx

    def partners(self):
        return [self.device(k=k) for k in range(1, self.nz)] + [
            self.device(x=1),
            self.device(y=1),
            self.device(c=1),
        ]


def meet(place):
    barrier = pltpu.get_barrier_semaphore()
    partners = place.partners()
    for partner in partners:
        pl.semaphore_signal(barrier, inc=1, device_id=partner, device_id_type=MESH)
    pl.semaphore_wait(barrier, len(partners))


class Sender:
    def __init__(self, send_sem, recv_sem):
        self.send_sem, self.recv_sem = send_sem, recv_sem
        self.count = 0
        self.open = []

    def send(self, src, dst, device):
        copy = pltpu.make_async_remote_copy(
            src_ref=src,
            dst_ref=dst,
            send_sem=self.send_sem.at[self.count],
            recv_sem=self.recv_sem.at[self.count],
            device_id=device,
            device_id_type=MESH,
        )
        self.count += 1
        copy.start()
        self.open.append(copy)
        return copy

    def close(self):
        for copy in self.open:
            copy.wait_send()
        self.open = []


def gather_copies(nz):
    return (nz - 1) + 2 * (nz + 2) + 5


def gather_steps(place, sender, shard, full):
    nz = place.nz
    half = nz // 2
    mine = place.column()
    own = full.at[place.z, mine]
    by_z = [sender.send(shard, own, place.device(k=k)) for k in range(1, nz)]
    from_x = [sender.send(shard, own, place.device(x=1))]
    from_y = [sender.send(shard, own, place.device(y=1))]
    yield
    for k in range(1, nz):
        by_z[k - 1].wait_recv()
        piece = full.at[place.zth(k), mine]
        from_x.append(sender.send(piece, piece, place.device(x=1)))
        from_y.append(sender.send(piece, piece, place.device(y=1)))
    line = full.at[:, mine]
    to_core = [sender.send(line, line, place.device(c=1))]
    yield
    for copy in from_x:
        copy.wait_recv()
    at_x = place.column(x=1)
    line = full.at[:, at_x]
    part = full.at[pl.ds(0, half), at_x]
    diag_a = sender.send(part, part, place.device(y=1))
    to_core.append(sender.send(line, line, place.device(c=1)))
    yield
    for copy in from_y:
        copy.wait_recv()
    at_y = place.column(y=1)
    line = full.at[:, at_y]
    part = full.at[pl.ds(half, nz - half), at_y]
    diag_b = sender.send(part, part, place.device(x=1))
    to_core.append(sender.send(line, line, place.device(c=1)))
    yield
    diag = place.column(x=1, y=1)
    for copy, start, size in ((diag_a, 0, half), (diag_b, half, nz - half)):
        copy.wait_recv()
        part = full.at[pl.ds(start, size), diag]
        to_core.append(sender.send(part, part, place.device(c=1)))
    yield
    for copy in to_core:
        copy.wait_recv()

NN = (((1,), (0,)), ((), ()))
NT = (((1,), (1,)), ((), ()))
TN = (((0,), (0,)), ((), ()))
LOW = jnp.bfloat16
F32 = jnp.float32


def mm(left, right, dims=NN):
    return lax.dot_general(left, right, dims, preferred_element_type=F32)


def loop(count, step):
    lax.fori_loop(0, count, lambda i, _: (step(i), 0)[1], 0)


def tile(index, size):
    return pl.ds(pl.multiple_of(index * size, size), size)


def run_out(steps):
    for _ in steps:
        pass


def expand(packed, offset, share, start, length):
    n, wide = packed.shape
    place = lax.broadcasted_iota(jnp.int32, (wide, length), 1) + start
    lane = lax.broadcasted_iota(jnp.int32, (wide, length), 0)
    pick = (lane == offset + lax.rem(place, share)).astype(F32).astype(LOW)
    spread = mm(packed, pick)
    row = lax.broadcasted_iota(jnp.int32, (n, length), 0)
    column = lax.broadcasted_iota(jnp.int32, (n, length), 1) + start
    return jnp.sum(jnp.where(row == lax.div(column, share), spread, 0.0), axis=0, keepdims=True)


def normalize(resid):
    centre = resid - jnp.mean(resid, axis=-1, keepdims=True)
    spread = jnp.mean(centre * centre, axis=-1, keepdims=True)
    rstd = lax.rsqrt(spread + eps_norm)
    return centre * rstd, rstd


def column_sum(value):
    return jnp.sum(value, axis=0, keepdims=True)


def reduce_copies(nz):
    return 4 + 2 + 4 + nz - 1


def reduce_buffers(nz, rows, cols):
    return dict(
        core=pltpu.VMEM((4, nz, rows, cols), LOW),
        diag=pltpu.VMEM((nz, rows, cols), LOW),
        line=pltpu.VMEM((2, nz, rows, cols), LOW),
        column=pltpu.VMEM((nz - 1, rows, cols), LOW),
    )


def add_rows(store, terms, count, rows):
    step = min(rows, 16)
    per = rows // step

    def one(j):
        i, start = j // per, (j % per) * step
        at = pl.ds(pl.multiple_of(start, step), step)
        total = terms[0](i, at).astype(F32)
        for term in terms[1:]:
            total = total + term(i, at).astype(F32)
        store(i, at, total)

    loop(count * per, one)


def reduce_steps(place, sender, grad, buffers, out, split):
    nz = place.nz
    rows = grad.shape[2]
    core, diag, line, column = (buffers[k] for k in ("core", "diag", "line", "column"))
    groups = ((1, 1), (0, 1), (1, 0), (0, 0))
    here = [place.column(y=fy, x=fx) for fy, fx in groups]
    by_core = [
        sender.send(grad.at[:, place.column(y=fy, c=1, x=fx)], core.at[i], place.device(c=1))
        for i, (fy, fx) in enumerate(groups)
    ]
    yield

    def put(slot, start=0):
        def store(i, at, value):
            grad[i + start, here[slot], at, :] = value.astype(LOW)

        return store

    def held(slot, start=0):
        return lambda i, at: grad[i + start, here[slot], at, :]

    def add_core(slot):
        by_core[slot].wait_recv()
        add_rows(put(slot), [held(slot), lambda i, at: core[slot, i, at, :]], nz, rows)

    def part(slot, start, size):
        return grad.at[pl.ds(start, size), here[slot]]

    low, high = pl.ds(0, split), pl.ds(split, nz - split)
    by_y = by_x = x_high = y_low = x_low = y_high = None
    add_core(0)
    if split > 0:
        by_y = sender.send(part(0, 0, split), diag.at[low], place.device(y=1))
    if split < nz:
        by_x = sender.send(part(0, split, nz - split), diag.at[high], place.device(x=1))
    add_core(1)
    if split < nz:
        x_high = sender.send(part(1, split, nz - split), line.at[0, high], place.device(x=1))
    add_core(2)
    if split > 0:
        y_low = sender.send(part(2, 0, split), line.at[1, low], place.device(y=1))
    add_core(3)
    yield
    if split > 0:
        by_y.wait_recv()
        add_rows(put(1), [held(1), lambda i, at: diag[i, at, :]], split, rows)
        x_low = sender.send(part(1, 0, split), line.at[0, low], place.device(x=1))
    if split < nz:
        by_x.wait_recv()
        add_rows(put(2, split), [held(2, split), lambda i, at: diag[i + split, at, :]], nz - split, rows)
        y_high = sender.send(part(2, split, nz - split), line.at[1, high], place.device(y=1))
    yield
    for copy in (x_high, y_low, x_low, y_high):
        if copy is not None:
            copy.wait_recv()
    add_rows(
        put(3),
        [held(3), lambda i, at: line[0, i, at, :], lambda i, at: line[1, i, at, :]],
        nz,
        rows,
    )
    by_z = [
        sender.send(grad.at[place.zth(k), here[3]], column.at[k - 1], place.device(k=k))
        for k in range(1, nz)
    ]
    yield
    for copy in by_z:
        copy.wait_recv()

    def last(i, at, value):
        out[at, :] = value

    add_rows(
        last,
        [lambda i, at: grad[place.z, here[3], at, :]]
        + [lambda i, at, k=k: column[k, at, :] for k in range(nz - 1)],
        1,
        rows,
    )


def sum_steps(place, sender, levels, taken):
    partners = [place.device(c=1), place.device(x=1), place.device(y=1)]
    bit = 1
    while bit < place.nz:
        partners.append(place.device(k=bit))
        bit *= 2
    for s, partner in enumerate(partners):
        copy = sender.send(levels.at[s], taken.at[s], partner)
        yield
        copy.wait_recv()
        levels[s + 1] = levels[s] + taken[s]


def forward_kernel(by_hand, items, half_len, names_in, names_out, names_scratch, *refs):
    names = names_in + names_out + names_scratch
    r = dict(zip(names, refs))
    width = r["input"].shape[1]
    rows = items * half_len
    blocks = r["act"].shape[0]
    place = Place()
    sender = Sender(r["send"], r["recv"])
    local = r["local"]
    local_count = [0]

    def copy(src, dst):
        made = pltpu.make_async_copy(src, dst, local.at[local_count[0]])
        local_count[0] += 1
        made.start()
        return made

    saved = []
    cot_in = copy(r["cotangent"], r["cot"])
    params = ["w_qkv", "small", "w_o", "w_in", "w_out"]
    if by_hand:
        full = {p: r["all_" + p] for p in params}
        kept = [copy(r[p], full[p].at[place.z, place.column()]) for p in params]
    else:
        full = {p: r[p] for p in params}
        kept = []
    meet(place)
    for made in kept:
        made.wait()
    if by_hand:
        gens = {p: gather_steps(place, sender, r[p], full[p]) for p in params}

    def pump(*which):
        if by_hand:
            for p in which:
                next(gens[p], None)

    across = place.device(x=1)
    pump("w_qkv", "small")
    codes_over = sender.send(r["codes"], r["codes_taken"], across)
    cols_over = sender.send(r["cols"], r["cols_taken"], across)
    half_item = [pl.ds(i * half_len, half_len) for i in range(items)]
    input_over = []
    for at in half_item[:2]:
        input_over.append(sender.send(r["input"].at[at], r["taken"].at[at], across))
    stream, sums = r["stream"], r["sums"]
    sums[...] = jnp.zeros_like(sums)
    sums[7:8, 0:128] = column_sum(r["cols"][...])
    for i in range(items):
        embed = r["embed"][i : i + 1, :]

        def make_stream(j, i=i, embed=embed):
            at = pl.ds(pl.multiple_of(i * half_len + j * 32, 32), 32)
            value = r["input"][at, :].astype(F32) + embed
            stream[at, :] = value.astype(LOW)
            weight = r["cols"][tile(j, 32), items + i : items + i + 1]
            sums[0:1, :] += column_sum(value * value * weight)

        loop(half_len // 32, make_stream)
    save_stream = copy(stream.at[pl.ds(0, rows)], r["save_stream"])
    pump("w_qkv", "small", "w_o", "w_in")
    pump("w_qkv", "small")
    pump("w_qkv", "small")
    for at in half_item[2:]:
        input_over.append(sender.send(r["input"].at[at], r["taken"].at[at], across))
    pump("w_qkv", "small", "w_o")
    pump("w_qkv", "small")
    load_qkv = [
        copy(full["w_qkv"].at[:, :, :, pl.ds(t * width, width)], r["v_qkv"].at[t]) for t in range(3)
    ]
    load_small = copy(full["small"], r["v_small"])
    load_small.wait()
    shards = r["v_small"].shape[0] * r["v_small"].shape[1]
    for d in range(shards):
        r["packed"][d : d + 1, :] = r["v_small"][d // 8, d % 8, 0:1, :]
    packed = r["packed"][...].astype(LOW)
    share = width // shards
    b_share = share * blocks
    vectors, b_in = r["vectors"], r["v_b_in"]
    for t in range(8):
        vectors[t : t + 1, :] = expand(packed, b_share + t * share, share, 0, width)
    for t in range(blocks):
        b_in[t : t + 1, :] = expand(packed, 0, b_share, t * width, width)
    bias_q, bias_v, bias_o, bias_out = (vectors[t : t + 1, :] for t in range(4))
    gain_one, gain_two, shift_one, shift_two = (vectors[t : t + 1, :] for t in range(4, 8))
    heads = r["heads"]
    step = 256

    def weight(name, t, at):
        value = r[name][t, :, :, :, at]
        return value.reshape(-1, value.shape[-1])

    for made in load_qkv:
        made.wait()

    def project_own(j):
        at = tile(j, step)
        mine = stream[0:rows, :]
        heads[0, :, at] = (mm(mine, weight("v_qkv", 0, at)) + vectors[0:1, at]).astype(LOW)
        heads[1, :, at] = mm(mine, weight("v_qkv", 1, at)).astype(LOW)
        heads[3, :, at] = (mm(mine, weight("v_qkv", 2, at)) + vectors[1:2, at]).astype(LOW)

    def project_other(j):
        at = tile(j, step)
        theirs = stream[rows : 2 * rows, :]
        heads[5, :, at] = (mm(theirs, weight("v_qkv", 0, at)) + vectors[0:1, at]).astype(LOW)
        heads[2, :, at] = mm(theirs, weight("v_qkv", 1, at)).astype(LOW)
        heads[4, :, at] = (mm(theirs, weight("v_qkv", 2, at)) + vectors[1:2, at]).astype(LOW)

    pump("w_in")
    loop(width // step, project_own)
    pump("w_o", "w_out")
    codes_over.wait_recv()
    same = lax.broadcasted_iota(jnp.int32, (half_len, half_len), 0) == lax.broadcasted_iota(
        jnp.int32, (half_len, half_len), 1
    )
    for i in range(items):
        asked = r["cols"][:, i : i + 1]
        own = (r["codes"][i : i + 1, :] <= asked) | same
        other = r["codes_taken"][i : i + 1, :] <= asked
        r["permit"][i, :, 0:half_len] = jnp.where(own, 0.0, fill_value)
        r["permit"][i, :, half_len : 2 * half_len] = jnp.where(other, 0.0, fill_value)
    for made in input_over:
        made.wait_recv()
    for i in range(items):
        embed = r["embed"][i : i + 1, :]

        def make_other(j, i=i, embed=embed):
            at = pl.ds(pl.multiple_of(i * half_len + j * 32, 32), 32)
            to = pl.ds(pl.multiple_of(rows + i * half_len + j * 32, 32), 32)
            stream[to, :] = (r["taken"][at, :].astype(F32) + embed).astype(LOW)

        loop(half_len // 32, make_other)
    loop(width // step, project_other)
    saved.append(copy(heads, r["save_heads"]))
    saved.append(copy(r["codes_taken"], r["save_codes"]))
    save_stream.wait()
    pump("w_o", "w_o", "w_in")
    lane = lax.broadcasted_iota(jnp.int32, (half_len, 2 * HD), 1)
    key_lane = lax.broadcasted_iota(jnp.int32, (2 * half_len, 2 * HD), 1)

    def attend(i):
        at_rows = pl.ds(i * half_len, half_len)

        def pair(p):
            at = tile(p, 2 * HD)
            query = heads[0, at_rows, at] * (1.0 / math.sqrt(HD))
            keys = jnp.concatenate([heads[1, at_rows, at], heads[2, at_rows, at]], axis=0)
            values = jnp.concatenate([heads[3, at_rows, at], heads[4, at_rows, at]], axis=0)
            nothing = jnp.zeros((), LOW)
            mixed = None
            logs = r["logs"][i]
            for h in range(2):
                scores = mm(jnp.where((lane < HD) == (h == 0), query, nothing), keys, NT) + r["permit"][i]
                peak = jnp.max(scores, axis=1, keepdims=True)
                expo = jnp.exp(scores - peak)
                total = jnp.sum(expo, axis=1, keepdims=True)
                probs = (expo * (1.0 / total)).astype(LOW)
                part = mm(probs, jnp.where((key_lane < HD) == (h == 0), values, nothing))
                mixed = part if mixed is None else mixed + part
                logs = jnp.where(lane == 2 * p + h, peak + jnp.log(total), logs)
            r["logs"][i] = logs
            stream[at_rows, at] = mixed.astype(LOW)

        loop(width // (2 * HD), pair)
        r["log_rows"][i] = r["logs"][i].T[:HEADS]
        logs_over.append(sender.send(r["log_rows"].at[i], r["logs_taken"].at[i], across))

    logs_over = []
    attend(0)
    pump("w_in", "w_in")
    if items > 1:
        attend(1)
    pump("w_in", "w_out")
    for i in range(2, items):
        attend(i)
    mixed = stream
    saved.append(copy(stream.at[pl.ds(0, rows)], r["save_mixed"]))
    saved.append(copy(r["log_rows"], r["save_logs"]))
    if by_hand:
        run_out(gens["w_o"])
    load_o = copy(full["w_o"], r["v_o"])
    load_o.wait()
    xhat = r["xhat"]
    for i in range(items):
        at_rows = pl.ds(i * half_len, half_len)
        w_o = r["v_o"][...].reshape(width, width)
        r["work"][...] = mm(mixed[at_rows, :], w_o) + bias_o
        embed = r["embed"][i : i + 1, :]

        def first_norm(j, i=i, embed=embed):
            at = pl.ds(pl.multiple_of(i * half_len + j * 32, 32), 32)
            to = pl.ds(pl.multiple_of(rows + i * half_len + j * 32, 32), 32)
            weight_rows = r["cols"][tile(j, 32), items + i : items + i + 1]
            attn = r["work"][tile(j, 32), :]
            sums[1:2, :] += column_sum(attn * attn * weight_rows)
            value, rstd = normalize(r["input"][at, :].astype(F32) + embed + attn)
            xhat[at, :] = value
            r["rstd"][at, :] = jnp.broadcast_to(rstd, (32, 128))
            stream[to, :] = (value * gain_one + shift_one).astype(LOW)

        loop(half_len // 32, first_norm)
    save_hidden = copy(stream.at[pl.ds(rows, rows)], r["save_hidden"])
    saved.append(copy(xhat, r["save_xhat"]))
    saved.append(copy(r["rstd"], r["save_rstd"]))
    if by_hand:
        run_out(gens["w_in"])
    load_in = [copy(full["w_in"].at[:, :, :, pl.ds(t * width, width)], r["v_in"].at[t]) for t in range(blocks)]
    for made in saved[:1]:
        made.wait()
    act, slope = heads, r["slope"]
    for t in range(blocks):
        load_in[t].wait()

        def feed(j, t=t):
            at = tile(j, step)
            w_in = weight("v_in", t, at)
            for i in range(items):
                own = pl.ds(i * half_len, half_len)
                pre = mm(stream[pl.ds(rows + i * half_len, half_len), :], w_in) + b_in[t : t + 1, at]
                cdf = 0.5 + 0.5 * lax.erf(pre * (1.0 / math.sqrt(2.0)))
                act[t, own, at] = (pre * cdf).astype(LOW)
                pdf = jnp.exp(pre * pre * -0.5) * (1.0 / math.sqrt(2.0 * math.pi))
                slope[t, own, at] = (cdf + pre * pdf).astype(LOW)

        loop(width // step, feed)
        if t == 1:
            pump("w_out")
        if t == 2:
            pump("w_out")
    saved.append(copy(heads.at[pl.ds(0, blocks)], r["act"]))
    saved.append(copy(slope, r["save_slope"]))
    if by_hand:
        run_out(gens["w_out"])
    load_out = [copy(full["w_out"].at[t], r["v_out"].at[t]) for t in range(blocks)]
    for made in load_out:
        made.wait()
    cot_in.wait()
    saved[2].wait()
    save_hidden.wait()
    for i in range(items):
        at_rows = pl.ds(i * half_len, half_len)
        total = None
        for t in range(blocks):
            part = mm(act[t, at_rows, :], r["v_out"][t].reshape(width, width))
            total = part if total is None else total + part
        r["work"][...] = total + bias_out

        def second_norm(j, i=i):
            at = pl.ds(pl.multiple_of(i * half_len + j * 32, 32), 32)
            to = pl.ds(pl.multiple_of(rows + i * half_len + j * 32, 32), 32)
            weight_rows = r["cols"][tile(j, 32), items + i : items + i + 1]
            branch = r["work"][tile(j, 32), :]
            sums[2:3, :] += column_sum(branch * branch * weight_rows)
            value, rstd = normalize(xhat[at, :] * gain_one + shift_one + branch)
            result = value * gain_two + shift_two
            sums[3:4, :] += column_sum(result * result * weight_rows)
            stream[at, :] = result.astype(LOW)
            grad = r["cot"][at, :].astype(F32)
            sums[5:6, :] += column_sum(grad * value)
            sums[6:7, :] += column_sum(grad)
            scaled = grad * gain_two
            back = rstd * (
                scaled
                - jnp.mean(scaled, axis=-1, keepdims=True)
                - value * jnp.mean(scaled * value, axis=-1, keepdims=True)
            )
            r["back"][at, :] = back
            back_low = back.astype(LOW)
            stream[to, :] = back_low
            sums[4:5, :] += column_sum(back_low.astype(F32))

        loop(half_len // 32, second_norm)
    saved.append(copy(stream.at[pl.ds(0, rows)], r["output"]))
    saved.append(copy(stream.at[pl.ds(rows, rows)], r["save_back_low"]))
    saved.append(copy(r["back"], r["save_back"]))
    saved.append(copy(vectors, r["save_vectors"]))
    for made in logs_over:
        made.wait_recv()
    saved.append(copy(r["logs_taken"], r["save_logs_taken"]))
    cols_over.wait_recv()
    saved.append(copy(r["cols_taken"], r["save_cols"]))
    for i, made in enumerate(saved):
        if i not in (0, 2):
            made.wait()
    sender.close()


def forward(by_hand, items, half_len, weights, small, block_input, embed, codes, cols, cotangent, collective_id):
    rows, width = block_input.shape
    full_len = 2 * half_len
    blocks = 4
    nz = lax.axis_size("dp") // 4
    shape = jax.ShapeDtypeStruct
    vmem, hbm = pl.BlockSpec(memory_space=pltpu.VMEM), pl.BlockSpec(memory_space=pl.ANY)
    params = ["w_qkv", "small", "w_o", "w_in", "w_out"]
    ins = dict(zip(params, [weights[0], small] + weights[1:]))
    spaces_in = [vmem if by_hand else hbm] * 5
    ins.update(input=block_input, embed=embed, codes=codes, cols=cols, cotangent=cotangent)
    spaces_in += [vmem] * 4 + [hbm]
    outs, spaces_out = {}, []
    if by_hand:
        for p in params:
            outs["all_" + p] = shape((nz, 8) + ins[p].shape, ins[p].dtype)
            spaces_out.append(hbm)
    outs.update(
        save_heads=shape((6, rows, width), LOW),
        save_codes=shape(codes.shape, F32),
        save_cols=shape(cols.shape, F32),
        save_stream=shape((rows, width), LOW),
        save_hidden=shape((rows, width), LOW),
        save_mixed=shape((rows, width), LOW),
        save_logs=shape((items, HEADS, half_len), F32),
        save_logs_taken=shape((items, HEADS, half_len), F32),
        save_xhat=shape((rows, width), F32),
        save_rstd=shape((rows, 128), F32),
        act=shape((blocks, rows, width), LOW),
        save_slope=shape((blocks, rows, width), LOW),
        output=shape((rows, width), LOW),
        save_back_low=shape((rows, width), LOW),
        save_back=shape((rows, width), F32),
        save_vectors=shape((8, width), F32),
        sums=shape((8, width), F32),
    )
    spaces_out += [hbm] * 16 + [vmem]
    if by_hand:
        small_full = (nz, 8) + small.shape
    else:
        small_full = small.shape
    copies = 5 * gather_copies(nz) + 2 * items + 2
    scratch = dict(
        send=pltpu.SemaphoreType.DMA((copies,)),
        recv=pltpu.SemaphoreType.DMA((copies,)),
        local=pltpu.SemaphoreType.DMA((40,)),
        taken=pltpu.VMEM((rows, width), LOW),
        codes_taken=pltpu.VMEM(codes.shape, F32),
        cols_taken=pltpu.VMEM(cols.shape, F32),
        stream=pltpu.VMEM((2 * rows, width), LOW),
        v_qkv=pltpu.VMEM((3, 4, 8, 32, width), LOW),
        v_small=pltpu.VMEM(small_full, F32),
        packed=pltpu.VMEM((small_full[0] * 8, small_full[-1]), F32),
        vectors=pltpu.VMEM((8, width), F32),
        v_b_in=pltpu.VMEM((8, width), F32),
        heads=pltpu.VMEM((6, rows, width), LOW),
        permit=pltpu.VMEM((items, half_len, full_len), F32),
        logs=pltpu.VMEM((items, half_len, 128), F32),
        log_rows=pltpu.VMEM((items, HEADS, half_len), F32),
        logs_taken=pltpu.VMEM((items, HEADS, half_len), F32),
        v_o=pltpu.VMEM((4, 8, 32, width), LOW),
        work=pltpu.VMEM((half_len, width), F32),
        xhat=pltpu.VMEM((rows, width), F32),
        rstd=pltpu.VMEM((rows, 128), F32),
        v_in=pltpu.VMEM((blocks, 4, 8, 32, width), LOW),
        slope=pltpu.VMEM((blocks, rows, width), LOW),
        v_out=pltpu.VMEM((blocks, 8, 128, width), LOW),
        cot=pltpu.VMEM((rows, width), LOW),
        back=pltpu.VMEM((rows, width), F32),
    )
    results = pl.pallas_call(
        partial(forward_kernel, by_hand, items, half_len, list(ins), list(outs), list(scratch)),
        out_shape=list(outs.values()),
        in_specs=spaces_in,
        out_specs=spaces_out,
        scratch_shapes=list(scratch.values()),
        compiler_params=pltpu.CompilerParams(
            collective_id=collective_id, has_side_effects=True, vmem_limit_bytes=62 << 20
        ),
    )(*ins.values())
    return dict(zip(outs, results), codes=codes, cols=cols)


class Kernel:
    def __init__(self, names, refs):
        self.refs = dict(zip(names, refs))
        self.place = Place()
        self.sender = Sender(self["send"], self["recv"])
        self.count = 0
        self.saved = []

    def __getitem__(self, name):
        return self.refs[name]

    def copy(self, src, dst):
        made = pltpu.make_async_copy(src, dst, self["local"].at[self.count])
        self.count += 1
        made.start()
        return made

    def save(self, src, dst):
        self.saved.append(self.copy(src, dst))

    def close(self):
        for made in self.saved:
            made.wait()
        self.sender.close()


def call(body, ins, spaces_in, outs, scratch, copies, collective_id):
    vmem, hbm = pl.BlockSpec(memory_space=pltpu.VMEM), pl.BlockSpec(memory_space=pl.ANY)
    scratch = dict(
        send=pltpu.SemaphoreType.DMA((copies,)),
        recv=pltpu.SemaphoreType.DMA((copies,)),
        local=pltpu.SemaphoreType.DMA((48,)),
        **scratch,
    )
    names = list(ins) + list(outs) + list(scratch)

    def kernel(*refs):
        body(Kernel(names, refs))

    results = pl.pallas_call(
        kernel,
        out_shape=[jax.ShapeDtypeStruct(s, d) for s, d, _ in outs.values()],
        in_specs=[vmem if name in spaces_in else hbm for name in ins],
        out_specs=[vmem if space == "vmem" else hbm for _, _, space in outs.values()],
        scratch_shapes=list(scratch.values()),
        compiler_params=pltpu.CompilerParams(
            collective_id=collective_id, has_side_effects=True, vmem_limit_bytes=63 << 20
        ),
    )(*ins.values())
    return dict(zip(outs, results))


def feed_back(by_hand, items, half_len, fw, weights, collective_id):
    blocks, rows, width = fw["act"].shape
    nz = lax.axis_size("dp") // 4
    half_width = width // 2
    step = 256

    def body(k):
        place, sender = k.place, k.sender
        load_low = k.copy(k["back_low"], k["v_low"])
        load_act = [k.copy(k["act"].at[t], k["v_act"].at[t]) for t in range(blocks)]
        load_out = k.copy(k["w_out"], k["v_out"])
        load_slope = k.copy(k["slope"], k["v_slope"])
        load_in = [
            k.copy(k["w_in"].at[:, :, :, pl.ds(t * width, width)], k["v_in"].at[t]) for t in range(blocks)
        ]
        load_rest = [
            k.copy(k["back"], k["v_back"]),
            k.copy(k["xhat"], k["v_xhat"]),
            k.copy(k["rstd"], k["v_rstd"]),
            k.copy(k["w_o"], k["v_o"]),
        ]
        meet(place)
        load_low.wait()
        low, act, grad = k["v_low"], k["v_act"], k["grad"]
        gens = []
        if by_hand:
            for q in range(2):
                buffers = {name: k[f"{name}{q}"] for name in ("core", "diag", "line", "column")}
                target = k["grad_out"].at[:, pl.ds(q * half_width, half_width)]
                gens.append(reduce_steps(place, sender, grad.at[q], buffers, target, nz))

        def pump(q):
            if by_hand:
                next(gens[q], None)

        for t in range(blocks):
            load_act[t].wait()

            def outer(j, t=t):
                part = mm(act[t, :, tile(j, step)], low[...], TN).astype(LOW)
                part = part.reshape(step // 128, 128, width)
                to = pl.ds(j * (step // 128), step // 128)
                grad[0, t, to] = part[:, :, :half_width]
                grad[1, t, to] = part[:, :, half_width:]

            loop(width // step, outer)
        pump(0)
        pump(1)
        if not by_hand:
            for q in range(2):
                k.save(grad.at[q], k["grad_out"].at[:, :, :, pl.ds(q * half_width, half_width)])
        load_out.wait()
        load_slope.wait()
        sums = k["sums"]
        sums[...] = jnp.zeros_like(sums)
        for t in range(blocks):

            def pull(j, t=t):
                at = tile(j, step)
                w_out = k["v_out"][t, pl.ds(j * (step // 128), step // 128)].reshape(step, width)
                part = mm(low[...], w_out, NT) * k["v_slope"][t, :, at].astype(F32)
                part = part.astype(LOW)
                act[t, :, at] = part
                sums[t : t + 1, at] = column_sum(part.astype(F32))

            loop(width // step, pull)
            if t < 2:
                pump(t)
        k.save(act, k["pre_grad"])
        for made in load_in + load_rest:
            made.wait()
        gain = k["vectors"][4:5, :]
        for i in range(items):
            at_rows = pl.ds(i * half_len, half_len)
            total = None
            for t in range(blocks):
                part = mm(act[t, at_rows, :], k["v_in"][t].reshape(width, width), NT)
                total = part if total is None else total + part
            k["work"][...] = total

            def first_back(j, i=i):
                at = pl.ds(pl.multiple_of(i * half_len + j * 32, 32), 32)
                hidden = k["work"][tile(j, 32), :] + k["v_back"][at, :]
                xhat = k["v_xhat"][at, :]
                rstd = k["v_rstd"][at, 0:1]
                sums[4:5, :] += column_sum(hidden * xhat)
                sums[5:6, :] += column_sum(hidden)
                scaled = hidden * gain
                value = rstd * (
                    scaled
                    - jnp.mean(scaled, axis=-1, keepdims=True)
                    - xhat * jnp.mean(scaled * xhat, axis=-1, keepdims=True)
                )
                k["v_back"][at, :] = value
                value_low = value.astype(LOW)
                low[at, :] = value_low
                sums[6:7, :] += column_sum(value_low.astype(F32))

            loop(half_len // 32, first_back)
            if i < 2:
                pump(i)
        w_o = k["v_o"][...].reshape(width, width)
        for i in range(items):
            at_rows = pl.ds(i * half_len, half_len)
            k["v_mixed_grad"][at_rows, :] = mm(low[at_rows, :], w_o, NT).astype(LOW)
        over = sender.send(k["v_mixed_grad"], k["v_taken"], place.device(x=1))
        k.save(k["v_back"], k["input_part"])
        k.save(low, k["attn_grad"])
        k.save(k["v_mixed_grad"], k["mixed_grad"])
        for q in range(2):
            pump(q)
        for gen in gens:
            run_out(gen)
        over.wait_recv()
        k.save(k["v_taken"], k["mixed_grad_taken"])
        k.close()

    ins = dict(
        back_low=fw["save_back_low"],
        act=fw["act"],
        w_out=weights[3],
        slope=fw["save_slope"],
        w_in=weights[2],
        back=fw["save_back"],
        xhat=fw["save_xhat"],
        rstd=fw["save_rstd"],
        w_o=weights[1],
        vectors=fw["save_vectors"],
    )
    outs = dict(
        pre_grad=((blocks, rows, width), LOW, "hbm"),
        input_part=((rows, width), F32, "hbm"),
        attn_grad=((rows, width), LOW, "hbm"),
        mixed_grad=((rows, width), LOW, "hbm"),
        mixed_grad_taken=((rows, width), LOW, "hbm"),
        sums=((8, width), F32, "vmem"),
    )
    if by_hand:
        outs["grad_out"] = ((128, width), F32, "vmem")
    else:
        outs["grad_out"] = ((4, 8, 128, width), LOW, "hbm")
    scratch = dict(
        v_low=pltpu.VMEM((rows, width), LOW),
        v_act=pltpu.VMEM((blocks, rows, width), LOW),
        v_out=pltpu.VMEM((blocks, 8, 128, width), LOW),
        v_slope=pltpu.VMEM((blocks, rows, width), LOW),
        v_in=pltpu.VMEM((blocks, 4, 8, 32, width), LOW),
        v_back=pltpu.VMEM((rows, width), F32),
        v_xhat=pltpu.VMEM((rows, width), F32),
        v_rstd=pltpu.VMEM((rows, 128), F32),
        v_o=pltpu.VMEM((4, 8, 32, width), LOW),
        v_mixed_grad=pltpu.VMEM((rows, width), LOW),
        v_taken=pltpu.VMEM((rows, width), LOW),
        work=pltpu.VMEM((half_len, width), F32),
        grad=pltpu.VMEM((2, 4, 8, 128, half_width), LOW),
    )
    copies = 1
    if by_hand:
        copies += 2 * reduce_copies(nz)
        for q in range(2):
            for name, buffer in reduce_buffers(nz, 128, half_width).items():
                scratch[f"{name}{q}"] = buffer
    return call(body, ins, ("vectors",), outs, scratch, copies, collective_id)


def attend_back(by_hand, items, half_len, fw, fb, collective_id):
    blocks, rows, width = fw["act"].shape
    nz = lax.axis_size("dp") // 4
    chunks = blocks + 1
    step = 256
    scale = 1.0 / math.sqrt(HD)

    def body(k):
        place, sender = k.place, k.sender
        load_hidden = k.copy(k["hidden"], k["v_left"])
        load_pre = [k.copy(k["pre_grad"].at[t], k["v_pre"].at[t]) for t in range(blocks)]
        load_mixed = [k.copy(k["attn_grad"], k["v_attn"])]
        load_heads = [
            k.copy(k["heads"], k["v_heads"]),
            k.copy(k["mixed_grad"], k["v_grad"].at[0]),
            k.copy(k["mixed_grad_taken"], k["v_grad"].at[1]),
        ]
        meet(place)
        grad = k["grad"]
        gens = []
        if by_hand:
            for q in range(chunks):
                buffers = {name: k[f"{name}{q}"] for name in ("core", "diag", "line", "column")}
                if q < blocks:
                    target = k["grad_in"].at[:, pl.ds(q * width, width)]
                else:
                    target = k["grad_o"]
                gens.append(reduce_steps(place, sender, grad.at[q], buffers, target, nz // 2))

        def pump(*which):
            if by_hand:
                for q in which:
                    next(gens[q], None)

        load_hidden.wait()
        left, turned = k["v_left"], k["v_turned"]

        def turn(j):
            turned[tile(j, 128), :] = left[:, tile(j, 128)].T

        def outer(q, right):
            def one(j):
                at = tile(j, step)
                part = mm(turned[...], right[:, at]).astype(LOW)
                grad[q, :, :, :, at] = part.reshape(4, 8, 32, step)

            loop(width // step, one)

        loop(width // 128, turn)
        load_left = None
        for t in range(blocks):
            load_pre[t].wait()
            outer(t, k["v_pre"].at[t])
            pump(t)
            if t == 0:
                load_left = k.copy(k["mixed"], left)
            if t >= 1:
                pump(t - 1)
        load_left.wait()
        for made in load_mixed:
            made.wait()
        loop(width // 128, turn)
        outer(blocks, k["v_attn"])
        pump(blocks)
        for made in load_heads:
            made.wait()
        same = lax.broadcasted_iota(jnp.int32, (half_len, half_len), 0) == lax.broadcasted_iota(
            jnp.int32, (half_len, half_len), 1
        )
        for i in range(items):
            asked = k["codes"][items + i : items + i + 1, :]
            asked_taken = k["codes_taken"][items + i : items + i + 1, :]
            code = k["cols"][:, 2 * items + i : 2 * items + i + 1]
            code_taken = k["cols_taken"][:, 2 * items + i : 2 * items + i + 1]
            k["permit"][i, 0:half_len, :] = jnp.where((code <= asked) | same, 0.0, fill_value)
            k["permit"][i, half_len : 2 * half_len, :] = jnp.where(code_taken <= asked, 0.0, fill_value)
            k["permit_taken"][i] = jnp.where(code <= asked_taken, 0.0, fill_value)
        heads, grads, result = k["v_heads"], k["v_grad"], k["v_pre"]
        lane = lax.broadcasted_iota(jnp.int32, (half_len, 2 * HD), 1)
        key_lane = lax.broadcasted_iota(jnp.int32, (2 * half_len, 2 * HD), 1)
        nothing = jnp.zeros((), LOW)

        def ours(i):
            at_rows = pl.ds(i * half_len, half_len)

            def pair(p):
                at = tile(p, 2 * HD)
                query = heads[0, at_rows, at]
                keys = jnp.concatenate([heads[1, at_rows, at], heads[2, at_rows, at]], axis=0)
                values = jnp.concatenate([heads[3, at_rows, at], heads[4, at_rows, at]], axis=0)
                grad_row = grads[0, at_rows, at]
                query_part = key_part = value_part = None
                for h in range(2):
                    mine = (lane < HD) == (h == 0)
                    key_mine = (key_lane < HD) == (h == 0)
                    query_h = jnp.where(mine, query, nothing)
                    grad_h = jnp.where(mine, grad_row, nothing)
                    keys_h = jnp.where(key_mine, keys, nothing)
                    at_head = pl.ds(2 * p + h, 1)
                    scores = mm(keys, query_h * scale, NT) + (k["permit"][i] - k["logs"][i, at_head, :])
                    probs = jnp.exp(scores)
                    prob_grad = mm(values, grad_h, NT)
                    centre = column_sum(probs * prob_grad)
                    k["centre"][i, at_head, :] = centre
                    score_grad = (probs * (prob_grad - centre)).astype(LOW)
                    parts = (
                        mm(score_grad, keys_h, TN),
                        mm(score_grad[:half_len], query_h),
                        mm(probs[:half_len].astype(LOW), grad_h),
                    )
                    if h == 0:
                        query_part, key_part, value_part = parts
                    else:
                        query_part = query_part + parts[0]
                        key_part = key_part + parts[1]
                        value_part = value_part + parts[2]
                query_low = (query_part * scale).astype(LOW)
                result[0, at_rows, at] = query_low
                k["sums"][0:1, at] += column_sum(query_low.astype(F32))
                k["parts"][0, at_rows, at] = key_part
                k["parts"][1, at_rows, at] = value_part

            loop(width // (2 * HD), pair)

        def theirs(i):
            at_rows = pl.ds(i * half_len, half_len)

            def pair(p):
                at = tile(p, 2 * HD)
                query = heads[5, at_rows, at]
                keys, values = heads[1, at_rows, at], heads[3, at_rows, at]
                grad_row = grads[1, at_rows, at]
                key_part, value_part = k["parts"][0, at_rows, at], k["parts"][1, at_rows, at]
                for h in range(2):
                    mine = (lane < HD) == (h == 0)
                    query_h = jnp.where(mine, query, nothing)
                    grad_h = jnp.where(mine, grad_row, nothing)
                    at_head = pl.ds(2 * p + h, 1)
                    scores = mm(keys, query_h * scale, NT) + (
                        k["permit_taken"][i] - k["logs_taken"][i, at_head, :]
                    )
                    probs = jnp.exp(scores)
                    prob_grad = mm(values, grad_h, NT)
                    score_grad = (probs * (prob_grad - k["centre_taken"][i, at_head, :])).astype(LOW)
                    key_part = key_part + mm(score_grad, query_h)
                    value_part = value_part + mm(probs.astype(LOW), grad_h)
                result[1, at_rows, at] = (key_part * scale).astype(LOW)
                value_low = value_part.astype(LOW)
                result[2, at_rows, at] = value_low
                k["sums"][1:2, at] += column_sum(value_low.astype(F32))

            loop(width // (2 * HD), pair)

        k["sums"][...] = jnp.zeros_like(k["sums"])
        over = []
        plan = {0: (0, 1, 2, 3, 4), 1: (3, 0, 1, 2), 2: (3, 4)}
        for i in range(items):
            ours(i)
            over.append(sender.send(k["centre"].at[i], k["centre_taken"].at[i], place.device(x=1)))
            pump(*plan.get(i, ()))
        k.save(result.at[0], k["joint_grad"].at[0])
        for i in range(items):
            over[i].wait_recv()
            theirs(i)
            if i == 0:
                pump(0, 1, 2, 3, 4)
        k.save(result.at[1], k["joint_grad"].at[1])
        k.save(result.at[2], k["joint_grad"].at[2])
        for gen in gens:
            run_out(gen)
        if not by_hand:
            for q in range(blocks):
                k.save(grad.at[q], k["grad_in"].at[:, :, :, pl.ds(q * width, width)])
            k.save(grad.at[blocks], k["grad_o"])
        k.close()

    ins = dict(
        hidden=fw["save_hidden"],
        pre_grad=fb["pre_grad"],
        mixed=fw["save_mixed"],
        attn_grad=fb["attn_grad"],
        heads=fw["save_heads"],
        mixed_grad=fb["mixed_grad"],
        mixed_grad_taken=fb["mixed_grad_taken"],
        codes=fw["codes"],
        codes_taken=fw["save_codes"],
        cols=fw["cols"],
        cols_taken=fw["save_cols"],
        logs=fw["save_logs"],
        logs_taken=fw["save_logs_taken"],
    )
    outs = dict(
        joint_grad=((3, rows, width), LOW, "hbm"),
        sums=((8, width), F32, "vmem"),
    )
    if by_hand:
        outs["grad_in"] = ((32, blocks * width), F32, "vmem")
        outs["grad_o"] = ((32, width), F32, "vmem")
    else:
        outs["grad_in"] = ((4, 8, 32, blocks * width), LOW, "hbm")
        outs["grad_o"] = ((4, 8, 32, width), LOW, "hbm")
    scratch = dict(
        v_left=pltpu.VMEM((rows, width), LOW),
        v_turned=pltpu.VMEM((width, rows), LOW),
        v_pre=pltpu.VMEM((blocks, rows, width), LOW),
        v_attn=pltpu.VMEM((rows, width), LOW),
        v_heads=pltpu.VMEM((6, rows, width), LOW),
        v_grad=pltpu.VMEM((2, rows, width), LOW),
        grad=pltpu.VMEM((chunks, 4, 8, 32, width), LOW),
        permit=pltpu.VMEM((items, 2 * half_len, half_len), F32),
        permit_taken=pltpu.VMEM((items, half_len, half_len), F32),
        parts=pltpu.VMEM((2, rows, width), F32),
        centre=pltpu.VMEM((items, HEADS, half_len), F32),
        centre_taken=pltpu.VMEM((items, HEADS, half_len), F32),
    )
    copies = items
    if by_hand:
        copies += chunks * reduce_copies(nz)
        for q in range(chunks):
            for name, buffer in reduce_buffers(nz, 32, width).items():
                scratch[f"{name}{q}"] = buffer
    spaces = ("codes", "codes_taken", "cols", "cols_taken", "logs", "logs_taken")
    return call(body, ins, spaces, outs, scratch, copies, collective_id)


def project_back(by_hand, items, half_len, fw, fb, ab, weights, collective_id):
    _, rows, width = ab["joint_grad"].shape
    nz = lax.axis_size("dp") // 4
    step = 256
    stages = 3 + (nz - 1).bit_length()

    def body(k):
        place, sender = k.place, k.sender
        load_stream = k.copy(k["stream"], k["v_left"])
        load_joint = [k.copy(k["joint_grad"].at[t], k["v_joint"].at[t]) for t in range(3)]
        load_qkv = [
            k.copy(k["w_qkv"].at[:, :, :, pl.ds(t * width, width)], k["v_qkv"].at[t]) for t in range(3)
        ]
        load_part = k.copy(k["input_part"], k["v_part"])
        meet(place)
        levels = k["levels"]
        for s, name in enumerate(("sums_one", "sums_two", "sums_three")):
            levels[0, 8 * s : 8 * s + 8, :] = k[name][...]
        small = sum_steps(place, sender, levels, k["levels_taken"])
        next(small)
        grad = k["grad"]
        gens = []
        if by_hand:
            for q in range(3):
                buffers = {name: k[f"{name}{q}"] for name in ("core", "diag", "line", "column")}
                target = k["grad_qkv"].at[:, pl.ds(q * width, width)]
                gens.append(reduce_steps(place, sender, grad.at[q], buffers, target, nz // 2))

        def pump(*which):
            if by_hand:
                for q in which:
                    next(gens[q], None)

        load_stream.wait()
        left, turned = k["v_left"], k["v_turned"]

        def turn(j):
            turned[tile(j, 128), :] = left[:, tile(j, 128)].T

        loop(width // 128, turn)
        for q in range(3):
            load_joint[q].wait()

            def outer(j, q=q):
                at = tile(j, step)
                part = mm(turned[...], k["v_joint"][q, :, at]).astype(LOW)
                grad[q, :, :, :, at] = part.reshape(4, 8, 32, step)

            loop(width // step, outer)
            pump(q)
        pump(0)
        next(small, None)
        for made in load_qkv + [load_part]:
            made.wait()
        for i in range(items):
            at_rows = pl.ds(i * half_len, half_len)
            total = k["v_part"][at_rows, :]
            for q in range(3):
                total = total + mm(k["v_joint"][q, at_rows, :], k["v_qkv"][q].reshape(width, width), NT)
            left[at_rows, :] = total.astype(LOW)
            if i == 0:
                pump(1)
            if i == 1:
                pump(2, 0)
                next(small, None)
        k.save(left, k["input_grad"])
        pump(1, 2)
        next(small, None)
        pump(0, 1, 2)
        for gen in gens + [small]:
            run_out(gen)
        k["totals"][...] = levels[stages]
        if not by_hand:
            for q in range(3):
                k.save(grad.at[q], k["grad_qkv"].at[:, :, :, pl.ds(q * width, width)])
        k.close()

    ins = dict(
        stream=fw["save_stream"],
        joint_grad=ab["joint_grad"],
        w_qkv=weights[0],
        input_part=fb["input_part"],
        sums_one=fw["sums"],
        sums_two=fb["sums"],
        sums_three=ab["sums"],
    )
    outs = dict(
        input_grad=((rows, width), LOW, "hbm"),
        totals=((24, width), F32, "vmem"),
    )
    if by_hand:
        outs["grad_qkv"] = ((32, 3 * width), F32, "vmem")
    else:
        outs["grad_qkv"] = ((4, 8, 32, 3 * width), LOW, "hbm")
    scratch = dict(
        v_left=pltpu.VMEM((rows, width), LOW),
        v_turned=pltpu.VMEM((width, rows), LOW),
        v_joint=pltpu.VMEM((3, rows, width), LOW),
        v_qkv=pltpu.VMEM((3, 4, 8, 32, width), LOW),
        v_part=pltpu.VMEM((rows, width), F32),
        grad=pltpu.VMEM((3, 4, 8, 32, width), LOW),
        levels=pltpu.VMEM((stages + 1, 24, width), F32),
        levels_taken=pltpu.VMEM((stages, 24, width), F32),
    )
    copies = stages
    if by_hand:
        copies += 3 * reduce_copies(nz)
        for q in range(3):
            for name, buffer in reduce_buffers(nz, 32, width).items():
                scratch[f"{name}{q}"] = buffer
    return call(body, ins, ("sums_one", "sums_two", "sums_three"), outs, scratch, copies, collective_id)


def body(
    block_input,
    lengths,
    mask,
    blocks,
    timesteps,
    w_qkv,
    w_o,
    w_in,
    w_out,
    b_in,
    biases,
    gains,
    shifts,
    cotangent,
):
    items, half_len, width = block_input.shape
    rows = items * half_len
    f32 = jnp.float32
    n = n_devices()
    share = width // n
    b_count = b_in.shape[0]
    positions = lax.axis_index("ctx") * half_len + jnp.arange(half_len, dtype=jnp.int32)
    valid = (positions[None, :] < lengths[:, None]) & ((mask == 1) | (positions[None, :] == 0))
    numbers = blocks.astype(f32)
    key_codes = jnp.where(valid, numbers, code_absent)
    codes = jnp.pad(jnp.concatenate([key_codes, numbers]), ((0, 8 - 2 * items), (0, 0)))
    cols = jnp.concatenate([numbers, valid.astype(f32), key_codes]).T
    cols = jnp.pad(cols, ((0, 0), (0, 128 - 3 * items)))
    embed = jnp.pad(time_embed(timesteps, width), ((0, 8 - items), (0, 0)))
    small = jnp.concatenate([b_in, biases.reshape(-1), gains.reshape(-1), shifts.reshape(-1)])
    small_wide = -(-small.shape[0] // 128) * 128
    small = jnp.pad(small.astype(f32), (0, small_wide - small.shape[0]))
    small = jnp.broadcast_to(small[None, :], (8, small_wide))
    by_hand = w_qkv.shape[0] == 32
    weights = [w_qkv, w_o, w_in, w_out]
    if not by_hand:
        weights = [lax.all_gather(w, AXES, axis=0, tiled=True) for w in weights]
        weights = [w.reshape(4, 8, w.shape[0] // 32, w.shape[1]) for w in weights]
        small = lax.all_gather(small, AXES, axis=0).reshape(n // 8, 8, 8, small_wide)
    fw = forward(
        by_hand,
        items,
        half_len,
        weights,
        small,
        block_input.reshape(rows, width),
        embed,
        codes,
        cols,
        cotangent.reshape(rows, width),
        1,
    )
    if by_hand:
        weights = [fw["all_" + p] for p in ("w_qkv", "w_o", "w_in", "w_out")]
    fb = feed_back(by_hand, items, half_len, fw, weights, 2)
    ab = attend_back(by_hand, items, half_len, fw, fb, 3)
    pb = project_back(by_hand, items, half_len, fw, fb, ab, weights, 4)
    grads = [pb["grad_qkv"], ab["grad_o"], ab["grad_in"], fb["grad_out"]]
    if not by_hand:
        grads = [
            lax.psum_scatter(
                part.astype(f32).reshape(-1, part.shape[-1]), AXES, scatter_dimension=0, tiled=True
            )
            for part in grads
        ]
    totals = pb["totals"]
    me = my_index()
    grad_b_in = lax.dynamic_slice(totals[8:12].reshape(-1), (me * b_count,), (b_count,))
    order = (16, 17, 14, 4, 12, 5, 13, 6)
    mine = lax.dynamic_slice(totals, (0, me * share), (24, share))
    mine = jnp.stack([mine[row] for row in order])
    count = jnp.sum(totals[7, items : 2 * items])
    rms = jnp.sqrt(jnp.sum(totals[:4], axis=1) / (count * width))
    return (
        fw["output"].reshape(block_input.shape),
        pb["input_grad"].reshape(block_input.shape),
        *grads,
        grad_b_in,
        mine[:4],
        mine[4:6],
        mine[6:8],
        rms,
    )


def solution(mesh):
    in_specs = (
        P("dp", "ctx", None),
        P("dp"),
        P("dp", "ctx"),
        P("dp", "ctx"),
        P("dp"),
        P(("dp", "ctx"), None),
        P(("dp", "ctx"), None),
        P(("dp", "ctx"), None),
        P(("dp", "ctx"), None),
        P(("dp", "ctx")),
        P(None, ("dp", "ctx")),
        P(None, ("dp", "ctx")),
        P(None, ("dp", "ctx")),
        P("dp", "ctx", None),
    )
    out_specs = (
        P("dp", "ctx", None),
        P("dp", "ctx", None),
        P(("dp", "ctx"), None),
        P(("dp", "ctx"), None),
        P(("dp", "ctx"), None),
        P(("dp", "ctx"), None),
        P(("dp", "ctx")),
        P(None, ("dp", "ctx")),
        P(None, ("dp", "ctx")),
        P(None, ("dp", "ctx")),
        P(),
    )
    return jax.shard_map(body, mesh=mesh, in_specs=in_specs, out_specs=out_specs, check_vma=False)
```

```python
from functools import partial
import math

import jax
import jax.numpy as jnp
from jax import lax
from jax.experimental import pallas as pl
from jax.experimental.pallas import tpu as pltpu
from jax.sharding import PartitionSpec as P

HEADS = 16
HD = 64

AXES = ("dp", "ctx")
X = 1


def my_index():
    return lax.axis_index("dp") * lax.axis_size("ctx") + lax.axis_index("ctx")


def n_devices():
    return lax.axis_size("dp") * lax.axis_size("ctx")


fill_value = -1e30
eps_norm = 1e-05
code_absent = 30000.0


def time_embed(steps, width):
    half = width // 2
    freqs = jnp.exp(jnp.arange(half, dtype=jnp.float32) * (-math.log(10000.0) / half))
    angle = steps.astype(jnp.float32)[:, None] * freqs[None, :]
    return jnp.concatenate([jnp.sin(angle), jnp.cos(angle)], axis=-1)


MESH = pl.DeviceIdType.MESH


class Place:
    def __init__(self):
        dp = lax.axis_index("dp")
        self.nz = lax.axis_size("dp") // 4
        self.x = lax.axis_index("ctx")
        self.c = dp % 2
        self.y = (dp // 2) % 2
        self.z = dp // 4

    def zth(self, k):
        z, bit = self.z, 1
        while bit < self.nz:
            if k & bit:
                z = z + bit * (1 - 2 * ((self.z // bit) % 2))
            bit *= 2
        return z

    def flips(self, y=0, c=0, x=0):
        return (
            1 - self.y if y else self.y,
            1 - self.c if c else self.c,
            1 - self.x if x else self.x,
        )

    def device(self, k=0, y=0, c=0, x=0):
        fy, fc, fx = self.flips(y, c, x)
        return ((self.zth(k) * 2 + fy) * 2 + fc, fx)

    def shard(self, k=0, y=0, c=0, x=0):
        fy, fc, fx = self.flips(y, c, x)
        return ((self.zth(k) * 2 + fy) * 2 + fc) * 2 + fx

    def column(self, y=0, c=0, x=0):
        fy, fc, fx = self.flips(y, c, x)
        return (fy * 2 + fc) * 2 + fx

    def partners(self):
        return [self.device(k=k) for k in range(1, self.nz)] + [
            self.device(x=1),
            self.device(y=1),
            self.device(c=1),
        ]


def meet(place):
    barrier = pltpu.get_barrier_semaphore()
    partners = place.partners()
    for partner in partners:
        pl.semaphore_signal(barrier, inc=1, device_id=partner, device_id_type=MESH)
    pl.semaphore_wait(barrier, len(partners))


class Sender:
    def __init__(self, send_sem, recv_sem):
        self.send_sem, self.recv_sem = send_sem, recv_sem
        self.count = 0
        self.open = []

    def send(self, src, dst, device):
        copy = pltpu.make_async_remote_copy(
            src_ref=src,
            dst_ref=dst,
            send_sem=self.send_sem.at[self.count],
            recv_sem=self.recv_sem.at[self.count],
            device_id=device,
            device_id_type=MESH,
        )
        self.count += 1
        copy.start()
        self.open.append(copy)
        return copy

    def close(self):
        for copy in self.open:
            copy.wait_send()
        self.open = []


def gather_copies(nz):
    return 4 * nz + 5


def gather_steps(place, sender, shard, full, split):
    nz = place.nz
    mine, at_x, at_y, diag = (place.column(x=fx, y=fy) for fy, fx in ((0, 0), (0, 1), (1, 0), (1, 1)))
    own = full.at[place.z, mine]
    by_z = [sender.send(shard, own, place.device(k=k)) for k in range(1, nz)]
    yield
    from_x = [sender.send(shard, own, place.device(x=1))]
    from_y = [sender.send(shard, own, place.device(y=1))]
    yield
    for k in range(1, nz):
        by_z[k - 1].wait_recv()
        piece = full.at[place.zth(k), mine]
        from_x.append(sender.send(piece, piece, place.device(x=1)))
        from_y.append(sender.send(piece, piece, place.device(y=1)))
        yield
    to_core = [sender.send(full.at[:, mine], full.at[:, mine], place.device(c=1))]
    from_diag = []
    yield
    for k in range(nz):
        from_x[k].wait_recv()
        if k < split:
            piece = full.at[place.zth(k), at_x]
            from_diag.append(sender.send(piece, piece, place.device(y=1)))
        else:
            from_y[k].wait_recv()
            piece = full.at[place.zth(k), at_y]
            from_diag.append(sender.send(piece, piece, place.device(x=1)))
        yield
    to_core.append(sender.send(full.at[:, at_x], full.at[:, at_x], place.device(c=1)))
    for k in range(split):
        from_y[k].wait_recv()
    to_core.append(sender.send(full.at[:, at_y], full.at[:, at_y], place.device(c=1)))
    yield
    half = nz // 2
    for start, size in ((0, half), (half, nz - half)):
        for copy in from_diag if start == 0 else ():
            copy.wait_recv()
        part = full.at[pl.ds(start, size), diag]
        to_core.append(sender.send(part, part, place.device(c=1)))
    yield
    for copy in to_core:
        copy.wait_recv()


NN = (((1,), (0,)), ((), ()))
NT = (((1,), (1,)), ((), ()))
TN = (((0,), (0,)), ((), ()))
LOW = jnp.bfloat16
F32 = jnp.float32


def mm(left, right, dims=NN):
    return lax.dot_general(left, right, dims, preferred_element_type=F32)


def loop(count, step):
    lax.fori_loop(0, count, lambda i, _: (step(i), 0)[1], 0)


def tile(index, size):
    return pl.ds(pl.multiple_of(index * size, size), size)


def expand(packed, offset, share, start, length):
    n, wide = packed.shape
    place = lax.broadcasted_iota(jnp.int32, (wide, length), 1) + start
    lane = lax.broadcasted_iota(jnp.int32, (wide, length), 0)
    pick = (lane == offset + lax.rem(place, share)).astype(F32).astype(LOW)
    spread = mm(packed, pick)
    row = lax.broadcasted_iota(jnp.int32, (n, length), 0)
    column = lax.broadcasted_iota(jnp.int32, (n, length), 1) + start
    return jnp.sum(jnp.where(row == lax.div(column, share), spread, 0.0), axis=0, keepdims=True)


def normalize(resid):
    centre = resid - jnp.mean(resid, axis=-1, keepdims=True)
    spread = jnp.mean(centre * centre, axis=-1, keepdims=True)
    rstd = lax.rsqrt(spread + eps_norm)
    return centre * rstd, rstd


def column_sum(value):
    return jnp.sum(value, axis=0, keepdims=True)


def reduce_copies(nz):
    return nz + 6 + nz - 1


def reduce_buffers(nz, rows, cols):
    return dict(
        core=pltpu.VMEM((nz, 2, 2, rows, cols), LOW),
        diag=pltpu.VMEM((nz, rows, cols), LOW),
        line=pltpu.VMEM((2, nz, rows, cols), LOW),
        column=pltpu.VMEM((nz - 1, rows, cols), LOW),
    )


def add_rows(store, terms, count, rows):
    step = min(rows, 16)
    per = rows // step

    def one(j):
        i, start = j // per, (j % per) * step
        at = pl.ds(pl.multiple_of(start, step), step)
        total = terms[0](i, at).astype(F32)
        for term in terms[1:]:
            total = total + term(i, at).astype(F32)
        store(i, at, total)

    loop(count * per, one)


def reduce_steps(place, sender, grad, buffers, out, split, parts):
    nz = place.nz
    rows = grad.shape[4]
    core, diag, line, column = (buffers[k] for k in ("core", "diag", "line", "column"))
    groups = ((1, 1), (0, 1), (1, 0), (0, 0))
    here = [place.flips(y=fy, x=fx) for fy, fx in groups]
    by_core = []
    size = nz // parts
    for t in range(parts):
        if t:
            yield
        at = pl.ds(t * size, size)
        by_core.append(sender.send(grad.at[at, :, 1 - place.c], core.at[at], place.device(c=1)))
    yield

    def put(slot, start=0):
        fy, fc, fx = here[slot]

        def store(i, at, value):
            grad[i + start, fy, fc, fx, at, :] = value.astype(LOW)

        return store

    def held(slot, start=0):
        fy, fc, fx = here[slot]
        return lambda i, at: grad[i + start, fy, fc, fx, at, :]

    def add_core(slot):
        fy, _, fx = here[slot]
        add_rows(put(slot), [held(slot), lambda i, at: core[i, fy, fx, at, :]], nz, rows)

    def part(slot, start, count):
        fy, fc, fx = here[slot]
        return grad.at[pl.ds(start, count), fy, fc, fx]

    low, high = pl.ds(0, split), pl.ds(split, nz - split)
    by_y = by_x = x_high = y_low = x_low = y_high = None
    for copy in by_core:
        copy.wait_recv()
    add_core(0)
    if split > 0:
        by_y = sender.send(part(0, 0, split), diag.at[low], place.device(y=1))
    if split < nz:
        by_x = sender.send(part(0, split, nz - split), diag.at[high], place.device(x=1))
    yield
    add_core(1)
    if split < nz:
        x_high = sender.send(part(1, split, nz - split), line.at[0, high], place.device(x=1))
    add_core(2)
    if split > 0:
        y_low = sender.send(part(2, 0, split), line.at[1, low], place.device(y=1))
    yield
    add_core(3)
    yield
    if split > 0:
        by_y.wait_recv()
        add_rows(put(1), [held(1), lambda i, at: diag[i, at, :]], split, rows)
        x_low = sender.send(part(1, 0, split), line.at[0, low], place.device(x=1))
    yield
    if split < nz:
        by_x.wait_recv()
        add_rows(put(2, split), [held(2, split), lambda i, at: diag[i + split, at, :]], nz - split, rows)
        y_high = sender.send(part(2, split, nz - split), line.at[1, high], place.device(y=1))
    yield
    for copy in (x_high, y_low, x_low, y_high):
        if copy is not None:
            copy.wait_recv()
    add_rows(
        put(3),
        [held(3), lambda i, at: line[0, i, at, :], lambda i, at: line[1, i, at, :]],
        nz,
        rows,
    )
    fy, fc, fx = here[3]
    by_z = [
        sender.send(grad.at[place.zth(k), fy, fc, fx], column.at[k - 1], place.device(k=k))
        for k in range(1, nz)
    ]
    yield
    for copy in by_z:
        copy.wait_recv()

    def last(i, at, value):
        out[at, :] = value

    add_rows(
        last,
        [lambda i, at: grad[place.z, fy, fc, fx, at, :]]
        + [lambda i, at, k=k: column[k, at, :] for k in range(nz - 1)],
        1,
        rows,
    )


def sum_steps(place, sender, levels, taken):
    partners = [place.device(c=1), place.device(x=1), place.device(y=1)]
    bit = 1
    while bit < place.nz:
        partners.append(place.device(k=bit))
        bit *= 2
    for s, partner in enumerate(partners):
        copy = sender.send(levels.at[s], taken.at[s], partner)
        yield
        copy.wait_recv()
        levels[s + 1] = levels[s] + taken[s]


class Kernel:
    def __init__(self, name, names, refs):
        self.refs = dict(zip(names, refs))
        self.place = Place()
        self.sender = Sender(self["send"], self["recv"])
        self.plan = PLANS.get(name, ())
        self.count = self.points = 0
        self.saved, self.transfers = [], []

    def __getitem__(self, name):
        return self.refs[name]

    def copy(self, src, dst):
        made = pltpu.make_async_copy(src, dst, self["local"].at[self.count])
        self.count += 1
        made.start()
        return made

    def save(self, src, dst):
        made = self.copy(src, dst)
        self.saved.append(made)
        return made

    def add(self, steps):
        self.transfers.append(steps)
        return len(self.transfers) - 1

    def step(self, number):
        return next(self.transfers[number], self) is not self

    def point(self):
        turn = self.plan[self.points] if self.points < len(self.plan) else ()
        self.points += 1
        for number in turn:
            self.step(number)

    def finish(self, *numbers):
        for number in numbers:
            while self.step(number):
                pass

    def close(self):
        self.finish(*range(len(self.transfers)))
        for made in self.saved:
            made.wait()
        self.sender.close()


PLANS = {
    "forward": (
        (0, 7, 1, 0, 0, 1, 3, 1, 3, 1, 0, 2, 5, 0),
        (7, 3, 1, 2, 5, 2),
        (6, 2, 9),
        (0, 2, 0),
        (6, 2),
        (3, 0),
        (0, 0, 6, 5),
        (5, 4),
        (2, 2, 8, 4),
        (3, 4),
        (),
        (7, 9, 3, 2, 9),
        (2, 3),
        (),
        (3,),
        (),
        (4,),
        (4,),
        (),
        (3, 4),
        (4, 4),
        (3,),
        (),
        (4,),
        (3,),
        (11,),
        (11, 4),
        (4, 11),
        (10, 12),
        (),
        (4,),
        (),
        (12,),
    ),
    "feed_back": (
        (0, 1, 0),
        (0,),
        (),
        (0, 0),
        (1, 1, 1),
        (0,),
        (1,),
        (1,),
        (),
        (),
        (0,),
        (),
        (),
        (1,),
    ),
    "attend_back": (
        (),
        (3, 3),
        (),
        (),
        (3, 6),
        (5, 5, 0, 5),
        (6, 7, 4, 7),
        (6, 6, 0),
        (1, 3, 6, 4),
        (7, 3, 4, 5, 2),
        (6, 5),
        (1, 3, 7),
        (7, 5, 4),
        (7, 4),
        (2, 10, 6),
        (4,),
        (5,),
        (7,),
    ),
    "project_back": (
        (0, 0, 1),
        (1, 2, 2, 0),
        (1, 2, 1, 1),
        (2, 2, 0, 1, 3, 3, 3, 2),
        (3, 3, 0, 3),
        (1, 2, 1, 3),
    ),
}


def call(name, body, ins, spaces_in, outs, scratch, copies, collective_id):
    vmem, hbm = pl.BlockSpec(memory_space=pltpu.VMEM), pl.BlockSpec(memory_space=pl.ANY)
    scratch = dict(
        send=pltpu.SemaphoreType.DMA((copies,)),
        recv=pltpu.SemaphoreType.DMA((copies,)),
        local=pltpu.SemaphoreType.DMA((56,)),
        **scratch,
    )
    names = list(ins) + list(outs) + list(scratch)

    def kernel(*refs):
        body(Kernel(name, names, refs))

    results = pl.pallas_call(
        kernel,
        out_shape=[jax.ShapeDtypeStruct(s, d) for s, d, _ in outs.values()],
        in_specs=[vmem if given in spaces_in else hbm for given in ins],
        out_specs=[vmem if space == "vmem" else hbm for _, _, space in outs.values()],
        scratch_shapes=list(scratch.values()),
        compiler_params=pltpu.CompilerParams(
            collective_id=collective_id, has_side_effects=True, vmem_limit_bytes=63 << 20
        ),
    )(*ins.values())
    return dict(zip(outs, results))


def exchange(k, src, dst):
    copy = k.sender.send(src, dst, k.place.device(x=1))
    yield
    copy.wait_recv()


def row_sum(value):
    return jnp.sum(value.reshape(-1, 8, value.shape[-1]), axis=0)


NORM_ROWS = 128


def forward(by_hand, items, half_len, weights, small, block_input, embed, codes, cols, cotangent, collective_id):
    rows, width = block_input.shape
    full_len = 2 * half_len
    blocks = 4
    nz = lax.axis_size("dp") // 4
    step = 256
    params = ["w_qkv", "small", "w_o", "w_in", "w_out"]

    def body(k):
        place = k.place
        cot_in = k.copy(k["cotangent"], k["cot"])
        full = {p: k["all_" + p] if by_hand else k[p] for p in params}
        kept = [k.copy(k[p], full[p].at[place.z, place.column()]) for p in params if by_hand]
        meet(place)
        for made in kept:
            made.wait()
        number = {}
        if by_hand:
            for p in params:
                number[p] = k.add(gather_steps(place, k.sender, k[p], full[p], nz - nz // 4))

        def arrive(p):
            if by_hand:
                k.finish(number[p])

        codes_over = k.add(exchange(k, k["codes"], k["codes_taken"]))
        cols_over = k.add(exchange(k, k["cols"], k["cols_taken"]))
        input_over = [
            k.add(exchange(k, k["input"].at[pl.ds(i * half_len, half_len)], k["taken"].at[pl.ds(i * half_len, half_len)]))
            for i in range(items)
        ]
        k.point()
        stream, partial_sums = k["stream"], k["partial_sums"]
        partial_sums[...] = jnp.zeros_like(partial_sums)

        def gather_sum(kind, value):
            partial_sums[kind] += row_sum(value)

        for i in range(items):
            item_embed = k["embed"][i : i + 1, :]

            def make_stream(j, i=i, item_embed=item_embed):
                at = pl.ds(pl.multiple_of(i * half_len + j * 64, 64), 64)
                value = k["input"][at, :].astype(F32) + item_embed
                stream[at, :] = value.astype(LOW)
                gather_sum(0, value * value * k["cols"][tile(j, 64), items + i : items + i + 1])

            loop(half_len // 64, make_stream)
        save_stream = k.copy(stream.at[pl.ds(0, rows)], k["save_stream"])
        k.point()
        arrive("small")
        load_small = k.copy(full["small"], k["v_small"])
        load_small.wait()
        shards = k["v_small"].shape[0] * k["v_small"].shape[1]
        for d in range(shards):
            k["packed"][d : d + 1, :] = k["v_small"][d // 8, d % 8, 0:1, :]
        packed = k["packed"][...].astype(LOW)
        share = width // shards
        b_share = share * blocks
        vectors, b_in = k["vectors"], k["v_b_in"]
        for t in range(8):
            vectors[t : t + 1, :] = expand(packed, b_share + t * share, share, 0, width)
            if t in (0, 1, 3, 5):
                k.point()
        for t in range(blocks):
            b_in[t : t + 1, :] = expand(packed, 0, b_share, t * width, width)
            k.point()
        bias_o, bias_out, gain_one, gain_two, shift_one, shift_two = (vectors[t : t + 1, :] for t in range(2, 8))
        heads = k["heads"]

        def weight(name, t, at):
            value = k[name][t, :, :, :, at]
            return value.reshape(-1, value.shape[-1])

        arrive("w_qkv")
        load_qkv = [
            k.copy(full["w_qkv"].at[:, :, :, pl.ds(t * width, width)], k["v_qkv"].at[t]) for t in range(3)
        ]
        k.point()
        mine, theirs = stream.at[pl.ds(0, rows)], stream.at[pl.ds(rows, rows)]

        def project(source, slot, t, bias):
            def one(j):
                at = tile(j, step)
                value = mm(source[...], weight("v_qkv", t, at))
                if bias is not None:
                    value = value + vectors[bias : bias + 1, at]
                heads[slot, :, at] = value.astype(LOW)

            loop(width // step, one)

        for slot, t, bias in ((0, 0, 0), (1, 1, None), (3, 2, 1)):
            load_qkv[t].wait()
            project(mine, slot, t, bias)
            k.point()
        k.finish(codes_over)
        same = lax.broadcasted_iota(jnp.int32, (half_len, half_len), 0) == lax.broadcasted_iota(
            jnp.int32, (half_len, half_len), 1
        )
        for i in range(items):
            asked = k["cols"][:, i : i + 1]
            own = (k["codes"][i : i + 1, :] <= asked) | same
            other = k["codes_taken"][i : i + 1, :] <= asked
            k["permit"][i, :, 0:half_len] = jnp.where(own, 0.0, fill_value)
            k["permit"][i, :, half_len : 2 * half_len] = jnp.where(other, 0.0, fill_value)
        k.save(k["codes_taken"], k["save_codes"])
        k.point()
        for i in range(items):
            item_embed = k["embed"][i : i + 1, :]
            k.finish(input_over[i])

            def make_other(j, i=i, item_embed=item_embed):
                at = pl.ds(pl.multiple_of(i * half_len + j * 64, 64), 64)
                to = pl.ds(pl.multiple_of(rows + i * half_len + j * 64, 64), 64)
                stream[to, :] = (k["taken"][at, :].astype(F32) + item_embed).astype(LOW)

            loop(half_len // 64, make_other)
        for slot, t, bias in ((2, 1, None), (4, 2, 1), (5, 0, 0)):
            project(theirs, slot, t, bias)
            k.point()
        save_heads = k.copy(heads, k["save_heads"])
        save_stream.wait()
        lane = lax.broadcasted_iota(jnp.int32, (half_len, 2 * HD), 1)
        key_lane = lax.broadcasted_iota(jnp.int32, (2 * half_len, 2 * HD), 1)
        pairs = width // (2 * HD)
        for i in range(items):
            at_rows = pl.ds(i * half_len, half_len)

            def pair(p, i=i, at_rows=at_rows):
                at = tile(p, 2 * HD)
                query = heads[0, at_rows, at] * (1.0 / math.sqrt(HD))
                keys = jnp.concatenate([heads[1, at_rows, at], heads[2, at_rows, at]], axis=0)
                values = jnp.concatenate([heads[3, at_rows, at], heads[4, at_rows, at]], axis=0)
                nothing = jnp.zeros((), LOW)
                mixed = None
                logs = k["logs"][i]
                for h in range(2):
                    scores = mm(jnp.where((lane < HD) == (h == 0), query, nothing), keys, NT) + k["permit"][i]
                    peak = jnp.max(scores, axis=1, keepdims=True)
                    expo = jnp.exp(scores - peak)
                    total = jnp.sum(expo, axis=1, keepdims=True)
                    probs = (expo * (1.0 / total)).astype(LOW)
                    part = mm(probs, jnp.where((key_lane < HD) == (h == 0), values, nothing))
                    mixed = part if mixed is None else mixed + part
                    logs = jnp.where(lane == 2 * p + h, peak + jnp.log(total), logs)
                k["logs"][i] = logs
                stream[at_rows, at] = mixed.astype(LOW)

            loop(pairs // 2, pair)
            k.point()
            loop(pairs // 2, lambda p, pair=pair: pair(p + pairs // 2))
            k["log_rows"][i] = k["logs"][i].T[:HEADS]
            k.add(exchange(k, k["log_rows"].at[i], k["logs_taken"].at[i]))
            k.point()
        save_mixed = k.copy(stream.at[pl.ds(0, rows)], k["save_mixed"])
        k.save(k["log_rows"], k["save_logs"])
        arrive("w_o")
        k.copy(full["w_o"], k["v_o"]).wait()
        xhat = k["xhat"]
        for i in range(items):
            at_rows = pl.ds(i * half_len, half_len)
            k["work"][...] = mm(stream[at_rows, :], k["v_o"][...].reshape(width, width)) + bias_o
            item_embed = k["embed"][i : i + 1, :]

            def first_norm(j, i=i, item_embed=item_embed):
                at = pl.ds(pl.multiple_of(i * half_len + j * NORM_ROWS, NORM_ROWS), NORM_ROWS)
                to = pl.ds(pl.multiple_of(rows + i * half_len + j * NORM_ROWS, NORM_ROWS), NORM_ROWS)
                attn = k["work"][tile(j, NORM_ROWS), :]
                gather_sum(1, attn * attn * k["cols"][tile(j, NORM_ROWS), items + i : items + i + 1])
                value, rstd = normalize(k["input"][at, :].astype(F32) + item_embed + attn)
                xhat[at, :] = value
                k["rstd"][at, :] = jnp.broadcast_to(rstd, (NORM_ROWS, 128))
                stream[to, :] = (value * gain_one + shift_one).astype(LOW)

            loop(half_len // NORM_ROWS, first_norm)
            k.point()
        save_hidden = k.copy(stream.at[pl.ds(rows, rows)], k["save_hidden"])
        k.save(xhat, k["save_xhat"])
        k.save(k["rstd"], k["save_rstd"])
        arrive("w_in")
        load_in = [
            k.copy(full["w_in"].at[:, :, :, pl.ds(t * width, width)], k["v_in"].at[t]) for t in range(blocks)
        ]
        k.point()
        save_heads.wait()
        act, slope = heads, k["slope"]
        for t in range(blocks):
            load_in[t].wait()

            def feed(j, t=t):
                at = tile(j, step)
                w_in = weight("v_in", t, at)
                for i in range(items):
                    own = pl.ds(i * half_len, half_len)
                    pre = mm(stream[pl.ds(rows + i * half_len, half_len), :], w_in) + b_in[t : t + 1, at]
                    cdf = 0.5 + 0.5 * lax.erf(pre * (1.0 / math.sqrt(2.0)))
                    act[t, own, at] = (pre * cdf).astype(LOW)
                    pdf = jnp.exp(pre * pre * -0.5) * (1.0 / math.sqrt(2.0 * math.pi))
                    slope[t, own, at] = (cdf + pre * pdf).astype(LOW)

            loop(width // step, feed)
            k.save(act.at[t], k["act"].at[t])
            k.save(slope.at[t], k["save_slope"].at[t])
            k.point()
        arrive("w_out")
        load_out = [k.copy(full["w_out"].at[t], k["v_out"].at[t]) for t in range(blocks)]
        k.point()
        cot_in.wait()
        save_mixed.wait()
        save_hidden.wait()
        for made in load_out:
            made.wait()
        for i in range(items):
            at_rows = pl.ds(i * half_len, half_len)
            total = None
            for t in range(blocks):
                part = mm(act[t, at_rows, :], k["v_out"][t].reshape(width, width))
                total = part if total is None else total + part
            k["work"][...] = total + bias_out

            def second_norm(j, i=i):
                at = pl.ds(pl.multiple_of(i * half_len + j * NORM_ROWS, NORM_ROWS), NORM_ROWS)
                to = pl.ds(pl.multiple_of(rows + i * half_len + j * NORM_ROWS, NORM_ROWS), NORM_ROWS)
                weight_rows = k["cols"][tile(j, NORM_ROWS), items + i : items + i + 1]
                branch = k["work"][tile(j, NORM_ROWS), :]
                gather_sum(2, branch * branch * weight_rows)
                value, rstd = normalize(xhat[at, :] * gain_one + shift_one + branch)
                result = value * gain_two + shift_two
                gather_sum(3, result * result * weight_rows)
                stream[at, :] = result.astype(LOW)
                grad = k["cot"][at, :].astype(F32)
                gather_sum(5, grad * value)
                gather_sum(6, grad)
                scaled = grad * gain_two
                back = rstd * (
                    scaled
                    - jnp.mean(scaled, axis=-1, keepdims=True)
                    - value * jnp.mean(scaled * value, axis=-1, keepdims=True)
                )
                k["back"][at, :] = back
                back_low = back.astype(LOW)
                stream[to, :] = back_low
                gather_sum(4, back_low.astype(F32))

            loop(half_len // NORM_ROWS, second_norm)
            at_other = pl.ds(rows + i * half_len, half_len)
            k.save(stream.at[at_rows], k["output"].at[at_rows])
            k.save(stream.at[at_other], k["save_back_low"].at[at_rows])
            k.save(k["back"].at[at_rows], k["save_back"].at[at_rows])
        for kind in range(7):
            k["sums"][kind : kind + 1, :] = column_sum(partial_sums[kind])
        k["sums"][7:8, :] = jnp.zeros((1, width), F32)
        k["sums"][7:8, 0:128] = column_sum(k["cols"][...])
        k.save(vectors, k["save_vectors"])
        k.finish(*range(len(k.transfers)))
        k.save(k["logs_taken"], k["save_logs_taken"])
        k.save(k["cols_taken"], k["save_cols"])
        k.close()

    ins = dict(zip(params, [weights[0], small] + weights[1:]))
    spaces_in = list(params) if by_hand else []
    spaces_in += ["input", "embed", "codes", "cols"]
    ins.update(input=block_input, embed=embed, codes=codes, cols=cols, cotangent=cotangent)
    outs = {}
    if by_hand:
        for p in params:
            outs["all_" + p] = ((nz, 8) + ins[p].shape, ins[p].dtype, "hbm")
    outs.update(
        save_heads=((6, rows, width), LOW, "hbm"),
        save_codes=(codes.shape, F32, "hbm"),
        save_cols=(cols.shape, F32, "hbm"),
        save_stream=((rows, width), LOW, "hbm"),
        save_hidden=((rows, width), LOW, "hbm"),
        save_mixed=((rows, width), LOW, "hbm"),
        save_logs=((items, HEADS, half_len), F32, "hbm"),
        save_logs_taken=((items, HEADS, half_len), F32, "hbm"),
        save_xhat=((rows, width), F32, "hbm"),
        save_rstd=((rows, 128), F32, "hbm"),
        act=((blocks, rows, width), LOW, "hbm"),
        save_slope=((blocks, rows, width), LOW, "hbm"),
        output=((rows, width), LOW, "hbm"),
        save_back_low=((rows, width), LOW, "hbm"),
        save_back=((rows, width), F32, "hbm"),
        save_vectors=((8, width), F32, "hbm"),
        sums=((8, width), F32, "vmem"),
    )
    small_full = (nz, 8) + small.shape if by_hand else small.shape
    copies = 5 * gather_copies(nz) + 2 * items + 2
    scratch = dict(
        partial_sums=pltpu.VMEM((7, 8, width), F32),
        taken=pltpu.VMEM((rows, width), LOW),
        codes_taken=pltpu.VMEM(codes.shape, F32),
        cols_taken=pltpu.VMEM(cols.shape, F32),
        stream=pltpu.VMEM((2 * rows, width), LOW),
        v_qkv=pltpu.VMEM((3, 4, 8, 32, width), LOW),
        v_small=pltpu.VMEM(small_full, F32),
        packed=pltpu.VMEM((small_full[0] * 8, small_full[-1]), F32),
        vectors=pltpu.VMEM((8, width), F32),
        v_b_in=pltpu.VMEM((8, width), F32),
        heads=pltpu.VMEM((6, rows, width), LOW),
        permit=pltpu.VMEM((items, half_len, full_len), F32),
        logs=pltpu.VMEM((items, half_len, 128), F32),
        log_rows=pltpu.VMEM((items, HEADS, half_len), F32),
        logs_taken=pltpu.VMEM((items, HEADS, half_len), F32),
        v_o=pltpu.VMEM((4, 8, 32, width), LOW),
        work=pltpu.VMEM((half_len, width), F32),
        xhat=pltpu.VMEM((rows, width), F32),
        rstd=pltpu.VMEM((rows, 128), F32),
        v_in=pltpu.VMEM((blocks, 4, 8, 32, width), LOW),
        slope=pltpu.VMEM((blocks, rows, width), LOW),
        v_out=pltpu.VMEM((blocks, 8, 128, width), LOW),
        cot=pltpu.VMEM((rows, width), LOW),
        back=pltpu.VMEM((rows, width), F32),
    )
    results = call("forward" if by_hand else "", body, ins, spaces_in, outs, scratch, copies, collective_id)
    return dict(results, codes=codes, cols=cols)


def feed_back(by_hand, items, half_len, fw, weights, collective_id):
    blocks, rows, width = fw["act"].shape
    nz = lax.axis_size("dp") // 4
    half_width = width // 2
    step = 256

    def body(k):
        place, sender = k.place, k.sender
        load_low = k.copy(k["back_low"], k["v_low"])
        load_act = [k.copy(k["act"].at[t], k["v_act"].at[t]) for t in range(blocks)]
        load_out = k.copy(k["w_out"], k["v_out"])
        load_slope = k.copy(k["slope"], k["v_slope"])
        load_in = [
            k.copy(k["w_in"].at[:, :, :, pl.ds(t * width, width)], k["v_in"].at[t]) for t in range(blocks)
        ]
        load_rest = [
            k.copy(k["back"], k["v_back"]),
            k.copy(k["xhat"], k["v_xhat"]),
            k.copy(k["rstd"], k["v_rstd"]),
            k.copy(k["w_o"], k["v_o"]),
        ]
        meet(place)
        load_low.wait()
        low, act, grad = k["v_low"], k["v_act"], k["grad"]
        halves = []
        if by_hand:
            for q in range(2):
                buffers = {name: k[f"{name}{q}"] for name in ("core", "diag", "line", "column")}
                target = k["grad_out"].at[:, pl.ds(q * half_width, half_width)]
                halves.append(k.add(reduce_steps(place, sender, grad.at[q], buffers, target, nz // 2, nz)))
        for t in range(blocks):
            load_act[t].wait()

            def outer(j, t=t):
                part = mm(act[t, :, tile(j, step)], low[...], TN).astype(LOW)
                part = part.reshape(2, 128, width)
                y, c = j // 2, j % 2
                grad[0, t, y, c] = part[:, :, :half_width]
                grad[1, t, y, c] = part[:, :, half_width:]

            loop(width // step, outer)
            for q in halves:
                k.step(q)
        k.point()
        if not by_hand:
            for q in range(2):
                k.save(grad.at[q], k["grad_out"].at[:, :, :, :, :, pl.ds(q * half_width, half_width)])
        load_out.wait()
        load_slope.wait()
        sums = k["sums"]
        sums[...] = jnp.zeros_like(sums)
        for t in range(blocks):

            def pull(j, t=t):
                at = tile(j, step)
                w_out = k["v_out"][t, pl.ds(j * (step // 128), step // 128)].reshape(step, width)
                part = mm(low[...], w_out, NT) * k["v_slope"][t, :, at].astype(F32)
                part = part.astype(LOW)
                act[t, :, at] = part
                sums[t : t + 1, at] = column_sum(part.astype(F32))

            loop(width // step, pull)
            k.save(act.at[t], k["pre_grad"].at[t])
            k.point()
        for made in load_in + load_rest:
            made.wait()
        gain = k["vectors"][4:5, :]
        partial_sums = k["partial_sums"]
        partial_sums[...] = jnp.zeros_like(partial_sums)
        for i in range(items):
            at_rows = pl.ds(i * half_len, half_len)
            total = None
            for t in range(blocks):
                part = mm(act[t, at_rows, :], k["v_in"][t].reshape(width, width), NT)
                total = part if total is None else total + part
            k["work"][...] = total
            k.point()

            def first_back(j, i=i):
                at = pl.ds(pl.multiple_of(i * half_len + j * NORM_ROWS, NORM_ROWS), NORM_ROWS)
                hidden = k["work"][tile(j, NORM_ROWS), :] + k["v_back"][at, :]
                xhat = k["v_xhat"][at, :]
                rstd = k["v_rstd"][at, 0:1]
                partial_sums[0] += row_sum(hidden * xhat)
                partial_sums[1] += row_sum(hidden)
                scaled = hidden * gain
                value = rstd * (
                    scaled
                    - jnp.mean(scaled, axis=-1, keepdims=True)
                    - xhat * jnp.mean(scaled * xhat, axis=-1, keepdims=True)
                )
                k["v_back"][at, :] = value
                value_low = value.astype(LOW)
                low[at, :] = value_low
                partial_sums[2] += row_sum(value_low.astype(F32))

            loop(half_len // NORM_ROWS, first_back)
            k.save(k["v_back"].at[at_rows], k["input_part"].at[at_rows])
            k.save(low.at[at_rows], k["attn_grad"].at[at_rows])
            k.point()
        for kind in range(3):
            sums[4 + kind : 5 + kind, :] = column_sum(partial_sums[kind])
        w_o = k["v_o"][...].reshape(width, width)
        for i in range(items):
            at_rows = pl.ds(i * half_len, half_len)
            k["v_mixed_grad"][at_rows, :] = mm(low[at_rows, :], w_o, NT).astype(LOW)
            k.save(k["v_mixed_grad"].at[at_rows], k["mixed_grad"].at[at_rows])
            k.point()
        k.close()

    ins = dict(
        back_low=fw["save_back_low"],
        act=fw["act"],
        w_out=weights[3],
        slope=fw["save_slope"],
        w_in=weights[2],
        back=fw["save_back"],
        xhat=fw["save_xhat"],
        rstd=fw["save_rstd"],
        w_o=weights[1],
        vectors=fw["save_vectors"],
    )
    outs = dict(
        pre_grad=((blocks, rows, width), LOW, "hbm"),
        input_part=((rows, width), F32, "hbm"),
        attn_grad=((rows, width), LOW, "hbm"),
        mixed_grad=((rows, width), LOW, "hbm"),
        sums=((8, width), F32, "vmem"),
    )
    if by_hand:
        outs["grad_out"] = ((128, width), F32, "vmem")
    else:
        outs["grad_out"] = ((4, 2, 2, 2, 128, width), LOW, "hbm")
    scratch = dict(
        v_low=pltpu.VMEM((rows, width), LOW),
        v_act=pltpu.VMEM((blocks, rows, width), LOW),
        v_out=pltpu.VMEM((blocks, 8, 128, width), LOW),
        v_slope=pltpu.VMEM((blocks, rows, width), LOW),
        v_in=pltpu.VMEM((blocks, 4, 8, 32, width), LOW),
        v_back=pltpu.VMEM((rows, width), F32),
        v_xhat=pltpu.VMEM((rows, width), F32),
        v_rstd=pltpu.VMEM((rows, 128), F32),
        v_o=pltpu.VMEM((4, 8, 32, width), LOW),
        v_mixed_grad=pltpu.VMEM((rows, width), LOW),
        work=pltpu.VMEM((half_len, width), F32),
        grad=pltpu.VMEM((2, 4, 2, 2, 2, 128, half_width), LOW),
        partial_sums=pltpu.VMEM((3, 8, width), F32),
    )
    copies = 1
    if by_hand:
        copies += 2 * reduce_copies(nz)
        for q in range(2):
            for name, buffer in reduce_buffers(nz, 128, half_width).items():
                scratch[f"{name}{q}"] = buffer
    return call("feed_back" if by_hand else "", body, ins, ("vectors",), outs, scratch, copies, collective_id)


def attend_back(by_hand, items, half_len, fw, fb, collective_id):
    blocks, rows, width = fw["act"].shape
    nz = lax.axis_size("dp") // 4
    chunks = blocks + 1
    step = 256
    scale = 1.0 / math.sqrt(HD)

    def body(k):
        place, sender = k.place, k.sender
        load_hidden = k.copy(k["hidden"], k["v_left"])
        load_pre = [k.copy(k["pre_grad"].at[t], k["v_pre"].at[t]) for t in range(blocks)]
        load_mixed = [k.copy(k["attn_grad"], k["v_attn"])]
        load_heads = [
            k.copy(k["heads"], k["v_heads"]),
            k.copy(k["mixed_grad"], k["v_grad"].at[0]),
        ]
        load_heads[1].wait()
        meet(place)
        over_grad = []
        for i in range(items):
            at_rows = pl.ds(i * half_len, half_len)
            over_grad.append(k.add(exchange(k, k["v_grad"].at[0, at_rows], k["v_grad"].at[1, at_rows])))
            k.step(over_grad[i])
        grad = k["grad"]
        chunk = []

        def ready(q):
            if by_hand:
                buffers = {name: k[f"{name}{q}"] for name in ("core", "diag", "line", "column")}
                target = k["grad_in"].at[:, pl.ds(q * width, width)] if q < blocks else k["grad_o"]
                k.step(k.add(reduce_steps(place, sender, grad.at[q], buffers, target, nz, 1)))
            k.point()

        load_hidden.wait()
        left, turned = k["v_left"], k["v_turned"]

        def turn(j):
            turned[tile(j, 128), :] = left[:, tile(j, 128)].T

        def outer(q, right):
            def one(j):
                at = tile(j, step)
                part = mm(turned[...], right[:, at]).astype(LOW)
                grad[q, :, :, :, :, :, at] = part.reshape(4, 2, 2, 2, 32, step)

            loop(width // step, one)
            ready(q)

        loop(width // 128, turn)
        for t in range(blocks):
            load_pre[t].wait()
            outer(t, k["v_pre"].at[t])
        load_left = k.copy(k["mixed"], left)
        load_left.wait()
        for made in load_mixed:
            made.wait()
        loop(width // 128, turn)
        outer(blocks, k["v_attn"])
        load_heads[0].wait()
        same = lax.broadcasted_iota(jnp.int32, (half_len, half_len), 0) == lax.broadcasted_iota(
            jnp.int32, (half_len, half_len), 1
        )
        for i in range(items):
            asked = k["codes"][items + i : items + i + 1, :]
            asked_taken = k["codes_taken"][items + i : items + i + 1, :]
            code = k["cols"][:, 2 * items + i : 2 * items + i + 1]
            code_taken = k["cols_taken"][:, 2 * items + i : 2 * items + i + 1]
            k["permit"][i, 0:half_len, :] = jnp.where((code <= asked) | same, 0.0, fill_value)
            k["permit"][i, half_len : 2 * half_len, :] = jnp.where(code_taken <= asked, 0.0, fill_value)
            k["permit_taken"][i] = jnp.where(code <= asked_taken, 0.0, fill_value)
        k.point()
        heads, grads, result = k["v_heads"], k["v_grad"], k["v_pre"]
        lane = lax.broadcasted_iota(jnp.int32, (half_len, 2 * HD), 1)
        key_lane = lax.broadcasted_iota(jnp.int32, (2 * half_len, 2 * HD), 1)
        nothing = jnp.zeros((), LOW)
        pairs = width // (2 * HD)

        def ours(i):
            at_rows = pl.ds(i * half_len, half_len)

            def pair(p):
                at = tile(p, 2 * HD)
                query = heads[0, at_rows, at]
                keys = jnp.concatenate([heads[1, at_rows, at], heads[2, at_rows, at]], axis=0)
                values = jnp.concatenate([heads[3, at_rows, at], heads[4, at_rows, at]], axis=0)
                grad_row = grads[0, at_rows, at]
                query_part = key_part = value_part = None
                for h in range(2):
                    mine = (lane < HD) == (h == 0)
                    key_mine = (key_lane < HD) == (h == 0)
                    query_h = jnp.where(mine, query, nothing)
                    grad_h = jnp.where(mine, grad_row, nothing)
                    keys_h = jnp.where(key_mine, keys, nothing)
                    at_head = pl.ds(2 * p + h, 1)
                    scores = mm(keys, query_h * scale, NT) + (k["permit"][i] - k["logs"][i, at_head, :])
                    probs = jnp.exp(scores)
                    prob_grad = mm(values, grad_h, NT)
                    centre = column_sum(probs * prob_grad)
                    k["centre"][i, at_head, :] = centre
                    score_grad = (probs * (prob_grad - centre)).astype(LOW)
                    parts = (
                        mm(score_grad, keys_h, TN),
                        mm(score_grad[:half_len], query_h),
                        mm(probs[:half_len].astype(LOW), grad_h),
                    )
                    if h == 0:
                        query_part, key_part, value_part = parts
                    else:
                        query_part = query_part + parts[0]
                        key_part = key_part + parts[1]
                        value_part = value_part + parts[2]
                query_low = (query_part * scale).astype(LOW)
                result[0, at_rows, at] = query_low
                k["sums"][0:1, at] += column_sum(query_low.astype(F32))
                k["parts"][0, at_rows, at] = key_part
                k["parts"][1, at_rows, at] = value_part

            loop(pairs // 2, pair)
            k.point()
            loop(pairs // 2, lambda p: pair(p + pairs // 2))

        def theirs(i):
            at_rows = pl.ds(i * half_len, half_len)

            def pair(p):
                at = tile(p, 2 * HD)
                query = heads[5, at_rows, at]
                keys, values = heads[1, at_rows, at], heads[3, at_rows, at]
                grad_row = grads[1, at_rows, at]
                key_part, value_part = k["parts"][0, at_rows, at], k["parts"][1, at_rows, at]
                for h in range(2):
                    mine = (lane < HD) == (h == 0)
                    query_h = jnp.where(mine, query, nothing)
                    grad_h = jnp.where(mine, grad_row, nothing)
                    at_head = pl.ds(2 * p + h, 1)
                    scores = mm(keys, query_h * scale, NT) + (
                        k["permit_taken"][i] - k["logs_taken"][i, at_head, :]
                    )
                    probs = jnp.exp(scores)
                    prob_grad = mm(values, grad_h, NT)
                    score_grad = (probs * (prob_grad - k["centre_taken"][i, at_head, :])).astype(LOW)
                    key_part = key_part + mm(score_grad, query_h)
                    value_part = value_part + mm(probs.astype(LOW), grad_h)
                result[1, at_rows, at] = (key_part * scale).astype(LOW)
                value_low = value_part.astype(LOW)
                result[2, at_rows, at] = value_low
                k["sums"][1:2, at] += column_sum(value_low.astype(F32))

            loop(pairs // 2, pair)
            k.point()
            loop(pairs // 2, lambda p: pair(p + pairs // 2))

        k["sums"][...] = jnp.zeros_like(k["sums"])
        over = []
        for i in range(items):
            ours(i)
            over.append(k.add(exchange(k, k["centre"].at[i], k["centre_taken"].at[i])))
            k.step(over[i])
            k.point()
        k.save(result.at[0], k["joint_grad"].at[0])
        for i in range(items):
            k.finish(over[i], over_grad[i])
            theirs(i)
            k.point()
        k.save(result.at[1], k["joint_grad"].at[1])
        k.save(result.at[2], k["joint_grad"].at[2])
        if not by_hand:
            for q in range(blocks):
                k.save(grad.at[q], k["grad_in"].at[:, :, :, :, :, pl.ds(q * width, width)])
            k.save(grad.at[blocks], k["grad_o"])
        k.close()

    ins = dict(
        hidden=fw["save_hidden"],
        pre_grad=fb["pre_grad"],
        mixed=fw["save_mixed"],
        attn_grad=fb["attn_grad"],
        heads=fw["save_heads"],
        mixed_grad=fb["mixed_grad"],
        codes=fw["codes"],
        codes_taken=fw["save_codes"],
        cols=fw["cols"],
        cols_taken=fw["save_cols"],
        logs=fw["save_logs"],
        logs_taken=fw["save_logs_taken"],
    )
    outs = dict(
        joint_grad=((3, rows, width), LOW, "hbm"),
        sums=((8, width), F32, "vmem"),
    )
    if by_hand:
        outs["grad_in"] = ((32, blocks * width), F32, "vmem")
        outs["grad_o"] = ((32, width), F32, "vmem")
    else:
        outs["grad_in"] = ((4, 2, 2, 2, 32, blocks * width), LOW, "hbm")
        outs["grad_o"] = ((4, 2, 2, 2, 32, width), LOW, "hbm")
    scratch = dict(
        v_left=pltpu.VMEM((rows, width), LOW),
        v_turned=pltpu.VMEM((width, rows), LOW),
        v_pre=pltpu.VMEM((blocks, rows, width), LOW),
        v_attn=pltpu.VMEM((rows, width), LOW),
        v_heads=pltpu.VMEM((6, rows, width), LOW),
        v_grad=pltpu.VMEM((2, rows, width), LOW),
        grad=pltpu.VMEM((chunks, 4, 2, 2, 2, 32, width), LOW),
        permit=pltpu.VMEM((items, 2 * half_len, half_len), F32),
        permit_taken=pltpu.VMEM((items, half_len, half_len), F32),
        parts=pltpu.VMEM((2, rows, width), F32),
        centre=pltpu.VMEM((items, HEADS, half_len), F32),
        centre_taken=pltpu.VMEM((items, HEADS, half_len), F32),
    )
    copies = 2 * items
    if by_hand:
        copies += chunks * reduce_copies(nz)
        for q in range(chunks):
            for name, buffer in reduce_buffers(nz, 32, width).items():
                scratch[f"{name}{q}"] = buffer
    spaces = ("codes", "codes_taken", "cols", "cols_taken", "logs", "logs_taken")
    return call("attend_back" if by_hand else "", body, ins, spaces, outs, scratch, copies, collective_id)


def project_back(by_hand, items, half_len, fw, fb, ab, weights, collective_id):
    _, rows, width = ab["joint_grad"].shape
    nz = lax.axis_size("dp") // 4
    step = 256
    stages = 3 + (nz - 1).bit_length()

    def body(k):
        place, sender = k.place, k.sender
        load_stream = k.copy(k["stream"], k["v_left"])
        load_joint = [k.copy(k["joint_grad"].at[t], k["v_joint"].at[t]) for t in range(3)]
        load_qkv = [
            k.copy(k["w_qkv"].at[:, :, :, pl.ds(t * width, width)], k["v_qkv"].at[t]) for t in range(3)
        ]
        load_part = k.copy(k["input_part"], k["v_part"])
        meet(place)
        levels = k["levels"]
        for s, name in enumerate(("sums_one", "sums_two", "sums_three")):
            levels[0, 8 * s : 8 * s + 8, :] = k[name][...]
        k.add(sum_steps(place, sender, levels, k["levels_taken"]))
        k.step(0)
        grad = k["grad"]
        load_stream.wait()
        left, turned = k["v_left"], k["v_turned"]

        def turn(j):
            turned[tile(j, 128), :] = left[:, tile(j, 128)].T

        loop(width // 128, turn)
        for q in range(3):
            load_joint[q].wait()

            def outer(j, q=q):
                at = tile(j, step)
                part = mm(turned[...], k["v_joint"][q, :, at]).astype(LOW)
                grad[q, :, :, :, :, :, at] = part.reshape(4, 2, 2, 2, 32, step)

            loop(width // step, outer)
            if by_hand:
                buffers = {name: k[f"{name}{q}"] for name in ("core", "diag", "line", "column")}
                target = k["grad_qkv"].at[:, pl.ds(q * width, width)]
                k.step(k.add(reduce_steps(place, sender, grad.at[q], buffers, target, nz // 2, 1)))
            k.point()
        for made in load_qkv + [load_part]:
            made.wait()
        for i in range(items):
            at_rows = pl.ds(i * half_len, half_len)
            total = k["v_part"][at_rows, :]
            for q in range(3):
                total = total + mm(k["v_joint"][q, at_rows, :], k["v_qkv"][q].reshape(width, width), NT)
            left[at_rows, :] = total.astype(LOW)
            k.save(left.at[at_rows], k["input_grad"].at[at_rows])
            k.point()
        k.finish(*range(len(k.transfers)))
        k["totals"][...] = levels[stages]
        if not by_hand:
            for q in range(3):
                k.save(grad.at[q], k["grad_qkv"].at[:, :, :, :, :, pl.ds(q * width, width)])
        k.close()

    ins = dict(
        stream=fw["save_stream"],
        joint_grad=ab["joint_grad"],
        w_qkv=weights[0],
        input_part=fb["input_part"],
        sums_one=fw["sums"],
        sums_two=fb["sums"],
        sums_three=ab["sums"],
    )
    outs = dict(
        input_grad=((rows, width), LOW, "hbm"),
        totals=((24, width), F32, "vmem"),
    )
    if by_hand:
        outs["grad_qkv"] = ((32, 3 * width), F32, "vmem")
    else:
        outs["grad_qkv"] = ((4, 2, 2, 2, 32, 3 * width), LOW, "hbm")
    scratch = dict(
        v_left=pltpu.VMEM((rows, width), LOW),
        v_turned=pltpu.VMEM((width, rows), LOW),
        v_joint=pltpu.VMEM((3, rows, width), LOW),
        v_qkv=pltpu.VMEM((3, 4, 8, 32, width), LOW),
        v_part=pltpu.VMEM((rows, width), F32),
        grad=pltpu.VMEM((3, 4, 2, 2, 2, 32, width), LOW),
        levels=pltpu.VMEM((stages + 1, 24, width), F32),
        levels_taken=pltpu.VMEM((stages, 24, width), F32),
    )
    copies = stages
    if by_hand:
        copies += 3 * reduce_copies(nz)
        for q in range(3):
            for name, buffer in reduce_buffers(nz, 32, width).items():
                scratch[f"{name}{q}"] = buffer
    return call("project_back" if by_hand else "", body, ins, ("sums_one", "sums_two", "sums_three"), outs, scratch, copies, collective_id)


def body(
    block_input,
    lengths,
    mask,
    blocks,
    timesteps,
    w_qkv,
    w_o,
    w_in,
    w_out,
    b_in,
    biases,
    gains,
    shifts,
    cotangent,
):
    items, half_len, width = block_input.shape
    rows = items * half_len
    f32 = jnp.float32
    n = n_devices()
    share = width // n
    b_count = b_in.shape[0]
    positions = lax.axis_index("ctx") * half_len + jnp.arange(half_len, dtype=jnp.int32)
    valid = (positions[None, :] < lengths[:, None]) & ((mask == 1) | (positions[None, :] == 0))
    numbers = blocks.astype(f32)
    key_codes = jnp.where(valid, numbers, code_absent)
    codes = jnp.pad(jnp.concatenate([key_codes, numbers]), ((0, 8 - 2 * items), (0, 0)))
    cols = jnp.concatenate([numbers, valid.astype(f32), key_codes]).T
    cols = jnp.pad(cols, ((0, 0), (0, 128 - 3 * items)))
    embed = jnp.pad(time_embed(timesteps, width), ((0, 8 - items), (0, 0)))
    small = jnp.concatenate([b_in, biases.reshape(-1), gains.reshape(-1), shifts.reshape(-1)])
    small_wide = -(-small.shape[0] // 128) * 128
    small = jnp.pad(small.astype(f32), (0, small_wide - small.shape[0]))
    small = jnp.broadcast_to(small[None, :], (8, small_wide))
    by_hand = w_qkv.shape[0] == 32
    weights = [w_qkv, w_o, w_in, w_out]
    if not by_hand:
        weights = [lax.all_gather(w, AXES, axis=0, tiled=True) for w in weights]
        weights = [w.reshape(4, 8, w.shape[0] // 32, w.shape[1]) for w in weights]
        small = lax.all_gather(small, AXES, axis=0).reshape(n // 8, 8, 8, small_wide)
    fw = forward(
        by_hand,
        items,
        half_len,
        weights,
        small,
        block_input.reshape(rows, width),
        embed,
        codes,
        cols,
        cotangent.reshape(rows, width),
        1,
    )
    if by_hand:
        weights = [fw["all_" + p] for p in ("w_qkv", "w_o", "w_in", "w_out")]
    fb = feed_back(by_hand, items, half_len, fw, weights, 2)
    ab = attend_back(by_hand, items, half_len, fw, fb, 3)
    pb = project_back(by_hand, items, half_len, fw, fb, ab, weights, 4)
    grads = [pb["grad_qkv"], ab["grad_o"], ab["grad_in"], fb["grad_out"]]
    if not by_hand:
        grads = [
            lax.psum_scatter(
                part.astype(f32).reshape(-1, part.shape[-1]), AXES, scatter_dimension=0, tiled=True
            )
            for part in grads
        ]
    totals = pb["totals"]
    me = my_index()
    grad_b_in = lax.dynamic_slice(totals[8:12].reshape(-1), (me * b_count,), (b_count,))
    order = (16, 17, 14, 4, 12, 5, 13, 6)
    mine = lax.dynamic_slice(totals, (0, me * share), (24, share))
    mine = jnp.stack([mine[row] for row in order])
    count = jnp.sum(totals[7, items : 2 * items])
    rms = jnp.sqrt(jnp.sum(totals[:4], axis=1) / (count * width))
    return (
        fw["output"].reshape(block_input.shape),
        pb["input_grad"].reshape(block_input.shape),
        *grads,
        grad_b_in,
        mine[:4],
        mine[4:6],
        mine[6:8],
        rms,
    )


def solution(mesh):
    in_specs = (
        P("dp", "ctx", None),
        P("dp"),
        P("dp", "ctx"),
        P("dp", "ctx"),
        P("dp"),
        P(("dp", "ctx"), None),
        P(("dp", "ctx"), None),
        P(("dp", "ctx"), None),
        P(("dp", "ctx"), None),
        P(("dp", "ctx")),
        P(None, ("dp", "ctx")),
        P(None, ("dp", "ctx")),
        P(None, ("dp", "ctx")),
        P("dp", "ctx", None),
    )
    out_specs = (
        P("dp", "ctx", None),
        P("dp", "ctx", None),
        P(("dp", "ctx"), None),
        P(("dp", "ctx"), None),
        P(("dp", "ctx"), None),
        P(("dp", "ctx"), None),
        P(("dp", "ctx")),
        P(None, ("dp", "ctx")),
        P(None, ("dp", "ctx")),
        P(None, ("dp", "ctx")),
        P(),
    )
    return jax.shard_map(body, mesh=mesh, in_specs=in_specs, out_specs=out_specs, check_vma=False)
```

```python
from functools import partial
import math

import jax
import jax.numpy as jnp
from jax import lax
from jax.experimental import pallas as pl
from jax.experimental.pallas import tpu as pltpu
from jax.sharding import PartitionSpec as P

HEADS = 16
HD = 64

AXES = ("dp", "ctx")
X = 1


def my_index():
    return lax.axis_index("dp") * lax.axis_size("ctx") + lax.axis_index("ctx")


def n_devices():
    return lax.axis_size("dp") * lax.axis_size("ctx")


fill_value = -1e30
eps_norm = 1e-05
code_absent = 30000.0


def time_embed(steps, width):
    half = width // 2
    freqs = jnp.exp(jnp.arange(half, dtype=jnp.float32) * (-math.log(10000.0) / half))
    angle = steps.astype(jnp.float32)[:, None] * freqs[None, :]
    return jnp.concatenate([jnp.sin(angle), jnp.cos(angle)], axis=-1)


MESH = pl.DeviceIdType.MESH


class Place:
    def __init__(self):
        dp = lax.axis_index("dp")
        self.nz = lax.axis_size("dp") // 4
        self.x = lax.axis_index("ctx")
        self.c = dp % 2
        self.y = (dp // 2) % 2
        self.z = dp // 4

    def zth(self, k):
        z, bit = self.z, 1
        while bit < self.nz:
            if k & bit:
                z = z + bit * (1 - 2 * ((self.z // bit) % 2))
            bit *= 2
        return z

    def flips(self, y=0, c=0, x=0):
        return (
            1 - self.y if y else self.y,
            1 - self.c if c else self.c,
            1 - self.x if x else self.x,
        )

    def device(self, k=0, y=0, c=0, x=0):
        fy, fc, fx = self.flips(y, c, x)
        return ((self.zth(k) * 2 + fy) * 2 + fc, fx)

    def shard(self, k=0, y=0, c=0, x=0):
        fy, fc, fx = self.flips(y, c, x)
        return ((self.zth(k) * 2 + fy) * 2 + fc) * 2 + fx

    def column(self, y=0, c=0, x=0):
        fy, fc, fx = self.flips(y, c, x)
        return (fy * 2 + fc) * 2 + fx

    def partners(self):
        return [self.device(k=k) for k in range(1, self.nz)] + [
            self.device(x=1),
            self.device(y=1),
            self.device(c=1),
        ]


def meet(place):
    barrier = pltpu.get_barrier_semaphore()
    partners = place.partners()
    for partner in partners:
        pl.semaphore_signal(barrier, inc=1, device_id=partner, device_id_type=MESH)
    pl.semaphore_wait(barrier, len(partners))


class Sender:
    def __init__(self, send_sem, recv_sem):
        self.send_sem, self.recv_sem = send_sem, recv_sem
        self.count = 0
        self.open = []

    def send(self, src, dst, device, keep=None):
        copy = pltpu.make_async_remote_copy(
            src_ref=src,
            dst_ref=dst,
            send_sem=self.send_sem.at[self.count],
            recv_sem=self.recv_sem.at[self.count],
            device_id=device,
            device_id_type=MESH,
        )
        self.count += 1
        copy.start()
        (self.open if keep is None else keep).append(copy)
        return copy

    def close(self):
        for copy in self.open:
            copy.wait_send()
        self.open = []


def gather_copies(nz):
    return 4 * nz + 5


def gather_steps(place, sender, shard, full, split):
    nz = place.nz
    mine, at_x, at_y, diag = (place.column(x=fx, y=fy) for fy, fx in ((0, 0), (0, 1), (1, 0), (1, 1)))
    own = full.at[place.z, mine]
    by_z = [sender.send(shard, own, place.device(k=k)) for k in range(1, nz)]
    yield
    from_x = [sender.send(shard, own, place.device(x=1))]
    from_y = [sender.send(shard, own, place.device(y=1))]
    yield
    for k in range(1, nz):
        by_z[k - 1].wait_recv()
        piece = full.at[place.zth(k), mine]
        from_x.append(sender.send(piece, piece, place.device(x=1)))
        from_y.append(sender.send(piece, piece, place.device(y=1)))
        yield
    to_core = [sender.send(full.at[:, mine], full.at[:, mine], place.device(c=1))]
    from_diag = []
    yield
    for k in range(nz):
        from_x[k].wait_recv()
        if k < split:
            piece = full.at[place.zth(k), at_x]
            from_diag.append(sender.send(piece, piece, place.device(y=1)))
        else:
            from_y[k].wait_recv()
            piece = full.at[place.zth(k), at_y]
            from_diag.append(sender.send(piece, piece, place.device(x=1)))
        yield
    to_core.append(sender.send(full.at[:, at_x], full.at[:, at_x], place.device(c=1)))
    for k in range(split):
        from_y[k].wait_recv()
    to_core.append(sender.send(full.at[:, at_y], full.at[:, at_y], place.device(c=1)))
    yield
    half = nz // 2
    for start, size in ((0, half), (half, nz - half)):
        for copy in from_diag if start == 0 else ():
            copy.wait_recv()
        part = full.at[pl.ds(start, size), diag]
        to_core.append(sender.send(part, part, place.device(c=1)))
    yield
    for copy in to_core:
        copy.wait_recv()


def gather_late_steps(place, sender, shard, full):
    nz = place.nz
    own = full.at[place.z, place.column()]
    from_x = sender.send(shard, own, place.device(x=1))
    from_y = sender.send(shard, own, place.device(y=1))
    yield
    from_x.wait_recv()
    piece = full.at[place.z, place.column(x=1)]
    from_diag = sender.send(piece, piece, place.device(y=1))
    yield
    from_y.wait_recv()
    from_diag.wait_recv()
    by_z = []
    for k in range(1, nz):
        for fy in range(2):
            for fx in range(2):
                piece = full.at[place.z, place.column(y=fy, x=fx)]
                by_z.append(sender.send(piece, piece, place.device(k=k)))
    yield
    for copy in by_z:
        copy.wait_recv()
    to_core = []
    for fy in range(2):
        for fx in range(2):
            piece = full.at[:, place.column(y=fy, x=fx)]
            to_core.append(sender.send(piece, piece, place.device(c=1)))
    yield
    for copy in to_core:
        copy.wait_recv()


NN = (((1,), (0,)), ((), ()))
NT = (((1,), (1,)), ((), ()))
TN = (((0,), (0,)), ((), ()))
LOW = jnp.bfloat16
F32 = jnp.float32


def mm(left, right, dims=NN):
    return lax.dot_general(left, right, dims, preferred_element_type=F32)


def loop(count, step):
    lax.fori_loop(0, count, lambda i, _: (step(i), 0)[1], 0)


def tile(index, size):
    return pl.ds(pl.multiple_of(index * size, size), size)


def expand(packed, offset, share, start, length):
    n, wide = packed.shape
    place = lax.broadcasted_iota(jnp.int32, (wide, length), 1) + start
    lane = lax.broadcasted_iota(jnp.int32, (wide, length), 0)
    pick = (lane == offset + lax.rem(place, share)).astype(F32).astype(LOW)
    spread = mm(packed, pick)
    row = lax.broadcasted_iota(jnp.int32, (n, length), 0)
    column = lax.broadcasted_iota(jnp.int32, (n, length), 1) + start
    return jnp.sum(jnp.where(row == lax.div(column, share), spread, 0.0), axis=0, keepdims=True)


def normalize(resid):
    centre = resid - jnp.mean(resid, axis=-1, keepdims=True)
    spread = jnp.mean(centre * centre, axis=-1, keepdims=True)
    rstd = lax.rsqrt(spread + eps_norm)
    return centre * rstd, rstd


def column_sum(value):
    return jnp.sum(value, axis=0, keepdims=True)


def reduce_copies(nz):
    return nz + 6 + nz - 1


def reduce_buffers(nz, rows, cols):
    return dict(
        core=pltpu.VMEM((nz, 2, 2, rows, cols), LOW),
        diag=pltpu.VMEM((nz, rows, cols), LOW),
        line=pltpu.VMEM((2, nz, rows, cols), LOW),
        column=pltpu.VMEM((nz - 1, rows, cols), LOW),
    )


def add_rows(store, terms, count, rows):
    step = min(rows, 16)
    per = rows // step

    def one(j):
        i, start = j // per, (j % per) * step
        at = pl.ds(pl.multiple_of(start, step), step)
        total = terms[0](i, at).astype(F32)
        for term in terms[1:]:
            total = total + term(i, at).astype(F32)
        store(i, at, total)

    loop(count * per, one)


def reduce_steps(place, sender, grad, buffers, out, split, parts):
    nz = place.nz
    rows = grad.shape[4]
    core, diag, line, column = (buffers[k] for k in ("core", "diag", "line", "column"))
    groups = ((1, 1), (0, 1), (1, 0), (0, 0))
    here = [place.flips(y=fy, x=fx) for fy, fx in groups]
    sent, by_core = [], []
    size = nz // parts
    for t in range(parts):
        if t:
            yield
        at = pl.ds(t * size, size)
        by_core.append(sender.send(grad.at[at, :, 1 - place.c], core.at[at], place.device(c=1), sent))
    yield

    def put(slot, start=0):
        fy, fc, fx = here[slot]

        def store(i, at, value):
            grad[i + start, fy, fc, fx, at, :] = value.astype(LOW)

        return store

    def held(slot, start=0):
        fy, fc, fx = here[slot]
        return lambda i, at: grad[i + start, fy, fc, fx, at, :]

    def add_core(slot):
        fy, _, fx = here[slot]
        add_rows(put(slot), [held(slot), lambda i, at: core[i, fy, fx, at, :]], nz, rows)

    def part(slot, start, count):
        fy, fc, fx = here[slot]
        return grad.at[pl.ds(start, count), fy, fc, fx]

    low, high = pl.ds(0, split), pl.ds(split, nz - split)
    by_y = by_x = x_high = y_low = x_low = y_high = None
    for copy in by_core:
        copy.wait_recv()
    add_core(0)
    if split > 0:
        by_y = sender.send(part(0, 0, split), diag.at[low], place.device(y=1), sent)
    if split < nz:
        by_x = sender.send(part(0, split, nz - split), diag.at[high], place.device(x=1), sent)
    yield
    add_core(1)
    if split < nz:
        x_high = sender.send(part(1, split, nz - split), line.at[0, high], place.device(x=1), sent)
    add_core(2)
    if split > 0:
        y_low = sender.send(part(2, 0, split), line.at[1, low], place.device(y=1), sent)
    yield
    add_core(3)
    yield
    if split > 0:
        by_y.wait_recv()
        add_rows(put(1), [held(1), lambda i, at: diag[i, at, :]], split, rows)
        x_low = sender.send(part(1, 0, split), line.at[0, low], place.device(x=1), sent)
    yield
    if split < nz:
        by_x.wait_recv()
        add_rows(put(2, split), [held(2, split), lambda i, at: diag[i + split, at, :]], nz - split, rows)
        y_high = sender.send(part(2, split, nz - split), line.at[1, high], place.device(y=1), sent)
    yield
    for copy in (x_high, y_low, x_low, y_high):
        if copy is not None:
            copy.wait_recv()
    add_rows(
        put(3),
        [held(3), lambda i, at: line[0, i, at, :], lambda i, at: line[1, i, at, :]],
        nz,
        rows,
    )
    fy, fc, fx = here[3]
    by_z = [
        sender.send(grad.at[place.zth(k), fy, fc, fx], column.at[k - 1], place.device(k=k), sent)
        for k in range(1, nz)
    ]
    yield
    for copy in by_z:
        copy.wait_recv()

    def last(i, at, value):
        out[at, :] = value

    add_rows(
        last,
        [lambda i, at: grad[place.z, fy, fc, fx, at, :]]
        + [lambda i, at, k=k: column[k, at, :] for k in range(nz - 1)],
        1,
        rows,
    )
    for copy in sent:
        copy.wait_send()


def sum_steps(place, sender, levels, taken):
    partners = [place.device(c=1), place.device(x=1), place.device(y=1)]
    bit = 1
    while bit < place.nz:
        partners.append(place.device(k=bit))
        bit *= 2
    for s, partner in enumerate(partners):
        copy = sender.send(levels.at[s], taken.at[s], partner)
        yield
        copy.wait_recv()
        levels[s + 1] = levels[s] + taken[s]


class Kernel:
    def __init__(self, name, names, refs):
        self.refs = dict(zip(names, refs))
        self.place = Place()
        self.sender = Sender(self["send"], self["recv"])
        self.plan = PLANS.get(name, ())
        self.count = self.points = 0
        self.saved, self.transfers = [], []

    def __getitem__(self, name):
        return self.refs[name]

    def copy(self, src, dst):
        made = pltpu.make_async_copy(src, dst, self["local"].at[self.count])
        self.count += 1
        made.start()
        return made

    def save(self, src, dst):
        made = self.copy(src, dst)
        self.saved.append(made)
        return made

    def add(self, steps):
        self.transfers.append(steps)
        return len(self.transfers) - 1

    def step(self, number):
        return next(self.transfers[number], self) is not self

    def point(self):
        turn = self.plan[self.points] if self.points < len(self.plan) else ()
        self.points += 1
        for number in turn:
            self.step(number)

    def finish(self, *numbers):
        for number in numbers:
            while self.step(number):
                pass

    def close(self):
        self.finish(*range(len(self.transfers)))
        for made in self.saved:
            made.wait()
        self.sender.close()


PARTS = (
    ("w_qkv", None, None, False),
    ("small", None, None, False),
    ("w_o", None, None, True),
    ("w_in", 0, 2048, False),
    ("w_in", 2048, 3072, False),
    ("w_in", 3072, 4096, True),
    ("w_out", 0, 512, False),
    ("w_out", 512, 1024, False),
)
PLANS = {
    "forward": (
        (9, 0, 0, 6, 0, 5, 4, 11, 2, 5, 14, 0, 2, 1, 0, 0, 3),
        (11, 2, 8, 0, 9, 9, 12, 0),
        (10, 8, 13, 0, 8),
        (8, 11, 3),
        (0, 5, 10, 0, 15, 4),
        (3, 4, 6, 3, 3, 4, 0, 14),
        (13, 4, 13, 0),
        (3,),
        (12, 2, 14),
        (7, 10, 13, 4, 15),
        (10, 3, 6),
        (15,),
        (12, 2),
        (7,),
        (4, 4),
        (2,),
        (6, 3, 7),
        (),
        (),
        (3, 3, 4, 6, 5),
        (6,),
        (6, 4, 5),
        (7, 16, 3, 17),
        (3, 7, 7),
        (4, 6),
        (6, 6),
        (18, 4, 7),
        (7, 5),
        (17, 6, 7, 7),
        (),
        (6,),
        (7, 18),
        (16,),
        (7,),
        (),
        (17,),
    ),
    "feed_back": (
        (0,),
        (0, 1, 0),
        (),
        (0, 0),
        (1,),
        (1,),
        (1, 0, 1),
        (),
        (),
        (1, 0),
    ),
    "attend_back": (
        (3,),
        (),
        (),
        (),
        (5, 6),
        (4, 6, 6, 4, 0),
        (3, 4),
        (7, 1),
        (1, 5, 6),
        (3, 3, 0, 6),
        (2, 5, 7, 1),
        (4, 9, 3, 5, 6),
        (7, 5, 2, 3),
        (9, 4),
        (7, 9, 2),
        (11, 4, 7, 3),
        (6,),
        (11, 6),
        (),
        (7, 11, 12),
        (11, 11, 5, 12, 13, 7),
        (14, 11),
        (12, 14, 14, 7),
        (14, 14, 13, 12, 14, 12),
    ),
}


def call(name, body, ins, spaces_in, outs, scratch, copies, collective_id):
    vmem, hbm = pl.BlockSpec(memory_space=pltpu.VMEM), pl.BlockSpec(memory_space=pl.ANY)
    scratch = dict(
        send=pltpu.SemaphoreType.DMA((copies,)),
        recv=pltpu.SemaphoreType.DMA((copies,)),
        local=pltpu.SemaphoreType.DMA((64,)),
        **scratch,
    )
    names = list(ins) + list(outs) + list(scratch)

    def kernel(*refs):
        body(Kernel(name, names, refs))

    results = pl.pallas_call(
        kernel,
        out_shape=[jax.ShapeDtypeStruct(s, d) for s, d, _ in outs.values()],
        in_specs=[vmem if given in spaces_in else hbm for given in ins],
        out_specs=[vmem if space == "vmem" else hbm for _, _, space in outs.values()],
        scratch_shapes=list(scratch.values()),
        compiler_params=pltpu.CompilerParams(
            collective_id=collective_id, has_side_effects=True, vmem_limit_bytes=63 << 20
        ),
    )(*ins.values())
    return dict(zip(outs, results))


def exchange(k, src, dst):
    copy = k.sender.send(src, dst, k.place.device(x=1))
    yield
    copy.wait_recv()


def row_sum(value):
    return jnp.sum(value.reshape(-1, 8, value.shape[-1]), axis=0)


NORM_ROWS = 128


def forward(by_hand, items, half_len, weights, small, block_input, embed, codes, cols, cotangent, collective_id):
    rows, width = block_input.shape
    full_len = 2 * half_len
    blocks = 4
    nz = lax.axis_size("dp") // 4
    step = 256
    params = ["w_qkv", "small", "w_o", "w_in", "w_out"]

    def body(k):
        place = k.place
        cot_in = k.copy(k["cotangent"], k["cot"])
        full = {p: k["v_" + p] for p in params}
        kept = [k.copy(k[p], full[p].at[place.z, place.column()] if by_hand else full[p]) for p in params]
        meet(place)
        for made in kept:
            made.wait()
        number = {}
        if by_hand:
            for p, start, stop, late in PARTS:
                if start is None:
                    shard, whole = k[p], full[p]
                else:
                    shard = k[p].at[:, pl.ds(start, stop - start)]
                    whole = full[p].at[:, :, :, pl.ds(start, stop - start)]
                if late:
                    steps = gather_late_steps(place, k.sender, shard, whole)
                else:
                    steps = gather_steps(place, k.sender, shard, whole, nz - nz // 4)
                number.setdefault(p, []).append(k.add(steps))

        def arrive(p, *which):
            if by_hand:
                k.finish(*[number[p][i] for i in which or range(len(number[p]))])

        codes_over = k.add(exchange(k, k["codes"], k["codes_taken"]))
        cols_over = k.add(exchange(k, k["cols"], k["cols_taken"]))
        quarter = half_len // 2
        input_over = [
            k.add(exchange(k, k["input"].at[pl.ds(i * quarter, quarter)], k["taken"].at[pl.ds(i * quarter, quarter)]))
            for i in range(2 * items)
        ]
        k.point()
        stream, partial_sums = k["stream"], k["partial_sums"]
        partial_sums[...] = jnp.zeros_like(partial_sums)

        def gather_sum(kind, value):
            partial_sums[kind] += row_sum(value)

        for i in range(items):
            item_embed = k["embed"][i : i + 1, :]

            def make_stream(j, i=i, item_embed=item_embed):
                at = pl.ds(pl.multiple_of(i * half_len + j * 64, 64), 64)
                value = k["input"][at, :].astype(F32) + item_embed
                stream[at, :] = value.astype(LOW)
                gather_sum(0, value * value * k["cols"][tile(j, 64), items + i : items + i + 1])

            loop(half_len // 64, make_stream)
        save_stream = k.copy(stream.at[pl.ds(0, rows)], k["save_stream"])
        k.point()
        arrive("small")
        shards = k["v_small"].shape[0] * k["v_small"].shape[1]
        for d in range(shards):
            k["packed"][d : d + 1, :] = k["v_small"][d // 8, d % 8, 0:1, :]
        packed = k["packed"][...].astype(LOW)
        share = width // shards
        b_share = share * blocks
        vectors, b_in = k["vectors"], k["v_b_in"]
        for t in range(8):
            vectors[t : t + 1, :] = expand(packed, b_share + t * share, share, 0, width)
            if t in (0, 1, 3, 5):
                k.point()
        for t in range(blocks):
            b_in[t : t + 1, :] = expand(packed, 0, b_share, t * width, width)
            k.point()
        bias_o = vectors[2:3, :]
        gain_one, gain_two, shift_one, shift_two = (vectors[t : t + 1, :] for t in range(4, 8))
        heads = k["heads"]

        def weight(name, t, j):
            value = full[name][:, :, :, pl.ds(pl.multiple_of(t * width + j * step, step), step)]
            return value.reshape(-1, step)

        def keep(name):
            if by_hand:
                k.save(full[name], k["all_" + name])

        arrive("w_qkv")
        keep("w_qkv")
        k.point()

        def project(slot, t, bias):
            def one(j):
                at = tile(j, step)
                value = mm(stream[pl.ds(0, rows), :], weight("w_qkv", t, j))
                if bias is not None:
                    value = value + vectors[bias : bias + 1, at]
                heads[slot, :, at] = value.astype(LOW)

            loop(width // step, one)

        for slot, t, bias in ((0, 0, 0), (1, 1, None), (3, 2, 1)):
            project(slot, t, bias)
            k.point()
        k.finish(codes_over)
        same = lax.broadcasted_iota(jnp.int32, (half_len, half_len), 0) == lax.broadcasted_iota(
            jnp.int32, (half_len, half_len), 1
        )
        for i in range(items):
            asked = k["cols"][:, i : i + 1]
            own = (k["codes"][i : i + 1, :] <= asked) | same
            other = k["codes_taken"][i : i + 1, :] <= asked
            k["permit"][i, :, 0:half_len] = jnp.where(own, 0.0, fill_value)
            k["permit"][i, :, half_len : 2 * half_len] = jnp.where(other, 0.0, fill_value)
        k.save(k["codes_taken"], k["save_codes"])
        k.point()
        save_stream.wait()
        lane = lax.broadcasted_iota(jnp.int32, (half_len, 2 * HD), 1)
        key_lane = lax.broadcasted_iota(jnp.int32, (2 * half_len, 2 * HD), 1)
        pairs = width // (2 * HD)
        for i in range(items):
            at_rows = pl.ds(i * half_len, half_len)
            at_theirs = pl.ds(rows + i * half_len, half_len)
            item_embed = k["embed"][i : i + 1, :]
            k.finish(input_over[2 * i], input_over[2 * i + 1])

            def make_other(j, i=i, item_embed=item_embed):
                at = pl.ds(pl.multiple_of(i * half_len + j * 64, 64), 64)
                to = pl.ds(pl.multiple_of(rows + i * half_len + j * 64, 64), 64)
                stream[to, :] = (k["taken"][at, :].astype(F32) + item_embed).astype(LOW)

            def project_other(j, at_rows=at_rows, at_theirs=at_theirs):
                at = tile(j, step)
                source = stream[at_theirs, :]
                heads[2, at_rows, at] = mm(source, weight("w_qkv", 1, j)).astype(LOW)
                heads[4, at_rows, at] = (mm(source, weight("w_qkv", 2, j)) + vectors[1:2, at]).astype(LOW)
                heads[5, at_rows, at] = (mm(source, weight("w_qkv", 0, j)) + vectors[0:1, at]).astype(LOW)

            loop(half_len // 64, make_other)
            loop(width // step, project_other)
            if i == items - 1:
                save_heads = k.copy(heads, k["save_heads"])
            k.point()

            def pair(p, i=i, at_rows=at_rows):
                at = tile(p, 2 * HD)
                query = heads[0, at_rows, at] * (1.0 / math.sqrt(HD))
                keys = jnp.concatenate([heads[1, at_rows, at], heads[2, at_rows, at]], axis=0)
                values = jnp.concatenate([heads[3, at_rows, at], heads[4, at_rows, at]], axis=0)
                nothing = jnp.zeros((), LOW)
                mixed = None
                logs = k["logs"][i]
                for h in range(2):
                    scores = mm(jnp.where((lane < HD) == (h == 0), query, nothing), keys, NT) + k["permit"][i]
                    peak = jnp.max(scores, axis=1, keepdims=True)
                    expo = jnp.exp(scores - peak)
                    total = jnp.sum(expo, axis=1, keepdims=True)
                    probs = (expo * (1.0 / total)).astype(LOW)
                    part = mm(probs, jnp.where((key_lane < HD) == (h == 0), values, nothing))
                    mixed = part if mixed is None else mixed + part
                    logs = jnp.where(lane == 2 * p + h, peak + jnp.log(total), logs)
                k["logs"][i] = logs
                stream[at_rows, at] = mixed.astype(LOW)

            loop(pairs // 2, pair)
            k.point()
            loop(pairs // 2, lambda p, pair=pair: pair(p + pairs // 2))
            k["log_rows"][i] = k["logs"][i].T[:HEADS]
            k.add(exchange(k, k["log_rows"].at[i], k["logs_taken"].at[i]))
            k.point()
        save_mixed = k.copy(stream.at[pl.ds(0, rows)], k["save_mixed"])
        k.save(k["log_rows"], k["save_logs"])
        arrive("w_o")
        keep("w_o")
        xhat = k["xhat"]
        for i in range(items):
            at_rows = pl.ds(i * half_len, half_len)
            k["work"][...] = mm(stream[at_rows, :], full["w_o"][...].reshape(width, width)) + bias_o
            item_embed = k["embed"][i : i + 1, :]

            def first_norm(j, i=i, item_embed=item_embed):
                at = pl.ds(pl.multiple_of(i * half_len + j * NORM_ROWS, NORM_ROWS), NORM_ROWS)
                to = pl.ds(pl.multiple_of(rows + i * half_len + j * NORM_ROWS, NORM_ROWS), NORM_ROWS)
                attn = k["work"][tile(j, NORM_ROWS), :]
                gather_sum(1, attn * attn * k["cols"][tile(j, NORM_ROWS), items + i : items + i + 1])
                value, rstd = normalize(k["input"][at, :].astype(F32) + item_embed + attn)
                xhat[at, :] = value
                k["rstd"][at, :] = jnp.broadcast_to(rstd, (NORM_ROWS, 128))
                stream[to, :] = (value * gain_one + shift_one).astype(LOW)

            loop(half_len // NORM_ROWS, first_norm)
            k.point()
        save_hidden = k.copy(stream.at[pl.ds(rows, rows)], k["save_hidden"])
        k.save(xhat, k["save_xhat"])
        k.save(k["rstd"], k["save_rstd"])
        save_heads.wait()
        act, slope = heads, k["slope"]
        in_parts = {start: i for i, (start, _) in enumerate(part[1:3] for part in PARTS if part[0] == "w_in")}
        for t in range(blocks):
            if t * width in in_parts:
                arrive("w_in", in_parts[t * width])
                k.point()

            def feed(j, t=t):
                at = tile(j, step)
                w_in = weight("w_in", t, j)
                for i in range(items):
                    own = pl.ds(i * half_len, half_len)
                    pre = mm(stream[pl.ds(rows + i * half_len, half_len), :], w_in) + b_in[t : t + 1, at]
                    cdf = 0.5 + 0.5 * lax.erf(pre * (1.0 / math.sqrt(2.0)))
                    act[t, own, at] = (pre * cdf).astype(LOW)
                    pdf = jnp.exp(pre * pre * -0.5) * (1.0 / math.sqrt(2.0 * math.pi))
                    slope[t, own, at] = (cdf + pre * pdf).astype(LOW)

            loop(width // step, feed)
            k.save(act.at[t], k["act"].at[t])
            k.save(slope.at[t], k["save_slope"].at[t])
            k.point()
        keep("w_in")
        cot_in.wait()
        save_mixed.wait()
        save_hidden.wait()
        back = k["back"]
        out_parts = [(start, stop) for p, start, stop, _ in PARTS if p == "w_out"] if by_hand else [(0, width)]
        for which, (start, stop) in enumerate(out_parts):
            columns = pl.ds(start, stop - start)
            arrive("w_out", which)
            for i in range(items):
                at_rows = pl.ds(i * half_len, half_len)
                total = None
                for t in range(blocks):
                    part = mm(act[t, at_rows, :], full["w_out"][t, :, :, columns].reshape(width, stop - start))
                    total = part if total is None else total + part
                back[at_rows, columns] = total + vectors[3:4, columns]
            k.point()
        keep("w_out")
        for i in range(items):
            at_rows = pl.ds(i * half_len, half_len)

            def second_norm(j, i=i):
                at = pl.ds(pl.multiple_of(i * half_len + j * NORM_ROWS, NORM_ROWS), NORM_ROWS)
                to = pl.ds(pl.multiple_of(rows + i * half_len + j * NORM_ROWS, NORM_ROWS), NORM_ROWS)
                weight_rows = k["cols"][tile(j, NORM_ROWS), items + i : items + i + 1]
                branch = back[at, :]
                gather_sum(2, branch * branch * weight_rows)
                value, rstd = normalize(xhat[at, :] * gain_one + shift_one + branch)
                result = value * gain_two + shift_two
                gather_sum(3, result * result * weight_rows)
                stream[at, :] = result.astype(LOW)
                grad = k["cot"][at, :].astype(F32)
                gather_sum(5, grad * value)
                gather_sum(6, grad)
                scaled = grad * gain_two
                passed = rstd * (
                    scaled
                    - jnp.mean(scaled, axis=-1, keepdims=True)
                    - value * jnp.mean(scaled * value, axis=-1, keepdims=True)
                )
                back[at, :] = passed
                back_low = passed.astype(LOW)
                stream[to, :] = back_low
                gather_sum(4, back_low.astype(F32))

            loop(half_len // NORM_ROWS, second_norm)
            at_other = pl.ds(rows + i * half_len, half_len)
            k.save(stream.at[at_rows], k["output"].at[at_rows])
            k.save(stream.at[at_other], k["save_back_low"].at[at_rows])
            k.save(back.at[at_rows], k["save_back"].at[at_rows])
        for kind in range(7):
            k["sums"][kind : kind + 1, :] = column_sum(partial_sums[kind])
        k["sums"][7:8, :] = jnp.zeros((1, width), F32)
        k["sums"][7:8, 0:128] = column_sum(k["cols"][...])
        k.save(vectors, k["save_vectors"])
        k.finish(*range(len(k.transfers)))
        k.save(k["logs_taken"], k["save_logs_taken"])
        k.save(k["cols_taken"], k["save_cols"])
        k.close()

    ins = dict(zip(params, [weights[0], small] + weights[1:]))
    spaces_in = list(params) if by_hand else []
    spaces_in += ["input", "embed", "codes", "cols"]
    ins.update(input=block_input, embed=embed, codes=codes, cols=cols, cotangent=cotangent)
    outs = {}
    if by_hand:
        for p in params:
            if p != "small":
                outs["all_" + p] = ((nz, 8) + ins[p].shape, ins[p].dtype, "hbm")
    outs.update(
        save_heads=((6, rows, width), LOW, "hbm"),
        save_codes=(codes.shape, F32, "hbm"),
        save_cols=(cols.shape, F32, "hbm"),
        save_stream=((rows, width), LOW, "hbm"),
        save_hidden=((rows, width), LOW, "hbm"),
        save_mixed=((rows, width), LOW, "hbm"),
        save_logs=((items, HEADS, half_len), F32, "hbm"),
        save_logs_taken=((items, HEADS, half_len), F32, "hbm"),
        save_xhat=((rows, width), F32, "hbm"),
        save_rstd=((rows, 128), F32, "hbm"),
        act=((blocks, rows, width), LOW, "hbm"),
        save_slope=((blocks, rows, width), LOW, "hbm"),
        output=((rows, width), LOW, "hbm"),
        save_back_low=((rows, width), LOW, "hbm"),
        save_back=((rows, width), F32, "hbm"),
        save_vectors=((8, width), F32, "hbm"),
        sums=((8, width), F32, "vmem"),
    )
    small_full = (nz, 8) + small.shape if by_hand else small.shape
    copies = len(PARTS) * max(gather_copies(nz), 4 * nz + 4) + 3 * items + 2
    scratch = dict(
        partial_sums=pltpu.VMEM((7, 8, width), F32),
        taken=pltpu.VMEM((rows, width), LOW),
        codes_taken=pltpu.VMEM(codes.shape, F32),
        cols_taken=pltpu.VMEM(cols.shape, F32),
        stream=pltpu.VMEM((2 * rows, width), LOW),
        v_w_qkv=pltpu.VMEM((4, 8, 32, 3 * width), LOW),
        v_small=pltpu.VMEM(small_full, F32),
        packed=pltpu.VMEM((small_full[0] * 8, small_full[-1]), F32),
        vectors=pltpu.VMEM((8, width), F32),
        v_b_in=pltpu.VMEM((8, width), F32),
        heads=pltpu.VMEM((6, rows, width), LOW),
        permit=pltpu.VMEM((items, half_len, full_len), F32),
        logs=pltpu.VMEM((items, half_len, 128), F32),
        log_rows=pltpu.VMEM((items, HEADS, half_len), F32),
        logs_taken=pltpu.VMEM((items, HEADS, half_len), F32),
        v_w_o=pltpu.VMEM((4, 8, 32, width), LOW),
        work=pltpu.VMEM((half_len, width), F32),
        xhat=pltpu.VMEM((rows, width), F32),
        rstd=pltpu.VMEM((rows, 128), F32),
        v_w_in=pltpu.VMEM((4, 8, 32, blocks * width), LOW),
        slope=pltpu.VMEM((blocks, rows, width), LOW),
        v_w_out=pltpu.VMEM((4, 8, 128, width), LOW),
        cot=pltpu.VMEM((rows, width), LOW),
        back=pltpu.VMEM((rows, width), F32),
    )
    results = call("forward" if by_hand else "", body, ins, spaces_in, outs, scratch, copies, collective_id)
    return dict(results, codes=codes, cols=cols)


def feed_back(by_hand, items, half_len, fw, weights, collective_id):
    blocks, rows, width = fw["act"].shape
    nz = lax.axis_size("dp") // 4
    half_width = width // 2
    step = 256

    def body(k):
        place, sender = k.place, k.sender
        load_low = k.copy(k["back_low"], k["v_low"])
        load_act = [k.copy(k["act"].at[t], k["v_act"].at[t]) for t in range(blocks)]
        load_out = k.copy(k["w_out"], k["v_w"])
        load_slope = k.copy(k["slope"], k["v_slope"])
        load_hidden = k.copy(k["hidden"], k["v_left"])
        load_rest = [
            k.copy(k["back"], k["v_back"]),
            k.copy(k["xhat"], k["v_xhat"]),
            k.copy(k["rstd"], k["v_rstd"]),
            k.copy(k["w_o"], k["v_o"]),
        ]
        meet(place)
        load_low.wait()
        low, act, grad = k["v_low"], k["v_act"], k["grad"]
        halves = []
        if by_hand:
            for q in range(2):
                buffers = {name: k[f"{name}{q}"] for name in ("core", "diag", "line", "column")}
                target = k["grad_out"].at[:, pl.ds(q * half_width, half_width)]
                halves.append(k.add(reduce_steps(place, sender, grad.at[q], buffers, target, nz // 2, nz)))
        for t in range(blocks):
            load_act[t].wait()

            def outer(j, t=t):
                part = mm(act[t, :, tile(j, step)], low[...], TN).astype(LOW)
                part = part.reshape(2, 128, width)
                y, c = j // 2, j % 2
                grad[0, t, y, c] = part[:, :, :half_width]
                grad[1, t, y, c] = part[:, :, half_width:]

            loop(width // step, outer)
            for q in halves:
                k.step(q)
        k.point()
        if not by_hand:
            for q in range(2):
                k.save(grad.at[q], k["grad_out"].at[:, :, :, :, :, pl.ds(q * half_width, half_width)])
        load_out.wait()
        load_slope.wait()
        sums = k["sums"]
        sums[...] = jnp.zeros_like(sums)
        for t in range(blocks):

            def pull(j, t=t):
                at = tile(j, step)
                w_out = k["v_w"][t, j].reshape(step, width)
                part = mm(low[...], w_out, NT) * k["v_slope"][t, :, at].astype(F32)
                part = part.astype(LOW)
                act[t, :, at] = part
                sums[t : t + 1, at] = column_sum(part.astype(F32))

            loop(width // step, pull)
            k.point()
        load_in = [k.copy(k["w_in"].at[:, :, :, pl.ds(t * width, width)], k["v_w"].at[t]) for t in range(blocks)]
        load_hidden.wait()
        left, turned = k["v_left"], k["v_turned"]

        def turn(j):
            turned[tile(j, 128), :] = left[:, tile(j, 128)].T

        loop(width // 128, turn)
        save_in = []
        for t in range(blocks):
            if t >= 2:
                save_in[t - 2].wait()

            def outer_in(j, t=t):
                at = tile(j, step)
                part = mm(turned[...], act[t, :, at]).astype(LOW)
                k["grad_in_part"][t % 2, :, :, :, :, :, at] = part.reshape(4, 2, 2, 2, 32, step)

            loop(width // step, outer_in)
            save_in.append(k.copy(k["grad_in_part"].at[t % 2], k["grad_in"].at[t]))
            k.point()
        for made in load_in + load_rest + save_in[2:]:
            made.wait()
        gain = k["vectors"][4:5, :]
        partial_sums = k["partial_sums"]
        partial_sums[...] = jnp.zeros_like(partial_sums)
        for i in range(items):
            at_rows = pl.ds(i * half_len, half_len)
            total = None
            for t in range(blocks):
                part = mm(act[t, at_rows, :], k["v_w"][t].reshape(width, width), NT)
                total = part if total is None else total + part
            k["work"][...] = total
            k.point()

            def first_back(j, i=i):
                at = pl.ds(pl.multiple_of(i * half_len + j * NORM_ROWS, NORM_ROWS), NORM_ROWS)
                hidden = k["work"][tile(j, NORM_ROWS), :] + k["v_back"][at, :]
                xhat = k["v_xhat"][at, :]
                rstd = k["v_rstd"][at, 0:1]
                partial_sums[0] += row_sum(hidden * xhat)
                partial_sums[1] += row_sum(hidden)
                scaled = hidden * gain
                value = rstd * (
                    scaled
                    - jnp.mean(scaled, axis=-1, keepdims=True)
                    - xhat * jnp.mean(scaled * xhat, axis=-1, keepdims=True)
                )
                k["v_back"][at, :] = value
                value_low = value.astype(LOW)
                low[at, :] = value_low
                partial_sums[2] += row_sum(value_low.astype(F32))

            loop(half_len // NORM_ROWS, first_back)
            k.save(k["v_back"].at[at_rows], k["input_part"].at[at_rows])
            k.save(low.at[at_rows], k["attn_grad"].at[at_rows])
            k.point()
        for kind in range(3):
            sums[4 + kind : 5 + kind, :] = column_sum(partial_sums[kind])
        w_o = k["v_o"][...].reshape(width, width)
        for i in range(items):
            at_rows = pl.ds(i * half_len, half_len)
            k["v_mixed_grad"][at_rows, :] = mm(low[at_rows, :], w_o, NT).astype(LOW)
            k.save(k["v_mixed_grad"].at[at_rows], k["mixed_grad"].at[at_rows])
            k.point()
        k.close()

    ins = dict(
        back_low=fw["save_back_low"],
        act=fw["act"],
        w_out=weights[3].reshape(blocks, 4, 8, 32, width),
        slope=fw["save_slope"],
        w_in=weights[2],
        back=fw["save_back"],
        xhat=fw["save_xhat"],
        rstd=fw["save_rstd"],
        hidden=fw["save_hidden"],
        w_o=weights[1],
        vectors=fw["save_vectors"],
    )
    outs = dict(
        grad_in=((blocks, 4, 2, 2, 2, 32, width), LOW, "hbm"),
        input_part=((rows, width), F32, "hbm"),
        attn_grad=((rows, width), LOW, "hbm"),
        mixed_grad=((rows, width), LOW, "hbm"),
        sums=((8, width), F32, "vmem"),
    )
    if by_hand:
        outs["grad_out"] = ((128, width), F32, "vmem")
    else:
        outs["grad_out"] = ((4, 2, 2, 2, 128, width), LOW, "hbm")
    scratch = dict(
        v_low=pltpu.VMEM((rows, width), LOW),
        v_act=pltpu.VMEM((blocks, rows, width), LOW),
        v_left=pltpu.VMEM((rows, width), LOW),
        v_turned=pltpu.VMEM((width, rows), LOW),
        grad_in_part=pltpu.VMEM((2, 4, 2, 2, 2, 32, width), LOW),
        v_slope=pltpu.VMEM((blocks, rows, width), LOW),
        v_w=pltpu.VMEM((blocks, 4, 8, 32, width), LOW),
        v_back=pltpu.VMEM((rows, width), F32),
        v_xhat=pltpu.VMEM((rows, width), F32),
        v_rstd=pltpu.VMEM((rows, 128), F32),
        v_o=pltpu.VMEM((4, 8, 32, width), LOW),
        v_mixed_grad=pltpu.VMEM((rows, width), LOW),
        work=pltpu.VMEM((half_len, width), F32),
        grad=pltpu.VMEM((2, 4, 2, 2, 2, 128, half_width), LOW),
        partial_sums=pltpu.VMEM((3, 8, width), F32),
    )
    copies = 1
    if by_hand:
        copies += 2 * reduce_copies(nz)
        for q in range(2):
            for name, buffer in reduce_buffers(nz, 128, half_width).items():
                scratch[f"{name}{q}"] = buffer
    return call("feed_back" if by_hand else "", body, ins, ("vectors",), outs, scratch, copies, collective_id)


def attend_back(by_hand, items, half_len, fw, fb, weights, collective_id):
    blocks, rows, width = fw["act"].shape
    nz = lax.axis_size("dp") // 4
    chunks = blocks + 2
    step = 256
    scale = 1.0 / math.sqrt(HD)
    stages = 3 + (nz - 1).bit_length()

    def body(k):
        place, sender = k.place, k.sender
        load_grad = k.copy(k["mixed_grad"], k["v_grad"].at[0])
        grad = k["grad"]
        load_in = [k.copy(k["grad_in_part"].at[q], grad.at[q]) for q in range(blocks) if by_hand]
        load_mixed = [k.copy(k["mixed"], k["v_left"]), k.copy(k["attn_grad"], k["joint"].at[0])]
        load_heads = k.copy(k["heads"], k["v_heads"])
        load_qkv = [
            k.copy(k["w_qkv"].at[:, :, :, pl.ds(t * width, width)], k["v_qkv"].at[t]) for t in range(3)
        ]
        load_grad.wait()
        meet(place)
        over_grad = []
        for i in range(items):
            at_rows = pl.ds(i * half_len, half_len)
            over_grad.append(k.add(exchange(k, k["v_grad"].at[0, at_rows], k["v_grad"].at[1, at_rows])))
            k.step(over_grad[i])
        going = []

        def reduce(slot, target, split):
            if by_hand:
                buffers = {name: k[f"{name}{slot}"] for name in ("core", "diag", "line", "column")}
                going.append(k.add(reduce_steps(place, sender, grad.at[slot], buffers, target(), split, 1)))
                k.step(going[-1])
            k.point()

        for q in range(len(load_in)):
            load_in[q].wait()
            reduce(q, lambda q=q: k["grad_in"].at[:, pl.ds(q * width, width)], nz)
        left, turned, joint = k["v_left"], k["v_turned"], k["joint"]

        def turn(j):
            turned[tile(j, 128), :] = left[:, tile(j, 128)].T

        def outer(slot, right):
            def one(j):
                at = tile(j, step)
                part = mm(turned[...], right[:, at]).astype(LOW)
                grad[slot, :, :, :, :, :, at] = part.reshape(4, 2, 2, 2, 32, step)

            loop(width // step, one)

        for made in load_mixed:
            made.wait()
        loop(width // 128, turn)
        load_stream = k.copy(k["stream"], left)
        outer(blocks, joint.at[0])
        if not by_hand:
            k.save(grad.at[blocks], k["grad_o"])
        reduce(blocks, lambda: k["grad_o"], nz)
        load_heads.wait()
        same = lax.broadcasted_iota(jnp.int32, (half_len, half_len), 0) == lax.broadcasted_iota(
            jnp.int32, (half_len, half_len), 1
        )
        for i in range(items):
            asked = k["codes"][items + i : items + i + 1, :]
            asked_taken = k["codes_taken"][items + i : items + i + 1, :]
            code = k["cols"][:, 2 * items + i : 2 * items + i + 1]
            code_taken = k["cols_taken"][:, 2 * items + i : 2 * items + i + 1]
            k["permit"][i, 0:half_len, :] = jnp.where((code <= asked) | same, 0.0, fill_value)
            k["permit"][i, half_len : 2 * half_len, :] = jnp.where(code_taken <= asked, 0.0, fill_value)
            k["permit_taken"][i] = jnp.where(code <= asked_taken, 0.0, fill_value)
        k.point()
        heads, grads, result = k["v_heads"], k["v_grad"], joint
        lane = lax.broadcasted_iota(jnp.int32, (half_len, 2 * HD), 1)
        key_lane = lax.broadcasted_iota(jnp.int32, (2 * half_len, 2 * HD), 1)
        nothing = jnp.zeros((), LOW)
        pairs = width // (2 * HD)

        def ours(i):
            at_rows = pl.ds(i * half_len, half_len)

            def pair(p):
                at = tile(p, 2 * HD)
                query = heads[0, at_rows, at]
                keys = jnp.concatenate([heads[1, at_rows, at], heads[2, at_rows, at]], axis=0)
                values = jnp.concatenate([heads[3, at_rows, at], heads[4, at_rows, at]], axis=0)
                grad_row = grads[0, at_rows, at]
                query_part = key_part = value_part = None
                for h in range(2):
                    mine = (lane < HD) == (h == 0)
                    key_mine = (key_lane < HD) == (h == 0)
                    query_h = jnp.where(mine, query, nothing)
                    grad_h = jnp.where(mine, grad_row, nothing)
                    keys_h = jnp.where(key_mine, keys, nothing)
                    at_head = pl.ds(2 * p + h, 1)
                    scores = mm(keys, query_h * scale, NT) + (k["permit"][i] - k["logs"][i, at_head, :])
                    probs = jnp.exp(scores)
                    prob_grad = mm(values, grad_h, NT)
                    centre = column_sum(probs * prob_grad)
                    k["centre"][i, at_head, :] = centre
                    score_grad = (probs * (prob_grad - centre)).astype(LOW)
                    parts = (
                        mm(score_grad, keys_h, TN),
                        mm(score_grad[:half_len], query_h),
                        mm(probs[:half_len].astype(LOW), grad_h),
                    )
                    if h == 0:
                        query_part, key_part, value_part = parts
                    else:
                        query_part = query_part + parts[0]
                        key_part = key_part + parts[1]
                        value_part = value_part + parts[2]
                query_low = (query_part * scale).astype(LOW)
                result[0, at_rows, at] = query_low
                k["sums"][0:1, at] += column_sum(query_low.astype(F32))
                k["parts"][0, at_rows, at] = key_part
                k["parts"][1, at_rows, at] = value_part

            loop(pairs // 2, pair)
            k.point()
            loop(pairs // 2, lambda p: pair(p + pairs // 2))

        def theirs(i):
            at_rows = pl.ds(i * half_len, half_len)

            def pair(p):
                at = tile(p, 2 * HD)
                query = heads[5, at_rows, at]
                keys, values = heads[1, at_rows, at], heads[3, at_rows, at]
                grad_row = grads[1, at_rows, at]
                key_part, value_part = k["parts"][0, at_rows, at], k["parts"][1, at_rows, at]
                for h in range(2):
                    mine = (lane < HD) == (h == 0)
                    query_h = jnp.where(mine, query, nothing)
                    grad_h = jnp.where(mine, grad_row, nothing)
                    at_head = pl.ds(2 * p + h, 1)
                    scores = mm(keys, query_h * scale, NT) + (
                        k["permit_taken"][i] - k["logs_taken"][i, at_head, :]
                    )
                    probs = jnp.exp(scores)
                    prob_grad = mm(values, grad_h, NT)
                    score_grad = (probs * (prob_grad - k["centre_taken"][i, at_head, :])).astype(LOW)
                    key_part = key_part + mm(score_grad, query_h)
                    value_part = value_part + mm(probs.astype(LOW), grad_h)
                result[1, at_rows, at] = (key_part * scale).astype(LOW)
                value_low = value_part.astype(LOW)
                result[2, at_rows, at] = value_low
                k["sums"][1:2, at] += column_sum(value_low.astype(F32))

            loop(pairs // 2, pair)
            k.point()
            loop(pairs // 2, lambda p: pair(p + pairs // 2))

        k["sums"][...] = jnp.zeros_like(k["sums"])
        over = []
        for i in range(items):
            ours(i)
            over.append(k.add(exchange(k, k["centre"].at[i], k["centre_taken"].at[i])))
            k.step(over[i])
            k.point()
        load_stream.wait()
        loop(width // 128, turn)

        def outer_joint(q, slot):
            outer(slot, joint.at[q])
            if not by_hand:
                k.save(grad.at[slot], k["grad_qkv"].at[:, :, :, :, :, pl.ds(q * width, width)])
            reduce(slot, lambda: k["grad_qkv"].at[:, pl.ds(q * width, width)], nz // 2)

        outer_joint(0, blocks + 1)
        for i in range(items):
            k.finish(over[i], over_grad[i])
            theirs(i)
            k.point()
        levels = k["levels"]
        for s, name in enumerate(("sums_one", "sums_two")):
            levels[0, 8 * s : 8 * s + 8, :] = k[name][...]
        levels[0, 16:24, :] = k["sums"][...]
        small = k.add(sum_steps(place, sender, levels, k["levels_taken"]))
        k.step(small)
        k.finish(*going[:2])
        partners = place.partners()
        for partner in partners:
            pl.semaphore_signal(k["through"], inc=1, device_id=partner, device_id_type=MESH)
        load_part = k.copy(k["input_part"], k["parts"].at[0])
        pl.semaphore_wait(k["through"], len(partners))
        outer_joint(1, 0)
        outer_joint(2, 1)
        for made in load_qkv + [load_part]:
            made.wait()
        for i in range(items):
            at_rows = pl.ds(i * half_len, half_len)
            total = k["parts"][0, at_rows, :]
            for q in range(3):
                total = total + mm(joint[q, at_rows, :], k["v_qkv"][q].reshape(width, width), NT)
            left[at_rows, :] = total.astype(LOW)
            k.save(left.at[at_rows], k["input_grad"].at[at_rows])
            k.point()
        k.finish(*range(len(k.transfers)))
        k["totals"][...] = levels[stages]
        k.close()

    ins = dict(
        grad_in_part=fb["grad_in"],
        mixed=fw["save_mixed"],
        attn_grad=fb["attn_grad"],
        heads=fw["save_heads"],
        mixed_grad=fb["mixed_grad"],
        stream=fw["save_stream"],
        w_qkv=weights[0],
        input_part=fb["input_part"],
        codes=fw["codes"],
        codes_taken=fw["save_codes"],
        cols=fw["cols"],
        cols_taken=fw["save_cols"],
        logs=fw["save_logs"],
        logs_taken=fw["save_logs_taken"],
        sums_one=fw["sums"],
        sums_two=fb["sums"],
    )
    outs = dict(
        input_grad=((rows, width), LOW, "hbm"),
        totals=((24, width), F32, "vmem"),
    )
    if by_hand:
        outs["grad_in"] = ((32, blocks * width), F32, "vmem")
        outs["grad_o"] = ((32, width), F32, "vmem")
        outs["grad_qkv"] = ((32, 3 * width), F32, "vmem")
    else:
        outs["grad_o"] = ((4, 2, 2, 2, 32, width), LOW, "hbm")
        outs["grad_qkv"] = ((4, 2, 2, 2, 32, 3 * width), LOW, "hbm")
    scratch = dict(
        v_left=pltpu.VMEM((rows, width), LOW),
        v_turned=pltpu.VMEM((width, rows), LOW),
        joint=pltpu.VMEM((3, rows, width), LOW),
        v_heads=pltpu.VMEM((6, rows, width), LOW),
        v_grad=pltpu.VMEM((2, rows, width), LOW),
        v_qkv=pltpu.VMEM((3, 4, 8, 32, width), LOW),
        grad=pltpu.VMEM((chunks, 4, 2, 2, 2, 32, width), LOW),
        permit=pltpu.VMEM((items, 2 * half_len, half_len), F32),
        permit_taken=pltpu.VMEM((items, half_len, half_len), F32),
        parts=pltpu.VMEM((2, rows, width), F32),
        centre=pltpu.VMEM((items, HEADS, half_len), F32),
        centre_taken=pltpu.VMEM((items, HEADS, half_len), F32),
        sums=pltpu.VMEM((8, width), F32),
        levels=pltpu.VMEM((stages + 1, 24, width), F32),
        levels_taken=pltpu.VMEM((stages, 24, width), F32),
        through=pltpu.SemaphoreType.REGULAR,
    )
    copies = 2 * items + stages
    if by_hand:
        copies += (blocks + 4) * reduce_copies(nz)
        for q in range(chunks):
            for name, buffer in reduce_buffers(nz, 32, width).items():
                scratch[f"{name}{q}"] = buffer
    spaces = ("codes", "codes_taken", "cols", "cols_taken", "logs", "logs_taken", "sums_one", "sums_two")
    return call("attend_back" if by_hand else "", body, ins, spaces, outs, scratch, copies, collective_id)


def body(
    block_input,
    lengths,
    mask,
    blocks,
    timesteps,
    w_qkv,
    w_o,
    w_in,
    w_out,
    b_in,
    biases,
    gains,
    shifts,
    cotangent,
):
    items, half_len, width = block_input.shape
    rows = items * half_len
    f32 = jnp.float32
    n = n_devices()
    share = width // n
    b_count = b_in.shape[0]
    positions = lax.axis_index("ctx") * half_len + jnp.arange(half_len, dtype=jnp.int32)
    valid = (positions[None, :] < lengths[:, None]) & ((mask == 1) | (positions[None, :] == 0))
    numbers = blocks.astype(f32)
    key_codes = jnp.where(valid, numbers, code_absent)
    codes = jnp.pad(jnp.concatenate([key_codes, numbers]), ((0, 8 - 2 * items), (0, 0)))
    cols = jnp.concatenate([numbers, valid.astype(f32), key_codes]).T
    cols = jnp.pad(cols, ((0, 0), (0, 128 - 3 * items)))
    embed = jnp.pad(time_embed(timesteps, width), ((0, 8 - items), (0, 0)))
    small = jnp.concatenate([b_in, biases.reshape(-1), gains.reshape(-1), shifts.reshape(-1)])
    small_wide = -(-small.shape[0] // 128) * 128
    small = jnp.pad(small.astype(f32), (0, small_wide - small.shape[0]))
    small = jnp.broadcast_to(small[None, :], (8, small_wide))
    by_hand = w_qkv.shape[0] == 32
    weights = [w_qkv, w_o, w_in, w_out]
    if not by_hand:
        weights = [lax.all_gather(w, AXES, axis=0, tiled=True) for w in weights]
        weights = [w.reshape(4, 8, w.shape[0] // 32, w.shape[1]) for w in weights]
        small = lax.all_gather(small, AXES, axis=0).reshape(n // 8, 8, 8, small_wide)
    fw = forward(
        by_hand,
        items,
        half_len,
        weights,
        small,
        block_input.reshape(rows, width),
        embed,
        codes,
        cols,
        cotangent.reshape(rows, width),
        1,
    )
    if by_hand:
        weights = [fw["all_" + p] for p in ("w_qkv", "w_o", "w_in", "w_out")]
    fb = feed_back(by_hand, items, half_len, fw, weights, 2)
    ab = attend_back(by_hand, items, half_len, fw, fb, weights, 3)
    if by_hand:
        grads = [ab["grad_qkv"], ab["grad_o"], ab["grad_in"], fb["grad_out"]]
    else:
        grad_in = fb["grad_in"].reshape(4, width, width).transpose(1, 0, 2)
        grads = [
            lax.psum_scatter(
                part.astype(f32).reshape(rows_of, -1), AXES, scatter_dimension=0, tiled=True
            )
            for part, rows_of in (
                (ab["grad_qkv"], width),
                (ab["grad_o"], width),
                (grad_in, width),
                (fb["grad_out"], 4 * width),
            )
        ]
    totals = ab["totals"]
    me = my_index()
    grad_b_in = lax.dynamic_slice(totals[8:12].reshape(-1), (me * b_count,), (b_count,))
    order = (16, 17, 14, 4, 12, 5, 13, 6)
    mine = lax.dynamic_slice(totals, (0, me * share), (24, share))
    mine = jnp.stack([mine[row] for row in order])
    count = jnp.sum(totals[7, items : 2 * items])
    rms = jnp.sqrt(jnp.sum(totals[:4], axis=1) / (count * width))
    return (
        fw["output"].reshape(block_input.shape),
        ab["input_grad"].reshape(block_input.shape),
        *grads,
        grad_b_in,
        mine[:4],
        mine[4:6],
        mine[6:8],
        rms,
    )


def solution(mesh):
    in_specs = (
        P("dp", "ctx", None),
        P("dp"),
        P("dp", "ctx"),
        P("dp", "ctx"),
        P("dp"),
        P(("dp", "ctx"), None),
        P(("dp", "ctx"), None),
        P(("dp", "ctx"), None),
        P(("dp", "ctx"), None),
        P(("dp", "ctx")),
        P(None, ("dp", "ctx")),
        P(None, ("dp", "ctx")),
        P(None, ("dp", "ctx")),
        P("dp", "ctx", None),
    )
    out_specs = (
        P("dp", "ctx", None),
        P("dp", "ctx", None),
        P(("dp", "ctx"), None),
        P(("dp", "ctx"), None),
        P(("dp", "ctx"), None),
        P(("dp", "ctx"), None),
        P(("dp", "ctx")),
        P(None, ("dp", "ctx")),
        P(None, ("dp", "ctx")),
        P(None, ("dp", "ctx")),
        P(),
    )
    return jax.shard_map(body, mesh=mesh, in_specs=in_specs, out_specs=out_specs, check_vma=False)
```

```python
from functools import partial
import math

import jax
import jax.numpy as jnp
from jax import lax
from jax.experimental import pallas as pl
from jax.experimental.pallas import tpu as pltpu
from jax.sharding import PartitionSpec as P

HEADS = 16
HD = 64

AXES = ("dp", "ctx")
X = 1


def my_index():
    return lax.axis_index("dp") * lax.axis_size("ctx") + lax.axis_index("ctx")


def n_devices():
    return lax.axis_size("dp") * lax.axis_size("ctx")


fill_value = -1e30
eps_norm = 1e-05
code_absent = 30000.0


def time_embed(steps, width):
    half = width // 2
    freqs = jnp.exp(jnp.arange(half, dtype=jnp.float32) * (-math.log(10000.0) / half))
    angle = steps.astype(jnp.float32)[:, None] * freqs[None, :]
    return jnp.concatenate([jnp.sin(angle), jnp.cos(angle)], axis=-1)


MESH = pl.DeviceIdType.MESH


class Place:
    def __init__(self):
        dp = lax.axis_index("dp")
        self.nz = lax.axis_size("dp") // 4
        self.x = lax.axis_index("ctx")
        self.c = dp % 2
        self.y = (dp // 2) % 2
        self.z = dp // 4

    def zth(self, k):
        z, bit = self.z, 1
        while bit < self.nz:
            if k & bit:
                z = z + bit * (1 - 2 * ((self.z // bit) % 2))
            bit *= 2
        return z

    def flips(self, y=0, c=0, x=0):
        return (
            1 - self.y if y else self.y,
            1 - self.c if c else self.c,
            1 - self.x if x else self.x,
        )

    def device(self, k=0, y=0, c=0, x=0):
        fy, fc, fx = self.flips(y, c, x)
        return ((self.zth(k) * 2 + fy) * 2 + fc, fx)

    def shard(self, k=0, y=0, c=0, x=0):
        fy, fc, fx = self.flips(y, c, x)
        return ((self.zth(k) * 2 + fy) * 2 + fc) * 2 + fx

    def column(self, y=0, c=0, x=0):
        fy, fc, fx = self.flips(y, c, x)
        return (fy * 2 + fc) * 2 + fx

    def partners(self):
        return [self.device(k=k) for k in range(1, self.nz)] + [
            self.device(x=1),
            self.device(y=1),
            self.device(c=1),
        ]


def meet(place):
    barrier = pltpu.get_barrier_semaphore()
    partners = place.partners()
    for partner in partners:
        pl.semaphore_signal(barrier, inc=1, device_id=partner, device_id_type=MESH)
    pl.semaphore_wait(barrier, len(partners))


class Sender:
    def __init__(self, send_sem, recv_sem):
        self.send_sem, self.recv_sem = send_sem, recv_sem
        self.count = 0
        self.open = []

    def send(self, src, dst, device, keep=None):
        copy = pltpu.make_async_remote_copy(
            src_ref=src,
            dst_ref=dst,
            send_sem=self.send_sem.at[self.count],
            recv_sem=self.recv_sem.at[self.count],
            device_id=device,
            device_id_type=MESH,
        )
        self.count += 1
        copy.start()
        (self.open if keep is None else keep).append(copy)
        return copy

    def close(self):
        for copy in self.open:
            copy.wait_send()
        self.open = []


def gather_copies(nz):
    return 4 * nz + 5


def gather_steps(place, sender, shard, full, split):
    nz = place.nz
    mine, at_x, at_y, diag = (place.column(x=fx, y=fy) for fy, fx in ((0, 0), (0, 1), (1, 0), (1, 1)))
    own = full.at[place.z, mine]
    by_z = [sender.send(shard, own, place.device(k=k)) for k in range(1, nz)]
    yield
    from_x = [sender.send(shard, own, place.device(x=1))]
    from_y = [sender.send(shard, own, place.device(y=1))]
    yield
    for k in range(1, nz):
        by_z[k - 1].wait_recv()
        piece = full.at[place.zth(k), mine]
        from_x.append(sender.send(piece, piece, place.device(x=1)))
        from_y.append(sender.send(piece, piece, place.device(y=1)))
        yield
    to_core = [sender.send(full.at[:, mine], full.at[:, mine], place.device(c=1))]
    from_diag = []
    yield
    for k in range(nz):
        from_x[k].wait_recv()
        if k < split:
            piece = full.at[place.zth(k), at_x]
            from_diag.append(sender.send(piece, piece, place.device(y=1)))
        else:
            from_y[k].wait_recv()
            piece = full.at[place.zth(k), at_y]
            from_diag.append(sender.send(piece, piece, place.device(x=1)))
        yield
    to_core.append(sender.send(full.at[:, at_x], full.at[:, at_x], place.device(c=1)))
    for k in range(split):
        from_y[k].wait_recv()
    to_core.append(sender.send(full.at[:, at_y], full.at[:, at_y], place.device(c=1)))
    yield
    half = nz // 2
    for start, size in ((0, half), (half, nz - half)):
        for copy in from_diag if start == 0 else ():
            copy.wait_recv()
        part = full.at[pl.ds(start, size), diag]
        to_core.append(sender.send(part, part, place.device(c=1)))
    yield
    for copy in to_core:
        copy.wait_recv()


def gather_late_steps(place, sender, shard, full):
    nz = place.nz
    own = full.at[place.z, place.column()]
    from_x = sender.send(shard, own, place.device(x=1))
    from_y = sender.send(shard, own, place.device(y=1))
    yield
    from_x.wait_recv()
    piece = full.at[place.z, place.column(x=1)]
    from_diag = sender.send(piece, piece, place.device(y=1))
    yield
    from_y.wait_recv()
    from_diag.wait_recv()
    by_z = []
    for k in range(1, nz):
        for fy in range(2):
            for fx in range(2):
                piece = full.at[place.z, place.column(y=fy, x=fx)]
                by_z.append(sender.send(piece, piece, place.device(k=k)))
    yield
    for copy in by_z:
        copy.wait_recv()
    to_core = []
    for fy in range(2):
        for fx in range(2):
            piece = full.at[:, place.column(y=fy, x=fx)]
            to_core.append(sender.send(piece, piece, place.device(c=1)))
    yield
    for copy in to_core:
        copy.wait_recv()


NN = (((1,), (0,)), ((), ()))
NT = (((1,), (1,)), ((), ()))
TN = (((0,), (0,)), ((), ()))
LOW = jnp.bfloat16
F32 = jnp.float32


def mm(left, right, dims=NN):
    return lax.dot_general(left, right, dims, preferred_element_type=F32)


def loop(count, step):
    lax.fori_loop(0, count, lambda i, _: (step(i), 0)[1], 0)


def tile(index, size):
    return pl.ds(pl.multiple_of(index * size, size), size)


def expand(packed, offset, share, start, length):
    n, wide = packed.shape
    place = lax.broadcasted_iota(jnp.int32, (wide, length), 1) + start
    lane = lax.broadcasted_iota(jnp.int32, (wide, length), 0)
    pick = (lane == offset + lax.rem(place, share)).astype(F32).astype(LOW)
    spread = mm(packed, pick)
    row = lax.broadcasted_iota(jnp.int32, (n, length), 0)
    column = lax.broadcasted_iota(jnp.int32, (n, length), 1) + start
    return jnp.sum(jnp.where(row == lax.div(column, share), spread, 0.0), axis=0, keepdims=True)


def normalize(resid):
    centre = resid - jnp.mean(resid, axis=-1, keepdims=True)
    spread = jnp.mean(centre * centre, axis=-1, keepdims=True)
    rstd = lax.rsqrt(spread + eps_norm)
    return centre * rstd, rstd


def column_sum(value):
    return jnp.sum(value, axis=0, keepdims=True)


def reduce_copies(nz):
    return nz + 6 + nz - 1


def reduce_buffers(nz, rows, cols):
    return dict(
        core=pltpu.VMEM((nz, 2, 2, rows, cols), LOW),
        diag=pltpu.VMEM((nz, rows, cols), LOW),
        line=pltpu.VMEM((2, nz, rows, cols), LOW),
        column=pltpu.VMEM((nz - 1, rows, cols), LOW),
    )


def add_rows(store, terms, count, rows):
    step = min(rows, 16)
    per = rows // step

    def one(j):
        i, start = j // per, (j % per) * step
        at = pl.ds(pl.multiple_of(start, step), step)
        total = terms[0](i, at).astype(F32)
        for term in terms[1:]:
            total = total + term(i, at).astype(F32)
        store(i, at, total)

    loop(count * per, one)


def reduce_steps(place, sender, grad, buffers, out, split, parts):
    nz = place.nz
    rows = grad.shape[4]
    core, diag, line, column = (buffers[k] for k in ("core", "diag", "line", "column"))
    groups = ((1, 1), (0, 1), (1, 0), (0, 0))
    here = [place.flips(y=fy, x=fx) for fy, fx in groups]
    sent, by_core = [], []
    size = nz // parts
    for t in range(parts):
        if t:
            yield
        at = pl.ds(t * size, size)
        by_core.append(sender.send(grad.at[at, :, 1 - place.c], core.at[at], place.device(c=1), sent))
    yield

    def put(slot, start=0):
        fy, fc, fx = here[slot]

        def store(i, at, value):
            grad[i + start, fy, fc, fx, at, :] = value.astype(LOW)

        return store

    def held(slot, start=0):
        fy, fc, fx = here[slot]
        return lambda i, at: grad[i + start, fy, fc, fx, at, :]

    def add_core(slot):
        fy, _, fx = here[slot]
        add_rows(put(slot), [held(slot), lambda i, at: core[i, fy, fx, at, :]], nz, rows)

    def part(slot, start, count):
        fy, fc, fx = here[slot]
        return grad.at[pl.ds(start, count), fy, fc, fx]

    low, high = pl.ds(0, split), pl.ds(split, nz - split)
    by_y = by_x = x_high = y_low = x_low = y_high = None
    for copy in by_core:
        copy.wait_recv()
    add_core(0)
    if split > 0:
        by_y = sender.send(part(0, 0, split), diag.at[low], place.device(y=1), sent)
    if split < nz:
        by_x = sender.send(part(0, split, nz - split), diag.at[high], place.device(x=1), sent)
    yield
    add_core(1)
    if split < nz:
        x_high = sender.send(part(1, split, nz - split), line.at[0, high], place.device(x=1), sent)
    add_core(2)
    if split > 0:
        y_low = sender.send(part(2, 0, split), line.at[1, low], place.device(y=1), sent)
    yield
    add_core(3)
    yield
    if split > 0:
        by_y.wait_recv()
        add_rows(put(1), [held(1), lambda i, at: diag[i, at, :]], split, rows)
        x_low = sender.send(part(1, 0, split), line.at[0, low], place.device(x=1), sent)
    yield
    if split < nz:
        by_x.wait_recv()
        add_rows(put(2, split), [held(2, split), lambda i, at: diag[i + split, at, :]], nz - split, rows)
        y_high = sender.send(part(2, split, nz - split), line.at[1, high], place.device(y=1), sent)
    yield
    for copy in (x_high, y_low, x_low, y_high):
        if copy is not None:
            copy.wait_recv()
    add_rows(
        put(3),
        [held(3), lambda i, at: line[0, i, at, :], lambda i, at: line[1, i, at, :]],
        nz,
        rows,
    )
    fy, fc, fx = here[3]
    by_z = [
        sender.send(grad.at[place.zth(k), fy, fc, fx], column.at[k - 1], place.device(k=k), sent)
        for k in range(1, nz)
    ]
    yield
    for copy in by_z:
        copy.wait_recv()

    def last(i, at, value):
        out[at, :] = value

    add_rows(
        last,
        [lambda i, at: grad[place.z, fy, fc, fx, at, :]]
        + [lambda i, at, k=k: column[k, at, :] for k in range(nz - 1)],
        1,
        rows,
    )
    for copy in sent:
        copy.wait_send()


def sum_steps(place, sender, levels, taken):
    partners = [place.device(c=1), place.device(x=1), place.device(y=1)]
    bit = 1
    while bit < place.nz:
        partners.append(place.device(k=bit))
        bit *= 2
    for s, partner in enumerate(partners):
        copy = sender.send(levels.at[s], taken.at[s], partner)
        yield
        copy.wait_recv()
        levels[s + 1] = levels[s] + taken[s]


class Kernel:
    def __init__(self, name, names, refs):
        self.refs = dict(zip(names, refs))
        self.place = Place()
        self.sender = Sender(self["send"], self["recv"])
        self.plan = PLANS.get(name, ())
        self.count = self.points = 0
        self.saved, self.transfers = [], []

    def __getitem__(self, name):
        return self.refs[name]

    def copy(self, src, dst):
        made = pltpu.make_async_copy(src, dst, self["local"].at[self.count])
        self.count += 1
        made.start()
        return made

    def save(self, src, dst):
        made = self.copy(src, dst)
        self.saved.append(made)
        return made

    def add(self, steps):
        self.transfers.append(steps)
        return len(self.transfers) - 1

    def step(self, number):
        return next(self.transfers[number], self) is not self

    def point(self):
        turn = self.plan[self.points] if self.points < len(self.plan) else ()
        self.points += 1
        for number in turn:
            self.step(number)

    def finish(self, *numbers):
        for number in numbers:
            while self.step(number):
                pass

    def close(self):
        self.finish(*range(len(self.transfers)))
        for made in self.saved:
            made.wait()
        self.sender.close()


PARTS = (
    ("w_qkv", None, None, False),
    ("small", None, None, False),
    ("w_o", None, None, True),
    ("w_in", 0, 2048, False),
    ("w_in", 2048, 3072, False),
    ("w_in", 3072, 4096, True),
    ("w_out", 0, 512, False),
    ("w_out", 512, 1024, False),
)
PLANS = {
    "forward": (
        (8, 5, 1, 0, 2, 3, 0, 2, 13, 6, 5),
        (0, 0),
        (0, 8, 10, 13),
        (12, 13, 4),
        (7,),
        (13, 0),
        (0, 3, 4, 10),
        (0, 2, 0, 12, 0, 3, 10),
        (3, 3, 4, 11),
        (0, 6, 3),
        (4, 4, 8, 3, 15),
        (4, 14, 4, 5),
        (3, 8),
        (4, 3, 3, 7),
        (6,),
        (),
        (6,),
        (4, 4, 4, 6),
        (6,),
        (),
        (2, 7),
        (3, 6, 7),
        (),
        (3, 7),
        (6, 7, 4),
        (6,),
        (6,),
        (7,),
        (5, 7, 6, 17),
        (7,),
        (7,),
        (6,),
        (18, 9, 17, 7),
        (16, 7),
        (),
        (16, 17),
    ),
    "feed_back": (
        (0,),
        (0, 1, 0),
        (),
        (0, 0),
        (1,),
        (1,),
        (1, 0, 1),
        (),
        (),
        (1, 0),
    ),
    "attend_back": (
        (),
        (),
        (),
        (),
        (3, 3),
        (4, 4),
        (0, 5, 3, 4, 3),
        (0,),
        (),
        (6,),
        (4, 5, 6, 1, 4),
        (3, 5),
        (5, 2),
        (6, 9, 3),
        (2, 11, 6),
        (11, 4),
        (7,),
        (5, 11, 11, 5, 6),
        (11, 7),
        (6, 12, 7, 7),
        (5, 11, 12, 7, 13),
        (6, 13, 14, 12, 7),
        (13, 13),
        (13, 14, 12, 14, 14, 14, 13, 14),
    ),
}


def call(name, body, ins, spaces_in, outs, scratch, copies, collective_id):
    vmem, hbm = pl.BlockSpec(memory_space=pltpu.VMEM), pl.BlockSpec(memory_space=pl.ANY)
    scratch = dict(
        send=pltpu.SemaphoreType.DMA((copies,)),
        recv=pltpu.SemaphoreType.DMA((copies,)),
        local=pltpu.SemaphoreType.DMA((64,)),
        **scratch,
    )
    names = list(ins) + list(outs) + list(scratch)

    def kernel(*refs):
        body(Kernel(name, names, refs))

    results = pl.pallas_call(
        kernel,
        out_shape=[jax.ShapeDtypeStruct(s, d) for s, d, _ in outs.values()],
        in_specs=[vmem if given in spaces_in else hbm for given in ins],
        out_specs=[vmem if space == "vmem" else hbm for _, _, space in outs.values()],
        scratch_shapes=list(scratch.values()),
        compiler_params=pltpu.CompilerParams(
            collective_id=collective_id, has_side_effects=True, vmem_limit_bytes=63 << 20
        ),
    )(*ins.values())
    return dict(zip(outs, results))


def exchange(k, src, dst):
    copy = k.sender.send(src, dst, k.place.device(x=1))
    yield
    copy.wait_recv()


def row_sum(value):
    return jnp.sum(value.reshape(-1, 8, value.shape[-1]), axis=0)


NORM_ROWS = 128


def forward(by_hand, items, half_len, weights, small, block_input, embed, codes, cols, cotangent, collective_id):
    rows, width = block_input.shape
    full_len = 2 * half_len
    blocks = 4
    nz = lax.axis_size("dp") // 4
    step = 256
    params = ["w_qkv", "small", "w_o", "w_in", "w_out"]

    def body(k):
        place = k.place
        cot_in = k.copy(k["cotangent"], k["cot"])
        full = {p: k["v_" + p] for p in params}
        kept = [k.copy(k[p], full[p].at[place.z, place.column()] if by_hand else full[p]) for p in params]
        meet(place)
        for made in kept:
            made.wait()
        number = {}
        if by_hand:
            for p, start, stop, late in PARTS:
                if start is None:
                    shard, whole = k[p], full[p]
                else:
                    shard = k[p].at[:, pl.ds(start, stop - start)]
                    whole = full[p].at[:, :, :, pl.ds(start, stop - start)]
                if late:
                    steps = gather_late_steps(place, k.sender, shard, whole)
                else:
                    steps = gather_steps(place, k.sender, shard, whole, nz - nz // 4)
                number.setdefault(p, []).append(k.add(steps))

        def arrive(p, *which):
            if by_hand:
                k.finish(*[number[p][i] for i in which or range(len(number[p]))])

        codes_over = k.add(exchange(k, k["codes"], k["codes_taken"]))
        cols_over = k.add(exchange(k, k["cols"], k["cols_taken"]))
        quarter = half_len // 2
        input_over = [
            k.add(exchange(k, k["input"].at[pl.ds(i * quarter, quarter)], k["taken"].at[pl.ds(i * quarter, quarter)]))
            for i in range(2 * items)
        ]
        k.point()
        stream, partial_sums = k["stream"], k["partial_sums"]
        partial_sums[...] = jnp.zeros_like(partial_sums)

        def gather_sum(kind, value):
            partial_sums[kind] += row_sum(value)

        for i in range(items):
            item_embed = k["embed"][i : i + 1, :]

            def make_stream(j, i=i, item_embed=item_embed):
                at = pl.ds(pl.multiple_of(i * half_len + j * 64, 64), 64)
                value = k["input"][at, :].astype(F32) + item_embed
                stream[at, :] = value.astype(LOW)
                gather_sum(0, value * value * k["cols"][tile(j, 64), items + i : items + i + 1])

            loop(half_len // 64, make_stream)
        save_stream = k.copy(stream.at[pl.ds(0, rows)], k["save_stream"])
        k.point()
        arrive("small")
        shards = k["v_small"].shape[0] * k["v_small"].shape[1]
        for d in range(shards):
            k["packed"][d : d + 1, :] = k["v_small"][d // 8, d % 8, 0:1, :]
        packed = k["packed"][...].astype(LOW)
        share = width // shards
        b_share = share * blocks
        vectors, b_in = k["vectors"], k["v_b_in"]
        for t in range(8):
            vectors[t : t + 1, :] = expand(packed, b_share + t * share, share, 0, width)
            if t in (0, 1, 3, 5):
                k.point()
        for t in range(blocks):
            b_in[t : t + 1, :] = expand(packed, 0, b_share, t * width, width)
            k.point()
        bias_o = vectors[2:3, :]
        gain_one, gain_two, shift_one, shift_two = (vectors[t : t + 1, :] for t in range(4, 8))
        heads = k["heads"]

        def weight(name, t, j):
            value = full[name][:, :, :, pl.ds(pl.multiple_of(t * width + j * step, step), step)]
            return value.reshape(-1, step)

        def keep(name):
            if by_hand:
                k.save(full[name], k["all_" + name])

        arrive("w_qkv")
        keep("w_qkv")
        k.point()

        def project(slot, t, bias):
            def one(j):
                at = tile(j, step)
                value = mm(stream[pl.ds(0, rows), :], weight("w_qkv", t, j))
                if bias is not None:
                    value = value + vectors[bias : bias + 1, at]
                heads[slot, :, at] = value.astype(LOW)

            loop(width // step, one)

        for slot, t, bias in ((0, 0, 0), (1, 1, None), (3, 2, 1)):
            project(slot, t, bias)
            k.point()
        k.finish(codes_over)
        same = lax.broadcasted_iota(jnp.int32, (half_len, half_len), 0) == lax.broadcasted_iota(
            jnp.int32, (half_len, half_len), 1
        )
        for i in range(items):
            asked = k["cols"][:, i : i + 1]
            own = (k["codes"][i : i + 1, :] <= asked) | same
            other = k["codes_taken"][i : i + 1, :] <= asked
            k["permit"][i, :, 0:half_len] = jnp.where(own, 0.0, fill_value)
            k["permit"][i, :, half_len : 2 * half_len] = jnp.where(other, 0.0, fill_value)
        k.save(k["codes_taken"], k["save_codes"])
        k.point()
        save_stream.wait()
        lane = lax.broadcasted_iota(jnp.int32, (half_len, 2 * HD), 1)
        key_lane = lax.broadcasted_iota(jnp.int32, (2 * half_len, 2 * HD), 1)
        pairs = width // (2 * HD)
        for i in range(items):
            at_rows = pl.ds(i * half_len, half_len)
            at_theirs = pl.ds(rows + i * half_len, half_len)
            item_embed = k["embed"][i : i + 1, :]
            k.finish(input_over[2 * i], input_over[2 * i + 1])

            def make_other(j, i=i, item_embed=item_embed):
                at = pl.ds(pl.multiple_of(i * half_len + j * 64, 64), 64)
                to = pl.ds(pl.multiple_of(rows + i * half_len + j * 64, 64), 64)
                stream[to, :] = (k["taken"][at, :].astype(F32) + item_embed).astype(LOW)

            def project_other(j, at_rows=at_rows, at_theirs=at_theirs):
                at = tile(j, step)
                source = stream[at_theirs, :]
                heads[2, at_rows, at] = mm(source, weight("w_qkv", 1, j)).astype(LOW)
                heads[4, at_rows, at] = (mm(source, weight("w_qkv", 2, j)) + vectors[1:2, at]).astype(LOW)
                heads[5, at_rows, at] = (mm(source, weight("w_qkv", 0, j)) + vectors[0:1, at]).astype(LOW)

            loop(half_len // 64, make_other)
            loop(width // step, project_other)
            if i == items - 1:
                save_heads = k.copy(heads, k["save_heads"])
            k.point()

            def pair(p, i=i, at_rows=at_rows):
                at = tile(p, 2 * HD)
                query = heads[0, at_rows, at] * (1.0 / math.sqrt(HD))
                keys = jnp.concatenate([heads[1, at_rows, at], heads[2, at_rows, at]], axis=0)
                values = jnp.concatenate([heads[3, at_rows, at], heads[4, at_rows, at]], axis=0)
                nothing = jnp.zeros((), LOW)
                mixed = None
                logs = k["logs"][i]
                for h in range(2):
                    scores = mm(jnp.where((lane < HD) == (h == 0), query, nothing), keys, NT) + k["permit"][i]
                    peak = jnp.max(scores, axis=1, keepdims=True)
                    expo = jnp.exp(scores - peak)
                    total = jnp.sum(expo, axis=1, keepdims=True)
                    probs = (expo * (1.0 / total)).astype(LOW)
                    part = mm(probs, jnp.where((key_lane < HD) == (h == 0), values, nothing))
                    mixed = part if mixed is None else mixed + part
                    logs = jnp.where(lane == 2 * p + h, peak + jnp.log(total), logs)
                k["logs"][i] = logs
                stream[at_rows, at] = mixed.astype(LOW)

            loop(pairs // 2, pair)
            k.point()
            loop(pairs // 2, lambda p, pair=pair: pair(p + pairs // 2))
            k["log_rows"][i] = k["logs"][i].T[:HEADS]
            k.add(exchange(k, k["log_rows"].at[i], k["logs_taken"].at[i]))
            k.point()
        save_mixed = k.copy(stream.at[pl.ds(0, rows)], k["save_mixed"])
        k.save(k["log_rows"], k["save_logs"])
        arrive("w_o")
        keep("w_o")
        xhat = k["xhat"]
        for i in range(items):
            at_rows = pl.ds(i * half_len, half_len)
            k["work"][...] = mm(stream[at_rows, :], full["w_o"][...].reshape(width, width)) + bias_o
            item_embed = k["embed"][i : i + 1, :]

            def first_norm(j, i=i, item_embed=item_embed):
                at = pl.ds(pl.multiple_of(i * half_len + j * NORM_ROWS, NORM_ROWS), NORM_ROWS)
                to = pl.ds(pl.multiple_of(rows + i * half_len + j * NORM_ROWS, NORM_ROWS), NORM_ROWS)
                attn = k["work"][tile(j, NORM_ROWS), :]
                gather_sum(1, attn * attn * k["cols"][tile(j, NORM_ROWS), items + i : items + i + 1])
                value, rstd = normalize(k["input"][at, :].astype(F32) + item_embed + attn)
                xhat[at, :] = value
                k["rstd"][at, :] = jnp.broadcast_to(rstd, (NORM_ROWS, 128))
                stream[to, :] = (value * gain_one + shift_one).astype(LOW)

            loop(half_len // NORM_ROWS, first_norm)
            k.point()
        save_hidden = k.copy(stream.at[pl.ds(rows, rows)], k["save_hidden"])
        k.save(xhat, k["save_xhat"])
        k.save(k["rstd"], k["save_rstd"])
        save_heads.wait()
        act, slope = heads, k["slope"]
        in_parts = {start: i for i, (start, _) in enumerate(part[1:3] for part in PARTS if part[0] == "w_in")}
        for t in range(blocks):
            if t * width in in_parts:
                arrive("w_in", in_parts[t * width])
                k.point()

            def feed(j, t=t):
                at = tile(j, step)
                w_in = weight("w_in", t, j)
                for i in range(items):
                    own = pl.ds(i * half_len, half_len)
                    pre = mm(stream[pl.ds(rows + i * half_len, half_len), :], w_in) + b_in[t : t + 1, at]
                    cdf = 0.5 + 0.5 * lax.erf(pre * (1.0 / math.sqrt(2.0)))
                    act[t, own, at] = (pre * cdf).astype(LOW)
                    pdf = jnp.exp(pre * pre * -0.5) * (1.0 / math.sqrt(2.0 * math.pi))
                    slope[t, own, at] = (cdf + pre * pdf).astype(LOW)

            loop(width // step, feed)
            k.save(act.at[t], k["act"].at[t])
            k.save(slope.at[t], k["save_slope"].at[t])
            k.point()
        keep("w_in")
        cot_in.wait()
        save_mixed.wait()
        save_hidden.wait()
        back = k["back"]
        out_parts = [(start, stop) for p, start, stop, _ in PARTS if p == "w_out"] if by_hand else [(0, width)]
        for which, (start, stop) in enumerate(out_parts):
            columns = pl.ds(start, stop - start)
            arrive("w_out", which)
            for i in range(items):
                at_rows = pl.ds(i * half_len, half_len)
                total = None
                for t in range(blocks):
                    part = mm(act[t, at_rows, :], full["w_out"][t, :, :, columns].reshape(width, stop - start))
                    total = part if total is None else total + part
                back[at_rows, columns] = total + vectors[3:4, columns]
            k.point()
        keep("w_out")
        for i in range(items):
            at_rows = pl.ds(i * half_len, half_len)

            def second_norm(j, i=i):
                at = pl.ds(pl.multiple_of(i * half_len + j * NORM_ROWS, NORM_ROWS), NORM_ROWS)
                to = pl.ds(pl.multiple_of(rows + i * half_len + j * NORM_ROWS, NORM_ROWS), NORM_ROWS)
                weight_rows = k["cols"][tile(j, NORM_ROWS), items + i : items + i + 1]
                branch = back[at, :]
                gather_sum(2, branch * branch * weight_rows)
                value, rstd = normalize(xhat[at, :] * gain_one + shift_one + branch)
                result = value * gain_two + shift_two
                gather_sum(3, result * result * weight_rows)
                stream[at, :] = result.astype(LOW)
                grad = k["cot"][at, :].astype(F32)
                gather_sum(5, grad * value)
                gather_sum(6, grad)
                scaled = grad * gain_two
                passed = rstd * (
                    scaled
                    - jnp.mean(scaled, axis=-1, keepdims=True)
                    - value * jnp.mean(scaled * value, axis=-1, keepdims=True)
                )
                back[at, :] = passed
                back_low = passed.astype(LOW)
                stream[to, :] = back_low
                gather_sum(4, back_low.astype(F32))

            loop(half_len // NORM_ROWS, second_norm)
            at_other = pl.ds(rows + i * half_len, half_len)
            k.save(stream.at[at_rows], k["output"].at[at_rows])
            k.save(stream.at[at_other], k["save_back_low"].at[at_rows])
            k.save(back.at[at_rows], k["save_back"].at[at_rows])
        for kind in range(7):
            k["sums"][kind : kind + 1, :] = column_sum(partial_sums[kind])
        k["sums"][7:8, :] = jnp.zeros((1, width), F32)
        k["sums"][7:8, 0:128] = column_sum(k["cols"][...])
        k.save(vectors, k["save_vectors"])
        k.finish(*range(len(k.transfers)))
        k.save(k["logs_taken"], k["save_logs_taken"])
        k.save(k["cols_taken"], k["save_cols"])
        k.close()

    ins = dict(zip(params, [weights[0], small] + weights[1:]))
    spaces_in = list(params) if by_hand else []
    spaces_in += ["input", "embed", "codes", "cols"]
    ins.update(input=block_input, embed=embed, codes=codes, cols=cols, cotangent=cotangent)
    outs = {}
    if by_hand:
        for p in params:
            if p != "small":
                outs["all_" + p] = ((nz, 8) + ins[p].shape, ins[p].dtype, "hbm")
    outs.update(
        save_heads=((6, rows, width), LOW, "hbm"),
        save_codes=(codes.shape, F32, "hbm"),
        save_cols=(cols.shape, F32, "hbm"),
        save_stream=((rows, width), LOW, "hbm"),
        save_hidden=((rows, width), LOW, "hbm"),
        save_mixed=((rows, width), LOW, "hbm"),
        save_logs=((items, HEADS, half_len), F32, "hbm"),
        save_logs_taken=((items, HEADS, half_len), F32, "hbm"),
        save_xhat=((rows, width), F32, "hbm"),
        save_rstd=((rows, 128), F32, "hbm"),
        act=((blocks, rows, width), LOW, "hbm"),
        save_slope=((blocks, rows, width), LOW, "hbm"),
        output=((rows, width), LOW, "hbm"),
        save_back_low=((rows, width), LOW, "hbm"),
        save_back=((rows, width), F32, "hbm"),
        save_vectors=((8, width), F32, "hbm"),
        sums=((8, width), F32, "vmem"),
    )
    small_full = (nz, 8) + small.shape if by_hand else small.shape
    copies = len(PARTS) * max(gather_copies(nz), 4 * nz + 4) + 3 * items + 2
    scratch = dict(
        partial_sums=pltpu.VMEM((7, 8, width), F32),
        taken=pltpu.VMEM((rows, width), LOW),
        codes_taken=pltpu.VMEM(codes.shape, F32),
        cols_taken=pltpu.VMEM(cols.shape, F32),
        stream=pltpu.VMEM((2 * rows, width), LOW),
        v_w_qkv=pltpu.VMEM((4, 8, 32, 3 * width), LOW),
        v_small=pltpu.VMEM(small_full, F32),
        packed=pltpu.VMEM((small_full[0] * 8, small_full[-1]), F32),
        vectors=pltpu.VMEM((8, width), F32),
        v_b_in=pltpu.VMEM((8, width), F32),
        heads=pltpu.VMEM((6, rows, width), LOW),
        permit=pltpu.VMEM((items, half_len, full_len), F32),
        logs=pltpu.VMEM((items, half_len, 128), F32),
        log_rows=pltpu.VMEM((items, HEADS, half_len), F32),
        logs_taken=pltpu.VMEM((items, HEADS, half_len), F32),
        v_w_o=pltpu.VMEM((4, 8, 32, width), LOW),
        work=pltpu.VMEM((half_len, width), F32),
        xhat=pltpu.VMEM((rows, width), F32),
        rstd=pltpu.VMEM((rows, 128), F32),
        v_w_in=pltpu.VMEM((4, 8, 32, blocks * width), LOW),
        slope=pltpu.VMEM((blocks, rows, width), LOW),
        v_w_out=pltpu.VMEM((4, 8, 128, width), LOW),
        cot=pltpu.VMEM((rows, width), LOW),
        back=pltpu.VMEM((rows, width), F32),
    )
    results = call("forward" if by_hand else "", body, ins, spaces_in, outs, scratch, copies, collective_id)
    return dict(results, codes=codes, cols=cols)


def feed_back(by_hand, items, half_len, fw, weights, collective_id):
    blocks, rows, width = fw["act"].shape
    nz = lax.axis_size("dp") // 4
    half_width = width // 2
    step = 256

    def body(k):
        place, sender = k.place, k.sender
        load_low = k.copy(k["back_low"], k["v_low"])
        load_act = [k.copy(k["act"].at[t], k["v_act"].at[t]) for t in range(blocks)]
        load_out = k.copy(k["w_out"], k["v_w"])
        load_slope = k.copy(k["slope"], k["v_slope"])
        load_hidden = k.copy(k["hidden"], k["v_left"])
        load_rest = [
            k.copy(k["back"], k["v_back"]),
            k.copy(k["xhat"], k["v_xhat"]),
            k.copy(k["rstd"], k["v_rstd"]),
            k.copy(k["w_o"], k["v_o"]),
        ]
        meet(place)
        load_low.wait()
        low, act, grad = k["v_low"], k["v_act"], k["grad"]
        halves = []
        if by_hand:
            for q in range(2):
                buffers = {name: k[f"{name}{q}"] for name in ("core", "diag", "line", "column")}
                target = k["grad_out"].at[:, pl.ds(q * half_width, half_width)]
                halves.append(k.add(reduce_steps(place, sender, grad.at[q], buffers, target, nz // 2, nz)))
        for t in range(blocks):
            load_act[t].wait()

            def outer(j, t=t):
                part = mm(act[t, :, tile(j, step)], low[...], TN).astype(LOW)
                part = part.reshape(2, 128, width)
                y, c = j // 2, j % 2
                grad[0, t, y, c] = part[:, :, :half_width]
                grad[1, t, y, c] = part[:, :, half_width:]

            loop(width // step, outer)
            for q in halves:
                k.step(q)
        k.point()
        if not by_hand:
            for q in range(2):
                k.save(grad.at[q], k["grad_out"].at[:, :, :, :, :, pl.ds(q * half_width, half_width)])
        load_out.wait()
        load_slope.wait()
        sums = k["sums"]
        sums[...] = jnp.zeros_like(sums)
        for t in range(blocks):

            def pull(j, t=t):
                at = tile(j, step)
                w_out = k["v_w"][t, j].reshape(step, width)
                part = mm(low[...], w_out, NT) * k["v_slope"][t, :, at].astype(F32)
                part = part.astype(LOW)
                act[t, :, at] = part
                sums[t : t + 1, at] = column_sum(part.astype(F32))

            loop(width // step, pull)
            k.point()
        load_in = [k.copy(k["w_in"].at[:, :, :, pl.ds(t * width, width)], k["v_w"].at[t]) for t in range(blocks)]
        load_hidden.wait()
        left, turned = k["v_left"], k["v_turned"]

        def turn(j):
            turned[tile(j, 128), :] = left[:, tile(j, 128)].T

        loop(width // 128, turn)
        save_in = []
        for t in range(blocks):
            if t >= 2:
                save_in[t - 2].wait()

            def outer_in(j, t=t):
                at = tile(j, step)
                part = mm(turned[...], act[t, :, at]).astype(LOW)
                k["grad_in_part"][t % 2, :, :, :, :, :, at] = part.reshape(4, 2, 2, 2, 32, step)

            loop(width // step, outer_in)
            save_in.append(k.copy(k["grad_in_part"].at[t % 2], k["grad_in"].at[t]))
            k.point()
        for made in load_in + load_rest + save_in[2:]:
            made.wait()
        gain = k["vectors"][4:5, :]
        partial_sums = k["partial_sums"]
        partial_sums[...] = jnp.zeros_like(partial_sums)
        for i in range(items):
            at_rows = pl.ds(i * half_len, half_len)
            total = None
            for t in range(blocks):
                part = mm(act[t, at_rows, :], k["v_w"][t].reshape(width, width), NT)
                total = part if total is None else total + part
            k["work"][...] = total
            k.point()

            def first_back(j, i=i):
                at = pl.ds(pl.multiple_of(i * half_len + j * NORM_ROWS, NORM_ROWS), NORM_ROWS)
                hidden = k["work"][tile(j, NORM_ROWS), :] + k["v_back"][at, :]
                xhat = k["v_xhat"][at, :]
                rstd = k["v_rstd"][at, 0:1]
                partial_sums[0] += row_sum(hidden * xhat)
                partial_sums[1] += row_sum(hidden)
                scaled = hidden * gain
                value = rstd * (
                    scaled
                    - jnp.mean(scaled, axis=-1, keepdims=True)
                    - xhat * jnp.mean(scaled * xhat, axis=-1, keepdims=True)
                )
                k["v_back"][at, :] = value
                value_low = value.astype(LOW)
                low[at, :] = value_low
                partial_sums[2] += row_sum(value_low.astype(F32))

            loop(half_len // NORM_ROWS, first_back)
            k.save(k["v_back"].at[at_rows], k["input_part"].at[at_rows])
            k.save(low.at[at_rows], k["attn_grad"].at[at_rows])
            k.point()
        for kind in range(3):
            sums[4 + kind : 5 + kind, :] = column_sum(partial_sums[kind])
        w_o = k["v_o"][...].reshape(width, width)
        for i in range(items):
            at_rows = pl.ds(i * half_len, half_len)
            k["v_mixed_grad"][at_rows, :] = mm(low[at_rows, :], w_o, NT).astype(LOW)
            k.save(k["v_mixed_grad"].at[at_rows], k["mixed_grad"].at[at_rows])
            k.point()
        k.close()

    ins = dict(
        back_low=fw["save_back_low"],
        act=fw["act"],
        w_out=weights[3].reshape(blocks, 4, 8, 32, width),
        slope=fw["save_slope"],
        w_in=weights[2],
        back=fw["save_back"],
        xhat=fw["save_xhat"],
        rstd=fw["save_rstd"],
        hidden=fw["save_hidden"],
        w_o=weights[1],
        vectors=fw["save_vectors"],
    )
    outs = dict(
        grad_in=((blocks, 4, 2, 2, 2, 32, width), LOW, "hbm"),
        input_part=((rows, width), F32, "hbm"),
        attn_grad=((rows, width), LOW, "hbm"),
        mixed_grad=((rows, width), LOW, "hbm"),
        sums=((8, width), F32, "vmem"),
    )
    if by_hand:
        outs["grad_out"] = ((128, width), F32, "vmem")
    else:
        outs["grad_out"] = ((4, 2, 2, 2, 128, width), LOW, "hbm")
    scratch = dict(
        v_low=pltpu.VMEM((rows, width), LOW),
        v_act=pltpu.VMEM((blocks, rows, width), LOW),
        v_left=pltpu.VMEM((rows, width), LOW),
        v_turned=pltpu.VMEM((width, rows), LOW),
        grad_in_part=pltpu.VMEM((2, 4, 2, 2, 2, 32, width), LOW),
        v_slope=pltpu.VMEM((blocks, rows, width), LOW),
        v_w=pltpu.VMEM((blocks, 4, 8, 32, width), LOW),
        v_back=pltpu.VMEM((rows, width), F32),
        v_xhat=pltpu.VMEM((rows, width), F32),
        v_rstd=pltpu.VMEM((rows, 128), F32),
        v_o=pltpu.VMEM((4, 8, 32, width), LOW),
        v_mixed_grad=pltpu.VMEM((rows, width), LOW),
        work=pltpu.VMEM((half_len, width), F32),
        grad=pltpu.VMEM((2, 4, 2, 2, 2, 128, half_width), LOW),
        partial_sums=pltpu.VMEM((3, 8, width), F32),
    )
    copies = 1
    if by_hand:
        copies += 2 * reduce_copies(nz)
        for q in range(2):
            for name, buffer in reduce_buffers(nz, 128, half_width).items():
                scratch[f"{name}{q}"] = buffer
    return call("feed_back" if by_hand else "", body, ins, ("vectors",), outs, scratch, copies, collective_id)


def attend_back(by_hand, items, half_len, fw, fb, weights, collective_id):
    blocks, rows, width = fw["act"].shape
    nz = lax.axis_size("dp") // 4
    chunks = blocks + 2
    step = 256
    scale = 1.0 / math.sqrt(HD)
    stages = 3 + (nz - 1).bit_length()

    def body(k):
        place, sender = k.place, k.sender
        load_grad = k.copy(k["mixed_grad"], k["v_grad"].at[0])
        grad = k["grad"]
        load_in = [k.copy(k["grad_in_part"].at[q], grad.at[q]) for q in range(blocks) if by_hand]
        load_mixed = [k.copy(k["mixed"], k["v_left"]), k.copy(k["attn_grad"], k["joint"].at[0])]
        load_heads = k.copy(k["heads"], k["v_heads"])
        load_qkv = [
            k.copy(k["w_qkv"].at[:, :, :, pl.ds(t * width, width)], k["v_qkv"].at[t]) for t in range(3)
        ]
        load_grad.wait()
        meet(place)
        over_grad = []
        for i in range(items):
            at_rows = pl.ds(i * half_len, half_len)
            over_grad.append(k.add(exchange(k, k["v_grad"].at[0, at_rows], k["v_grad"].at[1, at_rows])))
            k.step(over_grad[i])
        going = []

        def reduce(slot, target, split):
            if by_hand:
                buffers = {name: k[f"{name}{slot}"] for name in ("core", "diag", "line", "column")}
                going.append(k.add(reduce_steps(place, sender, grad.at[slot], buffers, target(), split, 1)))
                k.step(going[-1])
            k.point()

        for q in range(len(load_in)):
            load_in[q].wait()
            reduce(q, lambda q=q: k["grad_in"].at[:, pl.ds(q * width, width)], nz)
        left, turned, joint = k["v_left"], k["v_turned"], k["joint"]

        def turn(j):
            turned[tile(j, 128), :] = left[:, tile(j, 128)].T

        def outer(slot, right):
            def one(j):
                at = tile(j, step)
                part = mm(turned[...], right[:, at]).astype(LOW)
                grad[slot, :, :, :, :, :, at] = part.reshape(4, 2, 2, 2, 32, step)

            loop(width // step, one)

        for made in load_mixed:
            made.wait()
        loop(width // 128, turn)
        load_stream = k.copy(k["stream"], left)
        outer(blocks, joint.at[0])
        if not by_hand:
            k.save(grad.at[blocks], k["grad_o"])
        reduce(blocks, lambda: k["grad_o"], nz)
        load_heads.wait()
        same = lax.broadcasted_iota(jnp.int32, (half_len, half_len), 0) == lax.broadcasted_iota(
            jnp.int32, (half_len, half_len), 1
        )
        for i in range(items):
            asked = k["codes"][items + i : items + i + 1, :]
            asked_taken = k["codes_taken"][items + i : items + i + 1, :]
            code = k["cols"][:, 2 * items + i : 2 * items + i + 1]
            code_taken = k["cols_taken"][:, 2 * items + i : 2 * items + i + 1]
            k["permit"][i, 0:half_len, :] = jnp.where((code <= asked) | same, 0.0, fill_value)
            k["permit"][i, half_len : 2 * half_len, :] = jnp.where(code_taken <= asked, 0.0, fill_value)
            k["permit_taken"][i] = jnp.where(code <= asked_taken, 0.0, fill_value)
        k.point()
        heads, grads, result = k["v_heads"], k["v_grad"], joint
        lane = lax.broadcasted_iota(jnp.int32, (half_len, 2 * HD), 1)
        key_lane = lax.broadcasted_iota(jnp.int32, (2 * half_len, 2 * HD), 1)
        nothing = jnp.zeros((), LOW)
        pairs = width // (2 * HD)

        def ours(i):
            at_rows = pl.ds(i * half_len, half_len)

            def pair(p):
                at = tile(p, 2 * HD)
                query = heads[0, at_rows, at]
                keys = jnp.concatenate([heads[1, at_rows, at], heads[2, at_rows, at]], axis=0)
                values = jnp.concatenate([heads[3, at_rows, at], heads[4, at_rows, at]], axis=0)
                grad_row = grads[0, at_rows, at]
                query_part = key_part = value_part = None
                for h in range(2):
                    mine = (lane < HD) == (h == 0)
                    key_mine = (key_lane < HD) == (h == 0)
                    query_h = jnp.where(mine, query, nothing)
                    grad_h = jnp.where(mine, grad_row, nothing)
                    keys_h = jnp.where(key_mine, keys, nothing)
                    at_head = pl.ds(2 * p + h, 1)
                    scores = mm(keys, query_h * scale, NT) + (k["permit"][i] - k["logs"][i, at_head, :])
                    probs = jnp.exp(scores)
                    prob_grad = mm(values, grad_h, NT)
                    centre = column_sum(probs * prob_grad)
                    k["centre"][i, at_head, :] = centre
                    score_grad = (probs * (prob_grad - centre)).astype(LOW)
                    parts = (
                        mm(score_grad, keys_h, TN),
                        mm(score_grad[:half_len], query_h),
                        mm(probs[:half_len].astype(LOW), grad_h),
                    )
                    if h == 0:
                        query_part, key_part, value_part = parts
                    else:
                        query_part = query_part + parts[0]
                        key_part = key_part + parts[1]
                        value_part = value_part + parts[2]
                query_low = (query_part * scale).astype(LOW)
                result[0, at_rows, at] = query_low
                k["sums"][0:1, at] += column_sum(query_low.astype(F32))
                k["parts"][0, at_rows, at] = key_part
                k["parts"][1, at_rows, at] = value_part

            loop(pairs // 2, pair)
            k.point()
            loop(pairs // 2, lambda p: pair(p + pairs // 2))

        def theirs(i):
            at_rows = pl.ds(i * half_len, half_len)

            def pair(p):
                at = tile(p, 2 * HD)
                query = heads[5, at_rows, at]
                keys, values = heads[1, at_rows, at], heads[3, at_rows, at]
                grad_row = grads[1, at_rows, at]
                key_part, value_part = k["parts"][0, at_rows, at], k["parts"][1, at_rows, at]
                for h in range(2):
                    mine = (lane < HD) == (h == 0)
                    query_h = jnp.where(mine, query, nothing)
                    grad_h = jnp.where(mine, grad_row, nothing)
                    at_head = pl.ds(2 * p + h, 1)
                    scores = mm(keys, query_h * scale, NT) + (
                        k["permit_taken"][i] - k["logs_taken"][i, at_head, :]
                    )
                    probs = jnp.exp(scores)
                    prob_grad = mm(values, grad_h, NT)
                    score_grad = (probs * (prob_grad - k["centre_taken"][i, at_head, :])).astype(LOW)
                    key_part = key_part + mm(score_grad, query_h)
                    value_part = value_part + mm(probs.astype(LOW), grad_h)
                result[1, at_rows, at] = (key_part * scale).astype(LOW)
                value_low = value_part.astype(LOW)
                result[2, at_rows, at] = value_low
                k["sums"][1:2, at] += column_sum(value_low.astype(F32))

            loop(pairs // 2, pair)
            k.point()
            loop(pairs // 2, lambda p: pair(p + pairs // 2))

        k["sums"][...] = jnp.zeros_like(k["sums"])
        over = []
        for i in range(items):
            ours(i)
            over.append(k.add(exchange(k, k["centre"].at[i], k["centre_taken"].at[i])))
            k.step(over[i])
            k.point()
        load_stream.wait()
        loop(width // 128, turn)

        def outer_joint(q, slot):
            outer(slot, joint.at[q])
            if not by_hand:
                k.save(grad.at[slot], k["grad_qkv"].at[:, :, :, :, :, pl.ds(q * width, width)])
            reduce(slot, lambda: k["grad_qkv"].at[:, pl.ds(q * width, width)], nz // 2)

        outer_joint(0, blocks + 1)
        for i in range(items):
            k.finish(over[i], over_grad[i])
            theirs(i)
            k.point()
        levels = k["levels"]
        for s, name in enumerate(("sums_one", "sums_two")):
            levels[0, 8 * s : 8 * s + 8, :] = k[name][...]
        levels[0, 16:24, :] = k["sums"][...]
        small = k.add(sum_steps(place, sender, levels, k["levels_taken"]))
        k.step(small)
        k.finish(*going[:2])
        partners = place.partners()
        for partner in partners:
            pl.semaphore_signal(k["through"], inc=1, device_id=partner, device_id_type=MESH)
        load_part = k.copy(k["input_part"], k["parts"].at[0])
        pl.semaphore_wait(k["through"], len(partners))
        outer_joint(1, 0)
        outer_joint(2, 1)
        for made in load_qkv + [load_part]:
            made.wait()
        for i in range(items):
            at_rows = pl.ds(i * half_len, half_len)
            total = k["parts"][0, at_rows, :]
            for q in range(3):
                total = total + mm(joint[q, at_rows, :], k["v_qkv"][q].reshape(width, width), NT)
            left[at_rows, :] = total.astype(LOW)
            k.save(left.at[at_rows], k["input_grad"].at[at_rows])
            k.point()
        k.finish(*range(len(k.transfers)))
        k["totals"][...] = levels[stages]
        k.close()

    ins = dict(
        grad_in_part=fb["grad_in"],
        mixed=fw["save_mixed"],
        attn_grad=fb["attn_grad"],
        heads=fw["save_heads"],
        mixed_grad=fb["mixed_grad"],
        stream=fw["save_stream"],
        w_qkv=weights[0],
        input_part=fb["input_part"],
        codes=fw["codes"],
        codes_taken=fw["save_codes"],
        cols=fw["cols"],
        cols_taken=fw["save_cols"],
        logs=fw["save_logs"],
        logs_taken=fw["save_logs_taken"],
        sums_one=fw["sums"],
        sums_two=fb["sums"],
    )
    outs = dict(
        input_grad=((rows, width), LOW, "hbm"),
        totals=((24, width), F32, "vmem"),
    )
    if by_hand:
        outs["grad_in"] = ((32, blocks * width), F32, "vmem")
        outs["grad_o"] = ((32, width), F32, "vmem")
        outs["grad_qkv"] = ((32, 3 * width), F32, "vmem")
    else:
        outs["grad_o"] = ((4, 2, 2, 2, 32, width), LOW, "hbm")
        outs["grad_qkv"] = ((4, 2, 2, 2, 32, 3 * width), LOW, "hbm")
    scratch = dict(
        v_left=pltpu.VMEM((rows, width), LOW),
        v_turned=pltpu.VMEM((width, rows), LOW),
        joint=pltpu.VMEM((3, rows, width), LOW),
        v_heads=pltpu.VMEM((6, rows, width), LOW),
        v_grad=pltpu.VMEM((2, rows, width), LOW),
        v_qkv=pltpu.VMEM((3, 4, 8, 32, width), LOW),
        grad=pltpu.VMEM((chunks, 4, 2, 2, 2, 32, width), LOW),
        permit=pltpu.VMEM((items, 2 * half_len, half_len), F32),
        permit_taken=pltpu.VMEM((items, half_len, half_len), F32),
        parts=pltpu.VMEM((2, rows, width), F32),
        centre=pltpu.VMEM((items, HEADS, half_len), F32),
        centre_taken=pltpu.VMEM((items, HEADS, half_len), F32),
        sums=pltpu.VMEM((8, width), F32),
        levels=pltpu.VMEM((stages + 1, 24, width), F32),
        levels_taken=pltpu.VMEM((stages, 24, width), F32),
        through=pltpu.SemaphoreType.REGULAR,
    )
    copies = 2 * items + stages
    if by_hand:
        copies += (blocks + 4) * reduce_copies(nz)
        for q in range(chunks):
            for name, buffer in reduce_buffers(nz, 32, width).items():
                scratch[f"{name}{q}"] = buffer
    spaces = ("codes", "codes_taken", "cols", "cols_taken", "logs", "logs_taken", "sums_one", "sums_two")
    return call("attend_back" if by_hand else "", body, ins, spaces, outs, scratch, copies, collective_id)


def body(
    block_input,
    lengths,
    mask,
    blocks,
    timesteps,
    w_qkv,
    w_o,
    w_in,
    w_out,
    b_in,
    biases,
    gains,
    shifts,
    cotangent,
):
    items, half_len, width = block_input.shape
    rows = items * half_len
    f32 = jnp.float32
    n = n_devices()
    share = width // n
    b_count = b_in.shape[0]
    positions = lax.axis_index("ctx") * half_len + jnp.arange(half_len, dtype=jnp.int32)
    valid = (positions[None, :] < lengths[:, None]) & ((mask == 1) | (positions[None, :] == 0))
    numbers = blocks.astype(f32)
    key_codes = jnp.where(valid, numbers, code_absent)
    codes = jnp.pad(jnp.concatenate([key_codes, numbers]), ((0, 8 - 2 * items), (0, 0)))
    cols = jnp.concatenate([numbers, valid.astype(f32), key_codes]).T
    cols = jnp.pad(cols, ((0, 0), (0, 128 - 3 * items)))
    embed = jnp.pad(time_embed(timesteps, width), ((0, 8 - items), (0, 0)))
    small = jnp.concatenate([b_in, biases.reshape(-1), gains.reshape(-1), shifts.reshape(-1)])
    small_wide = -(-small.shape[0] // 128) * 128
    small = jnp.pad(small.astype(f32), (0, small_wide - small.shape[0]))
    small = jnp.broadcast_to(small[None, :], (8, small_wide))
    by_hand = w_qkv.shape[0] == 32
    weights = [w_qkv, w_o, w_in, w_out]
    if not by_hand:
        weights = [lax.all_gather(w, AXES, axis=0, tiled=True) for w in weights]
        weights = [w.reshape(4, 8, w.shape[0] // 32, w.shape[1]) for w in weights]
        small = lax.all_gather(small, AXES, axis=0).reshape(n // 8, 8, 8, small_wide)
    fw = forward(
        by_hand,
        items,
        half_len,
        weights,
        small,
        block_input.reshape(rows, width),
        embed,
        codes,
        cols,
        cotangent.reshape(rows, width),
        1,
    )
    if by_hand:
        weights = [fw["all_" + p] for p in ("w_qkv", "w_o", "w_in", "w_out")]
    fb = feed_back(by_hand, items, half_len, fw, weights, 2)
    ab = attend_back(by_hand, items, half_len, fw, fb, weights, 3)
    if by_hand:
        grads = [ab["grad_qkv"], ab["grad_o"], ab["grad_in"], fb["grad_out"]]
    else:
        grad_in = fb["grad_in"].reshape(4, width, width).transpose(1, 0, 2)
        grads = [
            lax.psum_scatter(
                part.astype(f32).reshape(rows_of, -1), AXES, scatter_dimension=0, tiled=True
            )
            for part, rows_of in (
                (ab["grad_qkv"], width),
                (ab["grad_o"], width),
                (grad_in, width),
                (fb["grad_out"], 4 * width),
            )
        ]
    totals = ab["totals"]
    me = my_index()
    grad_b_in = lax.dynamic_slice(totals[8:12].reshape(-1), (me * b_count,), (b_count,))
    order = (16, 17, 14, 4, 12, 5, 13, 6)
    mine = lax.dynamic_slice(totals, (0, me * share), (24, share))
    mine = jnp.stack([mine[row] for row in order])
    count = jnp.sum(totals[7, items : 2 * items])
    rms = jnp.sqrt(jnp.sum(totals[:4], axis=1) / (count * width))
    return (
        fw["output"].reshape(block_input.shape),
        ab["input_grad"].reshape(block_input.shape),
        *grads,
        grad_b_in,
        mine[:4],
        mine[4:6],
        mine[6:8],
        rms,
    )


def solution(mesh):
    in_specs = (
        P("dp", "ctx", None),
        P("dp"),
        P("dp", "ctx"),
        P("dp", "ctx"),
        P("dp"),
        P(("dp", "ctx"), None),
        P(("dp", "ctx"), None),
        P(("dp", "ctx"), None),
        P(("dp", "ctx"), None),
        P(("dp", "ctx")),
        P(None, ("dp", "ctx")),
        P(None, ("dp", "ctx")),
        P(None, ("dp", "ctx")),
        P("dp", "ctx", None),
    )
    out_specs = (
        P("dp", "ctx", None),
        P("dp", "ctx", None),
        P(("dp", "ctx"), None),
        P(("dp", "ctx"), None),
        P(("dp", "ctx"), None),
        P(("dp", "ctx"), None),
        P(("dp", "ctx")),
        P(None, ("dp", "ctx")),
        P(None, ("dp", "ctx")),
        P(None, ("dp", "ctx")),
        P(),
    )
    return jax.shard_map(body, mesh=mesh, in_specs=in_specs, out_specs=out_specs, check_vma=False)
```

```python
from functools import partial
import math

import jax
import jax.numpy as jnp
from jax import lax
from jax.experimental import pallas as pl
from jax.experimental.pallas import tpu as pltpu
from jax.sharding import PartitionSpec as P

HEADS = 16
HD = 64

AXES = ("dp", "ctx")
X = 1


def my_index():
    return lax.axis_index("dp") * lax.axis_size("ctx") + lax.axis_index("ctx")


def n_devices():
    return lax.axis_size("dp") * lax.axis_size("ctx")


fill_value = -1e30
eps_norm = 1e-05
code_absent = 30000.0


def time_embed(steps, width):
    half = width // 2
    freqs = jnp.exp(jnp.arange(half, dtype=jnp.float32) * (-math.log(10000.0) / half))
    angle = steps.astype(jnp.float32)[:, None] * freqs[None, :]
    return jnp.concatenate([jnp.sin(angle), jnp.cos(angle)], axis=-1)


MESH = pl.DeviceIdType.MESH


class Place:
    def __init__(self):
        dp = lax.axis_index("dp")
        self.nz = lax.axis_size("dp") // 4
        self.x = lax.axis_index("ctx")
        self.c = dp % 2
        self.y = (dp // 2) % 2
        self.z = dp // 4

    def zth(self, k):
        z, bit = self.z, 1
        while bit < self.nz:
            if k & bit:
                z = z + bit * (1 - 2 * ((self.z // bit) % 2))
            bit *= 2
        return z

    def flips(self, y=0, c=0, x=0):
        return (
            1 - self.y if y else self.y,
            1 - self.c if c else self.c,
            1 - self.x if x else self.x,
        )

    def device(self, k=0, y=0, c=0, x=0):
        fy, fc, fx = self.flips(y, c, x)
        return ((self.zth(k) * 2 + fy) * 2 + fc, fx)

    def shard(self, k=0, y=0, c=0, x=0):
        fy, fc, fx = self.flips(y, c, x)
        return ((self.zth(k) * 2 + fy) * 2 + fc) * 2 + fx

    def column(self, y=0, c=0, x=0):
        fy, fc, fx = self.flips(y, c, x)
        return (fy * 2 + fc) * 2 + fx

    def partners(self):
        return [self.device(k=k) for k in range(1, self.nz)] + [
            self.device(x=1),
            self.device(y=1),
            self.device(c=1),
        ]


def meet(place):
    barrier = pltpu.get_barrier_semaphore()
    partners = place.partners()
    for partner in partners:
        pl.semaphore_signal(barrier, inc=1, device_id=partner, device_id_type=MESH)
    pl.semaphore_wait(barrier, len(partners))


class Sender:
    def __init__(self, send_sem, recv_sem):
        self.send_sem, self.recv_sem = send_sem, recv_sem
        self.count = 0
        self.open = []

    def send(self, src, dst, device, keep=None):
        copy = pltpu.make_async_remote_copy(
            src_ref=src,
            dst_ref=dst,
            send_sem=self.send_sem.at[self.count],
            recv_sem=self.recv_sem.at[self.count],
            device_id=device,
            device_id_type=MESH,
        )
        self.count += 1
        copy.start()
        (self.open if keep is None else keep).append(copy)
        return copy

    def close(self):
        for copy in self.open:
            copy.wait_send()
        self.open = []


def gather_copies(nz):
    return 4 * nz + 5


def gather_steps(place, sender, shard, full, split):
    nz = place.nz
    mine, at_x, at_y, diag = (place.column(x=fx, y=fy) for fy, fx in ((0, 0), (0, 1), (1, 0), (1, 1)))
    own = full.at[place.z, mine]
    by_z = [sender.send(shard, own, place.device(k=k)) for k in range(1, nz)]
    yield
    from_x = [sender.send(shard, own, place.device(x=1))]
    from_y = [sender.send(shard, own, place.device(y=1))]
    yield
    for k in range(1, nz):
        by_z[k - 1].wait_recv()
        piece = full.at[place.zth(k), mine]
        from_x.append(sender.send(piece, piece, place.device(x=1)))
        from_y.append(sender.send(piece, piece, place.device(y=1)))
        yield
    to_core = [sender.send(full.at[:, mine], full.at[:, mine], place.device(c=1))]
    from_diag = []
    yield
    for k in range(nz):
        from_x[k].wait_recv()
        if k < split:
            piece = full.at[place.zth(k), at_x]
            from_diag.append(sender.send(piece, piece, place.device(y=1)))
        else:
            from_y[k].wait_recv()
            piece = full.at[place.zth(k), at_y]
            from_diag.append(sender.send(piece, piece, place.device(x=1)))
        yield
    to_core.append(sender.send(full.at[:, at_x], full.at[:, at_x], place.device(c=1)))
    for k in range(split):
        from_y[k].wait_recv()
    to_core.append(sender.send(full.at[:, at_y], full.at[:, at_y], place.device(c=1)))
    yield
    half = nz // 2
    for start, size in ((0, half), (half, nz - half)):
        for copy in from_diag if start == 0 else ():
            copy.wait_recv()
        part = full.at[pl.ds(start, size), diag]
        to_core.append(sender.send(part, part, place.device(c=1)))
    yield
    for copy in to_core:
        copy.wait_recv()


def gather_late_steps(place, sender, shard, full):
    nz = place.nz
    own = full.at[place.z, place.column()]
    from_x = sender.send(shard, own, place.device(x=1))
    from_y = sender.send(shard, own, place.device(y=1))
    yield
    from_x.wait_recv()
    piece = full.at[place.z, place.column(x=1)]
    from_diag = sender.send(piece, piece, place.device(y=1))
    yield
    from_y.wait_recv()
    from_diag.wait_recv()
    by_z = []
    for k in range(1, nz):
        for fy in range(2):
            for fx in range(2):
                piece = full.at[place.z, place.column(y=fy, x=fx)]
                by_z.append(sender.send(piece, piece, place.device(k=k)))
    yield
    for copy in by_z:
        copy.wait_recv()
    to_core = []
    for fy in range(2):
        for fx in range(2):
            piece = full.at[:, place.column(y=fy, x=fx)]
            to_core.append(sender.send(piece, piece, place.device(c=1)))
    yield
    for copy in to_core:
        copy.wait_recv()


NN = (((1,), (0,)), ((), ()))
NT = (((1,), (1,)), ((), ()))
TN = (((0,), (0,)), ((), ()))
LOW = jnp.bfloat16
F32 = jnp.float32


def mm(left, right, dims=NN):
    return lax.dot_general(left, right, dims, preferred_element_type=F32)


def loop(count, step):
    lax.fori_loop(0, count, lambda i, _: (step(i), 0)[1], 0)


def tile(index, size):
    return pl.ds(pl.multiple_of(index * size, size), size)


def expand(packed, offset, share, start, length):
    n, wide = packed.shape
    place = lax.broadcasted_iota(jnp.int32, (wide, length), 1) + start
    lane = lax.broadcasted_iota(jnp.int32, (wide, length), 0)
    pick = (lane == offset + lax.rem(place, share)).astype(F32).astype(LOW)
    spread = mm(packed, pick)
    row = lax.broadcasted_iota(jnp.int32, (n, length), 0)
    column = lax.broadcasted_iota(jnp.int32, (n, length), 1) + start
    return jnp.sum(jnp.where(row == lax.div(column, share), spread, 0.0), axis=0, keepdims=True)


def normalize(resid):
    centre = resid - jnp.mean(resid, axis=-1, keepdims=True)
    spread = jnp.mean(centre * centre, axis=-1, keepdims=True)
    rstd = lax.rsqrt(spread + eps_norm)
    return centre * rstd, rstd


def column_sum(value):
    return jnp.sum(value, axis=0, keepdims=True)


def reduce_copies(nz):
    return nz + 6 + nz - 1


def reduce_buffers(nz, rows, cols):
    return dict(
        core=pltpu.VMEM((nz, 2, 2, rows, cols), LOW),
        diag=pltpu.VMEM((nz, rows, cols), LOW),
        line=pltpu.VMEM((2, nz, rows, cols), LOW),
        column=pltpu.VMEM((nz - 1, rows, cols), LOW),
    )


def add_rows(store, terms, count, rows, cols):
    step = min(rows, 16 * max(1, 1024 // cols))
    per = rows // step

    def one(j):
        i, start = j // per, (j % per) * step
        at = pl.ds(pl.multiple_of(start, step), step)
        total = terms[0](i, at).astype(F32)
        for term in terms[1:]:
            total = total + term(i, at).astype(F32)
        store(i, at, total)

    loop(count * per, one)


def reduce_steps(place, sender, grad, buffers, out, split, parts):
    nz = place.nz
    rows, cols = grad.shape[4:]
    core, diag, line, column = (buffers[k] for k in ("core", "diag", "line", "column"))
    groups = ((1, 1), (0, 1), (1, 0), (0, 0))
    here = [place.flips(y=fy, x=fx) for fy, fx in groups]
    sent, by_core = [], []
    size = nz // parts
    for t in range(parts):
        if t:
            yield
        at = pl.ds(t * size, size)
        by_core.append(sender.send(grad.at[at, :, 1 - place.c], core.at[at], place.device(c=1), sent))
    yield

    def put(slot, start=0):
        fy, fc, fx = here[slot]

        def store(i, at, value):
            grad[i + start, fy, fc, fx, at, :] = value.astype(LOW)

        return store

    def held(slot, start=0):
        fy, fc, fx = here[slot]
        return lambda i, at: grad[i + start, fy, fc, fx, at, :]

    def add_core(slot):
        fy, _, fx = here[slot]
        add_rows(put(slot), [held(slot), lambda i, at: core[i, fy, fx, at, :]], nz, rows, cols)

    def part(slot, start, count):
        fy, fc, fx = here[slot]
        return grad.at[pl.ds(start, count), fy, fc, fx]

    low, high = pl.ds(0, split), pl.ds(split, nz - split)
    by_y = by_x = x_high = y_low = x_low = y_high = None
    for copy in by_core:
        copy.wait_recv()
    add_core(0)
    if split > 0:
        by_y = sender.send(part(0, 0, split), diag.at[low], place.device(y=1), sent)
    if split < nz:
        by_x = sender.send(part(0, split, nz - split), diag.at[high], place.device(x=1), sent)
    yield
    add_core(1)
    if split < nz:
        x_high = sender.send(part(1, split, nz - split), line.at[0, high], place.device(x=1), sent)
    add_core(2)
    if split > 0:
        y_low = sender.send(part(2, 0, split), line.at[1, low], place.device(y=1), sent)
    yield
    add_core(3)
    yield
    if split > 0:
        by_y.wait_recv()
        add_rows(put(1), [held(1), lambda i, at: diag[i, at, :]], split, rows, cols)
        x_low = sender.send(part(1, 0, split), line.at[0, low], place.device(x=1), sent)
    yield
    if split < nz:
        by_x.wait_recv()
        add_rows(put(2, split), [held(2, split), lambda i, at: diag[i + split, at, :]], nz - split, rows, cols)
        y_high = sender.send(part(2, split, nz - split), line.at[1, high], place.device(y=1), sent)
    yield
    for copy in (x_high, y_low, x_low, y_high):
        if copy is not None:
            copy.wait_recv()
    add_rows(
        put(3),
        [held(3), lambda i, at: line[0, i, at, :], lambda i, at: line[1, i, at, :]],
        nz,
        rows,
        cols,
    )
    fy, fc, fx = here[3]
    by_z = [
        sender.send(grad.at[place.zth(k), fy, fc, fx], column.at[k - 1], place.device(k=k), sent)
        for k in range(1, nz)
    ]
    yield
    for copy in by_z:
        copy.wait_recv()

    def last(i, at, value):
        out[at, :] = value

    add_rows(
        last,
        [lambda i, at: grad[place.z, fy, fc, fx, at, :]]
        + [lambda i, at, k=k: column[k, at, :] for k in range(nz - 1)],
        1,
        rows,
        cols,
    )
    for copy in sent:
        copy.wait_send()


def reduce_late_copies(nz):
    return 1 + nz - 1 + 3


def reduce_late_buffers(nz, rows, cols):
    return dict(
        core=pltpu.VMEM((nz, 2, 2, rows, cols), LOW),
        diag=pltpu.VMEM((1, rows, cols), LOW),
        line=pltpu.VMEM((2, 1, rows, cols), LOW),
        column=pltpu.VMEM((nz - 1, 2, 2, rows, cols), LOW),
    )


def reduce_late_steps(place, sender, grad, buffers, out):
    nz = place.nz
    rows, cols = grad.shape[4:]
    core, diag, line, column = (buffers[k] for k in ("core", "diag", "line", "column"))
    sent = []
    by_core = sender.send(grad.at[:, :, 1 - place.c], core, place.device(c=1), sent)
    yield
    by_core.wait_recv()
    for fy in range(2):
        for fx in range(2):

            def put(i, at, value, fy=fy, fx=fx):
                grad[i, fy, place.c, fx, at, :] = value.astype(LOW)

            add_rows(
                put,
                [
                    lambda i, at, fy=fy, fx=fx: grad[i, fy, place.c, fx, at, :],
                    lambda i, at, fy=fy, fx=fx: core[i, fy, fx, at, :],
                ],
                nz,
                rows,
                cols,
            )
    by_z = [
        sender.send(grad.at[place.zth(k), :, place.c], column.at[k - 1], place.device(k=k), sent)
        for k in range(1, nz)
    ]
    yield
    for copy in by_z:
        copy.wait_recv()

    def add(fy, fx, terms):
        ty, tc, tx = place.flips(y=fy, x=fx)

        def put(i, at, value):
            grad[place.z, ty, tc, tx, at, :] = value.astype(LOW)

        add_rows(put, [lambda i, at: grad[place.z, ty, tc, tx, at, :]] + terms(ty, tx), 1, rows, cols)
        return grad.at[place.z, ty, tc, tx]

    def columns(ty, tx):
        return [lambda i, at, k=k: column[k, ty, tx, at, :] for k in range(nz - 1)]

    part = add(1, 1, columns)
    by_y = sender.send(part, diag.at[0], place.device(y=1), sent)
    part = add(1, 0, columns)
    y_line = sender.send(part, line.at[1, 0], place.device(y=1), sent)
    add(0, 1, columns)
    add(0, 0, columns)
    yield
    by_y.wait_recv()
    part = add(0, 1, lambda ty, tx: [lambda i, at: diag[0, at, :]])
    x_line = sender.send(part, line.at[0, 0], place.device(x=1), sent)
    yield
    x_line.wait_recv()
    y_line.wait_recv()
    ty, tc, tx = place.flips()

    def last(i, at, value):
        out[at, :] = value

    add_rows(
        last,
        [
            lambda i, at: grad[place.z, ty, tc, tx, at, :],
            lambda i, at: line[0, 0, at, :],
            lambda i, at: line[1, 0, at, :],
        ],
        1,
        rows,
        cols,
    )
    for copy in sent:
        copy.wait_send()


def sum_steps(place, sender, levels, taken):
    partners = [place.device(c=1), place.device(x=1), place.device(y=1)]
    bit = 1
    while bit < place.nz:
        partners.append(place.device(k=bit))
        bit *= 2
    for s, partner in enumerate(partners):
        copy = sender.send(levels.at[s], taken.at[s], partner)
        yield
        copy.wait_recv()
        levels[s + 1] = levels[s] + taken[s]


class Kernel:
    def __init__(self, name, names, refs):
        self.refs = dict(zip(names, refs))
        self.place = Place()
        self.sender = Sender(self["send"], self["recv"])
        self.plan = PLANS.get(name, ())
        self.count = self.points = 0
        self.saved, self.transfers = [], []

    def __getitem__(self, name):
        return self.refs[name]

    def copy(self, src, dst):
        made = pltpu.make_async_copy(src, dst, self["local"].at[self.count])
        self.count += 1
        made.start()
        return made

    def save(self, src, dst):
        made = self.copy(src, dst)
        self.saved.append(made)
        return made

    def add(self, steps):
        self.transfers.append(steps)
        return len(self.transfers) - 1

    def step(self, number):
        return next(self.transfers[number], self) is not self

    def point(self):
        turn = self.plan[self.points] if self.points < len(self.plan) else ()
        self.points += 1
        for number in turn:
            self.step(number)

    def finish(self, *numbers):
        for number in numbers:
            while self.step(number):
                pass

    def close(self):
        self.finish(*range(len(self.transfers)))
        for made in self.saved:
            made.wait()
        self.sender.close()


PARTS = (
    ("w_qkv", None, None, False),
    ("small", None, None, False),
    ("w_o", None, None, True),
    ("w_in", 0, 2048, False),
    ("w_in", 2048, 3072, False),
    ("w_in", 3072, 4096, True),
    ("w_out", 0, 512, False),
    ("w_out", 512, 1024, False),
)
OUT_SPLITS = (2, 2, 2, None)
IN_SPLITS = (4, 4, 4, 4)
O_SPLIT = None
QKV_SPLITS = (2, 2, 2)
PLANS = {
    "forward": (
        (8, 5, 1, 0, 2, 3, 0, 2, 13, 6, 5),
        (0, 0),
        (0, 8, 10, 13),
        (12, 13, 4),
        (7,),
        (13, 0),
        (0, 3, 4, 10),
        (0, 2, 0, 12, 0, 3, 10),
        (3, 3, 4, 11),
        (0, 6, 3),
        (4, 4, 8, 3, 15),
        (4, 14, 4, 5),
        (3, 8),
        (4, 3, 3, 7),
        (6,),
        (),
        (6,),
        (4, 4, 4, 6),
        (6,),
        (),
        (2, 7),
        (3, 6, 7),
        (),
        (3, 7),
        (6, 7, 4),
        (6,),
        (6,),
        (7,),
        (5, 7, 6, 17),
        (7,),
        (7,),
        (6,),
        (18, 9, 17, 7),
        (16, 7),
        (),
        (16, 17),
    ),
    "feed_back": (
        (0, 0, 0, 2, 3, 1),
        (1,),
        (0, 1, 2),
        (0, 2),
        (2, 1),
        (0, 1),
        (),
        (2,),
        (3, 1),
        (),
        (3, 2),
        (),
        (),
        (),
        (),
        (3,),
        (1,),
    ),
    "attend_back": (
        (),
        (),
        (),
        (),
        (),
        (3,),
        (3, 5),
        (4,),
        (3, 7, 6),
        (),
        (4, 6, 3),
        (4, 5, 5),
        (4, 3),
        (6, 6, 4, 3),
        (11,),
        (11, 4),
        (6,),
        (11,),
        (11,),
        (12, 11, 6, 5),
        (12, 5, 13, 11, 13, 14, 12, 5),
        (13, 13, 13),
        (14, 6, 12, 14, 14),
        (14, 7, 6, 13, 14),
    ),
}


def call(name, body, ins, spaces_in, outs, scratch, copies, collective_id):
    vmem, hbm = pl.BlockSpec(memory_space=pltpu.VMEM), pl.BlockSpec(memory_space=pl.ANY)
    scratch = dict(
        send=pltpu.SemaphoreType.DMA((copies,)),
        recv=pltpu.SemaphoreType.DMA((copies,)),
        local=pltpu.SemaphoreType.DMA((64,)),
        **scratch,
    )
    names = list(ins) + list(outs) + list(scratch)

    def kernel(*refs):
        body(Kernel(name, names, refs))

    results = pl.pallas_call(
        kernel,
        out_shape=[jax.ShapeDtypeStruct(s, d) for s, d, _ in outs.values()],
        in_specs=[
            pl.BlockSpec(memory_space=pltpu.SMEM) if given == "lengths" else vmem if given in spaces_in else hbm
            for given in ins
        ],
        out_specs=[vmem if space == "vmem" else hbm for _, _, space in outs.values()],
        scratch_shapes=list(scratch.values()),
        compiler_params=pltpu.CompilerParams(
            collective_id=collective_id, has_side_effects=True, vmem_limit_bytes=63 << 20
        ),
    )(*ins.values())
    return dict(zip(outs, results))


def exchange(k, src, dst):
    copy = k.sender.send(src, dst, k.place.device(x=1))
    yield
    copy.wait_recv()


def row_sum(value):
    return jnp.sum(value.reshape(-1, 8, value.shape[-1]), axis=0)


NORM_ROWS = 128


def forward(by_hand, items, half_len, weights, small, block_input, embed, slots, cotangent, collective_id):
    rows, width = block_input.shape
    full_len = 2 * half_len
    blocks = 4
    nz = lax.axis_size("dp") // 4
    step = 256
    params = ["w_qkv", "small", "w_o", "w_in", "w_out"]

    def body(k):
        place = k.place
        cot_in = k.copy(k["cotangent"], k["cot"])
        full = {p: k["v_" + p] for p in params}
        if by_hand:
            pieces = [k["b_in"][...]]
            for name in ("biases", "gains", "shifts"):
                pieces += [k[name][t : t + 1, :] for t in range(k[name].shape[0])]
            line = jnp.concatenate([piece.astype(F32) for piece in pieces], axis=1)
            k["small"][...] = jnp.broadcast_to(line, k["small"].shape)
        kept = [k.copy(k[p], full[p].at[place.z, place.column()] if by_hand else full[p]) for p in params]
        slot = lax.broadcasted_iota(jnp.int32, (1, half_len), 1) + place.x * half_len
        codes, cols, table = k["codes"], k["cols"], k["table"]
        codes[...] = jnp.zeros_like(codes)
        table[...] = jnp.zeros_like(table)
        for i in range(items):
            valid = (slot < k["lengths"][i]) & ((k["mask"][i : i + 1, :] == 1) | (slot == 0))
            numbers = k["blocks"][i : i + 1, :].astype(F32)
            key_code = jnp.where(valid, numbers, code_absent)
            codes[i : i + 1, :] = key_code
            codes[items + i : items + i + 1, :] = numbers
            table[i : i + 1, :] = numbers
            table[items + i : items + i + 1, :] = valid.astype(F32)
            table[2 * items + i : 2 * items + i + 1, :] = key_code
        cols[...] = table[...].T
        k.save(codes, k["save_own_codes"])
        k.save(cols, k["save_own_cols"])
        meet(place)
        for made in kept:
            made.wait()
        number = {}
        if by_hand:
            for p, start, stop, late in PARTS:
                if start is None:
                    shard, whole = k[p], full[p]
                else:
                    shard = k[p].at[:, pl.ds(start, stop - start)]
                    whole = full[p].at[:, :, :, pl.ds(start, stop - start)]
                if late:
                    steps = gather_late_steps(place, k.sender, shard, whole)
                else:
                    steps = gather_steps(place, k.sender, shard, whole, nz - nz // 4)
                number.setdefault(p, []).append(k.add(steps))

        def arrive(p, *which):
            if by_hand:
                k.finish(*[number[p][i] for i in which or range(len(number[p]))])

        codes_over = k.add(exchange(k, k["codes"], k["codes_taken"]))
        cols_over = k.add(exchange(k, k["cols"], k["cols_taken"]))
        quarter = half_len // 2
        input_over = [
            k.add(exchange(k, k["input"].at[pl.ds(i * quarter, quarter)], k["taken"].at[pl.ds(i * quarter, quarter)]))
            for i in range(2 * items)
        ]
        k.point()
        stream, partial_sums = k["stream"], k["partial_sums"]
        partial_sums[...] = jnp.zeros_like(partial_sums)

        def gather_sum(kind, value):
            partial_sums[kind] += row_sum(value)

        for i in range(items):
            item_embed = k["embed"][i : i + 1, :]

            def make_stream(j, i=i, item_embed=item_embed):
                at = pl.ds(pl.multiple_of(i * half_len + j * 64, 64), 64)
                value = k["input"][at, :].astype(F32) + item_embed
                stream[at, :] = value.astype(LOW)
                gather_sum(0, value * value * k["cols"][tile(j, 64), items + i : items + i + 1])

            loop(half_len // 64, make_stream)
        save_stream = k.copy(stream.at[pl.ds(0, rows)], k["save_stream"])
        k.point()
        arrive("small")
        shards = k["v_small"].shape[0] * k["v_small"].shape[1]
        for d in range(shards):
            k["packed"][d : d + 1, :] = k["v_small"][d // 8, d % 8, 0:1, :]
        packed = k["packed"][...].astype(LOW)
        share = width // shards
        b_share = share * blocks
        vectors, b_in = k["vectors"], k["v_b_in"]
        for t in range(8):
            vectors[t : t + 1, :] = expand(packed, b_share + t * share, share, 0, width)
            if t in (0, 1, 3, 5):
                k.point()
        for t in range(blocks):
            b_in[t : t + 1, :] = expand(packed, 0, b_share, t * width, width)
            k.point()
        bias_o = vectors[2:3, :]
        gain_one, gain_two, shift_one, shift_two = (vectors[t : t + 1, :] for t in range(4, 8))
        heads = k["heads"]

        def weight(name, t, j):
            value = full[name][:, :, :, pl.ds(pl.multiple_of(t * width + j * step, step), step)]
            return value.reshape(-1, step)

        def keep(name):
            if by_hand:
                k.save(full[name], k["all_" + name])

        arrive("w_qkv")
        keep("w_qkv")
        k.point()

        def project(slot, t, bias):
            def one(j):
                at = tile(j, step)
                value = mm(stream[pl.ds(0, rows), :], weight("w_qkv", t, j))
                if bias is not None:
                    value = value + vectors[bias : bias + 1, at]
                heads[slot, :, at] = value.astype(LOW)

            loop(width // step, one)

        for slot, t, bias in ((0, 0, 0), (1, 1, None), (3, 2, 1)):
            project(slot, t, bias)
            k.point()
        k.finish(codes_over)
        same = lax.broadcasted_iota(jnp.int32, (half_len, half_len), 0) == lax.broadcasted_iota(
            jnp.int32, (half_len, half_len), 1
        )
        for i in range(items):
            asked = k["cols"][:, i : i + 1]
            own = (k["codes"][i : i + 1, :] <= asked) | same
            other = k["codes_taken"][i : i + 1, :] <= asked
            k["permit"][i, :, 0:half_len] = jnp.where(own, 0.0, fill_value)
            k["permit"][i, :, half_len : 2 * half_len] = jnp.where(other, 0.0, fill_value)
        k.save(k["codes_taken"], k["save_codes"])
        k.point()
        save_stream.wait()
        lane = lax.broadcasted_iota(jnp.int32, (half_len, 2 * HD), 1)
        key_lane = lax.broadcasted_iota(jnp.int32, (2 * half_len, 2 * HD), 1)
        pairs = width // (2 * HD)
        for i in range(items):
            at_rows = pl.ds(i * half_len, half_len)
            at_theirs = pl.ds(rows + i * half_len, half_len)
            item_embed = k["embed"][i : i + 1, :]
            k.finish(input_over[2 * i], input_over[2 * i + 1])

            def make_other(j, i=i, item_embed=item_embed):
                at = pl.ds(pl.multiple_of(i * half_len + j * 64, 64), 64)
                to = pl.ds(pl.multiple_of(rows + i * half_len + j * 64, 64), 64)
                stream[to, :] = (k["taken"][at, :].astype(F32) + item_embed).astype(LOW)

            def project_other(j, at_rows=at_rows, at_theirs=at_theirs):
                at = tile(j, step)
                source = stream[at_theirs, :]
                heads[2, at_rows, at] = mm(source, weight("w_qkv", 1, j)).astype(LOW)
                heads[4, at_rows, at] = (mm(source, weight("w_qkv", 2, j)) + vectors[1:2, at]).astype(LOW)
                heads[5, at_rows, at] = (mm(source, weight("w_qkv", 0, j)) + vectors[0:1, at]).astype(LOW)

            loop(half_len // 64, make_other)
            loop(width // step, project_other)
            if i == items - 1:
                save_heads = k.copy(heads, k["save_heads"])
            k.point()

            def pair(p, i=i, at_rows=at_rows):
                at = tile(p, 2 * HD)
                query = heads[0, at_rows, at] * (1.0 / math.sqrt(HD))
                keys = jnp.concatenate([heads[1, at_rows, at], heads[2, at_rows, at]], axis=0)
                values = jnp.concatenate([heads[3, at_rows, at], heads[4, at_rows, at]], axis=0)
                nothing = jnp.zeros((), LOW)
                mixed = None
                logs = k["logs"][i]
                for h in range(2):
                    scores = mm(jnp.where((lane < HD) == (h == 0), query, nothing), keys, NT) + k["permit"][i]
                    peak = jnp.max(scores, axis=1, keepdims=True)
                    expo = jnp.exp(scores - peak)
                    total = jnp.sum(expo, axis=1, keepdims=True)
                    probs = (expo * (1.0 / total)).astype(LOW)
                    part = mm(probs, jnp.where((key_lane < HD) == (h == 0), values, nothing))
                    mixed = part if mixed is None else mixed + part
                    logs = jnp.where(lane == 2 * p + h, peak + jnp.log(total), logs)
                k["logs"][i] = logs
                stream[at_rows, at] = mixed.astype(LOW)

            loop(pairs // 2, pair)
            k.point()
            loop(pairs // 2, lambda p, pair=pair: pair(p + pairs // 2))
            k["log_rows"][i] = k["logs"][i].T[:HEADS]
            k.add(exchange(k, k["log_rows"].at[i], k["logs_taken"].at[i]))
            k.point()
        save_mixed = k.copy(stream.at[pl.ds(0, rows)], k["save_mixed"])
        k.save(k["log_rows"], k["save_logs"])
        arrive("w_o")
        keep("w_o")
        xhat = k["xhat"]
        for i in range(items):
            at_rows = pl.ds(i * half_len, half_len)
            k["work"][...] = mm(stream[at_rows, :], full["w_o"][...].reshape(width, width)) + bias_o
            item_embed = k["embed"][i : i + 1, :]

            def first_norm(j, i=i, item_embed=item_embed):
                at = pl.ds(pl.multiple_of(i * half_len + j * NORM_ROWS, NORM_ROWS), NORM_ROWS)
                to = pl.ds(pl.multiple_of(rows + i * half_len + j * NORM_ROWS, NORM_ROWS), NORM_ROWS)
                attn = k["work"][tile(j, NORM_ROWS), :]
                gather_sum(1, attn * attn * k["cols"][tile(j, NORM_ROWS), items + i : items + i + 1])
                value, rstd = normalize(k["input"][at, :].astype(F32) + item_embed + attn)
                xhat[at, :] = value
                k["rstd"][at, :] = jnp.broadcast_to(rstd, (NORM_ROWS, 128))
                stream[to, :] = (value * gain_one + shift_one).astype(LOW)

            loop(half_len // NORM_ROWS, first_norm)
            k.point()
        save_hidden = k.copy(stream.at[pl.ds(rows, rows)], k["save_hidden"])
        k.save(xhat, k["save_xhat"])
        k.save(k["rstd"], k["save_rstd"])
        save_heads.wait()
        act, slope = heads, k["slope"]
        in_parts = {start: i for i, (start, _) in enumerate(part[1:3] for part in PARTS if part[0] == "w_in")}
        for t in range(blocks):
            if t * width in in_parts:
                arrive("w_in", in_parts[t * width])
                k.point()

            def feed(j, t=t):
                at = tile(j, step)
                w_in = weight("w_in", t, j)
                for i in range(items):
                    own = pl.ds(i * half_len, half_len)
                    pre = mm(stream[pl.ds(rows + i * half_len, half_len), :], w_in) + b_in[t : t + 1, at]
                    cdf = 0.5 + 0.5 * lax.erf(pre * (1.0 / math.sqrt(2.0)))
                    act[t, own, at] = (pre * cdf).astype(LOW)
                    pdf = jnp.exp(pre * pre * -0.5) * (1.0 / math.sqrt(2.0 * math.pi))
                    slope[t, own, at] = (cdf + pre * pdf).astype(LOW)

            loop(width // step, feed)
            k.save(act.at[t], k["act"].at[t])
            k.save(slope.at[t], k["save_slope"].at[t])
            k.point()
        keep("w_in")
        cot_in.wait()
        save_mixed.wait()
        save_hidden.wait()
        back = k["back"]
        out_parts = [(start, stop) for p, start, stop, _ in PARTS if p == "w_out"] if by_hand else [(0, width)]
        for which, (start, stop) in enumerate(out_parts):
            columns = pl.ds(start, stop - start)
            arrive("w_out", which)
            for i in range(items):
                at_rows = pl.ds(i * half_len, half_len)
                total = None
                for t in range(blocks):
                    part = mm(act[t, at_rows, :], full["w_out"][t, :, :, columns].reshape(width, stop - start))
                    total = part if total is None else total + part
                back[at_rows, columns] = total + vectors[3:4, columns]
            k.point()
        keep("w_out")
        for i in range(items):
            at_rows = pl.ds(i * half_len, half_len)

            def second_norm(j, i=i):
                at = pl.ds(pl.multiple_of(i * half_len + j * NORM_ROWS, NORM_ROWS), NORM_ROWS)
                to = pl.ds(pl.multiple_of(rows + i * half_len + j * NORM_ROWS, NORM_ROWS), NORM_ROWS)
                weight_rows = k["cols"][tile(j, NORM_ROWS), items + i : items + i + 1]
                branch = back[at, :]
                gather_sum(2, branch * branch * weight_rows)
                value, rstd = normalize(xhat[at, :] * gain_one + shift_one + branch)
                result = value * gain_two + shift_two
                gather_sum(3, result * result * weight_rows)
                stream[at, :] = result.astype(LOW)
                grad = k["cot"][at, :].astype(F32)
                gather_sum(5, grad * value)
                gather_sum(6, grad)
                scaled = grad * gain_two
                passed = rstd * (
                    scaled
                    - jnp.mean(scaled, axis=-1, keepdims=True)
                    - value * jnp.mean(scaled * value, axis=-1, keepdims=True)
                )
                back[at, :] = passed
                back_low = passed.astype(LOW)
                stream[to, :] = back_low
                gather_sum(4, back_low.astype(F32))

            loop(half_len // NORM_ROWS, second_norm)
            at_other = pl.ds(rows + i * half_len, half_len)
            k.save(stream.at[at_rows], k["output"].at[at_rows])
            k.save(stream.at[at_other], k["save_back_low"].at[at_rows])
            k.save(back.at[at_rows], k["save_back"].at[at_rows])
        for kind in range(7):
            k["sums"][kind : kind + 1, :] = column_sum(partial_sums[kind])
        k["sums"][7:8, :] = jnp.zeros((1, width), F32)
        k["sums"][7:8, 0:128] = column_sum(k["cols"][...])
        k.save(vectors, k["save_vectors"])
        k.finish(*range(len(k.transfers)))
        k.save(k["logs_taken"], k["save_logs_taken"])
        k.save(k["cols_taken"], k["save_cols"])
        k.close()

    ins = dict(zip(params, [weights[0], small] + weights[1:]))
    spaces_in = ["input", "embed", "mask", "blocks"]
    lengths, mask, numbers = slots
    if by_hand:
        spaces_in += params + ["b_in", "biases", "gains", "shifts"]
        b_in, biases, gains, shifts = small
        small_wide = b_in.shape[0] + 8 * biases.shape[1]
        small_shape = (8, small_wide)
        del ins["small"]
        ins.update(b_in=b_in[None, :], biases=biases, gains=gains, shifts=shifts)
    else:
        small_shape = small.shape
    ins.update(lengths=lengths, mask=mask, blocks=numbers)
    ins.update(input=block_input, embed=embed, cotangent=cotangent)
    codes_shape, cols_shape = (8, half_len), (half_len, 128)
    outs = {}
    if by_hand:
        for p in params:
            if p != "small":
                outs["all_" + p] = ((nz, 8) + ins[p].shape, ins[p].dtype, "hbm")
    outs.update(
        save_heads=((6, rows, width), LOW, "hbm"),
        save_own_codes=(codes_shape, F32, "hbm"),
        save_own_cols=(cols_shape, F32, "hbm"),
        save_codes=(codes_shape, F32, "hbm"),
        save_cols=(cols_shape, F32, "hbm"),
        save_stream=((rows, width), LOW, "hbm"),
        save_hidden=((rows, width), LOW, "hbm"),
        save_mixed=((rows, width), LOW, "hbm"),
        save_logs=((items, HEADS, half_len), F32, "hbm"),
        save_logs_taken=((items, HEADS, half_len), F32, "hbm"),
        save_xhat=((rows, width), F32, "hbm"),
        save_rstd=((rows, 128), F32, "hbm"),
        act=((blocks, rows, width), LOW, "hbm"),
        save_slope=((blocks, rows, width), LOW, "hbm"),
        output=((rows, width), LOW, "hbm"),
        save_back_low=((rows, width), LOW, "hbm"),
        save_back=((rows, width), F32, "hbm"),
        save_vectors=((8, width), F32, "hbm"),
        sums=((8, width), F32, "vmem"),
    )
    small_full = (nz, 8) + small_shape if by_hand else small_shape
    copies = len(PARTS) * max(gather_copies(nz), 4 * nz + 4) + 3 * items + 2
    scratch = dict(
        partial_sums=pltpu.VMEM((7, 8, width), F32),
        taken=pltpu.VMEM((rows, width), LOW),
        codes=pltpu.VMEM(codes_shape, F32),
        cols=pltpu.VMEM(cols_shape, F32),
        table=pltpu.VMEM((128, half_len), F32),
        codes_taken=pltpu.VMEM(codes_shape, F32),
        cols_taken=pltpu.VMEM(cols_shape, F32),
        stream=pltpu.VMEM((2 * rows, width), LOW),
        v_w_qkv=pltpu.VMEM((4, 8, 32, 3 * width), LOW),
        v_small=pltpu.VMEM(small_full, F32),
        packed=pltpu.VMEM((small_full[0] * 8, small_full[-1]), F32),
        vectors=pltpu.VMEM((8, width), F32),
        v_b_in=pltpu.VMEM((8, width), F32),
        heads=pltpu.VMEM((6, rows, width), LOW),
        permit=pltpu.VMEM((items, half_len, full_len), F32),
        logs=pltpu.VMEM((items, half_len, 128), F32),
        log_rows=pltpu.VMEM((items, HEADS, half_len), F32),
        logs_taken=pltpu.VMEM((items, HEADS, half_len), F32),
        v_w_o=pltpu.VMEM((4, 8, 32, width), LOW),
        work=pltpu.VMEM((half_len, width), F32),
        xhat=pltpu.VMEM((rows, width), F32),
        rstd=pltpu.VMEM((rows, 128), F32),
        v_w_in=pltpu.VMEM((4, 8, 32, blocks * width), LOW),
        slope=pltpu.VMEM((blocks, rows, width), LOW),
        v_w_out=pltpu.VMEM((4, 8, 128, width), LOW),
        cot=pltpu.VMEM((rows, width), LOW),
        back=pltpu.VMEM((rows, width), F32),
    )
    if by_hand:
        scratch["small"] = pltpu.VMEM(small_shape, F32)
    return call("forward" if by_hand else "", body, ins, spaces_in, outs, scratch, copies, collective_id)


def feed_back(by_hand, items, half_len, fw, weights, collective_id):
    blocks, rows, width = fw["act"].shape
    nz = lax.axis_size("dp") // 4
    chunk_width = width // len(OUT_SPLITS)
    step = 256

    def body(k):
        place, sender = k.place, k.sender
        load_low = k.copy(k["back_low"], k["v_low"])
        load_act = [k.copy(k["act"].at[t], k["v_act"].at[t]) for t in range(blocks)]
        load_out = k.copy(k["w_out"], k["v_w"])
        load_slope = k.copy(k["slope"], k["v_slope"])
        load_hidden = k.copy(k["hidden"], k["v_left"])
        load_rest = [
            k.copy(k["back"], k["v_back"]),
            k.copy(k["xhat"], k["v_xhat"]),
            k.copy(k["rstd"], k["v_rstd"]),
            k.copy(k["w_o"], k["v_o"]),
        ]
        meet(place)
        load_low.wait()
        low, act, grad = k["v_low"], k["v_act"], k["grad"]
        halves = []
        if by_hand:
            for q, split in enumerate(OUT_SPLITS):
                buffers = {name: k[f"{name}{q}"] for name in ("core", "diag", "line", "column")}
                target = k["grad_out"].at[:, pl.ds(q * chunk_width, chunk_width)]
                if split is None:
                    steps = reduce_late_steps(place, sender, grad.at[q], buffers, target)
                else:
                    steps = reduce_steps(place, sender, grad.at[q], buffers, target, split, nz)
                halves.append(k.add(steps))
        for t in range(blocks):
            load_act[t].wait()

            def outer(j, t=t):
                part = mm(act[t, :, tile(j, step)], low[...], TN).astype(LOW)
                part = part.reshape(2, 128, width)
                y, c = j // 2, j % 2
                for q in range(len(OUT_SPLITS)):
                    grad[q, t, y, c] = part[:, :, q * chunk_width : (q + 1) * chunk_width]

            loop(width // step, outer)
            for q, split in zip(halves, OUT_SPLITS):
                if split is not None or t == blocks - 1:
                    k.step(q)
        k.point()
        if not by_hand:
            for q in range(len(OUT_SPLITS)):
                k.save(grad.at[q], k["grad_out"].at[:, :, :, :, :, pl.ds(q * chunk_width, chunk_width)])
        load_out.wait()
        load_slope.wait()
        sums = k["sums"]
        sums[...] = jnp.zeros_like(sums)
        for t in range(blocks):

            def pull(j, t=t):
                at = tile(j, step)
                w_out = k["v_w"][t, j].reshape(step, width)
                part = mm(low[...], w_out, NT) * k["v_slope"][t, :, at].astype(F32)
                part = part.astype(LOW)
                act[t, :, at] = part
                sums[t : t + 1, at] = column_sum(part.astype(F32))

            loop(width // step, pull)
            k.point()
        load_in = [k.copy(k["w_in"].at[:, :, :, pl.ds(t * width, width)], k["v_w"].at[t]) for t in range(blocks)]
        load_hidden.wait()
        left, turned = k["v_left"], k["v_turned"]

        def turn(j):
            turned[tile(j, 128), :] = left[:, tile(j, 128)].T

        loop(width // 128, turn)
        save_in = []
        for t in range(blocks):
            if t >= 2:
                save_in[t - 2].wait()

            def outer_in(j, t=t):
                at = tile(j, step)
                part = mm(turned[...], act[t, :, at]).astype(LOW)
                k["grad_in_part"][t % 2, :, :, :, :, :, at] = part.reshape(4, 2, 2, 2, 32, step)

            loop(width // step, outer_in)
            save_in.append(k.copy(k["grad_in_part"].at[t % 2], k["grad_in"].at[t]))
            k.point()
        for made in load_in + load_rest + save_in[2:]:
            made.wait()
        gain = k["vectors"][4:5, :]
        partial_sums = k["partial_sums"]
        partial_sums[...] = jnp.zeros_like(partial_sums)
        for i in range(items):
            at_rows = pl.ds(i * half_len, half_len)
            total = None
            for t in range(blocks):
                part = mm(act[t, at_rows, :], k["v_w"][t].reshape(width, width), NT)
                total = part if total is None else total + part
            k["work"][...] = total
            k.point()

            def first_back(j, i=i):
                at = pl.ds(pl.multiple_of(i * half_len + j * NORM_ROWS, NORM_ROWS), NORM_ROWS)
                hidden = k["work"][tile(j, NORM_ROWS), :] + k["v_back"][at, :]
                xhat = k["v_xhat"][at, :]
                rstd = k["v_rstd"][at, 0:1]
                partial_sums[0] += row_sum(hidden * xhat)
                partial_sums[1] += row_sum(hidden)
                scaled = hidden * gain
                value = rstd * (
                    scaled
                    - jnp.mean(scaled, axis=-1, keepdims=True)
                    - xhat * jnp.mean(scaled * xhat, axis=-1, keepdims=True)
                )
                k["v_back"][at, :] = value
                value_low = value.astype(LOW)
                low[at, :] = value_low
                partial_sums[2] += row_sum(value_low.astype(F32))

            loop(half_len // NORM_ROWS, first_back)
            k.save(k["v_back"].at[at_rows], k["input_part"].at[at_rows])
            k.save(low.at[at_rows], k["attn_grad"].at[at_rows])
            k.point()
        for kind in range(3):
            sums[4 + kind : 5 + kind, :] = column_sum(partial_sums[kind])
        w_o = k["v_o"][...].reshape(width, width)
        for i in range(items):
            at_rows = pl.ds(i * half_len, half_len)
            k["v_mixed_grad"][at_rows, :] = mm(low[at_rows, :], w_o, NT).astype(LOW)
            k.save(k["v_mixed_grad"].at[at_rows], k["mixed_grad"].at[at_rows])
            k.point()
        k.close()

    ins = dict(
        back_low=fw["save_back_low"],
        act=fw["act"],
        w_out=weights[3].reshape(blocks, 4, 8, 32, width),
        slope=fw["save_slope"],
        w_in=weights[2],
        back=fw["save_back"],
        xhat=fw["save_xhat"],
        rstd=fw["save_rstd"],
        hidden=fw["save_hidden"],
        w_o=weights[1],
        vectors=fw["save_vectors"],
    )
    outs = dict(
        grad_in=((blocks, 4, 2, 2, 2, 32, width), LOW, "hbm"),
        input_part=((rows, width), F32, "hbm"),
        attn_grad=((rows, width), LOW, "hbm"),
        mixed_grad=((rows, width), LOW, "hbm"),
        sums=((8, width), F32, "vmem"),
    )
    if by_hand:
        outs["grad_out"] = ((128, width), F32, "vmem")
    else:
        outs["grad_out"] = ((4, 2, 2, 2, 128, width), LOW, "hbm")
    scratch = dict(
        v_low=pltpu.VMEM((rows, width), LOW),
        v_act=pltpu.VMEM((blocks, rows, width), LOW),
        v_left=pltpu.VMEM((rows, width), LOW),
        v_turned=pltpu.VMEM((width, rows), LOW),
        grad_in_part=pltpu.VMEM((2, 4, 2, 2, 2, 32, width), LOW),
        v_slope=pltpu.VMEM((blocks, rows, width), LOW),
        v_w=pltpu.VMEM((blocks, 4, 8, 32, width), LOW),
        v_back=pltpu.VMEM((rows, width), F32),
        v_xhat=pltpu.VMEM((rows, width), F32),
        v_rstd=pltpu.VMEM((rows, 128), F32),
        v_o=pltpu.VMEM((4, 8, 32, width), LOW),
        v_mixed_grad=pltpu.VMEM((rows, width), LOW),
        work=pltpu.VMEM((half_len, width), F32),
        grad=pltpu.VMEM((len(OUT_SPLITS), 4, 2, 2, 2, 128, chunk_width), LOW),
        partial_sums=pltpu.VMEM((3, 8, width), F32),
    )
    copies = 1
    if by_hand:
        copies += len(OUT_SPLITS) * max(reduce_copies(nz), reduce_late_copies(nz))
        for q, split in enumerate(OUT_SPLITS):
            buffers = reduce_late_buffers if split is None else reduce_buffers
            for name, buffer in buffers(nz, 128, chunk_width).items():
                scratch[f"{name}{q}"] = buffer
    return call("feed_back" if by_hand else "", body, ins, ("vectors",), outs, scratch, copies, collective_id)


def attend_back(by_hand, items, half_len, fw, fb, weights, collective_id):
    blocks, rows, width = fw["act"].shape
    nz = lax.axis_size("dp") // 4
    chunks = blocks + 2
    step = 256
    scale = 1.0 / math.sqrt(HD)
    stages = 3 + (nz - 1).bit_length()

    def body(k):
        place, sender = k.place, k.sender
        load_grad = k.copy(k["mixed_grad"], k["v_grad"].at[0])
        grad = k["grad"]
        load_in = [k.copy(k["grad_in_part"].at[q], grad.at[q]) for q in range(blocks) if by_hand]
        load_mixed = [k.copy(k["mixed"], k["v_left"]), k.copy(k["attn_grad"], k["joint"].at[0])]
        load_heads = k.copy(k["heads"], k["v_heads"])
        load_qkv = [
            k.copy(k["w_qkv"].at[:, :, :, pl.ds(t * width, width)], k["v_qkv"].at[t]) for t in range(3)
        ]
        load_grad.wait()
        meet(place)
        over_grad = []
        for i in range(items):
            at_rows = pl.ds(i * half_len, half_len)
            over_grad.append(k.add(exchange(k, k["v_grad"].at[0, at_rows], k["v_grad"].at[1, at_rows])))
            k.step(over_grad[i])
        going = []

        def reduce(slot, target, split):
            if by_hand:
                buffers = {name: k[f"{name}{slot}"] for name in ("core", "diag", "line", "column")}
                if split is None:
                    steps = reduce_late_steps(place, sender, grad.at[slot], buffers, target())
                else:
                    steps = reduce_steps(place, sender, grad.at[slot], buffers, target(), split, 1)
                going.append(k.add(steps))
                k.step(going[-1])
            k.point()

        for q in range(len(load_in)):
            load_in[q].wait()
            reduce(q, lambda q=q: k["grad_in"].at[:, pl.ds(q * width, width)], IN_SPLITS[q])
        left, turned, joint = k["v_left"], k["v_turned"], k["joint"]

        def turn(j):
            turned[tile(j, 128), :] = left[:, tile(j, 128)].T

        def outer(slot, right):
            def one(j):
                at = tile(j, step)
                part = mm(turned[...], right[:, at]).astype(LOW)
                grad[slot, :, :, :, :, :, at] = part.reshape(4, 2, 2, 2, 32, step)

            loop(width // step, one)

        for made in load_mixed:
            made.wait()
        loop(width // 128, turn)
        load_stream = k.copy(k["stream"], left)
        outer(blocks, joint.at[0])
        if not by_hand:
            k.save(grad.at[blocks], k["grad_o"])
        reduce(blocks, lambda: k["grad_o"], O_SPLIT)
        load_heads.wait()
        same = lax.broadcasted_iota(jnp.int32, (half_len, half_len), 0) == lax.broadcasted_iota(
            jnp.int32, (half_len, half_len), 1
        )
        for i in range(items):
            asked = k["codes"][items + i : items + i + 1, :]
            asked_taken = k["codes_taken"][items + i : items + i + 1, :]
            code = k["cols"][:, 2 * items + i : 2 * items + i + 1]
            code_taken = k["cols_taken"][:, 2 * items + i : 2 * items + i + 1]
            k["permit"][i, 0:half_len, :] = jnp.where((code <= asked) | same, 0.0, fill_value)
            k["permit"][i, half_len : 2 * half_len, :] = jnp.where(code_taken <= asked, 0.0, fill_value)
            k["permit_taken"][i] = jnp.where(code <= asked_taken, 0.0, fill_value)
        k.point()
        heads, grads, result = k["v_heads"], k["v_grad"], joint
        lane = lax.broadcasted_iota(jnp.int32, (half_len, 2 * HD), 1)
        key_lane = lax.broadcasted_iota(jnp.int32, (2 * half_len, 2 * HD), 1)
        nothing = jnp.zeros((), LOW)
        pairs = width // (2 * HD)

        def ours(i):
            at_rows = pl.ds(i * half_len, half_len)

            def pair(p):
                at = tile(p, 2 * HD)
                query = heads[0, at_rows, at]
                keys = jnp.concatenate([heads[1, at_rows, at], heads[2, at_rows, at]], axis=0)
                values = jnp.concatenate([heads[3, at_rows, at], heads[4, at_rows, at]], axis=0)
                grad_row = grads[0, at_rows, at]
                query_part = key_part = value_part = None
                for h in range(2):
                    mine = (lane < HD) == (h == 0)
                    key_mine = (key_lane < HD) == (h == 0)
                    query_h = jnp.where(mine, query, nothing)
                    grad_h = jnp.where(mine, grad_row, nothing)
                    keys_h = jnp.where(key_mine, keys, nothing)
                    at_head = pl.ds(2 * p + h, 1)
                    scores = mm(keys, query_h * scale, NT) + (k["permit"][i] - k["logs"][i, at_head, :])
                    probs = jnp.exp(scores)
                    prob_grad = mm(values, grad_h, NT)
                    centre = column_sum(probs * prob_grad)
                    k["centre"][i, at_head, :] = centre
                    score_grad = (probs * (prob_grad - centre)).astype(LOW)
                    parts = (
                        mm(score_grad, keys_h, TN),
                        mm(score_grad[:half_len], query_h),
                        mm(probs[:half_len].astype(LOW), grad_h),
                    )
                    if h == 0:
                        query_part, key_part, value_part = parts
                    else:
                        query_part = query_part + parts[0]
                        key_part = key_part + parts[1]
                        value_part = value_part + parts[2]
                query_low = (query_part * scale).astype(LOW)
                result[0, at_rows, at] = query_low
                k["sums"][0:1, at] += column_sum(query_low.astype(F32))
                k["parts"][0, at_rows, at] = key_part
                k["parts"][1, at_rows, at] = value_part

            loop(pairs // 2, pair)
            k.point()
            loop(pairs // 2, lambda p: pair(p + pairs // 2))

        def theirs(i):
            at_rows = pl.ds(i * half_len, half_len)

            def pair(p):
                at = tile(p, 2 * HD)
                query = heads[5, at_rows, at]
                keys, values = heads[1, at_rows, at], heads[3, at_rows, at]
                grad_row = grads[1, at_rows, at]
                key_part, value_part = k["parts"][0, at_rows, at], k["parts"][1, at_rows, at]
                for h in range(2):
                    mine = (lane < HD) == (h == 0)
                    query_h = jnp.where(mine, query, nothing)
                    grad_h = jnp.where(mine, grad_row, nothing)
                    at_head = pl.ds(2 * p + h, 1)
                    scores = mm(keys, query_h * scale, NT) + (
                        k["permit_taken"][i] - k["logs_taken"][i, at_head, :]
                    )
                    probs = jnp.exp(scores)
                    prob_grad = mm(values, grad_h, NT)
                    score_grad = (probs * (prob_grad - k["centre_taken"][i, at_head, :])).astype(LOW)
                    key_part = key_part + mm(score_grad, query_h)
                    value_part = value_part + mm(probs.astype(LOW), grad_h)
                result[1, at_rows, at] = (key_part * scale).astype(LOW)
                value_low = value_part.astype(LOW)
                result[2, at_rows, at] = value_low
                k["sums"][1:2, at] += column_sum(value_low.astype(F32))

            loop(pairs // 2, pair)
            k.point()
            loop(pairs // 2, lambda p: pair(p + pairs // 2))

        k["sums"][...] = jnp.zeros_like(k["sums"])
        over = []
        for i in range(items):
            ours(i)
            over.append(k.add(exchange(k, k["centre"].at[i], k["centre_taken"].at[i])))
            k.step(over[i])
            k.point()
        load_stream.wait()
        loop(width // 128, turn)

        def outer_joint(q, slot):
            outer(slot, joint.at[q])
            if not by_hand:
                k.save(grad.at[slot], k["grad_qkv"].at[:, :, :, :, :, pl.ds(q * width, width)])
            reduce(slot, lambda: k["grad_qkv"].at[:, pl.ds(q * width, width)], QKV_SPLITS[q])

        outer_joint(0, blocks + 1)
        for i in range(items):
            k.finish(over[i], over_grad[i])
            theirs(i)
            k.point()
        levels = k["levels"]
        for s, name in enumerate(("sums_one", "sums_two")):
            levels[0, 8 * s : 8 * s + 8, :] = k[name][...]
        levels[0, 16:24, :] = k["sums"][...]
        small = k.add(sum_steps(place, sender, levels, k["levels_taken"]))
        k.step(small)
        k.finish(*going[:2])
        partners = place.partners()
        for partner in partners:
            pl.semaphore_signal(k["through"], inc=1, device_id=partner, device_id_type=MESH)
        load_part = k.copy(k["input_part"], k["parts"].at[0])
        pl.semaphore_wait(k["through"], len(partners))
        outer_joint(1, 0)
        outer_joint(2, 1)
        for made in load_qkv + [load_part]:
            made.wait()
        for i in range(items):
            at_rows = pl.ds(i * half_len, half_len)
            total = k["parts"][0, at_rows, :]
            for q in range(3):
                total = total + mm(joint[q, at_rows, :], k["v_qkv"][q].reshape(width, width), NT)
            left[at_rows, :] = total.astype(LOW)
            k.save(left.at[at_rows], k["input_grad"].at[at_rows])
            k.point()
        k.finish(*range(len(k.transfers)))
        k["totals"][...] = levels[stages]
        k.close()

    ins = dict(
        grad_in_part=fb["grad_in"],
        mixed=fw["save_mixed"],
        attn_grad=fb["attn_grad"],
        heads=fw["save_heads"],
        mixed_grad=fb["mixed_grad"],
        stream=fw["save_stream"],
        w_qkv=weights[0],
        input_part=fb["input_part"],
        codes=fw["save_own_codes"],
        codes_taken=fw["save_codes"],
        cols=fw["save_own_cols"],
        cols_taken=fw["save_cols"],
        logs=fw["save_logs"],
        logs_taken=fw["save_logs_taken"],
        sums_one=fw["sums"],
        sums_two=fb["sums"],
    )
    outs = dict(
        input_grad=((rows, width), LOW, "hbm"),
        totals=((24, width), F32, "vmem"),
    )
    if by_hand:
        outs["grad_in"] = ((32, blocks * width), F32, "vmem")
        outs["grad_o"] = ((32, width), F32, "vmem")
        outs["grad_qkv"] = ((32, 3 * width), F32, "vmem")
    else:
        outs["grad_o"] = ((4, 2, 2, 2, 32, width), LOW, "hbm")
        outs["grad_qkv"] = ((4, 2, 2, 2, 32, 3 * width), LOW, "hbm")
    scratch = dict(
        v_left=pltpu.VMEM((rows, width), LOW),
        v_turned=pltpu.VMEM((width, rows), LOW),
        joint=pltpu.VMEM((3, rows, width), LOW),
        v_heads=pltpu.VMEM((6, rows, width), LOW),
        v_grad=pltpu.VMEM((2, rows, width), LOW),
        v_qkv=pltpu.VMEM((3, 4, 8, 32, width), LOW),
        grad=pltpu.VMEM((chunks, 4, 2, 2, 2, 32, width), LOW),
        permit=pltpu.VMEM((items, 2 * half_len, half_len), F32),
        permit_taken=pltpu.VMEM((items, half_len, half_len), F32),
        parts=pltpu.VMEM((2, rows, width), F32),
        centre=pltpu.VMEM((items, HEADS, half_len), F32),
        centre_taken=pltpu.VMEM((items, HEADS, half_len), F32),
        sums=pltpu.VMEM((8, width), F32),
        levels=pltpu.VMEM((stages + 1, 24, width), F32),
        levels_taken=pltpu.VMEM((stages, 24, width), F32),
        through=pltpu.SemaphoreType.REGULAR,
    )
    copies = 2 * items + stages
    if by_hand:
        copies += (blocks + 4) * max(reduce_copies(nz), reduce_late_copies(nz))
        for q, split in enumerate(IN_SPLITS + (O_SPLIT, QKV_SPLITS[0])):
            buffers = reduce_late_buffers if split is None else reduce_buffers
            for name, buffer in buffers(nz, 32, width).items():
                scratch[f"{name}{q}"] = buffer
    spaces = ("codes", "codes_taken", "cols", "cols_taken", "logs", "logs_taken", "sums_one", "sums_two")
    return call("attend_back" if by_hand else "", body, ins, spaces, outs, scratch, copies, collective_id)


def hand_over(arrays, totals, items):
    width = totals.shape[1]
    count = len(arrays)

    def kernel(*refs):
        sources, total = refs[:count], refs[count]
        targets, b_in, rest, rms = refs[count + 1 : 2 * count + 1], *refs[2 * count + 1 : 2 * count + 4]
        held, in_sem, out_sem = refs[2 * count + 4 : 3 * count + 4], refs[3 * count + 4], refs[3 * count + 5]
        loads = [pltpu.make_async_copy(s, h, in_sem.at[i]) for i, (s, h) in enumerate(zip(sources, held))]
        stores = [pltpu.make_async_copy(h, t, out_sem.at[i]) for i, (h, t) in enumerate(zip(held, targets))]
        for load in loads:
            load.start()
        me = my_index()
        group = pl.ds(pl.multiple_of((me % 8) * 128, 128), 128)
        for t in range(4):
            row = total[8 + t : 9 + t, group]
            b_in[...] = row if t == 0 else jnp.where(me // 8 == t, row, b_in[...])
        group = pl.ds(pl.multiple_of((me // 4) * 128, 128), 128)
        for to, row in enumerate((16, 17, 14, 4, 12, 5, 13, 6)):
            wide = total[row : row + 1, group]
            value = wide[:, :32]
            for q in range(1, 4):
                value = jnp.where(me % 4 == q, wide[:, 32 * q : 32 * q + 32], value)
            rest[to : to + 1, :] = value
        tokens = jnp.sum(total[7:8, items : 2 * items], axis=1, keepdims=True)
        means = jnp.sum(total[0:4, :], axis=1, keepdims=True) / (tokens * width)
        rms[...] = jnp.broadcast_to(jnp.sqrt(means), rms.shape)
        for load, store in zip(loads, stores):
            load.wait()
            store.start()
        for store in stores:
            store.wait()

    vmem, hbm = pl.BlockSpec(memory_space=pltpu.VMEM), pl.BlockSpec(memory_space=pl.ANY)
    shape = jax.ShapeDtypeStruct
    return pl.pallas_call(
        kernel,
        out_shape=[shape(a.shape, a.dtype) for a in arrays]
        + [shape((1, 128), F32), shape((8, 32), F32), shape((4, 128), F32)],
        in_specs=[hbm] * count + [vmem],
        out_specs=[hbm] * count + [vmem] * 3,
        scratch_shapes=[pltpu.VMEM(a.shape, a.dtype) for a in arrays]
        + [pltpu.SemaphoreType.DMA((count,)), pltpu.SemaphoreType.DMA((count,))],
        compiler_params=pltpu.CompilerParams(vmem_limit_bytes=62 << 20),
    )(*arrays, totals)


def body(
    block_input,
    lengths,
    mask,
    blocks,
    timesteps,
    w_qkv,
    w_o,
    w_in,
    w_out,
    b_in,
    biases,
    gains,
    shifts,
    cotangent,
):
    items, half_len, width = block_input.shape
    rows = items * half_len
    f32 = jnp.float32
    n = n_devices()
    share = width // n
    b_count = b_in.shape[0]
    embed = time_embed(timesteps, width)
    by_hand = w_qkv.shape[0] == 32
    weights = [w_qkv, w_o, w_in, w_out]
    small = [b_in, biases, gains, shifts]
    if not by_hand:
        weights = [lax.all_gather(w, AXES, axis=0, tiled=True) for w in weights]
        weights = [w.reshape(4, 8, w.shape[0] // 32, w.shape[1]) for w in weights]
        small = jnp.concatenate([piece.reshape(-1) for piece in small])
        small_wide = -(-small.shape[0] // 128) * 128
        small = jnp.pad(small.astype(f32), (0, small_wide - small.shape[0]))
        small = jnp.broadcast_to(small[None, :], (8, small_wide))
        small = lax.all_gather(small, AXES, axis=0).reshape(n // 8, 8, 8, small_wide)
    fw = forward(
        by_hand,
        items,
        half_len,
        weights,
        small,
        block_input.reshape(rows, width),
        embed,
        (lengths, mask, blocks),
        cotangent.reshape(rows, width),
        1,
    )
    if by_hand:
        weights = [fw["all_" + p] for p in ("w_qkv", "w_o", "w_in", "w_out")]
    fb = feed_back(by_hand, items, half_len, fw, weights, 2)
    ab = attend_back(by_hand, items, half_len, fw, fb, weights, 3)
    if by_hand:
        grads = [ab["grad_qkv"], ab["grad_o"], ab["grad_in"], fb["grad_out"]]
        *arrays, own_b_in, own, rms = hand_over([fw["output"], ab["input_grad"]] + grads, ab["totals"], items)
        return (
            arrays[0].reshape(block_input.shape),
            arrays[1].reshape(block_input.shape),
            *arrays[2:],
            own_b_in.reshape(-1),
            own[:4],
            own[4:6],
            own[6:8],
            rms[:, 0],
        )
    grad_in = fb["grad_in"].reshape(4, width, width).transpose(1, 0, 2)
    grads = [
            lax.psum_scatter(
                part.astype(f32).reshape(rows_of, -1), AXES, scatter_dimension=0, tiled=True
            )
            for part, rows_of in (
                (ab["grad_qkv"], width),
                (ab["grad_o"], width),
                (grad_in, width),
                (fb["grad_out"], 4 * width),
            )
        ]
    totals = ab["totals"]
    me = my_index()
    grad_b_in = lax.dynamic_slice(totals[8:12].reshape(-1), (me * b_count,), (b_count,))
    order = (16, 17, 14, 4, 12, 5, 13, 6)
    mine = lax.dynamic_slice(totals, (0, me * share), (24, share))
    mine = jnp.stack([mine[row] for row in order])
    count = jnp.sum(totals[7, items : 2 * items])
    rms = jnp.sqrt(jnp.sum(totals[:4], axis=1) / (count * width))
    return (
        fw["output"].reshape(block_input.shape),
        ab["input_grad"].reshape(block_input.shape),
        *grads,
        grad_b_in,
        mine[:4],
        mine[4:6],
        mine[6:8],
        rms,
    )


def solution(mesh):
    in_specs = (
        P("dp", "ctx", None),
        P("dp"),
        P("dp", "ctx"),
        P("dp", "ctx"),
        P("dp"),
        P(("dp", "ctx"), None),
        P(("dp", "ctx"), None),
        P(("dp", "ctx"), None),
        P(("dp", "ctx"), None),
        P(("dp", "ctx")),
        P(None, ("dp", "ctx")),
        P(None, ("dp", "ctx")),
        P(None, ("dp", "ctx")),
        P("dp", "ctx", None),
    )
    out_specs = (
        P("dp", "ctx", None),
        P("dp", "ctx", None),
        P(("dp", "ctx"), None),
        P(("dp", "ctx"), None),
        P(("dp", "ctx"), None),
        P(("dp", "ctx"), None),
        P(("dp", "ctx")),
        P(None, ("dp", "ctx")),
        P(None, ("dp", "ctx")),
        P(None, ("dp", "ctx")),
        P(),
    )
    return jax.shard_map(body, mesh=mesh, in_specs=in_specs, out_specs=out_specs, check_vma=False)
```

```python
from functools import partial
import math

import jax
import jax.numpy as jnp
from jax import lax
from jax.experimental import pallas as pl
from jax.experimental.pallas import tpu as pltpu
from jax.sharding import PartitionSpec as P

HEADS = 16
HD = 64

AXES = ("dp", "ctx")
X = 1


def my_index():
    return lax.axis_index("dp") * lax.axis_size("ctx") + lax.axis_index("ctx")


def n_devices():
    return lax.axis_size("dp") * lax.axis_size("ctx")


fill_value = -1e30
eps_norm = 1e-05
code_absent = 30000.0


def time_embed(steps, width):
    half = width // 2
    freqs = jnp.exp(jnp.arange(half, dtype=jnp.float32) * (-math.log(10000.0) / half))
    angle = steps.astype(jnp.float32)[:, None] * freqs[None, :]
    return jnp.concatenate([jnp.sin(angle), jnp.cos(angle)], axis=-1)


MESH = pl.DeviceIdType.MESH


class Place:
    def __init__(self):
        dp = lax.axis_index("dp")
        self.nz = lax.axis_size("dp") // 4
        self.x = lax.axis_index("ctx")
        self.c = dp % 2
        self.y = (dp // 2) % 2
        self.z = dp // 4

    def zth(self, k):
        z, bit = self.z, 1
        while bit < self.nz:
            if k & bit:
                z = z + bit * (1 - 2 * ((self.z // bit) % 2))
            bit *= 2
        return z

    def flips(self, y=0, c=0, x=0):
        return (
            1 - self.y if y else self.y,
            1 - self.c if c else self.c,
            1 - self.x if x else self.x,
        )

    def device(self, k=0, y=0, c=0, x=0):
        fy, fc, fx = self.flips(y, c, x)
        return ((self.zth(k) * 2 + fy) * 2 + fc, fx)

    def shard(self, k=0, y=0, c=0, x=0):
        fy, fc, fx = self.flips(y, c, x)
        return ((self.zth(k) * 2 + fy) * 2 + fc) * 2 + fx

    def column(self, y=0, c=0, x=0):
        fy, fc, fx = self.flips(y, c, x)
        return (fy * 2 + fc) * 2 + fx

    def partners(self):
        return [self.device(k=k) for k in range(1, self.nz)] + [
            self.device(x=1),
            self.device(y=1),
            self.device(c=1),
        ]


def meet(place):
    barrier = pltpu.get_barrier_semaphore()
    partners = place.partners()
    for partner in partners:
        pl.semaphore_signal(barrier, inc=1, device_id=partner, device_id_type=MESH)
    pl.semaphore_wait(barrier, len(partners))


class Sender:
    def __init__(self, send_sem, recv_sem):
        self.send_sem, self.recv_sem = send_sem, recv_sem
        self.count = 0
        self.open = []

    def send(self, src, dst, device, keep=None):
        copy = pltpu.make_async_remote_copy(
            src_ref=src,
            dst_ref=dst,
            send_sem=self.send_sem.at[self.count],
            recv_sem=self.recv_sem.at[self.count],
            device_id=device,
            device_id_type=MESH,
        )
        self.count += 1
        copy.start()
        (self.open if keep is None else keep).append(copy)
        return copy

    def close(self):
        for copy in self.open:
            copy.wait_send()
        self.open = []


def gather_copies(nz):
    return 4 * nz + 5


def gather_steps(place, sender, shard, full, split):
    nz = place.nz
    mine, at_x, at_y, diag = (place.column(x=fx, y=fy) for fy, fx in ((0, 0), (0, 1), (1, 0), (1, 1)))
    own = full.at[place.z, mine]
    by_z = [sender.send(shard, own, place.device(k=k)) for k in range(1, nz)]
    yield
    from_x = [sender.send(shard, own, place.device(x=1))]
    from_y = [sender.send(shard, own, place.device(y=1))]
    yield
    for k in range(1, nz):
        by_z[k - 1].wait_recv()
        piece = full.at[place.zth(k), mine]
        from_x.append(sender.send(piece, piece, place.device(x=1)))
        from_y.append(sender.send(piece, piece, place.device(y=1)))
        yield
    to_core = [sender.send(full.at[:, mine], full.at[:, mine], place.device(c=1))]
    from_diag = []
    yield
    for k in range(nz):
        from_x[k].wait_recv()
        if k < split:
            piece = full.at[place.zth(k), at_x]
            from_diag.append(sender.send(piece, piece, place.device(y=1)))
        else:
            from_y[k].wait_recv()
            piece = full.at[place.zth(k), at_y]
            from_diag.append(sender.send(piece, piece, place.device(x=1)))
        yield
    to_core.append(sender.send(full.at[:, at_x], full.at[:, at_x], place.device(c=1)))
    for k in range(split):
        from_y[k].wait_recv()
    to_core.append(sender.send(full.at[:, at_y], full.at[:, at_y], place.device(c=1)))
    yield
    half = nz // 2
    for start, size in ((0, half), (half, nz - half)):
        for copy in from_diag if start == 0 else ():
            copy.wait_recv()
        part = full.at[pl.ds(start, size), diag]
        to_core.append(sender.send(part, part, place.device(c=1)))
    yield
    for copy in to_core:
        copy.wait_recv()


def gather_late_steps(place, sender, shard, full):
    nz = place.nz
    own = full.at[place.z, place.column()]
    from_x = sender.send(shard, own, place.device(x=1))
    from_y = sender.send(shard, own, place.device(y=1))
    yield
    from_x.wait_recv()
    piece = full.at[place.z, place.column(x=1)]
    from_diag = sender.send(piece, piece, place.device(y=1))
    yield
    from_y.wait_recv()
    from_diag.wait_recv()
    by_z = []
    for k in range(1, nz):
        for fy in range(2):
            for fx in range(2):
                piece = full.at[place.z, place.column(y=fy, x=fx)]
                by_z.append(sender.send(piece, piece, place.device(k=k)))
    yield
    for copy in by_z:
        copy.wait_recv()
    to_core = []
    for fy in range(2):
        for fx in range(2):
            piece = full.at[:, place.column(y=fy, x=fx)]
            to_core.append(sender.send(piece, piece, place.device(c=1)))
    yield
    for copy in to_core:
        copy.wait_recv()


NN = (((1,), (0,)), ((), ()))
NT = (((1,), (1,)), ((), ()))
TN = (((0,), (0,)), ((), ()))
LOW = jnp.bfloat16
F32 = jnp.float32


def mm(left, right, dims=NN):
    return lax.dot_general(left, right, dims, preferred_element_type=F32)


def loop(count, step, unroll=1):
    lax.fori_loop(0, count, lambda i, _: (step(i), 0)[1], 0, unroll=min(unroll, count))


def tile(index, size):
    return pl.ds(pl.multiple_of(index * size, size), size)


def expand(packed, offset, share, start, length):
    n, wide = packed.shape
    place = lax.broadcasted_iota(jnp.int32, (wide, length), 1) + start
    lane = lax.broadcasted_iota(jnp.int32, (wide, length), 0)
    pick = (lane == offset + lax.rem(place, share)).astype(F32).astype(LOW)
    spread = mm(packed, pick)
    row = lax.broadcasted_iota(jnp.int32, (n, length), 0)
    column = lax.broadcasted_iota(jnp.int32, (n, length), 1) + start
    return jnp.sum(jnp.where(row == lax.div(column, share), spread, 0.0), axis=0, keepdims=True)


def normalize(resid):
    centre = resid - jnp.mean(resid, axis=-1, keepdims=True)
    spread = jnp.mean(centre * centre, axis=-1, keepdims=True)
    rstd = lax.rsqrt(spread + eps_norm)
    return centre * rstd, rstd


def column_sum(value):
    return jnp.sum(value, axis=0, keepdims=True)


def reduce_copies(nz):
    return nz + 6 + nz - 1


def reduce_buffers(nz, rows, cols):
    return dict(
        core=pltpu.VMEM((nz, 2, 2, rows, cols), LOW),
        diag=pltpu.VMEM((nz, rows, cols), LOW),
        line=pltpu.VMEM((2, nz, rows, cols), LOW),
        column=pltpu.VMEM((nz - 1, rows, cols), LOW),
    )


def add_rows(store, terms, count, rows, cols):
    step = min(rows, 16 * max(1, 1024 // cols))
    per = rows // step

    def one(j):
        i, start = j // per, (j % per) * step
        at = pl.ds(pl.multiple_of(start, step), step)
        total = terms[0](i, at).astype(F32)
        for term in terms[1:]:
            total = total + term(i, at).astype(F32)
        store(i, at, total)

    loop(count * per, one, 2)


def reduce_steps(place, sender, grad, buffers, out, split, parts):
    nz = place.nz
    rows, cols = grad.shape[4:]
    core, diag, line, column = (buffers[k] for k in ("core", "diag", "line", "column"))
    groups = ((1, 1), (0, 1), (1, 0), (0, 0))
    here = [place.flips(y=fy, x=fx) for fy, fx in groups]
    sent, by_core = [], []
    size = nz // parts
    for t in range(parts):
        if t:
            yield
        at = pl.ds(t * size, size)
        by_core.append(sender.send(grad.at[at, :, 1 - place.c], core.at[at], place.device(c=1), sent))
    yield

    def put(slot, start=0):
        fy, fc, fx = here[slot]

        def store(i, at, value):
            grad[i + start, fy, fc, fx, at, :] = value.astype(LOW)

        return store

    def held(slot, start=0):
        fy, fc, fx = here[slot]
        return lambda i, at: grad[i + start, fy, fc, fx, at, :]

    def add_core(slot):
        fy, _, fx = here[slot]
        add_rows(put(slot), [held(slot), lambda i, at: core[i, fy, fx, at, :]], nz, rows, cols)

    def part(slot, start, count):
        fy, fc, fx = here[slot]
        return grad.at[pl.ds(start, count), fy, fc, fx]

    low, high = pl.ds(0, split), pl.ds(split, nz - split)
    by_y = by_x = x_high = y_low = x_low = y_high = None
    for copy in by_core:
        copy.wait_recv()
    add_core(0)
    if split > 0:
        by_y = sender.send(part(0, 0, split), diag.at[low], place.device(y=1), sent)
    if split < nz:
        by_x = sender.send(part(0, split, nz - split), diag.at[high], place.device(x=1), sent)
    yield
    add_core(1)
    if split < nz:
        x_high = sender.send(part(1, split, nz - split), line.at[0, high], place.device(x=1), sent)
    add_core(2)
    if split > 0:
        y_low = sender.send(part(2, 0, split), line.at[1, low], place.device(y=1), sent)
    yield
    add_core(3)
    yield
    if split > 0:
        by_y.wait_recv()
        add_rows(put(1), [held(1), lambda i, at: diag[i, at, :]], split, rows, cols)
        x_low = sender.send(part(1, 0, split), line.at[0, low], place.device(x=1), sent)
    yield
    if split < nz:
        by_x.wait_recv()
        add_rows(put(2, split), [held(2, split), lambda i, at: diag[i + split, at, :]], nz - split, rows, cols)
        y_high = sender.send(part(2, split, nz - split), line.at[1, high], place.device(y=1), sent)
    yield
    for copy in (x_high, y_low, x_low, y_high):
        if copy is not None:
            copy.wait_recv()
    add_rows(
        put(3),
        [held(3), lambda i, at: line[0, i, at, :], lambda i, at: line[1, i, at, :]],
        nz,
        rows,
        cols,
    )
    fy, fc, fx = here[3]
    by_z = [
        sender.send(grad.at[place.zth(k), fy, fc, fx], column.at[k - 1], place.device(k=k), sent)
        for k in range(1, nz)
    ]
    yield
    for copy in by_z:
        copy.wait_recv()

    def last(i, at, value):
        out[at, :] = value

    add_rows(
        last,
        [lambda i, at: grad[place.z, fy, fc, fx, at, :]]
        + [lambda i, at, k=k: column[k, at, :] for k in range(nz - 1)],
        1,
        rows,
        cols,
    )
    for copy in sent:
        copy.wait_send()


def reduce_late_copies(nz):
    return 1 + nz - 1 + 3


def reduce_late_buffers(nz, rows, cols):
    return dict(
        core=pltpu.VMEM((nz, 2, 2, rows, cols), LOW),
        diag=pltpu.VMEM((1, rows, cols), LOW),
        line=pltpu.VMEM((2, 1, rows, cols), LOW),
        column=pltpu.VMEM((nz - 1, 2, 2, rows, cols), LOW),
    )


def reduce_late_steps(place, sender, grad, buffers, out):
    nz = place.nz
    rows, cols = grad.shape[4:]
    core, diag, line, column = (buffers[k] for k in ("core", "diag", "line", "column"))
    sent = []
    by_core = sender.send(grad.at[:, :, 1 - place.c], core, place.device(c=1), sent)
    yield
    by_core.wait_recv()
    for fy in range(2):
        for fx in range(2):

            def put(i, at, value, fy=fy, fx=fx):
                grad[i, fy, place.c, fx, at, :] = value.astype(LOW)

            add_rows(
                put,
                [
                    lambda i, at, fy=fy, fx=fx: grad[i, fy, place.c, fx, at, :],
                    lambda i, at, fy=fy, fx=fx: core[i, fy, fx, at, :],
                ],
                nz,
                rows,
                cols,
            )
    by_z = [
        sender.send(grad.at[place.zth(k), :, place.c], column.at[k - 1], place.device(k=k), sent)
        for k in range(1, nz)
    ]
    yield
    for copy in by_z:
        copy.wait_recv()

    def add(fy, fx, terms):
        ty, tc, tx = place.flips(y=fy, x=fx)

        def put(i, at, value):
            grad[place.z, ty, tc, tx, at, :] = value.astype(LOW)

        add_rows(put, [lambda i, at: grad[place.z, ty, tc, tx, at, :]] + terms(ty, tx), 1, rows, cols)
        return grad.at[place.z, ty, tc, tx]

    def columns(ty, tx):
        return [lambda i, at, k=k: column[k, ty, tx, at, :] for k in range(nz - 1)]

    part = add(1, 1, columns)
    by_y = sender.send(part, diag.at[0], place.device(y=1), sent)
    part = add(1, 0, columns)
    y_line = sender.send(part, line.at[1, 0], place.device(y=1), sent)
    add(0, 1, columns)
    add(0, 0, columns)
    yield
    by_y.wait_recv()
    part = add(0, 1, lambda ty, tx: [lambda i, at: diag[0, at, :]])
    x_line = sender.send(part, line.at[0, 0], place.device(x=1), sent)
    yield
    x_line.wait_recv()
    y_line.wait_recv()
    ty, tc, tx = place.flips()

    def last(i, at, value):
        out[at, :] = value

    add_rows(
        last,
        [
            lambda i, at: grad[place.z, ty, tc, tx, at, :],
            lambda i, at: line[0, 0, at, :],
            lambda i, at: line[1, 0, at, :],
        ],
        1,
        rows,
        cols,
    )
    for copy in sent:
        copy.wait_send()


def sum_steps(place, sender, levels, taken):
    partners = [place.device(c=1), place.device(x=1), place.device(y=1)]
    bit = 1
    while bit < place.nz:
        partners.append(place.device(k=bit))
        bit *= 2
    for s, partner in enumerate(partners):
        copy = sender.send(levels.at[s], taken.at[s], partner)
        yield
        copy.wait_recv()
        levels[s + 1] = levels[s] + taken[s]


class Kernel:
    def __init__(self, name, names, refs):
        self.refs = dict(zip(names, refs))
        self.place = Place()
        self.sender = Sender(self["send"], self["recv"])
        self.plan = PLANS.get(name, ())
        self.count = self.points = 0
        self.saved, self.transfers = [], []

    def __getitem__(self, name):
        return self.refs[name]

    def copy(self, src, dst):
        made = pltpu.make_async_copy(src, dst, self["local"].at[self.count])
        self.count += 1
        made.start()
        return made

    def save(self, src, dst):
        made = self.copy(src, dst)
        self.saved.append(made)
        return made

    def add(self, steps):
        self.transfers.append(steps)
        return len(self.transfers) - 1

    def step(self, number):
        return next(self.transfers[number], self) is not self

    def point(self):
        turn = self.plan[self.points] if self.points < len(self.plan) else ()
        self.points += 1
        for number in turn:
            self.step(number)

    def finish(self, *numbers):
        for number in numbers:
            while self.step(number):
                pass

    def close(self):
        self.finish(*range(len(self.transfers)))
        for made in self.saved:
            made.wait()
        self.sender.close()


PARTS = (
    ("w_qkv", None, None, False),
    ("small", None, None, False),
    ("w_o", None, None, True),
    ("w_in", 0, 2048, False),
    ("w_in", 2048, 3072, False),
    ("w_in", 3072, 4096, True),
    ("w_out", 0, 512, False),
    ("w_out", 512, 1024, False),
)
OUT_SPLITS = (3, 3, 3, 3, 3, 3, 3, None)
IN_SPLITS = (4, 4, 4, 4)
O_SPLIT = None
QKV_SPLITS = (2, 2, 2)
EARLY = 1
PLANS = {
    "forward": (
        (2, 5, 1, 0, 0, 3, 2, 14, 3, 4, 6),
        (2, 0, 5, 0),
        (0, 8, 3),
        (4, 0, 3),
        (0, 0, 4, 11, 6, 0, 0),
        (10, 14, 13, 0),
        (8, 3, 4, 12),
        (4, 11, 15),
        (3, 4, 7, 3),
        (8, 11, 0, 7),
        (6, 7),
        (8,),
        (3, 2),
        (4, 5),
        (4, 3, 6),
        (2,),
        (3,),
        (4, 3),
        (4, 2, 6),
        (),
        (7, 6),
        (6, 7),
        (7, 6),
        (7,),
        (4,),
        (3, 6),
        (7, 4),
        (6,),
        (5, 6),
        (7,),
        (7, 17),
        (9, 6),
        (7, 16),
        (18, 7),
        (),
        (17, 9, 17),
    ),
    "feed_back": (
        (0, 1, 3, 1, 2, 1, 6),
        (0, 3, 3, 0, 0),
        (0, 1, 5),
        (1, 3, 7, 3, 6),
        (2, 2, 6, 2, 2, 4),
        (6,),
        (6,),
        (0, 5),
        (5, 1, 5),
        (3, 5, 4),
        (2, 0, 4),
        (4, 6, 4),
        (7, 5),
        (3, 4, 7),
        (7, 1, 8, 6, 5),
    ),
    "attend_back": (
        (),
        (),
        (),
        (2,),
        (3, 3, 2, 4, 2),
        (),
        (5, 3, 0, 6, 2),
        (),
        (3, 3),
        (0,),
        (),
        (4, 5),
        (2, 2, 4, 4),
        (),
        (5, 3, 1, 5),
        (10, 10),
        (5,),
        (4,),
        (4,),
        (11, 10, 5, 10, 10),
        (11, 12, 12, 12, 4),
        (11, 10, 4),
        (13, 12, 5, 12),
        (13, 11, 13, 13, 13, 12, 6, 13),
    ),
}


def call(name, body, ins, spaces_in, outs, scratch, copies, collective_id):
    vmem, hbm = pl.BlockSpec(memory_space=pltpu.VMEM), pl.BlockSpec(memory_space=pl.ANY)
    scratch = dict(
        send=pltpu.SemaphoreType.DMA((copies,)),
        recv=pltpu.SemaphoreType.DMA((copies,)),
        local=pltpu.SemaphoreType.DMA((64,)),
        **scratch,
    )
    names = list(ins) + list(outs) + list(scratch)

    def kernel(*refs):
        body(Kernel(name, names, refs))

    results = pl.pallas_call(
        kernel,
        out_shape=[jax.ShapeDtypeStruct(s, d) for s, d, _ in outs.values()],
        in_specs=[
            pl.BlockSpec(memory_space=pltpu.SMEM) if given == "lengths" else vmem if given in spaces_in else hbm
            for given in ins
        ],
        out_specs=[vmem if space == "vmem" else hbm for _, _, space in outs.values()],
        scratch_shapes=list(scratch.values()),
        compiler_params=pltpu.CompilerParams(
            collective_id=collective_id, has_side_effects=True, vmem_limit_bytes=63 << 20
        ),
    )(*ins.values())
    return dict(zip(outs, results))


def exchange(k, src, dst):
    copy = k.sender.send(src, dst, k.place.device(x=1))
    yield
    copy.wait_recv()


def row_sum(value):
    return jnp.sum(value.reshape(-1, 8, value.shape[-1]), axis=0)


NORM_ROWS = 128


def forward(by_hand, items, half_len, weights, small, block_input, embed, slots, cotangent, collective_id):
    rows, width = block_input.shape
    full_len = 2 * half_len
    blocks = 4
    nz = lax.axis_size("dp") // 4
    step = 256
    params = ["w_qkv", "small", "w_o", "w_in", "w_out"]

    def body(k):
        place = k.place
        cot_in = k.copy(k["cotangent"], k["cot"])
        full = {p: k["v_" + p] for p in params}
        if by_hand:
            pieces = [k["b_in"][...]]
            for name in ("biases", "gains", "shifts"):
                pieces += [k[name][t : t + 1, :] for t in range(k[name].shape[0])]
            line = jnp.concatenate([piece.astype(F32) for piece in pieces], axis=1)
            k["small"][...] = jnp.broadcast_to(line, k["small"].shape)
        kept = [k.copy(k[p], full[p].at[place.z, place.column()] if by_hand else full[p]) for p in params]
        slot = lax.broadcasted_iota(jnp.int32, (1, half_len), 1) + place.x * half_len
        codes, cols, table = k["codes"], k["cols"], k["table"]
        codes[...] = jnp.zeros_like(codes)
        table[...] = jnp.zeros_like(table)
        for i in range(items):
            valid = (slot < k["lengths"][i]) & ((k["mask"][i : i + 1, :] == 1) | (slot == 0))
            numbers = k["blocks"][i : i + 1, :].astype(F32)
            key_code = jnp.where(valid, numbers, code_absent)
            codes[i : i + 1, :] = key_code
            codes[items + i : items + i + 1, :] = numbers
            table[i : i + 1, :] = numbers
            table[items + i : items + i + 1, :] = valid.astype(F32)
            table[2 * items + i : 2 * items + i + 1, :] = key_code
        cols[...] = table[...].T
        k.save(codes, k["save_own_codes"])
        k.save(cols, k["save_own_cols"])
        meet(place)
        for made in kept:
            made.wait()
        number = {}
        if by_hand:
            for p, start, stop, late in PARTS:
                if start is None:
                    shard, whole = k[p], full[p]
                else:
                    shard = k[p].at[:, pl.ds(start, stop - start)]
                    whole = full[p].at[:, :, :, pl.ds(start, stop - start)]
                if late:
                    steps = gather_late_steps(place, k.sender, shard, whole)
                else:
                    steps = gather_steps(place, k.sender, shard, whole, nz - nz // 4)
                number.setdefault(p, []).append(k.add(steps))

        def arrive(p, *which):
            if by_hand:
                k.finish(*[number[p][i] for i in which or range(len(number[p]))])

        codes_over = k.add(exchange(k, k["codes"], k["codes_taken"]))
        cols_over = k.add(exchange(k, k["cols"], k["cols_taken"]))
        quarter = half_len // 2
        input_over = [
            k.add(exchange(k, k["input"].at[pl.ds(i * quarter, quarter)], k["taken"].at[pl.ds(i * quarter, quarter)]))
            for i in range(2 * items)
        ]
        k.point()
        stream, partial_sums = k["stream"], k["partial_sums"]
        partial_sums[...] = jnp.zeros_like(partial_sums)

        def gather_sum(kind, value):
            partial_sums[kind] += row_sum(value)

        for i in range(items):
            item_embed = k["embed"][i : i + 1, :]

            def make_stream(j, i=i, item_embed=item_embed):
                at = pl.ds(pl.multiple_of(i * half_len + j * 64, 64), 64)
                value = k["input"][at, :].astype(F32) + item_embed
                stream[at, :] = value.astype(LOW)
                gather_sum(0, value * value * k["cols"][tile(j, 64), items + i : items + i + 1])

            loop(half_len // 64, make_stream)
        save_stream = k.copy(stream.at[pl.ds(0, rows)], k["save_stream"])
        k.point()
        arrive("small")
        shards = k["v_small"].shape[0] * k["v_small"].shape[1]
        for d in range(shards):
            k["packed"][d : d + 1, :] = k["v_small"][d // 8, d % 8, 0:1, :]
        packed = k["packed"][...].astype(LOW)
        share = width // shards
        b_share = share * blocks
        vectors, b_in = k["vectors"], k["v_b_in"]
        for t in range(8):
            vectors[t : t + 1, :] = expand(packed, b_share + t * share, share, 0, width)
            if t in (0, 1, 3, 5):
                k.point()
        for t in range(blocks):
            b_in[t : t + 1, :] = expand(packed, 0, b_share, t * width, width)
            k.point()
        bias_o = vectors[2:3, :]
        gain_one, gain_two, shift_one, shift_two = (vectors[t : t + 1, :] for t in range(4, 8))
        heads = k["heads"]

        def weight(name, t, j):
            value = full[name][:, :, :, pl.ds(pl.multiple_of(t * width + j * step, step), step)]
            return value.reshape(-1, step)

        def keep(name):
            if by_hand:
                k.save(full[name], k["all_" + name])

        arrive("w_qkv")
        keep("w_qkv")
        k.point()

        def project(slot, t, bias):
            def one(j):
                at = tile(j, step)
                value = mm(stream[pl.ds(0, rows), :], weight("w_qkv", t, j))
                if bias is not None:
                    value = value + vectors[bias : bias + 1, at]
                heads[slot, :, at] = value.astype(LOW)

            loop(width // step, one, 4)

        for slot, t, bias in ((0, 0, 0), (1, 1, None), (3, 2, 1)):
            project(slot, t, bias)
            k.point()
        k.finish(codes_over)
        same = lax.broadcasted_iota(jnp.int32, (half_len, half_len), 0) == lax.broadcasted_iota(
            jnp.int32, (half_len, half_len), 1
        )
        for i in range(items):
            asked = k["cols"][:, i : i + 1]
            own = (k["codes"][i : i + 1, :] <= asked) | same
            other = k["codes_taken"][i : i + 1, :] <= asked
            k["permit"][i, :, 0:half_len] = jnp.where(own, 0.0, fill_value)
            k["permit"][i, :, half_len : 2 * half_len] = jnp.where(other, 0.0, fill_value)
        k.save(k["codes_taken"], k["save_codes"])
        k.point()
        save_stream.wait()
        lane = lax.broadcasted_iota(jnp.int32, (half_len, 2 * HD), 1)
        key_lane = lax.broadcasted_iota(jnp.int32, (2 * half_len, 2 * HD), 1)
        pairs = width // (2 * HD)
        for i in range(items):
            at_rows = pl.ds(i * half_len, half_len)
            at_theirs = pl.ds(rows + i * half_len, half_len)
            item_embed = k["embed"][i : i + 1, :]
            k.finish(input_over[2 * i], input_over[2 * i + 1])

            def make_other(j, i=i, item_embed=item_embed):
                at = pl.ds(pl.multiple_of(i * half_len + j * 64, 64), 64)
                to = pl.ds(pl.multiple_of(rows + i * half_len + j * 64, 64), 64)
                stream[to, :] = (k["taken"][at, :].astype(F32) + item_embed).astype(LOW)

            def project_other(j, at_rows=at_rows, at_theirs=at_theirs):
                at = tile(j, step)
                source = stream[at_theirs, :]
                heads[2, at_rows, at] = mm(source, weight("w_qkv", 1, j)).astype(LOW)
                heads[4, at_rows, at] = (mm(source, weight("w_qkv", 2, j)) + vectors[1:2, at]).astype(LOW)
                heads[5, at_rows, at] = (mm(source, weight("w_qkv", 0, j)) + vectors[0:1, at]).astype(LOW)

            loop(half_len // 64, make_other)
            loop(width // step, project_other, 4)
            if i == items - 1:
                save_heads = k.copy(heads, k["save_heads"])
            k.point()

            def pair(p, i=i, at_rows=at_rows):
                at = tile(p, 2 * HD)
                query = heads[0, at_rows, at] * (1.0 / math.sqrt(HD))
                keys = jnp.concatenate([heads[1, at_rows, at], heads[2, at_rows, at]], axis=0)
                values = jnp.concatenate([heads[3, at_rows, at], heads[4, at_rows, at]], axis=0)
                nothing = jnp.zeros((), LOW)
                mixed = None
                logs = k["logs"][i]
                for h in range(2):
                    scores = mm(jnp.where((lane < HD) == (h == 0), query, nothing), keys, NT) + k["permit"][i]
                    peak = jnp.max(scores, axis=1, keepdims=True)
                    expo = jnp.exp(scores - peak)
                    total = jnp.sum(expo, axis=1, keepdims=True)
                    probs = (expo * (1.0 / total)).astype(LOW)
                    part = mm(probs, jnp.where((key_lane < HD) == (h == 0), values, nothing))
                    mixed = part if mixed is None else mixed + part
                    logs = jnp.where(lane == 2 * p + h, peak + jnp.log(total), logs)
                k["logs"][i] = logs
                stream[at_rows, at] = mixed.astype(LOW)

            loop(pairs // 2, pair, 4)
            k.point()
            loop(pairs // 2, lambda p, pair=pair: pair(p + pairs // 2), 4)
            k["log_rows"][i] = k["logs"][i].T[:HEADS]
            k.add(exchange(k, k["log_rows"].at[i], k["logs_taken"].at[i]))
            k.point()
        save_mixed = k.copy(stream.at[pl.ds(0, rows)], k["save_mixed"])
        k.save(k["log_rows"], k["save_logs"])
        arrive("w_o")
        keep("w_o")
        xhat = k["xhat"]
        for i in range(items):
            at_rows = pl.ds(i * half_len, half_len)
            k["work"][...] = mm(stream[at_rows, :], full["w_o"][...].reshape(width, width)) + bias_o
            item_embed = k["embed"][i : i + 1, :]

            def first_norm(j, i=i, item_embed=item_embed):
                at = pl.ds(pl.multiple_of(i * half_len + j * NORM_ROWS, NORM_ROWS), NORM_ROWS)
                to = pl.ds(pl.multiple_of(rows + i * half_len + j * NORM_ROWS, NORM_ROWS), NORM_ROWS)
                attn = k["work"][tile(j, NORM_ROWS), :]
                gather_sum(1, attn * attn * k["cols"][tile(j, NORM_ROWS), items + i : items + i + 1])
                value, rstd = normalize(k["input"][at, :].astype(F32) + item_embed + attn)
                xhat[at, :] = value
                k["rstd"][at, :] = jnp.broadcast_to(rstd, (NORM_ROWS, 128))
                stream[to, :] = (value * gain_one + shift_one).astype(LOW)

            loop(half_len // NORM_ROWS, first_norm)
            k.point()
        save_hidden = k.copy(stream.at[pl.ds(rows, rows)], k["save_hidden"])
        k.save(xhat, k["save_xhat"])
        k.save(k["rstd"], k["save_rstd"])
        save_heads.wait()
        act, slope = heads, k["slope"]
        in_parts = {start: i for i, (start, _) in enumerate(part[1:3] for part in PARTS if part[0] == "w_in")}
        for t in range(blocks):
            if t * width in in_parts:
                arrive("w_in", in_parts[t * width])
                k.point()

            def feed(j, t=t):
                at = tile(j, step)
                w_in = weight("w_in", t, j)
                for i in range(items):
                    own = pl.ds(i * half_len, half_len)
                    pre = mm(stream[pl.ds(rows + i * half_len, half_len), :], w_in) + b_in[t : t + 1, at]
                    cdf = 0.5 + 0.5 * lax.erf(pre * (1.0 / math.sqrt(2.0)))
                    act[t, own, at] = (pre * cdf).astype(LOW)
                    pdf = jnp.exp(pre * pre * -0.5) * (1.0 / math.sqrt(2.0 * math.pi))
                    slope[t, own, at] = (cdf + pre * pdf).astype(LOW)

            loop(width // step, feed, 4)
            k.save(act.at[t], k["act"].at[t])
            k.save(slope.at[t], k["save_slope"].at[t])
            k.point()
        keep("w_in")
        cot_in.wait()
        save_mixed.wait()
        save_hidden.wait()
        back = k["back"]
        out_parts = [(start, stop) for p, start, stop, _ in PARTS if p == "w_out"] if by_hand else [(0, width)]
        for which, (start, stop) in enumerate(out_parts):
            columns = pl.ds(start, stop - start)
            arrive("w_out", which)
            for i in range(items):
                at_rows = pl.ds(i * half_len, half_len)
                total = None
                for t in range(blocks):
                    part = mm(act[t, at_rows, :], full["w_out"][t, :, :, columns].reshape(width, stop - start))
                    total = part if total is None else total + part
                back[at_rows, columns] = total + vectors[3:4, columns]
            k.point()
        keep("w_out")
        for i in range(items):
            at_rows = pl.ds(i * half_len, half_len)

            def second_norm(j, i=i):
                at = pl.ds(pl.multiple_of(i * half_len + j * NORM_ROWS, NORM_ROWS), NORM_ROWS)
                to = pl.ds(pl.multiple_of(rows + i * half_len + j * NORM_ROWS, NORM_ROWS), NORM_ROWS)
                weight_rows = k["cols"][tile(j, NORM_ROWS), items + i : items + i + 1]
                branch = back[at, :]
                gather_sum(2, branch * branch * weight_rows)
                value, rstd = normalize(xhat[at, :] * gain_one + shift_one + branch)
                result = value * gain_two + shift_two
                gather_sum(3, result * result * weight_rows)
                stream[at, :] = result.astype(LOW)
                grad = k["cot"][at, :].astype(F32)
                gather_sum(5, grad * value)
                gather_sum(6, grad)
                scaled = grad * gain_two
                passed = rstd * (
                    scaled
                    - jnp.mean(scaled, axis=-1, keepdims=True)
                    - value * jnp.mean(scaled * value, axis=-1, keepdims=True)
                )
                back[at, :] = passed
                back_low = passed.astype(LOW)
                stream[to, :] = back_low
                gather_sum(4, back_low.astype(F32))

            loop(half_len // NORM_ROWS, second_norm)
            at_other = pl.ds(rows + i * half_len, half_len)
            k.save(stream.at[at_rows], k["output"].at[at_rows])
            k.save(stream.at[at_other], k["save_back_low"].at[at_rows])
            k.save(back.at[at_rows], k["save_back"].at[at_rows])
        for kind in range(7):
            k["sums"][kind : kind + 1, :] = column_sum(partial_sums[kind])
        k["sums"][7:8, :] = jnp.zeros((1, width), F32)
        k["sums"][7:8, 0:128] = column_sum(k["cols"][...])
        k.save(vectors, k["save_vectors"])
        k.finish(*range(len(k.transfers)))
        k.save(k["logs_taken"], k["save_logs_taken"])
        k.save(k["cols_taken"], k["save_cols"])
        k.close()

    ins = dict(zip(params, [weights[0], small] + weights[1:]))
    spaces_in = ["input", "embed", "mask", "blocks"]
    lengths, mask, numbers = slots
    if by_hand:
        spaces_in += params + ["b_in", "biases", "gains", "shifts"]
        b_in, biases, gains, shifts = small
        small_wide = b_in.shape[0] + 8 * biases.shape[1]
        small_shape = (8, small_wide)
        del ins["small"]
        ins.update(b_in=b_in[None, :], biases=biases, gains=gains, shifts=shifts)
    else:
        small_shape = small.shape
    ins.update(lengths=lengths, mask=mask, blocks=numbers)
    ins.update(input=block_input, embed=embed, cotangent=cotangent)
    codes_shape, cols_shape = (8, half_len), (half_len, 128)
    outs = {}
    if by_hand:
        for p in params:
            if p != "small":
                outs["all_" + p] = ((nz, 8) + ins[p].shape, ins[p].dtype, "hbm")
    outs.update(
        save_heads=((6, rows, width), LOW, "hbm"),
        save_own_codes=(codes_shape, F32, "hbm"),
        save_own_cols=(cols_shape, F32, "hbm"),
        save_codes=(codes_shape, F32, "hbm"),
        save_cols=(cols_shape, F32, "hbm"),
        save_stream=((rows, width), LOW, "hbm"),
        save_hidden=((rows, width), LOW, "hbm"),
        save_mixed=((rows, width), LOW, "hbm"),
        save_logs=((items, HEADS, half_len), F32, "hbm"),
        save_logs_taken=((items, HEADS, half_len), F32, "hbm"),
        save_xhat=((rows, width), F32, "hbm"),
        save_rstd=((rows, 128), F32, "hbm"),
        act=((blocks, rows, width), LOW, "hbm"),
        save_slope=((blocks, rows, width), LOW, "hbm"),
        output=((rows, width), LOW, "hbm"),
        save_back_low=((rows, width), LOW, "hbm"),
        save_back=((rows, width), F32, "hbm"),
        save_vectors=((8, width), F32, "hbm"),
        sums=((8, width), F32, "vmem"),
    )
    small_full = (nz, 8) + small_shape if by_hand else small_shape
    copies = len(PARTS) * max(gather_copies(nz), 4 * nz + 4) + 3 * items + 2
    scratch = dict(
        partial_sums=pltpu.VMEM((7, 8, width), F32),
        taken=pltpu.VMEM((rows, width), LOW),
        codes=pltpu.VMEM(codes_shape, F32),
        cols=pltpu.VMEM(cols_shape, F32),
        table=pltpu.VMEM((128, half_len), F32),
        codes_taken=pltpu.VMEM(codes_shape, F32),
        cols_taken=pltpu.VMEM(cols_shape, F32),
        stream=pltpu.VMEM((2 * rows, width), LOW),
        v_w_qkv=pltpu.VMEM((4, 8, 32, 3 * width), LOW),
        v_small=pltpu.VMEM(small_full, F32),
        packed=pltpu.VMEM((small_full[0] * 8, small_full[-1]), F32),
        vectors=pltpu.VMEM((8, width), F32),
        v_b_in=pltpu.VMEM((8, width), F32),
        heads=pltpu.VMEM((6, rows, width), LOW),
        permit=pltpu.VMEM((items, half_len, full_len), F32),
        logs=pltpu.VMEM((items, half_len, 128), F32),
        log_rows=pltpu.VMEM((items, HEADS, half_len), F32),
        logs_taken=pltpu.VMEM((items, HEADS, half_len), F32),
        v_w_o=pltpu.VMEM((4, 8, 32, width), LOW),
        work=pltpu.VMEM((half_len, width), F32),
        xhat=pltpu.VMEM((rows, width), F32),
        rstd=pltpu.VMEM((rows, 128), F32),
        v_w_in=pltpu.VMEM((4, 8, 32, blocks * width), LOW),
        slope=pltpu.VMEM((blocks, rows, width), LOW),
        v_w_out=pltpu.VMEM((4, 8, 128, width), LOW),
        cot=pltpu.VMEM((rows, width), LOW),
        back=pltpu.VMEM((rows, width), F32),
    )
    if by_hand:
        scratch["small"] = pltpu.VMEM(small_shape, F32)
    return call("forward" if by_hand else "", body, ins, spaces_in, outs, scratch, copies, collective_id)


def feed_back(by_hand, items, half_len, fw, weights, collective_id):
    blocks, rows, width = fw["act"].shape
    nz = lax.axis_size("dp") // 4
    chunk_width = width // len(OUT_SPLITS)
    step = 256

    def body(k):
        place, sender = k.place, k.sender
        load_low = k.copy(k["back_low"], k["v_low"])
        load_act = [k.copy(k["act"].at[t], k["v_act"].at[t]) for t in range(blocks)]
        load_out = k.copy(k["w_out"], k["v_w"])
        load_slope = k.copy(k["slope"], k["v_slope"])
        load_hidden = k.copy(k["hidden"], k["v_left"])
        load_rest = [
            k.copy(k["back"], k["v_back"]),
            k.copy(k["xhat"], k["v_xhat"]),
            k.copy(k["rstd"], k["v_rstd"]),
            k.copy(k["w_o"], k["v_o"]),
        ]
        meet(place)
        load_low.wait()
        low, act, grad = k["v_low"], k["v_act"], k["grad"]
        halves = []
        if by_hand:
            for q, split in enumerate(OUT_SPLITS):
                buffers = {name: k[f"{name}{q}"] for name in ("core", "diag", "line", "column")}
                target = k["grad_out"].at[:, pl.ds(q * chunk_width, chunk_width)]
                if split is None:
                    steps = reduce_late_steps(place, sender, grad.at[q], buffers, target)
                else:
                    steps = reduce_steps(place, sender, grad.at[q], buffers, target, split, nz)
                halves.append(k.add(steps))
        for t in range(blocks):
            load_act[t].wait()

            def outer(j, t=t):
                part = mm(act[t, :, tile(j, step)], low[...], TN).astype(LOW)
                part = part.reshape(2, 128, width)
                y, c = j // 2, j % 2
                for q in range(len(OUT_SPLITS)):
                    grad[q, t, y, c] = part[:, :, q * chunk_width : (q + 1) * chunk_width]

            loop(width // step, outer, 4)
            for q, split in zip(halves, OUT_SPLITS):
                if split is not None or t == blocks - 1:
                    k.step(q)
        k.point()
        if not by_hand:
            for q in range(len(OUT_SPLITS)):
                k.save(grad.at[q], k["grad_out"].at[:, :, :, :, :, pl.ds(q * chunk_width, chunk_width)])
        load_out.wait()
        load_slope.wait()
        sums = k["sums"]
        sums[...] = jnp.zeros_like(sums)
        load_in = []
        for t in range(blocks):

            def pull(j, t=t):
                at = tile(j, step)
                w_out = k["v_w"][t, j].reshape(step, width)
                part = mm(low[...], w_out, NT) * k["v_slope"][t, :, at].astype(F32)
                part = part.astype(LOW)
                act[t, :, at] = part
                sums[t : t + 1, at] = column_sum(part.astype(F32))

            loop(width // step, pull, 4)
            load_in.append(k.copy(k["w_in"].at[:, :, :, pl.ds(t * width, width)], k["v_w"].at[t]))
            k.point()
        for made in load_in + load_rest:
            made.wait()
        gain = k["vectors"][4:5, :]
        partial_sums = k["partial_sums"]
        partial_sums[...] = jnp.zeros_like(partial_sums)
        over = []
        for i in range(items):
            at_rows = pl.ds(i * half_len, half_len)
            total = None
            for t in range(blocks):
                part = mm(act[t, at_rows, :], k["v_w"][t].reshape(width, width), NT)
                total = part if total is None else total + part
            k["work"][...] = total
            k.point()

            def first_back(j, i=i):
                at = pl.ds(pl.multiple_of(i * half_len + j * NORM_ROWS, NORM_ROWS), NORM_ROWS)
                hidden = k["work"][tile(j, NORM_ROWS), :] + k["v_back"][at, :]
                xhat = k["v_xhat"][at, :]
                rstd = k["v_rstd"][at, 0:1]
                partial_sums[0] += row_sum(hidden * xhat)
                partial_sums[1] += row_sum(hidden)
                scaled = hidden * gain
                value = rstd * (
                    scaled
                    - jnp.mean(scaled, axis=-1, keepdims=True)
                    - xhat * jnp.mean(scaled * xhat, axis=-1, keepdims=True)
                )
                k["v_back"][at, :] = value
                value_low = value.astype(LOW)
                low[at, :] = value_low
                partial_sums[2] += row_sum(value_low.astype(F32))

            loop(half_len // NORM_ROWS, first_back)
            k.save(k["v_back"].at[at_rows], k["input_part"].at[at_rows])
            k.save(low.at[at_rows], k["attn_grad"].at[at_rows])
            w_o = k["v_o"][...].reshape(width, width)
            mixed_grad = k["v_mixed_grad"]
            mixed_grad[at_rows, :] = mm(low[at_rows, :], w_o, NT).astype(LOW)
            k.save(mixed_grad.at[at_rows], k["mixed_grad"].at[at_rows])
            if i < EARLY:
                over.append(k.add(exchange(k, mixed_grad.at[at_rows], k["v_taken"].at[at_rows])))
                k.step(over[i])
            k.point()
        for kind in range(3):
            sums[4 + kind : 5 + kind, :] = column_sum(partial_sums[kind])
        load_hidden.wait()
        left, turned = k["v_left"], k["v_turned"]

        def turn(j):
            turned[tile(j, 128), :] = left[:, tile(j, 128)].T

        loop(width // 128, turn, 4)
        save_in = []
        for t in range(blocks):
            if t >= 2:
                save_in[t - 2].wait()

            def outer_in(j, t=t):
                at = tile(j, step)
                part = mm(turned[...], act[t, :, at]).astype(LOW)
                k["grad_in_part"][t % 2, :, :, :, :, :, at] = part.reshape(4, 2, 2, 2, 32, step)

            loop(width // step, outer_in, 4)
            save_in.append(k.copy(k["grad_in_part"].at[t % 2], k["grad_in"].at[t]))
            k.point()
        for made in save_in[2:]:
            made.wait()
        for i, number in enumerate(over):
            at_rows = pl.ds(i * half_len, half_len)
            k.finish(number)
            k.save(k["v_taken"].at[at_rows], k["mixed_grad_taken"].at[at_rows])
        k.close()

    ins = dict(
        back_low=fw["save_back_low"],
        act=fw["act"],
        w_out=weights[3].reshape(blocks, 4, 8, 32, width),
        slope=fw["save_slope"],
        w_in=weights[2],
        back=fw["save_back"],
        xhat=fw["save_xhat"],
        rstd=fw["save_rstd"],
        hidden=fw["save_hidden"],
        w_o=weights[1],
        vectors=fw["save_vectors"],
    )
    outs = dict(
        grad_in=((blocks, 4, 2, 2, 2, 32, width), LOW, "hbm"),
        input_part=((rows, width), F32, "hbm"),
        attn_grad=((rows, width), LOW, "hbm"),
        mixed_grad=((rows, width), LOW, "hbm"),
        mixed_grad_taken=((rows, width), LOW, "hbm"),
        sums=((8, width), F32, "vmem"),
    )
    if by_hand:
        outs["grad_out"] = ((128, width), F32, "vmem")
    else:
        outs["grad_out"] = ((4, 2, 2, 2, 128, width), LOW, "hbm")
    scratch = dict(
        v_low=pltpu.VMEM((rows, width), LOW),
        v_act=pltpu.VMEM((blocks, rows, width), LOW),
        v_left=pltpu.VMEM((rows, width), LOW),
        v_turned=pltpu.VMEM((width, rows), LOW),
        grad_in_part=pltpu.VMEM((2, 4, 2, 2, 2, 32, width), LOW),
        v_slope=pltpu.VMEM((blocks, rows, width), LOW),
        v_w=pltpu.VMEM((blocks, 4, 8, 32, width), LOW),
        v_back=pltpu.VMEM((rows, width), F32),
        v_xhat=pltpu.VMEM((rows, width), F32),
        v_rstd=pltpu.VMEM((rows, 128), F32),
        v_o=pltpu.VMEM((4, 8, 32, width), LOW),
        v_mixed_grad=pltpu.VMEM((rows, width), LOW),
        v_taken=pltpu.VMEM((rows, width), LOW),
        work=pltpu.VMEM((half_len, width), F32),
        grad=pltpu.VMEM((len(OUT_SPLITS), 4, 2, 2, 2, 128, chunk_width), LOW),
        partial_sums=pltpu.VMEM((3, 8, width), F32),
    )
    copies = items
    if by_hand:
        copies += len(OUT_SPLITS) * max(reduce_copies(nz), reduce_late_copies(nz))
        for q, split in enumerate(OUT_SPLITS):
            buffers = reduce_late_buffers if split is None else reduce_buffers
            for name, buffer in buffers(nz, 128, chunk_width).items():
                scratch[f"{name}{q}"] = buffer
    return call("feed_back" if by_hand else "", body, ins, ("vectors",), outs, scratch, copies, collective_id)


def attend_back(by_hand, items, half_len, fw, fb, weights, collective_id):
    blocks, rows, width = fw["act"].shape
    nz = lax.axis_size("dp") // 4
    chunks = blocks + 2
    step = 256
    scale = 1.0 / math.sqrt(HD)
    stages = 3 + (nz - 1).bit_length()

    def body(k):
        place, sender = k.place, k.sender
        load_grad = k.copy(k["mixed_grad"], k["v_grad"].at[0])
        grad = k["grad"]
        load_in = [k.copy(k["grad_in_part"].at[q], grad.at[q]) for q in range(blocks) if by_hand]
        load_mixed = [k.copy(k["mixed"], k["v_left"]), k.copy(k["attn_grad"], k["joint"].at[0])]
        load_heads = k.copy(k["heads"], k["v_heads"])
        load_qkv = [
            k.copy(k["w_qkv"].at[:, :, :, pl.ds(t * width, width)], k["v_qkv"].at[t]) for t in range(3)
        ]
        load_grad.wait()
        meet(place)
        over_grad = []
        load_taken = []
        for i in range(items):
            at_rows = pl.ds(i * half_len, half_len)
            if i < EARLY:
                load_taken.append(k.copy(k["mixed_grad_taken"].at[at_rows], k["v_grad"].at[1, at_rows]))
            else:
                over_grad.append(k.add(exchange(k, k["v_grad"].at[0, at_rows], k["v_grad"].at[1, at_rows])))
                k.step(over_grad[-1])
        going = []

        def reduce(slot, target, split):
            if by_hand:
                buffers = {name: k[f"{name}{slot}"] for name in ("core", "diag", "line", "column")}
                if split is None:
                    steps = reduce_late_steps(place, sender, grad.at[slot], buffers, target())
                else:
                    steps = reduce_steps(place, sender, grad.at[slot], buffers, target(), split, 1)
                going.append(k.add(steps))
                k.step(going[-1])
            k.point()

        for q in range(len(load_in)):
            load_in[q].wait()
            reduce(q, lambda q=q: k["grad_in"].at[:, pl.ds(q * width, width)], IN_SPLITS[q])
        left, turned, joint = k["v_left"], k["v_turned"], k["joint"]

        def turn(j):
            turned[tile(j, 128), :] = left[:, tile(j, 128)].T

        def outer(slot, right):
            def one(j):
                at = tile(j, step)
                part = mm(turned[...], right[:, at]).astype(LOW)
                grad[slot, :, :, :, :, :, at] = part.reshape(4, 2, 2, 2, 32, step)

            loop(width // step, one, 4)

        for made in load_mixed:
            made.wait()
        loop(width // 128, turn, 4)
        load_stream = k.copy(k["stream"], left)
        outer(blocks, joint.at[0])
        if not by_hand:
            k.save(grad.at[blocks], k["grad_o"])
        reduce(blocks, lambda: k["grad_o"], O_SPLIT)
        load_heads.wait()
        same = lax.broadcasted_iota(jnp.int32, (half_len, half_len), 0) == lax.broadcasted_iota(
            jnp.int32, (half_len, half_len), 1
        )
        for i in range(items):
            asked = k["codes"][items + i : items + i + 1, :]
            asked_taken = k["codes_taken"][items + i : items + i + 1, :]
            code = k["cols"][:, 2 * items + i : 2 * items + i + 1]
            code_taken = k["cols_taken"][:, 2 * items + i : 2 * items + i + 1]
            k["permit"][i, 0:half_len, :] = jnp.where((code <= asked) | same, 0.0, fill_value)
            k["permit"][i, half_len : 2 * half_len, :] = jnp.where(code_taken <= asked, 0.0, fill_value)
            k["permit_taken"][i] = jnp.where(code <= asked_taken, 0.0, fill_value)
        k.point()
        heads, grads, result = k["v_heads"], k["v_grad"], joint
        lane = lax.broadcasted_iota(jnp.int32, (half_len, 2 * HD), 1)
        key_lane = lax.broadcasted_iota(jnp.int32, (2 * half_len, 2 * HD), 1)
        nothing = jnp.zeros((), LOW)
        pairs = width // (2 * HD)

        def ours(i):
            at_rows = pl.ds(i * half_len, half_len)

            def pair(p):
                at = tile(p, 2 * HD)
                query = heads[0, at_rows, at]
                keys = jnp.concatenate([heads[1, at_rows, at], heads[2, at_rows, at]], axis=0)
                values = jnp.concatenate([heads[3, at_rows, at], heads[4, at_rows, at]], axis=0)
                grad_row = grads[0, at_rows, at]
                query_part = key_part = value_part = None
                for h in range(2):
                    mine = (lane < HD) == (h == 0)
                    key_mine = (key_lane < HD) == (h == 0)
                    query_h = jnp.where(mine, query, nothing)
                    grad_h = jnp.where(mine, grad_row, nothing)
                    keys_h = jnp.where(key_mine, keys, nothing)
                    at_head = pl.ds(2 * p + h, 1)
                    scores = mm(keys, query_h * scale, NT) + (k["permit"][i] - k["logs"][i, at_head, :])
                    probs = jnp.exp(scores)
                    prob_grad = mm(values, grad_h, NT)
                    centre = column_sum(probs * prob_grad)
                    k["centre"][i, at_head, :] = centre
                    score_grad = (probs * (prob_grad - centre)).astype(LOW)
                    parts = (
                        mm(score_grad, keys_h, TN),
                        mm(score_grad[:half_len], query_h),
                        mm(probs[:half_len].astype(LOW), grad_h),
                    )
                    if h == 0:
                        query_part, key_part, value_part = parts
                    else:
                        query_part = query_part + parts[0]
                        key_part = key_part + parts[1]
                        value_part = value_part + parts[2]
                query_low = (query_part * scale).astype(LOW)
                result[0, at_rows, at] = query_low
                k["sums"][0:1, at] += column_sum(query_low.astype(F32))
                k["parts"][0, at_rows, at] = key_part
                k["parts"][1, at_rows, at] = value_part

            loop(pairs // 2, pair, 4)
            k.point()
            loop(pairs // 2, lambda p: pair(p + pairs // 2), 4)

        def theirs(i):
            at_rows = pl.ds(i * half_len, half_len)

            def pair(p):
                at = tile(p, 2 * HD)
                query = heads[5, at_rows, at]
                keys, values = heads[1, at_rows, at], heads[3, at_rows, at]
                grad_row = grads[1, at_rows, at]
                key_part, value_part = k["parts"][0, at_rows, at], k["parts"][1, at_rows, at]
                for h in range(2):
                    mine = (lane < HD) == (h == 0)
                    query_h = jnp.where(mine, query, nothing)
                    grad_h = jnp.where(mine, grad_row, nothing)
                    at_head = pl.ds(2 * p + h, 1)
                    scores = mm(keys, query_h * scale, NT) + (
                        k["permit_taken"][i] - k["logs_taken"][i, at_head, :]
                    )
                    probs = jnp.exp(scores)
                    prob_grad = mm(values, grad_h, NT)
                    score_grad = (probs * (prob_grad - k["centre_taken"][i, at_head, :])).astype(LOW)
                    key_part = key_part + mm(score_grad, query_h)
                    value_part = value_part + mm(probs.astype(LOW), grad_h)
                result[1, at_rows, at] = (key_part * scale).astype(LOW)
                value_low = value_part.astype(LOW)
                result[2, at_rows, at] = value_low
                k["sums"][1:2, at] += column_sum(value_low.astype(F32))

            loop(pairs // 2, pair, 4)
            k.point()
            loop(pairs // 2, lambda p: pair(p + pairs // 2), 4)

        k["sums"][...] = jnp.zeros_like(k["sums"])
        over = []
        for i in range(items):
            ours(i)
            over.append(k.add(exchange(k, k["centre"].at[i], k["centre_taken"].at[i])))
            k.step(over[i])
            k.point()
        load_stream.wait()
        loop(width // 128, turn, 4)

        def outer_joint(q, slot):
            outer(slot, joint.at[q])
            if not by_hand:
                k.save(grad.at[slot], k["grad_qkv"].at[:, :, :, :, :, pl.ds(q * width, width)])
            reduce(slot, lambda: k["grad_qkv"].at[:, pl.ds(q * width, width)], QKV_SPLITS[q])

        outer_joint(0, blocks + 1)
        for i in range(items):
            k.finish(over[i], *over_grad[max(i - EARLY, 0) : i - EARLY + 1])
            if i < EARLY:
                load_taken[i].wait()
            theirs(i)
            k.point()
        levels = k["levels"]
        for s, name in enumerate(("sums_one", "sums_two")):
            levels[0, 8 * s : 8 * s + 8, :] = k[name][...]
        levels[0, 16:24, :] = k["sums"][...]
        small = k.add(sum_steps(place, sender, levels, k["levels_taken"]))
        k.step(small)
        k.finish(*going[:2])
        partners = place.partners()
        for partner in partners:
            pl.semaphore_signal(k["through"], inc=1, device_id=partner, device_id_type=MESH)
        load_part = k.copy(k["input_part"], k["parts"].at[0])
        pl.semaphore_wait(k["through"], len(partners))
        outer_joint(1, 0)
        outer_joint(2, 1)
        for made in load_qkv + [load_part]:
            made.wait()
        for i in range(items):
            at_rows = pl.ds(i * half_len, half_len)
            total = k["parts"][0, at_rows, :]
            for q in range(3):
                total = total + mm(joint[q, at_rows, :], k["v_qkv"][q].reshape(width, width), NT)
            left[at_rows, :] = total.astype(LOW)
            k.save(left.at[at_rows], k["input_grad"].at[at_rows])
            k.point()
        k.finish(*range(len(k.transfers)))
        k["totals"][...] = levels[stages]
        k.close()

    ins = dict(
        grad_in_part=fb["grad_in"],
        mixed=fw["save_mixed"],
        attn_grad=fb["attn_grad"],
        heads=fw["save_heads"],
        mixed_grad=fb["mixed_grad"],
        mixed_grad_taken=fb["mixed_grad_taken"],
        stream=fw["save_stream"],
        w_qkv=weights[0],
        input_part=fb["input_part"],
        codes=fw["save_own_codes"],
        codes_taken=fw["save_codes"],
        cols=fw["save_own_cols"],
        cols_taken=fw["save_cols"],
        logs=fw["save_logs"],
        logs_taken=fw["save_logs_taken"],
        sums_one=fw["sums"],
        sums_two=fb["sums"],
    )
    outs = dict(
        input_grad=((rows, width), LOW, "hbm"),
        totals=((24, width), F32, "vmem"),
    )
    if by_hand:
        outs["grad_in"] = ((32, blocks * width), F32, "vmem")
        outs["grad_o"] = ((32, width), F32, "vmem")
        outs["grad_qkv"] = ((32, 3 * width), F32, "vmem")
    else:
        outs["grad_o"] = ((4, 2, 2, 2, 32, width), LOW, "hbm")
        outs["grad_qkv"] = ((4, 2, 2, 2, 32, 3 * width), LOW, "hbm")
    scratch = dict(
        v_left=pltpu.VMEM((rows, width), LOW),
        v_turned=pltpu.VMEM((width, rows), LOW),
        joint=pltpu.VMEM((3, rows, width), LOW),
        v_heads=pltpu.VMEM((6, rows, width), LOW),
        v_grad=pltpu.VMEM((2, rows, width), LOW),
        v_qkv=pltpu.VMEM((3, 4, 8, 32, width), LOW),
        grad=pltpu.VMEM((chunks, 4, 2, 2, 2, 32, width), LOW),
        permit=pltpu.VMEM((items, 2 * half_len, half_len), F32),
        permit_taken=pltpu.VMEM((items, half_len, half_len), F32),
        parts=pltpu.VMEM((2, rows, width), F32),
        centre=pltpu.VMEM((items, HEADS, half_len), F32),
        centre_taken=pltpu.VMEM((items, HEADS, half_len), F32),
        sums=pltpu.VMEM((8, width), F32),
        levels=pltpu.VMEM((stages + 1, 24, width), F32),
        levels_taken=pltpu.VMEM((stages, 24, width), F32),
        through=pltpu.SemaphoreType.REGULAR,
    )
    copies = 2 * items + stages
    if by_hand:
        copies += (blocks + 4) * max(reduce_copies(nz), reduce_late_copies(nz))
        for q, split in enumerate(IN_SPLITS + (O_SPLIT, QKV_SPLITS[0])):
            buffers = reduce_late_buffers if split is None else reduce_buffers
            for name, buffer in buffers(nz, 32, width).items():
                scratch[f"{name}{q}"] = buffer
    spaces = ("codes", "codes_taken", "cols", "cols_taken", "logs", "logs_taken", "sums_one", "sums_two")
    return call("attend_back" if by_hand else "", body, ins, spaces, outs, scratch, copies, collective_id)


def hand_over(arrays, totals, items):
    width = totals.shape[1]
    count = len(arrays)

    def kernel(*refs):
        sources, total = refs[:count], refs[count]
        targets, b_in, *rest, rms = refs[count + 1 : 2 * count + 1], *refs[2 * count + 1 : 2 * count + 6]
        held, in_sem, out_sem = refs[2 * count + 6 : 3 * count + 6], refs[3 * count + 6], refs[3 * count + 7]
        loads = [pltpu.make_async_copy(s, h, in_sem.at[i]) for i, (s, h) in enumerate(zip(sources, held))]
        stores = [pltpu.make_async_copy(h, t, out_sem.at[i]) for i, (h, t) in enumerate(zip(held, targets))]
        for load in loads:
            load.start()
        me = my_index()
        group = pl.ds(pl.multiple_of((me % 8) * 128, 128), 128)
        for t in range(4):
            row = total[8 + t : 9 + t, group]
            b_in[...] = row if t == 0 else jnp.where(me // 8 == t, row, b_in[...])
        group = pl.ds(pl.multiple_of((me // 4) * 128, 128), 128)
        for to, row in enumerate((16, 17, 14, 4, 12, 5, 13, 6)):
            wide = total[row : row + 1, group]
            value = wide[:, :32]
            for q in range(1, 4):
                value = jnp.where(me % 4 == q, wide[:, 32 * q : 32 * q + 32], value)
            target, at = (rest[0], to) if to < 4 else (rest[1], to - 4) if to < 6 else (rest[2], to - 6)
            target[at : at + 1, :] = value
        tokens = jnp.sum(total[7:8, items : 2 * items], axis=1, keepdims=True)
        means = jnp.sum(total[0:4, :], axis=1, keepdims=True) / (tokens * width)
        rms[...] = jnp.broadcast_to(jnp.sqrt(means), rms.shape)
        for load, store in zip(loads, stores):
            load.wait()
            store.start()
        for store in stores:
            store.wait()

    vmem, hbm = pl.BlockSpec(memory_space=pltpu.VMEM), pl.BlockSpec(memory_space=pl.ANY)
    shape = jax.ShapeDtypeStruct
    return pl.pallas_call(
        kernel,
        out_shape=[shape(a.shape, a.dtype) for a in arrays]
        + [shape((1, 128), F32), shape((4, 32), F32), shape((2, 32), F32), shape((2, 32), F32), shape((4, 128), F32)],
        in_specs=[hbm] * count + [vmem],
        out_specs=[hbm] * count + [vmem] * 5,
        scratch_shapes=[pltpu.VMEM(a.shape, a.dtype) for a in arrays]
        + [pltpu.SemaphoreType.DMA((count,)), pltpu.SemaphoreType.DMA((count,))],
        compiler_params=pltpu.CompilerParams(vmem_limit_bytes=62 << 20),
    )(*arrays, totals)


def body(
    block_input,
    lengths,
    mask,
    blocks,
    timesteps,
    w_qkv,
    w_o,
    w_in,
    w_out,
    b_in,
    biases,
    gains,
    shifts,
    cotangent,
):
    items, half_len, width = block_input.shape
    rows = items * half_len
    f32 = jnp.float32
    n = n_devices()
    share = width // n
    b_count = b_in.shape[0]
    embed = time_embed(timesteps, width)
    by_hand = w_qkv.shape[0] == 32
    weights = [w_qkv, w_o, w_in, w_out]
    small = [b_in, biases, gains, shifts]
    if not by_hand:
        weights = [lax.all_gather(w, AXES, axis=0, tiled=True) for w in weights]
        weights = [w.reshape(4, 8, w.shape[0] // 32, w.shape[1]) for w in weights]
        small = jnp.concatenate([piece.reshape(-1) for piece in small])
        small_wide = -(-small.shape[0] // 128) * 128
        small = jnp.pad(small.astype(f32), (0, small_wide - small.shape[0]))
        small = jnp.broadcast_to(small[None, :], (8, small_wide))
        small = lax.all_gather(small, AXES, axis=0).reshape(n // 8, 8, 8, small_wide)
    fw = forward(
        by_hand,
        items,
        half_len,
        weights,
        small,
        block_input.reshape(rows, width),
        embed,
        (lengths, mask, blocks),
        cotangent.reshape(rows, width),
        1,
    )
    if by_hand:
        weights = [fw["all_" + p] for p in ("w_qkv", "w_o", "w_in", "w_out")]
    fb = feed_back(by_hand, items, half_len, fw, weights, 2)
    ab = attend_back(by_hand, items, half_len, fw, fb, weights, 3)
    if by_hand:
        grads = [ab["grad_qkv"], ab["grad_o"], ab["grad_in"], fb["grad_out"]]
        *arrays, own_b_in, own_biases, own_gains, own_shifts, rms = hand_over([fw["output"], ab["input_grad"]] + grads, ab["totals"], items)
        return (
            arrays[0].reshape(block_input.shape),
            arrays[1].reshape(block_input.shape),
            *arrays[2:],
            own_b_in.reshape(-1),
            own_biases,
            own_gains,
            own_shifts,
            rms[:, 0],
        )
    grad_in = fb["grad_in"].reshape(4, width, width).transpose(1, 0, 2)
    grads = [
            lax.psum_scatter(
                part.astype(f32).reshape(rows_of, -1), AXES, scatter_dimension=0, tiled=True
            )
            for part, rows_of in (
                (ab["grad_qkv"], width),
                (ab["grad_o"], width),
                (grad_in, width),
                (fb["grad_out"], 4 * width),
            )
        ]
    totals = ab["totals"]
    me = my_index()
    grad_b_in = lax.dynamic_slice(totals[8:12].reshape(-1), (me * b_count,), (b_count,))
    order = (16, 17, 14, 4, 12, 5, 13, 6)
    mine = lax.dynamic_slice(totals, (0, me * share), (24, share))
    mine = jnp.stack([mine[row] for row in order])
    count = jnp.sum(totals[7, items : 2 * items])
    rms = jnp.sqrt(jnp.sum(totals[:4], axis=1) / (count * width))
    return (
        fw["output"].reshape(block_input.shape),
        ab["input_grad"].reshape(block_input.shape),
        *grads,
        grad_b_in,
        mine[:4],
        mine[4:6],
        mine[6:8],
        rms,
    )


def solution(mesh):
    in_specs = (
        P("dp", "ctx", None),
        P("dp"),
        P("dp", "ctx"),
        P("dp", "ctx"),
        P("dp"),
        P(("dp", "ctx"), None),
        P(("dp", "ctx"), None),
        P(("dp", "ctx"), None),
        P(("dp", "ctx"), None),
        P(("dp", "ctx")),
        P(None, ("dp", "ctx")),
        P(None, ("dp", "ctx")),
        P(None, ("dp", "ctx")),
        P("dp", "ctx", None),
    )
    out_specs = (
        P("dp", "ctx", None),
        P("dp", "ctx", None),
        P(("dp", "ctx"), None),
        P(("dp", "ctx"), None),
        P(("dp", "ctx"), None),
        P(("dp", "ctx"), None),
        P(("dp", "ctx")),
        P(None, ("dp", "ctx")),
        P(None, ("dp", "ctx")),
        P(None, ("dp", "ctx")),
        P(),
    )
    return jax.shard_map(body, mesh=mesh, in_specs=in_specs, out_specs=out_specs, check_vma=False)
```
